32 devices in a mesh: dp: 8 (over z, core), fsdp: 4 (over y, x).
Axes of the slice: x: 2, y: 2, z: 4, core: 2. Of those that a mesh axis runs over, the one named last changes fastest.
Arguments:
- tokens: bfloat16 [16384, 1024], P(('dp', 'fsdp')), may hold values from -6 to 6
- segments: int32 [16384], P(('dp', 'fsdp')), may hold values from 0 to 127, as said below
- cotangent: bfloat16 [16384, 1024], P(('dp', 'fsdp')), may hold values from -6 to 6
- attn_w: float32 [4, 1024, 1024], P(None, 'dp', 'fsdp'), may hold values from -1.5 to 1.5
- ffn_w: float32 [2, 1024, 4096], P(None, 'dp', 'fsdp'), may hold values from -0.1875 to 0.1875
- vectors: float32 [12, 1024], P(None, ('dp', 'fsdp')), may hold values from -1.2 to 1.4
- attn_mom: float32 [4, 1024, 1024], P(None, 'dp', 'fsdp'), may hold values from -768 to 768
- ffn_mom: float32 [2, 1024, 4096], P(None, 'dp', 'fsdp'), may hold values from -896 to 896
- vec_mom: float32 [12, 1024], P(None, ('dp', 'fsdp')), may hold values from -230.4 to 230.4
- attn_ema: float32 [4, 1024, 1024], P(None, 'dp', 'fsdp'), may hold values from -1.5 to 1.5
- ffn_ema: float32 [2, 1024, 4096], P(None, 'dp', 'fsdp'), may hold values from -0.1875 to 0.1875
- vec_ema: float32 [12, 1024], P(None, ('dp', 'fsdp')), may hold values from -1.2 to 1.4
Outputs:
- layer_out: bfloat16 [16384, 1024], P(('dp', 'fsdp'))
- input_grad: float32 [16384, 1024], P(('dp', 'fsdp'))
- attn_new: float32 [4, 1024, 1024], P(None, 'dp', 'fsdp')
- ffn_new: float32 [2, 1024, 4096], P(None, 'dp', 'fsdp')
- vec_new: float32 [12, 1024], P(None, ('dp', 'fsdp'))
- attn_mom_new: float32 [4, 1024, 1024], P(None, 'dp', 'fsdp')
- ffn_mom_new: float32 [2, 1024, 4096], P(None, 'dp', 'fsdp')
- vec_mom_new: float32 [12, 1024], P(None, ('dp', 'fsdp'))
- attn_ema_new: float32 [4, 1024, 1024], P(None, 'dp', 'fsdp')
- ffn_ema_new: float32 [2, 1024, 4096], P(None, 'dp', 'fsdp')
- vec_ema_new: float32 [12, 1024], P(None, ('dp', 'fsdp'))
- out_bias_grad: float32 [1024], P(('dp', 'fsdp'))
The draws below stay inside these ranges and needn't reach their ends.
Inputs may be any that keep to these rules, and one draw needn't show every extreme that they name: `segments`: each aligned block of 512 positions holds either one item or four items of 128 positions, and the last block four; ids never fall along the positions and differ between items.
All inputs are finite; a program needn't handle non-finite values.
Results may differ from the reference program's by a relative error of at most 0.035.
Values may be sent and summed in bfloat16 or wider, within the bound.
A program may use at most 256 MiB of HBM per device.

```python
import math
from functools import partial
import jax
import jax.numpy as jnp
from jax import lax

D = 1024
FF = 4096
HEADS = 16
HDIM = 64
TILE = 512
ITERS = 5
TOKENS = 16384


def rising(count, top_ratio):
    position = jnp.arange(count, dtype=jnp.float32) / max(count - 1, 1)
    return jnp.sqrt(1.0 + (top_ratio - 1.0) * position)


def attention_law(key):
    normal_noise = jax.random.truncated_normal(key, -4.0, 4.0, (4, D, D), jnp.float32)
    factors = jnp.array([1.0, 1.0, 1.0, 12.0], jnp.float32)
    return normal_noise * factors[:, None, None] / math.sqrt(D)


def vector_law(key):
    normal_noise = jax.random.truncated_normal(key, -4.0, 4.0, (12, D), jnp.float32)
    rows_index = jnp.arange(12)[:, None]
    gain_rows = (rows_index == 3) | (rows_index == 10)
    return jnp.where(gain_rows, 1.0 + 0.1 * normal_noise, 0.3 * normal_noise)


def moment_law(key, count, sizes, columns, top_ratio):
    normal_noise = jax.random.truncated_normal(key, -4.0, 4.0, (count, D, columns), jnp.float32)
    scales = jnp.array(sizes, jnp.float32) * math.sqrt(TOKENS)
    return normal_noise * scales[:, None, None] * rising(D, top_ratio)[None, :, None] * rising(columns, top_ratio)[None, None, :]


def draw_segments(key, part):
    key = jax.random.fold_in(key, 9)
    tile_count = TOKENS // TILE
    kinds = jax.random.randint(key, (tile_count,), 0, 2).astype(jnp.int32)
    kinds = kinds.at[tile_count - 1].set(1)
    position = jnp.arange(TOKENS, dtype=jnp.int32)
    tile_of = position // TILE
    inner = position % TILE // (TILE // 4)
    return (tile_of * 4 + inner * kinds[tile_of]).astype(jnp.int32)


def draw_attn_w(key, part):
    key = jax.random.fold_in(key, 3)
    return attention_law(key)


def draw_attn_ema(key, part):
    key = jax.random.fold_in(key, 4)
    return attention_law(key)


def draw_vectors(key, part):
    key = jax.random.fold_in(key, 5)
    return vector_law(key)


def draw_vec_ema(key, part):
    key = jax.random.fold_in(key, 6)
    return vector_law(key)


def draw_attn_mom(key, part):
    key = jax.random.fold_in(key, 7)
    top_ratio = 3.0
    return moment_law(key, 4, (0.2, 0.2, 0.3, 0.03), D, top_ratio)


def draw_ffn_mom(key, part):
    key = jax.random.fold_in(key, 8)
    top_ratio = 3.0
    return moment_law(key, 2, (0.35, 0.35), FF, top_ratio)


def levels(stream_key, shape, cuts, low, top_value):
    factor_of, own = 1.0, jax.random.fold_in(stream_key, 6)
    for axis_at, shards_of in cuts:
        heights = jnp.exp(jax.random.uniform(jax.random.fold_in(own, axis_at), (shards_of,), jnp.float32, low / len(cuts), top_value / len(cuts)))
        factor_of = factor_of * jnp.repeat(heights, shape[axis_at] // shards_of).reshape([-1 if axis == axis_at else 1 for axis in range(len(shape))])
    return factor_of


def normal_values(stream_key, extent, scale, most, pieces=(), kind=jnp.bfloat16):
    level = levels(stream_key, extent, pieces, -0.22, 0.18) if pieces else 1.0
    drawn = jax.random.normal(stream_key, extent, jnp.float32) * scale * level
    return jnp.minimum(jnp.maximum(drawn, -most), most).astype(kind)


def setup_inputs(seed: int = 0) -> dict:
    arg_keys = jax.random.split(jax.random.key(seed), 13)
    return {
        "tokens": normal_values(arg_keys[0], (TOKENS, D), 1.0, 6.0, ((0, 32),)),
        "segments": draw_segments(jax.random.fold_in(arg_keys[12], 71), 0),
        "cotangent": normal_values(arg_keys[2], (TOKENS, D), 1.0, 6.0, ((0, 32),)),
        "attn_w": draw_attn_w(jax.random.fold_in(arg_keys[12], 71), 0),
        "ffn_w": normal_values(arg_keys[4], (2, D, FF), D ** -0.5, 0.1875, ((1, 8), (2, 4)), jnp.float32),
        "vectors": draw_vectors(jax.random.fold_in(arg_keys[12], 71), 0),
        "attn_mom": draw_attn_mom(jax.random.fold_in(arg_keys[12], 71), 0),
        "ffn_mom": draw_ffn_mom(jax.random.fold_in(arg_keys[12], 71), 0),
        "vec_mom": normal_values(arg_keys[8], (12, D), (0.3 * TOKENS ** 0.5), 230.4, ((1, 32),), jnp.float32),
        "attn_ema": draw_attn_ema(jax.random.fold_in(arg_keys[12], 71), 0),
        "ffn_ema": normal_values(arg_keys[10], (2, D, FF), D ** -0.5, 0.1875, ((1, 8), (2, 4)), jnp.float32),
        "vec_ema": draw_vec_ema(jax.random.fold_in(arg_keys[12], 71), 0),
    }


@jax.custom_vjp
def low(v):
    return lax.optimization_barrier(v.astype(jnp.bfloat16)).astype(jnp.float32)

@jax.custom_vjp
def low_back(v):
    return v

def low_keep(v):
    return (low(v), None)

def low_pass(kept, grad):
    return (grad,)

def back_keep(v):
    return (v, None)

def back_low(kept, grad):
    return (low(grad),)
low.defvjp(low_keep, low_pass)
low_back.defvjp(back_keep, back_low)
highest = lax.Precision.HIGHEST
score_scale = 0.125
ln_epsilon = 1e-05
norm_epsilon = 1e-06
ns_linear = 3.4445
ns_square = -4.775
ns_cubic = 2.0315
matrix_decay = 0.95
vector_decay = 0.9
average_decay = 0.7
weight_decay = 0.01
attn_rates = (1.0, 1.0, 1.0, 10.0)
vector_step = 0.3

def matmul(left, right):
    return jnp.dot(left, right, precision=highest)

def layer_norm(values, gain, shift):
    center = values - lax.optimization_barrier(jnp.mean(values, axis=-1, keepdims=True))
    spread = lax.optimization_barrier(jnp.mean(center * center, axis=-1, keepdims=True))
    return center * lax.rsqrt(spread + ln_epsilon) * gain + shift

def block_forward(weights, token_rows, labels):
    attn_low, ffn_low, vec_low = weights
    width = token_rows.shape[0]
    queries = low_back(low(matmul(token_rows, attn_low[0]) + vec_low[0]))
    keys_all = low_back(low(matmul(token_rows, attn_low[1])))
    values_all = low_back(low(matmul(token_rows, attn_low[2]) + vec_low[1]))
    tile_count = width // TILE
    tile_shape = (tile_count, TILE, HEADS, HDIM)
    scores = jnp.einsum('tqhd,tkhd->thqk', queries.reshape(tile_shape), keys_all.reshape(tile_shape), precision=highest) * score_scale
    scores = low_back(scores)
    grouped = labels.reshape(tile_count, TILE)
    allowed = grouped[:, None, :, None] == grouped[:, None, None, :]
    scores = jnp.where(allowed, scores, -1e+30)
    row_top = lax.optimization_barrier(jnp.max(scores, axis=-1, keepdims=True))
    exponent = jnp.exp(scores - row_top)
    attention = low(exponent / lax.optimization_barrier(jnp.sum(exponent, axis=-1, keepdims=True)))
    mixture = jnp.einsum('thqk,tkhd->tqhd', attention, values_all.reshape(tile_shape), precision=highest)
    mixture = low_back(low(mixture.reshape(width, D)))
    branch = low_back(matmul(mixture, attn_low[3]) + vec_low[2])
    normed = layer_norm(token_rows + branch, vec_low[3], vec_low[4])
    up_proj = low_back(matmul(low(normed), ffn_low[0]) + vec_low[5:9].reshape(-1))
    active = low(jax.nn.gelu(up_proj, approximate=False))
    down_out = low_back(matmul(active, ffn_low[1].T) + vec_low[9])
    return layer_norm(normed + down_out, vec_low[10], vec_low[11])

def layer_forward(tokens_in, attn_w, ffn_w, vectors, segments):
    weights = (low(attn_w), low(ffn_w), low(vectors))
    block_rows = 8 * TILE
    block_count = TOKENS // block_rows
    token_blocks = tokens_in.reshape(block_count, block_rows, D)
    label_blocks = segments.reshape(block_count, block_rows)

    def one_block(carry, inputs):
        return (carry, jax.checkpoint(block_forward)(weights, inputs[0], inputs[1]))
    ignored, outputs = lax.scan(one_block, jnp.zeros((), jnp.float32), (token_blocks, label_blocks))
    return outputs.reshape(TOKENS, D)

def orthogonal(moment):
    current = moment / (jnp.sqrt(jnp.sum(moment * moment)) + norm_epsilon)
    for iteration in range(ITERS):
        current_low = current.astype(jnp.bfloat16)
        gram_low = jnp.dot(current_low, current_low.T, preferred_element_type=jnp.float32).astype(jnp.bfloat16)
        first_prod = jnp.dot(gram_low, current_low, preferred_element_type=jnp.float32)
        second_prod = jnp.dot(gram_low, first_prod.astype(jnp.bfloat16), preferred_element_type=jnp.float32)
        current = ns_linear * current + ns_square * first_prod + ns_cubic * second_prod
    return current

def reference(tokens, segments, cotangent, attn_w, ffn_w, vectors, attn_mom, ffn_mom, vec_mom, attn_ema, ffn_ema, vec_ema):
    tokens_in = tokens.astype(jnp.float32)
    layer_out, pullback = jax.vjp(partial(layer_forward, segments=segments), tokens_in, attn_w, ffn_w, vectors)
    input_grad, attn_grad, ffn_grad, vec_grad = pullback(cotangent.astype(jnp.float32))
    attn_mom_new = matrix_decay * attn_mom + attn_grad
    ffn_mom_new = matrix_decay * ffn_mom + ffn_grad
    attn_list = []
    for index in range(4):
        rate = attn_rates[index]
        attn_list.append(attn_w[index] * (1.0 - weight_decay * rate) - rate * orthogonal(attn_mom_new[index]))
    attn_new = jnp.stack(attn_list)
    shape_factor = math.sqrt(FF / D)
    ffn_list = []
    for index in range(2):
        ffn_list.append(ffn_w[index] * (1.0 - weight_decay) - shape_factor * orthogonal(ffn_mom_new[index]))
    ffn_new = jnp.stack(ffn_list)
    vec_mom_new = vector_decay * vec_mom + vec_grad
    vec_new = vectors - vector_step / math.sqrt(TOKENS) * vec_mom_new
    attn_ema_new = average_decay * attn_ema + (1.0 - average_decay) * attn_new
    ffn_ema_new = average_decay * ffn_ema + (1.0 - average_decay) * ffn_new
    vec_ema_new = average_decay * vec_ema + (1.0 - average_decay) * vec_new
    return (layer_out.astype(jnp.bfloat16), input_grad, attn_new, ffn_new, vec_new, attn_mom_new, ffn_mom_new, vec_mom_new, attn_ema_new, ffn_ema_new, vec_ema_new, vec_grad[2])
```

```python
import functools
import math

import jax
import jax.numpy as jnp
from jax import lax
from jax.experimental import pallas as pl
from jax.experimental.pallas import tpu as pltpu
from jax.sharding import PartitionSpec as P

D = 1024
FF = 4096
HEADS = 16
HDIM = 64
TILE = 512
ITERS = 5


score_scale = 0.125
ln_epsilon = 1e-05
norm_epsilon = 1e-06
ns_linear = 3.4445
ns_square = -4.775
ns_cubic = 2.0315
matrix_decay = 0.95
vector_decay = 0.9
average_decay = 0.7
weight_decay = 0.01
attn_rates = (1.0, 1.0, 1.0, 10.0)
vector_step = 0.3


def product(left, right):
    return jnp.dot(left, right, preferred_element_type=jnp.float32)


def contract_rows(left, right):
    return lax.dot_general(
        left, right, (((0,), (0,)), ((), ())), preferred_element_type=jnp.float32
    )


def contract_cols(left, right):
    return lax.dot_general(
        left, right, (((1,), (1,)), ((), ())), preferred_element_type=jnp.float32
    )


MESH = pl.DeviceIdType.MESH
ROLES = 8
STEP_ROWS = 512
NORM_ROWS = 128


def greet(partners):
    barrier = pltpu.get_barrier_semaphore()
    for partner in partners:
        pl.semaphore_signal(barrier, inc=1, device_id=partner, device_id_type=MESH)
    pl.semaphore_wait(barrier, len(partners))


def place(ndp, nf):
    dp, fs = lax.axis_index("dp"), lax.axis_index("fsdp")
    side = math.isqrt(nf)
    return lax.div(dp, 2), lax.rem(dp, 2), lax.div(fs, side), lax.rem(fs, side), ndp // 2, side


def line_partners(ndp, nf):
    z, core, y, x, nz, side = place(ndp, nf)
    mine = y * side + x
    return (
        [(z * 2 + 1 - core, mine)]
        + [(lax.rem(z + step, nz) * 2 + core, mine) for step in range(1, nz)]
        + [(z * 2 + core, y * side + lax.rem(x + step, side)) for step in range(1, side)]
        + [(z * 2 + core, lax.rem(y + step, side) * side + x) for step in range(1, side)]
    )


def remote(source, target, send_sem, recv_sem, device):
    return pltpu.make_async_remote_copy(
        src_ref=source,
        dst_ref=target,
        send_sem=send_sem,
        recv_sem=recv_sem,
        device_id=device,
        device_id_type=MESH,
    )


def loop(count, body, start=0):
    def step(index, carry):
        body(index)
        return carry

    lax.fori_loop(start, count, step, 0)


def gather_kernel(ndp, nf, chunks, *refs):
    shards, wholes = refs[:chunks], refs[chunks : 2 * chunks]
    own_sem, own_recv, pair_recv, z_send, first_send, second_send, pair_send = refs[2 * chunks :]
    z, core, y, x, nz, side = place(ndp, nf)
    dp, fs = z * 2 + core, y * side + x
    greet(line_partners(ndp, nf))

    def slot(chunk, plane_at, z_at):
        return wholes[chunk].at[plane_at, z_at * 2 + core]

    def source(chunk, plane_at, z_at, own):
        return shards[chunk] if own else slot(chunk, plane_at, z_at)

    def along(first, step):
        x_at = jnp.where(first, lax.rem(x + step, side), x)
        y_at = jnp.where(first, y, lax.rem(y + step, side))
        return y_at * side + x_at

    def first_copy(chunk, z_at, step, own):
        peer = along(lax.rem(z_at, 2) == 0, step)
        return remote(
            source(chunk, fs, z_at, own),
            slot(chunk, fs, z_at),
            first_send.at[chunk, z_at, step - 1],
            own_recv.at[chunk, fs, z_at],
            (dp, peer),
        )

    def second_copy(chunk, plane_at, z_at, step, own, line):
        peer = along(lax.rem(z_at, 2) != 0, step)
        return remote(
            source(chunk, plane_at, z_at, own),
            slot(chunk, plane_at, z_at),
            second_send.at[chunk, z_at, line, step - 1],
            own_recv.at[chunk, plane_at, z_at],
            (dp, peer),
        )

    def pair_copy(chunk, plane_at, z_at, own):
        return remote(
            source(chunk, plane_at, z_at, own),
            slot(chunk, plane_at, z_at),
            pair_send.at[chunk, plane_at, z_at],
            pair_recv.at[chunk, plane_at, z_at],
            (z * 2 + 1 - core, fs),
        )

    def z_copy(chunk, step):
        return remote(
            shards[chunk],
            slot(chunk, fs, z),
            z_send.at[chunk, step - 1],
            own_recv.at[chunk, fs, z],
            (lax.rem(z + step, nz) * 2 + core, fs),
        )

    def arrived(chunk, plane_at, z_at):
        here = slot(chunk, plane_at, z_at)
        remote(here, here, own_sem.at[chunk], own_recv.at[chunk, plane_at, z_at], (dp, fs)).wait_recv()

    def pass_on(chunk, z_at, own):
        for step in range(1, side):
            first_copy(chunk, z_at, step, own).start()
            second_copy(chunk, fs, z_at, step, own, 0).start()
        pair_copy(chunk, fs, z_at, own).start()

    def own_copy(chunk):
        return pltpu.make_async_copy(shards[chunk], slot(chunk, fs, z), own_sem.at[chunk])

    for chunk in range(chunks):
        for step in range(1, nz):
            z_copy(chunk, step).start()
        pass_on(chunk, z, True)
        own_copy(chunk).start(priority=1)

    def from_z(chunk):
        def each(step):
            z_at = lax.rem(z + step, nz)
            arrived(chunk, fs, z_at)
            pass_on(chunk, z_at, False)

        loop(nz, each, 1)

    def from_first(chunk):
        def each(hop):
            z_at = lax.rem(z + hop, nz)
            for line in range(1, side):
                plane_at = along(lax.rem(z_at, 2) == 0, line)
                arrived(chunk, plane_at, z_at)
                for step in range(1, side):
                    second_copy(chunk, plane_at, z_at, step, False, line).start()
                pair_copy(chunk, plane_at, z_at, False).start()

        loop(nz, each)

    def last_places(z_at):
        x_first = lax.rem(z_at, 2) == 0
        for line in range(side):
            for step in range(1, side):
                near_x, far_y = lax.rem(x + line, side), lax.rem(y + step, side)
                far_x, near_y = lax.rem(x + step, side), lax.rem(y + line, side)
                yield jnp.where(x_first, far_y * side + near_x, near_y * side + far_x)

    def from_second(chunk):
        def each(hop):
            z_at = lax.rem(z + hop, nz)
            for plane_at in last_places(z_at):
                arrived(chunk, plane_at, z_at)
                pair_copy(chunk, plane_at, z_at, False).start()

        loop(nz, each)

    stages = (from_z, from_first, from_second)
    for turn in range(chunks + 2):
        for stage in range(3):
            if 0 <= turn - stage < chunks:
                stages[stage](turn - stage)

    for chunk in range(chunks):
        own_copy(chunk).wait()
        for step in range(1, nz):
            z_copy(chunk, step).wait_send()

        def finish(z_at):
            for step in range(1, side):
                first_copy(chunk, z_at, step, False).wait_send()
                for line in range(side):
                    second_copy(chunk, fs, z_at, step, False, line).wait_send()

            def each(plane_at):
                pair_copy(chunk, plane_at, z_at, False).wait_send()
                there = wholes[chunk].at[plane_at, z_at * 2 + 1 - core]
                remote(
                    there, there, own_sem.at[chunk], pair_recv.at[chunk, plane_at, z_at], (dp, fs)
                ).wait_recv()

            loop(nf, each)

        loop(nz, finish)


def gather_all(ndp, nf, shards):
    nz, side, chunks = ndp // 2, math.isqrt(nf), len(shards)
    dma = pltpu.SemaphoreType.DMA
    return pl.pallas_call(
        functools.partial(gather_kernel, ndp, nf, chunks),
        name="gather_weights",
        out_shape=[jax.ShapeDtypeStruct((nf, ndp) + part.shape, part.dtype) for part in shards],
        in_specs=[pl.BlockSpec(memory_space=pl.ANY)] * chunks,
        out_specs=[pl.BlockSpec(memory_space=pl.ANY)] * chunks,
        scratch_shapes=[
            dma((chunks,)),
            dma((chunks, nf, nz)),
            dma((chunks, nf, nz)),
            dma((chunks, nz - 1)),
            dma((chunks, nz, side - 1)),
            dma((chunks, nz, side, side - 1)),
            dma((chunks, nf, nz)),
        ],
        compiler_params=pltpu.CompilerParams(collective_id=2, has_side_effects=True),
    )(*shards)


def ortho_kernel(
    ndp,
    nf,
    attn_ref,
    ffn_ref,
    attn_out,
    ffn_out,
    land_attn,
    land_ffn,
    iter_low,
    iter_full,
    gram,
    gram_send,
    gram_recv,
    off_low,
    poly_low,
    diag_row,
    diag_col,
    own_low,
    own_full,
    own_attn,
    own_ffn,
    own_sem,
    piece_send,
    piece_recv,
    first_send,
    second_send,
    plane_recv,
    gram_send_sem,
    gram_recv_sem,
    back_send,
    back_recv,
):
    z, core, y, x, nz, side = place(ndp, nf)
    dp, fs = z * 2 + core, y * side + x
    rows = attn_ref.shape[1]
    size = rows * ndp
    is_attn = jnp.logical_or(dp < 2, jnp.logical_and(dp >= 6, dp < ROLES))
    is_ffn = jnp.logical_and(dp >= 2, dp < 6)
    partner = z * 2 + 1 - core

    greet(
        [(lax.rem(dp + step, ndp), fs) for step in range(1, ndp)]
        + [(dp, y * side + lax.rem(x + step, side)) for step in range(1, side)]
        + [(dp, lax.rem(y + step, side) * side + x) for step in range(1, side)]
    )

    def piece(role):
        if role < 2 or role >= 6:
            return attn_ref.at[role if role < 2 else role - 4], land_attn
        return ffn_ref.at[(role - 2) // 2, (role - 2) % 2], land_ffn

    def piece_copy(role):
        source, land = piece(role)
        return remote(source, land.at[fs, dp], piece_send.at[role], piece_recv.at[dp], (role, fs))

    for role in (2, 4, 3, 5, 0, 6, 1, 7):
        @pl.when(dp != role)
        def _(role=role):
            piece_copy(role).start()

        @pl.when(dp == role)
        def _(role=role):
            source, land = piece(role)
            pltpu.make_async_copy(source, land.at[fs, dp], own_sem).start()

    def along(first, step):
        x_at = jnp.where(first, lax.rem(x + step, side), x)
        y_at = jnp.where(first, y, lax.rem(y + step, side))
        return y_at * side + x_at

    def iterate(land, source, own_out, target, role, paired):
        width = land.shape[-1]
        columns = width * nf
        tall = min(STEP_ROWS, size)
        steps = size // tall
        wide = min(1024, columns)

        def row_of(index):
            return lax.rem(z + index // 2, nz) * 2 + lax.rem(core + index, 2)

        def x_first(row):
            return lax.rem(row // 2, 2) == 0

        def first_copy(row, step):
            here = land.at[fs, row]
            peer = along(x_first(row), step)
            return remote(here, here, first_send.at[row, step - 1], plane_recv.at[fs, row], (dp, peer))

        def second_copy(plane_at, row, line, step):
            here = land.at[plane_at, row]
            peer = along(jnp.logical_not(x_first(row)), step)
            return remote(
                here, here, second_send.at[row, line, step - 1], plane_recv.at[plane_at, row], (dp, peer)
            )

        def arrived(plane_at, row):
            here = land.at[plane_at, row]
            remote(here, here, own_sem, plane_recv.at[plane_at, row], (dp, fs)).wait_recv()

        def take_piece(index):
            row = row_of(index)

            @pl.when(index == 0)
            def _():
                pltpu.make_async_copy(source, land.at[fs, row], own_sem).wait()

            @pl.when(index > 0)
            def _():
                remote(source, land.at[fs, row], own_sem, piece_recv.at[row], (dp, fs)).wait_recv()

            for step in range(1, side):
                first_copy(row, step).start()
                second_copy(fs, row, 0, step).start()

        loop(ndp, take_piece)

        def pass_on(index):
            row = row_of(index)
            for line in range(1, side):
                plane_at = along(x_first(row), line)
                arrived(plane_at, row)
                for step in range(1, side):
                    second_copy(plane_at, row, line, step).start()

        def add_gram(plane_at, fresh):
            block = land[plane_at].reshape(size, width)
            for step in range(steps):
                at = slice(step * tall, (step + 1) * tall)
                part = contract_cols(block[at], block)
                if fresh:
                    gram[at] = part
                else:
                    gram[at] += part

        add_gram(fs, True)
        loop(ndp, pass_on)

        for line in range(side):
            for step in range(1, side):

                def last(index, line=line, step=step):
                    row = row_of(index)
                    near = jnp.where(
                        x_first(row),
                        lax.rem(y + step, side) * side + lax.rem(x + line, side),
                        lax.rem(y + line, side) * side + lax.rem(x + step, side),
                    )
                    arrived(near, row)

                loop(ndp, last)
            if line == 0:
                for step in range(1, side):
                    add_gram(along(True, step), False)
                    add_gram(along(False, step), False)
        for far_y in range(1, side):
            for far_x in range(1, side):
                add_gram(lax.rem(y + far_y, side) * side + lax.rem(x + far_x, side), False)

        def gram_copy(slot, step):
            at = pl.ds(step * tall, tall)
            return remote(
                gram_send.at[slot, at],
                gram_recv.at[slot, at],
                gram_send_sem.at[slot, step],
                gram_recv_sem.at[slot, step],
                (partner, fs),
            )

        if paired:
            for step in range(steps):
                at = slice(step * tall, (step + 1) * tall)
                gram_send[0, at] = gram[at].astype(jnp.bfloat16)
                gram_copy(0, step).start()
        for index in range(nf):
            block = land[index].reshape(size, width)
            at = slice(index * width, (index + 1) * width)
            iter_low[0, :, at] = block
            iter_full[:, at] = block.astype(jnp.float32)

        def on_diagonal(step):
            row = lax.broadcasted_iota(jnp.int32, (tall, size), 0) + step * tall
            return row == lax.broadcasted_iota(jnp.int32, (tall, size), 1)

        def back_copy(row):
            return remote(own_out.at[row], target, back_send.at[row], back_recv.at[role], (row, fs))

        def iteration(count):
            now = lax.rem(count, 2)
            later = 1 - now

            @pl.when(count > 0)
            def _():
                def gram_rows(step):
                    at = pl.ds(pl.multiple_of(step * tall, tall), tall)
                    part = contract_cols(iter_low[now, at, :columns], iter_low[now, :, :columns])
                    if paired:
                        gram_send[now, at] = part.astype(jnp.bfloat16)
                        gram_copy(now, step).start()
                    else:
                        gram[at] = part

                loop(steps, gram_rows)

            diag_row[...] = jnp.zeros_like(diag_row)

            def gather_rows(step):
                at = pl.ds(pl.multiple_of(step * tall, tall), tall)
                if paired:
                    gram_copy(now, step).wait()
                    total = gram_send[now, at].astype(jnp.float32) + gram_recv[now, at].astype(jnp.float32)
                    gram[at] = total
                else:
                    total = gram[at]
                masked = jnp.where(on_diagonal(step), total, 0.0)
                diag_col[at] = jnp.sum(masked, axis=1, keepdims=True)
                diag_row[...] += jnp.sum(masked, axis=0, keepdims=True)

            loop(steps, gather_rows)
            norm = jnp.sqrt(jnp.sum(diag_row[...], axis=1, keepdims=True)) + norm_epsilon
            inverse = jnp.where(count == 0, 1.0 / norm, 1.0)
            square = inverse * inverse

            def scale_rows(step):
                at = pl.ds(pl.multiple_of(step * tall, tall), tall)
                scaled = jnp.where(on_diagonal(step), 0.0, gram[at] * square)
                gram[at] = scaled
                off_low[at] = scaled.astype(jnp.bfloat16)

            loop(steps, scale_rows)

            def poly_rows(step):
                at = pl.ds(pl.multiple_of(step * tall, tall), tall)
                again = product(off_low[at], off_low[...])
                mine = diag_col[at] * square
                both = mine + diag_row[...] * square
                off = gram[at]
                here = on_diagonal(step)
                again_diag = jnp.sum(jnp.where(here, again, 0.0), axis=1, keepdims=True)
                poly = ns_square * off + ns_cubic * (both * off + again)
                poly_low[at] = jnp.where(here, 0.0, poly).astype(jnp.bfloat16)
                factor = ns_linear + ns_square * mine + ns_cubic * (mine * mine + again_diag)

                @pl.when(count < ITERS - 1)
                def _():
                    for left in range(0, columns, wide):
                        part = slice(left, left + wide)
                        moved = product(poly_low[at], iter_low[now, :, part])
                        fresh = inverse * (factor * iter_full[at, part] + moved)
                        iter_full[at, part] = fresh
                        iter_low[later, at, part] = fresh.astype(jnp.bfloat16)

                @pl.when(count == ITERS - 1)
                def _():
                    for index in range(nf):
                        @pl.when(fs == index)
                        def _(index=index):
                            part = slice(index * width, (index + 1) * width)
                            own_full[at, :width] = iter_full[at, part]

                            @pl.when(step == 0)
                            def _():
                                own_low[:, :width] = iter_low[now, :, part]

                    moved = product(poly_low[at], own_low[:, :width])
                    fresh = inverse * (factor * own_full[at, :width] + moved)
                    blocks = tall // rows
                    own_out[pl.ds(step * blocks, blocks)] = fresh.astype(jnp.bfloat16).reshape(
                        blocks, rows, width
                    )

                    def give(index):
                        row = step * blocks + index

                        @pl.when(row != dp)
                        def _():
                            back_copy(row).start()

                        @pl.when(row == dp)
                        def _():
                            pltpu.make_async_copy(own_out.at[row], target, own_sem).start()

                    loop(blocks, give)

            loop(steps, poly_rows)

        loop(ITERS, iteration)

        def finish(row):
            for step in range(1, side):
                first_copy(row, step).wait_send()
                for line in range(side):
                    second_copy(fs, row, line, step).wait_send()

            @pl.when(row != dp)
            def _():
                back_copy(row).wait_send()

        loop(ndp, finish)
        pltpu.make_async_copy(own_out.at[dp], target, own_sem).wait()

    @pl.when(is_attn)
    def _():
        at = jnp.where(dp < 2, dp, dp - 4)
        iterate(land_attn, attn_ref.at[at], own_attn, attn_out.at[at], dp, False)

    @pl.when(is_ffn)
    def _():
        matrix, half = (dp - 2) // 2, lax.rem(dp - 2, 2)
        iterate(land_ffn, ffn_ref.at[matrix, half], own_ffn, ffn_out.at[matrix, half], dp, True)

    for role in range(ROLES):
        @pl.when(dp != role)
        def _(role=role):
            if role < 2 or role >= 6:
                target = attn_out.at[role if role < 2 else role - 4]
            else:
                target = ffn_out.at[(role - 2) // 2, (role - 2) % 2]
            piece_copy(role).wait_send()
            remote(target, target, own_sem, back_recv.at[role], (role, fs)).wait_recv()


def orthogonalize(ndp, nf, attn_low, ffn_low):
    rows, width_attn = attn_low.shape[1:]
    width_ffn = ffn_low.shape[3]
    side = math.isqrt(nf)
    size = rows * ndp
    columns = width_ffn * nf
    tall = min(STEP_ROWS, size)
    bf16, f32 = jnp.bfloat16, jnp.float32
    dma = pltpu.SemaphoreType.DMA
    return pl.pallas_call(
        functools.partial(ortho_kernel, ndp, nf),
        name="newton_schulz",
        out_shape=[
            jax.ShapeDtypeStruct(attn_low.shape, bf16),
            jax.ShapeDtypeStruct(ffn_low.shape, bf16),
        ],
        in_specs=[pl.BlockSpec(memory_space=pltpu.VMEM)] * 2,
        out_specs=[pl.BlockSpec(memory_space=pltpu.VMEM)] * 2,
        scratch_shapes=[
            pltpu.VMEM((nf, ndp, rows, width_attn), bf16),
            pltpu.VMEM((nf, ndp, rows, width_ffn), bf16),
            pltpu.VMEM((2, size, columns), bf16),
            pltpu.VMEM((size, columns), f32),
            pltpu.VMEM((size, size), f32),
            pltpu.VMEM((2, size, size), bf16),
            pltpu.VMEM((2, size, size), bf16),
            pltpu.VMEM((size, size), bf16),
            pltpu.VMEM((size, size), bf16),
            pltpu.VMEM((1, size), f32),
            pltpu.VMEM((size, 1), f32),
            pltpu.VMEM((size, width_ffn), bf16),
            pltpu.VMEM((size, width_ffn), f32),
            pltpu.VMEM((ndp, rows, width_attn), bf16),
            pltpu.VMEM((ndp, rows, width_ffn), bf16),
            dma,
            dma((ROLES,)),
            dma((ndp,)),
            dma((ndp, side - 1)),
            dma((ndp, side, side - 1)),
            dma((nf, ndp)),
            dma((2, size // tall)),
            dma((2, size // tall)),
            dma((ndp,)),
            dma((ROLES,)),
        ],
        compiler_params=pltpu.CompilerParams(
            collective_id=1, has_side_effects=True, vmem_limit_bytes=60 * 1024 * 1024
        ),
    )(attn_low, ffn_low)


def update_kernel(
    attn_w,
    ffn_w,
    vectors,
    attn_mom,
    ffn_mom,
    vec_mom,
    attn_ema,
    ffn_ema,
    vec_ema,
    attn_grad,
    up_grad,
    down_grad,
    vec_grad,
    attn_ortho,
    ffn_ortho,
    attn_new,
    ffn_new,
    vec_new,
    attn_mom_new,
    ffn_mom_new,
    vec_mom_new,
    attn_ema_new,
    ffn_ema_new,
    vec_ema_new,
    *,
    vector_rate,
):
    for index in range(4):
        rate = attn_rates[index]
        attn_mom_new[index] = matrix_decay * attn_mom[index] + attn_grad[index]
        new = attn_w[index] * (1.0 - weight_decay * rate) - rate * attn_ortho[index].astype(jnp.float32)
        attn_new[index] = new
        attn_ema_new[index] = average_decay * attn_ema[index] + (1.0 - average_decay) * new
    width = ffn_ortho.shape[-1]
    shape_factor = math.sqrt(FF / D)
    for index, grad in enumerate((up_grad, down_grad)):
        ffn_mom_new[index] = matrix_decay * ffn_mom[index] + grad[...]
        for half in range(2):
            at = slice(half * width, (half + 1) * width)
            ortho = ffn_ortho[index, half].astype(jnp.float32)
            new = ffn_w[index, :, at] * (1.0 - weight_decay) - shape_factor * ortho
            ffn_new[index, :, at] = new
            ffn_ema_new[index, :, at] = average_decay * ffn_ema[index, :, at] + (1.0 - average_decay) * new
    mom = vector_decay * vec_mom[...] + vec_grad[...]
    vec_mom_new[...] = mom
    new = vectors[...] - vector_rate * mom
    vec_new[...] = new
    vec_ema_new[...] = average_decay * vec_ema[...] + (1.0 - average_decay) * new


def update_all(vector_rate, *operands):
    states = operands[:9]
    return pl.pallas_call(
        functools.partial(update_kernel, vector_rate=vector_rate),
        name="update",
        out_shape=[jax.ShapeDtypeStruct(states[index % 3].shape, jnp.float32) for index in range(9)],
        in_specs=[pl.BlockSpec(memory_space=pltpu.VMEM)] * len(operands),
        out_specs=[pl.BlockSpec(memory_space=pltpu.VMEM)] * 9,
        compiler_params=pltpu.CompilerParams(vmem_limit_bytes=60 * 1024 * 1024),
    )(*operands)


ROOM = pltpu.CompilerParams(vmem_limit_bytes=56 * 1024 * 1024)
ROOT_HALF = math.sqrt(0.5)
BELL = 1.0 / math.sqrt(2.0 * math.pi)


def flat(block):
    return block.reshape(-1, block.shape[-1])


def head_lanes(values, head):
    if values.shape[1] == HDIM:
        return values
    lane = lax.broadcasted_iota(jnp.int32, values.shape, 1)
    return jnp.where(lax.div(lane, HDIM) == head, values, jnp.zeros_like(values))


def normalize(values):
    center = values - jnp.mean(values, axis=1, keepdims=True)
    inverse = lax.rsqrt(jnp.mean(center * center, axis=1, keepdims=True) + ln_epsilon)
    return center * inverse, inverse


def normalize_back(grad, scaled, inverse):
    return inverse * (
        grad
        - jnp.mean(grad, axis=1, keepdims=True)
        - scaled * jnp.mean(grad * scaled, axis=1, keepdims=True)
    )


def row_sum(values):
    return jnp.sum(values.astype(jnp.float32), axis=0, keepdims=True)


def attend_kernel(
    tokens_ref,
    label_col,
    label_row,
    query_w,
    key_w,
    value_w,
    out_w,
    bias_q,
    bias_v,
    bias_o,
    blocks_out,
    mixture_out,
    total_out,
    scaled_out,
    inverse_out,
    branch,
    parts,
):
    step = pl.program_id(0)
    tokens = tokens_ref[...]
    width = query_w.shape[-1]
    heads = width // HDIM
    queries = (product(tokens, flat(query_w[...])) + bias_q[0]).astype(jnp.bfloat16)
    keys_all = product(tokens, flat(key_w[...])).astype(jnp.bfloat16)
    values_all = (product(tokens, flat(value_w[...])) + bias_v[0]).astype(jnp.bfloat16)
    blocks_out[0, 0] = queries
    blocks_out[0, 1] = keys_all
    blocks_out[0, 2] = values_all
    allowed = label_col[...] == label_row[...]
    count = tokens.shape[0]
    lane = lax.broadcasted_iota(jnp.int32, (count, 128), 1)
    totals = jnp.zeros((count, 128), jnp.float32)
    mixture = jnp.zeros((count, width), jnp.float32)
    for head in range(heads):
        scores = contract_cols(head_lanes(queries, head) * score_scale, keys_all)
        scores = jnp.where(allowed, scores, -1e30)
        top = jnp.max(scores, axis=1, keepdims=True)
        exponent = jnp.exp(scores - top)
        total = jnp.sum(exponent, axis=1, keepdims=True)
        attention = (exponent * (1.0 / total)).astype(jnp.bfloat16)
        totals = jnp.where(lane == head, top + jnp.log(total), totals)
        mixture += product(attention, head_lanes(values_all, head))
    mixture = mixture.astype(jnp.bfloat16)
    parts[step] = mixture
    total_out[0] = jnp.transpose(totals)[:8]
    for index in range(out_w.shape[0]):
        side = slice(index * width, (index + 1) * width)
        moved = product(mixture, flat(out_w[index]))

        @pl.when(step == 0)
        def _():
            branch[:, side] = moved

        @pl.when(step > 0)
        def _():
            branch[:, side] += moved

    @pl.when(step == pl.num_programs(0) - 1)
    def _():
        scaled, inverse = normalize(tokens.astype(jnp.float32) + branch[...] + bias_o[...])
        scaled_out[...] = scaled
        inverse_out[...] = inverse
        for index in range(parts.shape[0]):
            mixture_out[:, index * width : (index + 1) * width] = parts[index]


def whole_spec(shape):
    return pl.BlockSpec(shape, lambda *at: (0,) * len(shape))


def attend(tokens, segments, attn_all, vectors):
    nf, ndp, _, width = attn_all.shape
    rows = D // ndp
    count = tokens.shape[0]
    bf16, f32 = jnp.bfloat16, jnp.float32

    def column(matrix):
        return pl.BlockSpec((1, ndp, rows, width), lambda at: (at, 0, matrix, 0))

    bias = pl.BlockSpec((1, 1, width), lambda at: (at, 0, 0))
    return pl.pallas_call(
        attend_kernel,
        name="attention",
        grid=(nf,),
        in_specs=[
            whole_spec((count, D)),
            whole_spec((count, 1)),
            whole_spec((1, count)),
            column(0),
            column(1),
            column(2),
            pl.BlockSpec((nf, ndp // nf, rows, width), lambda at: (0, at, 3, 0)),
            bias,
            bias,
            whole_spec((1, D)),
        ],
        out_specs=[
            pl.BlockSpec((1, 3, count, width), lambda at: (at, 0, 0, 0)),
            whole_spec((count, D)),
            pl.BlockSpec((1, 8, count), lambda at: (at, 0, 0)),
            whole_spec((count, D)),
            whole_spec((count, 1)),
        ],
        out_shape=[
            jax.ShapeDtypeStruct((nf, 3, count, width), bf16),
            jax.ShapeDtypeStruct((count, D), bf16),
            jax.ShapeDtypeStruct((nf, 8, count), f32),
            jax.ShapeDtypeStruct((count, D), f32),
            jax.ShapeDtypeStruct((count, 1), f32),
        ],
        scratch_shapes=[pltpu.VMEM((count, D), f32), pltpu.VMEM((nf, count, width), bf16)],
        compiler_params=ROOM,
    )(
        tokens,
        segments[:, None],
        segments[None, :],
        attn_all,
        attn_all,
        attn_all,
        attn_all,
        vectors[0].reshape(nf, 1, width),
        vectors[1].reshape(nf, 1, width),
        vectors[2:3],
    )


def feed_kernel(
    scaled_ref,
    gains,
    up_w,
    down_w,
    bias_up,
    cotangent_ref,
    low_out,
    active_out,
    slope_out,
    layer_out,
    d_second_out,
    sums_out,
    total,
):
    step = pl.program_id(0)

    @pl.when(step == 0)
    def _():
        normed = scaled_ref[...] * gains[0:1] + gains[1:2]
        low_out[...] = normed.astype(jnp.bfloat16)
        total[...] = normed + gains[2:3]

    up_proj = product(low_out[...], flat(up_w[...])) + bias_up[...]
    half = 0.5 * (1.0 + lax.erf(up_proj * ROOT_HALF))
    active = (up_proj * half).astype(jnp.bfloat16)
    slope = half + up_proj * (BELL * jnp.exp(-0.5 * up_proj * up_proj))
    active_out[...] = active
    slope_out[...] = slope.astype(jnp.bfloat16)
    total[...] += contract_cols(active, flat(down_w[...]))

    @pl.when(step == pl.num_programs(0) - 1)
    def _():
        scaled, inverse = normalize(total[...])
        layer_out[...] = (scaled * gains[3:4] + gains[4:5]).astype(jnp.bfloat16)
        grad = cotangent_ref[...].astype(jnp.float32)
        d_second = normalize_back(grad * gains[3:4], scaled, inverse)
        d_second_out[...] = d_second
        sums_out[0:1] = row_sum(d_second.astype(jnp.bfloat16))
        sums_out[1:2] = row_sum(grad * scaled)
        sums_out[2:3] = row_sum(grad)


def feed_width(part):
    return min(512, part.shape[-1])


def feed_blocks(part):
    nf, ndp, rows, columns = part.shape
    width = feed_width(part)
    per = columns // width
    return pl.BlockSpec((1, ndp, rows, width), lambda at: (at // per, 0, 0, at % per))


def feed_forward(scaled, vectors, up_all, down_all, cotangent):
    count = scaled.shape[0]
    width = feed_width(up_all)
    bf16, f32 = jnp.bfloat16, jnp.float32
    gains = jnp.concatenate([vectors[3:5], vectors[9:12], jnp.zeros((3, D), f32)])
    return pl.pallas_call(
        feed_kernel,
        name="feed_forward",
        grid=(FF // width,),
        in_specs=[
            whole_spec((count, D)),
            whole_spec((8, D)),
            feed_blocks(up_all),
            feed_blocks(down_all),
            pl.BlockSpec((1, width), lambda at: (0, at)),
            whole_spec((count, D)),
        ],
        out_specs=[
            whole_spec((count, D)),
            pl.BlockSpec((count, width), lambda at: (0, at)),
            pl.BlockSpec((count, width), lambda at: (0, at)),
            whole_spec((count, D)),
            whole_spec((count, D)),
            whole_spec((8, D)),
        ],
        out_shape=[
            jax.ShapeDtypeStruct((count, D), bf16),
            jax.ShapeDtypeStruct((count, FF), bf16),
            jax.ShapeDtypeStruct((count, FF), bf16),
            jax.ShapeDtypeStruct((count, D), bf16),
            jax.ShapeDtypeStruct((count, D), f32),
            jax.ShapeDtypeStruct((8, D), f32),
        ],
        scratch_shapes=[pltpu.VMEM((count, D), f32)],
        compiler_params=ROOM,
    )(scaled, gains, up_all, down_all, vectors[5:9].reshape(1, FF), cotangent)


def backward_kernel(
    ndp,
    nf,
    d_second_ref,
    low_ref,
    scaled_ref,
    inverse_ref,
    gain_ref,
    active_ref,
    slope_ref,
    up_ref,
    down_ref,
    tokens_ref,
    label_col,
    label_row,
    blocks_ref,
    mixture_ref,
    total_ref,
    attn_ref,
    tail_ref,
    attn_mom,
    ffn_mom,
    input_grad,
    up_out,
    down_out,
    attn_out,
    vec_out,
    attn_low,
    ffn_low,
    held_up,
    held_down,
    held_attn,
    first_up,
    first_down,
    first_attn,
    second_up,
    second_down,
    second_attn,
    z_up,
    z_down,
    z_attn,
    stages_out,
    land,
    ffn_weight,
    ffn_act,
    attn_weight,
    attn_block,
    wide_low,
    wide_two,
    turned_one,
    turned_two,
    branch,
    bias_up_sum,
    query_sum,
    value_sum,
    vec_land,
    load_sem,
    step_sem,
    pair_send,
    pair_recv,
    first_send,
    first_recv,
    second_send,
    second_recv,
    z_send,
    z_recv,
    vec_send,
    vec_recv,
):
    z, core, y, x, nz, side = place(ndp, nf)
    dp, fs = z * 2 + core, y * side + x
    other = (z * 2 + 1 - core, fs)
    held, outs = (held_up, held_down, held_attn), (up_out, down_out, attn_out)
    from_first, from_second = (first_up, first_down, first_attn), (second_up, second_down, second_attn)
    from_z = (z_up, z_down, z_attn)
    chunks = 3
    rows, width_ffn = held_up.shape[2:]
    width_attn = held_attn.shape[-1]
    width = ffn_weight.shape[-1]
    per = width_ffn // width
    greet(line_partners(ndp, nf))

    def place_of(turn):
        step = nf - 1 - turn
        return lax.rem(y + lax.div(step, side), side) * side + lax.rem(x + lax.rem(step, side), side)

    def first_copy(chunk, z_at, line, step):
        x_first = lax.rem(z_at, 2) == 0
        near, far = lax.rem(x + step, side), lax.rem(y + step, side)
        to = jnp.where(x_first, y * side + near, far * side + x)
        at = jnp.where(
            x_first,
            lax.rem(y + line, side) * side + near,
            far * side + lax.rem(x + line, side),
        )
        return remote(
            held[chunk].at[z_at, at],
            from_first[chunk].at[z_at, step - 1, line],
            first_send.at[chunk, z_at, step - 1, line],
            first_recv.at[chunk, z_at, step - 1, line],
            (dp, to),
        )

    lag = 2
    total_steps = nf * per + nf
    schedule = {}
    for sent, base, stride in (((0, 1), 0, per), ((2,), nf * per, 1)):
        for turns in ((0,), tuple(range(1, nf - 1))):
            ready = min(base + (turns[-1] + 1) * stride - 1 + lag, total_steps)
            for z_at in range(0, nz, 2):
                schedule.setdefault(ready, []).extend((chunk, turns, z_at) for chunk in sent)

    def send_first(chunk, turns, z_from):
        def each(z_at):
            x_first = lax.rem(z_at, 2) == 0
            for turn in turns:
                step_x, step_y = (nf - 1 - turn) % side, (nf - 1 - turn) // side
                step = jnp.where(x_first, step_x, step_y)
                line = jnp.where(x_first, step_y, step_x)

                @pl.when(step > 0)
                def _(line=line, step=step):
                    first_copy(chunk, z_at, line, step).start()

        loop(z_from + 2, each, z_from)

    def sends_at(step, steps):
        for when in steps:
            @pl.when(step == when)
            def _(when=when):
                for chunk, turns, z_at in schedule.get(when, ()):
                    send_first(chunk, turns, z_at)

    def line_place(z_at, line):
        x_first = lax.rem(z_at, 2) == 0
        return jnp.where(
            x_first, lax.rem(y + line, side) * side + x, y * side + lax.rem(x + line, side)
        )

    def second_copy(chunk, z_at, step):
        to = line_place(z_at, step)
        return remote(
            held[chunk].at[z_at, to],
            from_second[chunk].at[z_at, step - 1],
            second_send.at[chunk, z_at, step - 1],
            second_recv.at[chunk, z_at, step - 1],
            (dp, to),
        )

    def z_copy(chunk, step):
        z_at = lax.rem(z + step, nz)
        return remote(
            held[chunk].at[z_at, fs],
            from_z[chunk].at[step - 1],
            z_send.at[chunk, step - 1],
            z_recv.at[chunk, step - 1],
            (z_at * 2 + core, fs),
        )

    def take_first(chunk):
        def each(hop):
            z_at = lax.rem(z + 1 + hop, nz)
            for line in (*range(1, side), 0):
                at = line_place(z_at, line)
                for step in range(1, side):
                    first_copy(chunk, z_at, line, step).wait_recv()
                    held[chunk][z_at, at] += from_first[chunk][z_at, step - 1, line]
                if line:
                    second_copy(chunk, z_at, line).start()

        loop(nz, each)

    def take_second(chunk):
        def each(hop):
            z_at = lax.rem(z + 1 + hop, nz)
            for step in range(1, side):
                second_copy(chunk, z_at, step).wait_recv()
                held[chunk][z_at, fs] += from_second[chunk][z_at, step - 1]

            @pl.when(hop < nz - 1)
            def _():
                z_copy(chunk, hop + 1).start()

        loop(nz, each)

    def moments(chunk):
        source = ffn_mom.at[chunk] if chunk < 2 else attn_mom
        return pltpu.make_async_copy(source, outs[chunk], load_sem.at[3 + chunk])

    def take_z(chunk):
        total = held[chunk][z, fs].astype(jnp.float32)
        for step in range(1, nz):
            z_copy(chunk, step).wait_recv()
            total += from_z[chunk][step - 1].astype(jnp.float32)
        moments(chunk).wait()
        low = (matrix_decay * outs[chunk][...] + total).astype(jnp.bfloat16)
        outs[chunk][...] = total
        if chunk < 2:
            half = low.shape[1] // 2
            ffn_low[chunk, 0] = low[:, :half]
            ffn_low[chunk, 1] = low[:, half:]
        else:
            attn_low[...] = low

    vec_rounds = [[other]]
    vec_rounds.append([(dp, y * side + lax.rem(x + step, side)) for step in range(1, side)])
    vec_rounds.append([(dp, lax.rem(y + step, side) * side + x) for step in range(1, side)])
    vec_rounds.append([(lax.rem(z + step, nz) * 2 + core, fs) for step in range(1, nz)])
    starts = [sum(len(group) for group in vec_rounds[:index]) for index in range(4)]

    def vec_copy(index, step):
        at = starts[index] + step
        return remote(
            vec_land.at[index], vec_land.at[4 + at], vec_send.at[at], vec_recv.at[at], vec_rounds[index][step]
        )

    def vec_start(index):
        for step in range(len(vec_rounds[index])):
            vec_copy(index, step).start()

    def vec_take(index):
        total = vec_land[index]
        for step in range(len(vec_rounds[index])):
            vec_copy(index, step).wait_recv()
            total += vec_land[4 + starts[index] + step]
        if index < 3:
            vec_land[index + 1] = total
            vec_start(index + 1)
        else:
            vec_out[...] = total

    def split(values, keep, give):
        parts = values.astype(jnp.bfloat16).reshape(nz, 2, rows, values.shape[1])
        for which in range(2):
            @pl.when(core == which)
            def _(which=which):
                keep(parts[:, which])
                give(parts[:, 1 - which])

    def ffn_loads(slot, turn, part):
        block = place_of(turn)
        at = pl.ds(part * width, width)
        column = pl.ds(pl.multiple_of(block * width_ffn + part * width, width), width)
        pairs = (
            (up_ref.at[block, :, :, at], ffn_weight.at[slot, 0]),
            (down_ref.at[block, :, :, at], ffn_weight.at[slot, 1]),
            (active_ref.at[:, column], ffn_act.at[slot, 0]),
            (slope_ref.at[:, column], ffn_act.at[slot, 1]),
        )
        return [
            pltpu.make_async_copy(source, target, step_sem.at[slot, index])
            for index, (source, target) in enumerate(pairs)
        ]

    def load(index, source, target):
        return pltpu.make_async_copy(source, target, load_sem.at[index])

    load(0, low_ref, wide_low).start(priority=1)
    load(1, d_second_ref, input_grad).start(priority=1)
    for copy in ffn_loads(0, 0, 0):
        copy.start(priority=1)
    load(2, tokens_ref, wide_two).start(priority=1)
    for chunk in range(chunks):
        moments(chunk).start(priority=1)
    load(0, low_ref, wide_low).wait()
    turned_one[...] = jnp.transpose(wide_low[...])
    load(1, d_second_ref, input_grad).wait()
    wide_low[...] = input_grad[...].astype(jnp.bfloat16)
    turned_two[...] = jnp.transpose(wide_low[...])

    def pair_copy(step):
        stage, slot = lax.rem(step, lag), lax.rem(step, 2 * lag)
        return remote(stages_out.at[stage], land.at[slot], pair_send.at[stage], pair_recv.at[slot], other)

    def pair_take(step):
        pair_copy(step).wait()
        slot = lax.rem(step, 2 * lag)

        @pl.when(step < nf * per)
        def _():
            block, part = place_of(lax.div(step, per)), lax.rem(step, per)
            for index in range(2):
                for which in range(per):
                    @pl.when(part == which)
                    def _(index=index, which=which):
                        for half in range(2):
                            left = which * width + half * width_attn
                            at = slice(left, left + width_attn)
                            held[index][:, block, :, at] += land[slot, :, 2 * index + half]

        @pl.when(step >= nf * per)
        def _():
            held_attn[:, place_of(step - nf * per)] += land[slot]

    def ffn_turn(turn):
        block = place_of(turn)
        for part in range(per):
            now = turn * per + part
            slot = lax.rem(now, 2)
            if part < per - 1:
                for copy in ffn_loads(1 - slot, turn, part + 1):
                    copy.start(priority=1)
            else:
                @pl.when(turn < nf - 1)
                def _():
                    for copy in ffn_loads(1 - slot, turn + 1, 0):
                        copy.start(priority=1)

            for copy in ffn_loads(slot, turn, part):
                copy.wait()
            d_active = product(wide_low[...], flat(ffn_weight[slot, 1]))
            d_up = (d_active * ffn_act[slot, 1].astype(jnp.float32)).astype(jnp.bfloat16)
            bias_up_sum[block * per + part] = row_sum(d_up)
            input_grad[...] += contract_cols(d_up, flat(ffn_weight[slot, 0]))

            @pl.when(now >= lag)
            def _():
                pair_take(now - lag)

            sends_at(now, range(nf * per))
            at = slice(part * width, (part + 1) * width)
            for index in range(2):

                def keep(values, index=index):
                    held[index][:, block, :, at] = values

                def give(values, index=index):
                    for half in range(2):
                        side_at = slice(half * width_attn, (half + 1) * width_attn)
                        stages_out[lax.rem(now, lag), :, 2 * index + half] = values[:, :, side_at]

                if index == 0:
                    split(product(turned_one[...], d_up), keep, give)
                else:
                    split(product(turned_two[...], ffn_act[slot, 0]), keep, give)
            pair_copy(now).start()

    loop(nf, ffn_turn)

    load(2, tokens_ref, wide_two).wait()
    turned_one[...] = jnp.transpose(wide_two[...])
    load(0, mixture_ref, wide_two).start(priority=1)

    def attn_load(index, turn):
        block = place_of(turn)
        per_block = ndp // nf
        source, target = (
            (attn_ref.at[block, :, pl.ds(0, 3 * rows)], attn_weight[0]),
            (
                attn_ref.at[:, pl.ds(block * per_block, per_block), pl.ds(3 * rows, rows)],
                attn_weight[1],
            ),
            (blocks_ref.at[block], attn_block),
        )[index]
        return pltpu.make_async_copy(source, target, step_sem.at[0, index])

    for index in range(3):
        attn_load(index, 0).start(priority=1)
    vec_land[0] = jnp.zeros((16, D), jnp.float32)
    vec_land[0, 9:12] = tail_ref[0:3]

    def norm_back(index):
        at = pl.ds(pl.multiple_of(index * NORM_ROWS, NORM_ROWS), NORM_ROWS)
        grad = input_grad[at]
        scaled = scaled_ref[at]
        d_first = normalize_back(grad * gain_ref[...], scaled, inverse_ref[at])
        input_grad[at] = d_first
        low = d_first.astype(jnp.bfloat16)
        vec_land[0, 2:3] += row_sum(low)
        vec_land[0, 3:4] += row_sum(grad * scaled)
        vec_land[0, 4:5] += row_sum(grad)
        for column in range(nf):
            branch[column, at] = low[:, column * width_attn : (column + 1) * width_attn]

    loop(tokens_ref.shape[0] // NORM_ROWS, norm_back)
    load(0, mixture_ref, wide_two).wait()
    turned_two[...] = jnp.transpose(wide_two[...])

    def attn_turn(turn):
        block = place_of(turn)
        now = nf * per + turn

        def load_next(index):
            @pl.when(turn < nf - 1)
            def _():
                attn_load(index, turn + 1).start(priority=1)

        for index in range(3):
            attn_load(index, turn).wait()
        count = tokens_ref.shape[0]
        zero = jnp.zeros((count, width_attn), jnp.float32)
        d_mixture = zero
        for index in range(nf):
            d_mixture += contract_cols(branch[index], flat(attn_weight[1][index]))
        load_next(1)
        d_mixture = d_mixture.astype(jnp.bfloat16)
        queries, keys_all, values_all = (attn_block[index] for index in range(3))
        allowed = label_col[...] == label_row[...]
        d_queries, d_keys, d_values = zero, zero, zero
        for head in range(width_attn // HDIM):
            my_queries = head_lanes(queries, head) * score_scale
            my_mixture = head_lanes(d_mixture, head)
            scores = contract_cols(keys_all, my_queries) - total_ref[block, head : head + 1, :]
            attention = jnp.where(allowed, jnp.exp(scores), 0.0)
            d_attention = contract_cols(values_all, my_mixture)
            inner = jnp.sum(d_attention * attention, axis=0, keepdims=True)
            d_scores = (attention * (d_attention - inner)).astype(jnp.bfloat16)
            d_keys += product(d_scores, my_queries)
            d_values += product(attention.astype(jnp.bfloat16), my_mixture)
            d_queries += contract_rows(d_scores, head_lanes(keys_all, head) * score_scale)
        load_next(2)
        grads = [values.astype(jnp.bfloat16) for values in (d_queries, d_keys, d_values)]
        query_sum[block] = row_sum(grads[0])
        value_sum[block] = row_sum(grads[2])
        moved = jnp.zeros((count, D), jnp.float32)
        for index in range(3):
            weight = attn_weight[0][:, index * rows : (index + 1) * rows]
            moved += contract_cols(grads[index], flat(weight))
        input_grad[...] += moved
        load_next(0)

        pair_take(now - lag)
        for index in range(4):
            turned, grad = (turned_one, grads[index]) if index < 3 else (turned_two, branch[block])

            def keep(values, index=index):
                held_attn[:, block, index] = values

            def give(values, index=index):
                stages_out[lax.rem(now, lag), :, index] = values

            split(product(turned[...], grad), keep, give)
        pair_copy(now).start()
        sends_at(now, range(nf * per, total_steps))

        @pl.when(turn == nf - 2)
        def _():
            take_first(0)
            take_first(1)

        @pl.when(turn == nf - 1)
        def _():
            take_second(0)
            take_second(1)

    loop(nf, attn_turn)
    for index in range(nf):
        at = slice(index * width_attn, (index + 1) * width_attn)
        vec_land[0, 0:1, at] = query_sum[index]
        vec_land[0, 1:2, at] = value_sum[index]
    for index in range(nf * per):
        left = index * width
        vec_land[0, 5 + left // D : 6 + left // D, left % D : left % D + width] = bias_up_sum[index]
    vec_start(0)
    for step in range(total_steps - lag, total_steps):
        pair_take(step)
    sends_at(total_steps, (total_steps,))

    vec_take(0)
    take_first(2)
    vec_take(1)
    take_z(0)
    take_second(2)
    vec_take(2)
    take_z(1)
    vec_take(3)
    take_z(2)

    for chunk in range(chunks):

        def finish(z_at):
            for step in range(1, side):
                second_copy(chunk, z_at, step).wait_send()
                for line in range(side):
                    first_copy(chunk, z_at, line, step).wait_send()

        loop(nz, finish)
        for step in range(1, nz):
            z_copy(chunk, step).wait_send()
    for index in range(4):
        for step in range(len(vec_rounds[index])):
            vec_copy(index, step).wait_send()


def backward_kernel_entry(ndp, nf, *refs):
    at = 19 + 7 + 12 + 2 + 2
    backward_kernel(ndp, nf, *refs[:at], refs[at : at + 2], *refs[at + 2 :])


def backward(
    ndp, nf, d_second, low, scaled, inverse, vectors, active, slope, up_all, down_all,
    tokens, segments, blocks, mixture, totals, attn_all, tail_sums, attn_mom, ffn_mom,
):
    nz, side = ndp // 2, math.isqrt(nf)
    count = tokens.shape[0]
    rows, width_ffn = up_all.shape[2:]
    width_attn = attn_all.shape[-1]
    width = 2 * width_attn
    bf16, f32 = jnp.bfloat16, jnp.float32
    dma = pltpu.SemaphoreType.DMA
    anywhere, inside = pl.BlockSpec(memory_space=pl.ANY), pl.BlockSpec(memory_space=pltpu.VMEM)
    shapes = [(rows, width_ffn), (rows, width_ffn), (4, rows, width_attn)]
    vec_copies = 1 + 2 * (side - 1) + nz - 1
    sums = []
    for lead in ((nz, nf), (nz, side - 1, side), (nz, side - 1), (nz - 1,)):
        sums += [pltpu.VMEM(lead + shape, bf16) for shape in shapes]
    return pl.pallas_call(
        functools.partial(backward_kernel_entry, ndp, nf),
        name="backward",
        out_shape=[jax.ShapeDtypeStruct((count, D), f32)]
        + [jax.ShapeDtypeStruct(shape, f32) for shape in shapes]
        + [
            jax.ShapeDtypeStruct((16, D), f32),
            jax.ShapeDtypeStruct(attn_mom.shape, bf16),
            jax.ShapeDtypeStruct((2, 2, rows, width_ffn // 2), bf16),
        ],
        in_specs=[
            anywhere,
            anywhere,
            inside,
            inside,
            inside,
            anywhere,
            anywhere,
            anywhere,
            anywhere,
            anywhere,
            inside,
            inside,
            anywhere,
            anywhere,
            inside,
            anywhere,
            inside,
            anywhere,
            anywhere,
        ],
        out_specs=[inside] * 7,
        scratch_shapes=sums
        + [
            pltpu.VMEM((2, nz, 4, rows, width_attn), bf16),
            pltpu.VMEM((4, nz, 4, rows, width_attn), bf16),
            pltpu.VMEM((2, 2, ndp, rows, width), bf16),
            pltpu.VMEM((2, 2, count, width), bf16),
            pltpu.VMEM((ndp, 3 * rows, width_attn), bf16),
            pltpu.VMEM((nf, ndp // nf, rows, width_attn), bf16),
            pltpu.VMEM((3, count, width_attn), bf16),
            pltpu.VMEM((count, D), bf16),
            pltpu.VMEM((count, D), bf16),
            pltpu.VMEM((D, count), bf16),
            pltpu.VMEM((D, count), bf16),
            pltpu.VMEM((nf, count, width_attn), bf16),
            pltpu.VMEM((FF // width, 1, width), f32),
            pltpu.VMEM((nf, 1, width_attn), f32),
            pltpu.VMEM((nf, 1, width_attn), f32),
            pltpu.VMEM((4 + vec_copies, 16, D), f32),
            dma((6,)),
            dma((2, 4)),
            dma((2,)),
            dma((4,)),
            dma((3, nz, side - 1, side)),
            dma((3, nz, side - 1, side)),
            dma((3, nz, side - 1)),
            dma((3, nz, side - 1)),
            dma((3, nz - 1)),
            dma((3, nz - 1)),
            dma((vec_copies,)),
            dma((vec_copies,)),
        ],
        compiler_params=pltpu.CompilerParams(
            collective_id=3, has_side_effects=True, vmem_limit_bytes=63 * 1024 * 1024
        ),
    )(
        d_second, low, scaled, inverse, vectors[3:4], active, slope, up_all, down_all,
        tokens, segments[:, None], segments[None, :], blocks, mixture, totals, attn_all, tail_sums, attn_mom, ffn_mom,
    )


def on_device(
    tokens,
    segments,
    cotangent,
    attn_w,
    ffn_w,
    vectors,
    attn_mom,
    ffn_mom,
    vec_mom,
    attn_ema,
    ffn_ema,
    vec_ema,
):
    ndp, nf = lax.axis_size("dp"), lax.axis_size("fsdp")
    rows, width_attn = attn_w.shape[1:]
    share = vectors.shape[1]
    ffn_low = ffn_w.astype(jnp.bfloat16)
    vec_shard = jnp.pad(vectors, ((0, 4), (0, width_attn - share)))
    shard = jnp.concatenate([attn_w.reshape(4 * rows, width_attn), vec_shard]).astype(jnp.bfloat16)
    attn_all, up_all, down_all = gather_all(ndp, nf, [shard, ffn_low[0], ffn_low[1]])
    vec_full = attn_all[:, :, 4 * rows : 4 * rows + 12, :share].transpose(2, 1, 0, 3).reshape(12, D)
    vec_full = vec_full.astype(jnp.float32)
    blocks, mixture, totals, scaled, inverse = attend(tokens, segments, attn_all, vec_full)
    low, active, slope, layer_out, d_second, tail_sums = feed_forward(
        scaled, vec_full, up_all, down_all, cotangent
    )
    input_grad, up_grad, down_grad, attn_grad, vec_sum, attn_piece, ffn_piece = backward(
        ndp, nf, d_second, low, scaled, inverse, vec_full, active, slope, up_all, down_all,
        tokens, segments, blocks, mixture, totals, attn_all, tail_sums, attn_mom, ffn_mom,
    )
    mine = (lax.axis_index("dp") * nf + lax.axis_index("fsdp")) * share
    vec_grad = lax.dynamic_slice(vec_sum, (0, mine), (12, share))
    attn_ortho, ffn_ortho = orthogonalize(ndp, nf, attn_piece, ffn_piece)
    total_tokens = tokens.shape[0] * ndp * nf
    updated = update_all(
        vector_step / math.sqrt(total_tokens),
        attn_w,
        ffn_w,
        vectors,
        attn_mom,
        ffn_mom,
        vec_mom,
        attn_ema,
        ffn_ema,
        vec_ema,
        attn_grad,
        up_grad,
        down_grad,
        vec_grad,
        attn_ortho,
        ffn_ortho,
    )
    return (layer_out, input_grad, *updated, vec_grad[2])


def solution(mesh):
    in_specs = (
        P(("dp", "fsdp"), None),
        P(("dp", "fsdp")),
        P(("dp", "fsdp"), None),
        P(None, "dp", "fsdp"),
        P(None, "dp", "fsdp"),
        P(None, ("dp", "fsdp")),
        P(None, "dp", "fsdp"),
        P(None, "dp", "fsdp"),
        P(None, ("dp", "fsdp")),
        P(None, "dp", "fsdp"),
        P(None, "dp", "fsdp"),
        P(None, ("dp", "fsdp")),
    )
    out_specs = (
        P(("dp", "fsdp"), None),
        P(("dp", "fsdp"), None),
        P(None, "dp", "fsdp"),
        P(None, "dp", "fsdp"),
        P(None, ("dp", "fsdp")),
        P(None, "dp", "fsdp"),
        P(None, "dp", "fsdp"),
        P(None, ("dp", "fsdp")),
        P(None, "dp", "fsdp"),
        P(None, "dp", "fsdp"),
        P(None, ("dp", "fsdp")),
        P(("dp", "fsdp")),
    )
    return jax.shard_map(
        on_device, mesh=mesh, in_specs=in_specs, out_specs=out_specs, check_vma=False
    )
```

```python
import functools
import math

import jax
import jax.numpy as jnp
from jax import lax
from jax.experimental import pallas as pl
from jax.experimental.pallas import tpu as pltpu
from jax.sharding import PartitionSpec as P

D = 1024
FF = 4096
HEADS = 16
HDIM = 64
TILE = 512
ITERS = 5


score_scale = 0.125
ln_epsilon = 1e-05
norm_epsilon = 1e-06
ns_linear = 3.4445
ns_square = -4.775
ns_cubic = 2.0315
matrix_decay = 0.95
vector_decay = 0.9
average_decay = 0.7
weight_decay = 0.01
attn_rates = (1.0, 1.0, 1.0, 10.0)
vector_step = 0.3


def product(left, right):
    return jnp.dot(left, right, preferred_element_type=jnp.float32)


def contract_rows(left, right):
    return lax.dot_general(
        left, right, (((0,), (0,)), ((), ())), preferred_element_type=jnp.float32
    )


def contract_cols(left, right):
    return lax.dot_general(
        left, right, (((1,), (1,)), ((), ())), preferred_element_type=jnp.float32
    )


MESH = pl.DeviceIdType.MESH
ROLES = 8
STEP_ROWS = 512
NORM_ROWS = 128
TILE_ROWS = 128


def greet(partners):
    barrier = pltpu.get_barrier_semaphore()
    for partner in partners:
        pl.semaphore_signal(barrier, inc=1, device_id=partner, device_id_type=MESH)
    pl.semaphore_wait(barrier, len(partners))


def place(ndp, nf):
    dp, fs = lax.axis_index("dp"), lax.axis_index("fsdp")
    side = math.isqrt(nf)
    return lax.div(dp, 2), lax.rem(dp, 2), lax.div(fs, side), lax.rem(fs, side), ndp // 2, side


def line_partners(ndp, nf):
    z, core, y, x, nz, side = place(ndp, nf)
    mine = y * side + x
    return (
        [(z * 2 + 1 - core, mine)]
        + [(lax.rem(z + step, nz) * 2 + core, mine) for step in range(1, nz)]
        + [(z * 2 + core, y * side + lax.rem(x + step, side)) for step in range(1, side)]
        + [(z * 2 + core, lax.rem(y + step, side) * side + x) for step in range(1, side)]
    )


def remote(source, target, send_sem, recv_sem, device):
    return pltpu.make_async_remote_copy(
        src_ref=source,
        dst_ref=target,
        send_sem=send_sem,
        recv_sem=recv_sem,
        device_id=device,
        device_id_type=MESH,
    )


def loop(count, body, start=0):
    def step(index, carry):
        body(index)
        return carry

    lax.fori_loop(start, count, step, 0)


def ortho_kernel(
    ndp,
    nf,
    attn_ref,
    ffn_ref,
    attn_out,
    ffn_out,
    land_attn,
    land_ffn,
    iter_low,
    iter_full,
    gram,
    gram_send,
    gram_recv,
    off_low,
    poly_low,
    diag_row,
    diag_col,
    inverse_norm,
    own_low,
    own_full,
    own_attn,
    own_ffn,
    own_sem,
    piece_send,
    piece_recv,
    first_send,
    second_send,
    plane_recv,
    gram_send_sem,
    gram_recv_sem,
    back_send,
    back_recv,
):
    z, core, y, x, nz, side = place(ndp, nf)
    dp, fs = z * 2 + core, y * side + x
    rows = attn_ref.shape[1]
    size = rows * ndp
    is_attn = jnp.logical_or(dp < 2, jnp.logical_and(dp >= 6, dp < ROLES))
    is_ffn = jnp.logical_and(dp >= 2, dp < 6)
    partner = z * 2 + 1 - core

    greet(
        [(lax.rem(dp + step, ndp), fs) for step in range(1, ndp)]
        + [(dp, y * side + lax.rem(x + step, side)) for step in range(1, side)]
        + [(dp, lax.rem(y + step, side) * side + x) for step in range(1, side)]
    )

    def piece(role):
        if role < 2 or role >= 6:
            return attn_ref.at[role if role < 2 else role - 4], land_attn
        return ffn_ref.at[(role - 2) // 2, (role - 2) % 2], land_ffn

    def piece_copy(role):
        source, land = piece(role)
        return remote(source, land.at[fs, dp], piece_send.at[role], piece_recv.at[dp], (role, fs))

    for role in (2, 4, 3, 5, 0, 6, 1, 7):
        @pl.when(dp != role)
        def _(role=role):
            piece_copy(role).start()

        @pl.when(dp == role)
        def _(role=role):
            source, land = piece(role)
            pltpu.make_async_copy(source, land.at[fs, dp], own_sem).start()

    def along(first, step):
        x_at = jnp.where(first, lax.rem(x + step, side), x)
        y_at = jnp.where(first, y, lax.rem(y + step, side))
        return y_at * side + x_at

    def iterate(land, source, own_out, target, role, paired):
        width = land.shape[-1]
        columns = width * nf
        tall = min(STEP_ROWS, size)
        steps = size // tall
        wide = min(1024, columns)

        def row_of(index):
            return lax.rem(z + index // 2, nz) * 2 + lax.rem(core + index, 2)

        def x_first(row):
            return lax.rem(row // 2, 2) == 0

        def first_copy(row, step):
            here = land.at[fs, row]
            peer = along(x_first(row), step)
            return remote(here, here, first_send.at[row, step - 1], plane_recv.at[fs, row], (dp, peer))

        def second_copy(plane_at, row, line, step):
            here = land.at[plane_at, row]
            peer = along(jnp.logical_not(x_first(row)), step)
            return remote(
                here, here, second_send.at[row, line, step - 1], plane_recv.at[plane_at, row], (dp, peer)
            )

        def arrived(plane_at, row):
            here = land.at[plane_at, row]
            remote(here, here, own_sem, plane_recv.at[plane_at, row], (dp, fs)).wait_recv()

        def take_piece(index):
            row = row_of(index)

            @pl.when(index == 0)
            def _():
                pltpu.make_async_copy(source, land.at[fs, row], own_sem).wait()

            @pl.when(index > 0)
            def _():
                remote(source, land.at[fs, row], own_sem, piece_recv.at[row], (dp, fs)).wait_recv()

            for step in range(1, side):
                first_copy(row, step).start()
                second_copy(fs, row, 0, step).start()

        loop(ndp, take_piece)

        def pass_on(index):
            row = row_of(index)
            for line in range(1, side):
                plane_at = along(x_first(row), line)
                arrived(plane_at, row)
                for step in range(1, side):
                    second_copy(plane_at, row, line, step).start()

        def add_gram(plane_at, fresh):
            block = land[plane_at].reshape(size, width)
            for step in range(steps):
                at = slice(step * tall, (step + 1) * tall)
                part = contract_cols(block[at], block)
                if fresh:
                    gram[at] = part
                else:
                    gram[at] += part

        add_gram(fs, True)
        loop(ndp, pass_on)

        for line in range(side):
            for step in range(1, side):

                def last(index, line=line, step=step):
                    row = row_of(index)
                    near = jnp.where(
                        x_first(row),
                        lax.rem(y + step, side) * side + lax.rem(x + line, side),
                        lax.rem(y + line, side) * side + lax.rem(x + step, side),
                    )
                    arrived(near, row)

                loop(ndp, last)
            if line == 0:
                for step in range(1, side):
                    add_gram(along(True, step), False)
                    add_gram(along(False, step), False)
        for far_y in range(1, side):
            for far_x in range(1, side):
                add_gram(lax.rem(y + far_y, side) * side + lax.rem(x + far_x, side), False)

        def gram_copy(slot, step):
            at = pl.ds(step * tall, tall)
            return remote(
                gram_send.at[slot, at],
                gram_recv.at[slot, at],
                gram_send_sem.at[slot, step],
                gram_recv_sem.at[slot, step],
                (partner, fs),
            )

        if paired:
            for step in range(steps):
                at = slice(step * tall, (step + 1) * tall)
                gram_send[0, at] = gram[at].astype(jnp.bfloat16)
                gram_copy(0, step).start()
        for index in range(nf):
            block = land[index].reshape(size, width)
            at = slice(index * width, (index + 1) * width)
            iter_low[0, :, at] = block
            iter_full[:, at] = block.astype(jnp.float32)

        def back_copy(row):
            return remote(own_out.at[row], target, back_send.at[row], back_recv.at[role], (row, fs))

        def iteration(count):
            now = lax.rem(count, 2)
            later = 1 - now

            @pl.when(count > 0)
            def _():
                def gram_rows(step):
                    at = pl.ds(pl.multiple_of(step * tall, tall), tall)
                    part = contract_cols(iter_low[now, at, :columns], iter_low[now, :, :columns])
                    if paired:
                        gram_send[now, at] = part.astype(jnp.bfloat16)
                        gram_copy(now, step).start()
                    else:
                        gram[at] = part

                loop(steps, gram_rows)

            eye = lax.broadcasted_iota(jnp.int32, (TILE_ROWS, TILE_ROWS), 0) == lax.broadcasted_iota(
                jnp.int32, (TILE_ROWS, TILE_ROWS), 1
            )

            @pl.when(count == 0)
            def _():
                trace = jnp.zeros((TILE_ROWS, TILE_ROWS), jnp.float32)
                if paired:
                    for step in range(steps):
                        gram_copy(now, step).wait()
                for tile in range(size // TILE_ROWS):
                    at = slice(tile * TILE_ROWS, (tile + 1) * TILE_ROWS)
                    if paired:
                        square = gram_send[now, at, at].astype(jnp.float32)
                        trace += square + gram_recv[now, at, at].astype(jnp.float32)
                    else:
                        trace += gram[at, at]
                trace = jnp.sum(jnp.where(eye, trace, 0.0), axis=1, keepdims=True)
                trace = jnp.sum(trace, axis=0, keepdims=True)
                inverse_norm[...] = 1.0 / (jnp.sqrt(trace) + norm_epsilon)

            @pl.when(count > 0)
            def _():
                inverse_norm[...] = jnp.ones_like(inverse_norm)

            inverse = inverse_norm[...]
            shrink = inverse * inverse

            for step in range(steps):
                if paired:
                    @pl.when(count > 0)
                    def _(step=step):
                        gram_copy(now, step).wait()

                for tile in range(step * tall // TILE_ROWS, (step + 1) * tall // TILE_ROWS):
                    at = slice(tile * TILE_ROWS, (tile + 1) * TILE_ROWS)
                    if paired:
                        total = gram_send[now, at].astype(jnp.float32) + gram_recv[now, at].astype(jnp.float32)
                    else:
                        total = gram[at]
                    total = total * shrink
                    gram[at] = total
                    off_low[at] = total.astype(jnp.bfloat16)
                    square = total[:, at]
                    masked = jnp.where(eye, square, 0.0)
                    diag_col[at] = jnp.sum(masked, axis=1, keepdims=True)
                    diag_row[:, at] = jnp.sum(masked, axis=0, keepdims=True)
                    square = jnp.where(eye, 0.0, square)
                    gram[at, at] = square
                    off_low[at, at] = square.astype(jnp.bfloat16)

            linear, middle, cubic = ns_linear * inverse, ns_square * inverse, ns_cubic * inverse

            def poly_rows(step):
                at = pl.ds(step * tall, tall)
                again = product(off_low[at], off_low[...])
                mine = diag_col[at]
                poly = gram[at] * (middle + cubic * mine + cubic * diag_row[...]) + cubic * again
                poly_low[at] = poly.astype(jnp.bfloat16)
                again_diag = []
                for tile in range(tall // TILE_ROWS):
                    rows_at = slice(tile * TILE_ROWS, (tile + 1) * TILE_ROWS)
                    side_at = slice(step * tall + tile * TILE_ROWS, step * tall + (tile + 1) * TILE_ROWS)
                    again_diag.append(
                        jnp.sum(jnp.where(eye, again[rows_at, side_at], 0.0), axis=1, keepdims=True)
                    )
                    poly_low[side_at, side_at] = jnp.where(eye, 0.0, poly[rows_at, side_at]).astype(jnp.bfloat16)
                again_diag = jnp.concatenate(again_diag, axis=0)
                factor = linear + middle * mine + cubic * (mine * mine + again_diag)

                @pl.when(count < ITERS - 1)
                def _():
                    for left in range(0, columns, wide):
                        part = slice(left, left + wide)
                        moved = product(poly_low[at], iter_low[now, :, part])
                        fresh = factor * iter_full[at, part] + moved
                        iter_full[at, part] = fresh
                        iter_low[later, at, part] = fresh.astype(jnp.bfloat16)

                @pl.when(count == ITERS - 1)
                def _():
                    for index in range(nf):
                        @pl.when(fs == index)
                        def _(index=index):
                            part = slice(index * width, (index + 1) * width)
                            own_full[at, :width] = iter_full[at, part]

                            if step == 0:
                                own_low[:, :width] = iter_low[now, :, part]

                    moved = product(poly_low[at], own_low[:, :width])
                    fresh = factor * own_full[at, :width] + moved
                    blocks = tall // rows
                    own_out[pl.ds(step * blocks, blocks)] = fresh.astype(jnp.bfloat16).reshape(
                        blocks, rows, width
                    )

                    def give(index):
                        row = step * blocks + index

                        @pl.when(row != dp)
                        def _():
                            back_copy(row).start()

                        @pl.when(row == dp)
                        def _():
                            pltpu.make_async_copy(own_out.at[row], target, own_sem).start()

                    loop(blocks, give)

            for step in range(steps):
                poly_rows(step)

        loop(ITERS, iteration)

        def finish(row):
            for step in range(1, side):
                first_copy(row, step).wait_send()
                for line in range(side):
                    second_copy(fs, row, line, step).wait_send()

            @pl.when(row != dp)
            def _():
                back_copy(row).wait_send()

        loop(ndp, finish)
        pltpu.make_async_copy(own_out.at[dp], target, own_sem).wait()

    @pl.when(is_attn)
    def _():
        at = jnp.where(dp < 2, dp, dp - 4)
        iterate(land_attn, attn_ref.at[at], own_attn, attn_out.at[at], dp, False)

    @pl.when(is_ffn)
    def _():
        matrix, half = (dp - 2) // 2, lax.rem(dp - 2, 2)
        iterate(land_ffn, ffn_ref.at[matrix, half], own_ffn, ffn_out.at[matrix, half], dp, True)

    for role in range(ROLES):
        @pl.when(dp != role)
        def _(role=role):
            if role < 2 or role >= 6:
                target = attn_out.at[role if role < 2 else role - 4]
            else:
                target = ffn_out.at[(role - 2) // 2, (role - 2) % 2]
            piece_copy(role).wait_send()
            remote(target, target, own_sem, back_recv.at[role], (role, fs)).wait_recv()


def orthogonalize(ndp, nf, attn_low, ffn_low):
    rows, width_attn = attn_low.shape[1:]
    width_ffn = ffn_low.shape[3]
    side = math.isqrt(nf)
    size = rows * ndp
    columns = width_ffn * nf
    tall = min(STEP_ROWS, size)
    bf16, f32 = jnp.bfloat16, jnp.float32
    dma = pltpu.SemaphoreType.DMA
    return pl.pallas_call(
        functools.partial(ortho_kernel, ndp, nf),
        name="newton_schulz",
        out_shape=[
            jax.ShapeDtypeStruct(attn_low.shape, bf16),
            jax.ShapeDtypeStruct(ffn_low.shape, bf16),
        ],
        in_specs=[pl.BlockSpec(memory_space=pltpu.VMEM)] * 2,
        out_specs=[pl.BlockSpec(memory_space=pltpu.VMEM)] * 2,
        scratch_shapes=[
            pltpu.VMEM((nf, ndp, rows, width_attn), bf16),
            pltpu.VMEM((nf, ndp, rows, width_ffn), bf16),
            pltpu.VMEM((2, size, columns), bf16),
            pltpu.VMEM((size, columns), f32),
            pltpu.VMEM((size, size), f32),
            pltpu.VMEM((2, size, size), bf16),
            pltpu.VMEM((2, size, size), bf16),
            pltpu.VMEM((size, size), bf16),
            pltpu.VMEM((size, size), bf16),
            pltpu.VMEM((1, size), f32),
            pltpu.VMEM((size, 1), f32),
            pltpu.VMEM((1, 1), f32),
            pltpu.VMEM((size, width_ffn), bf16),
            pltpu.VMEM((size, width_ffn), f32),
            pltpu.VMEM((ndp, rows, width_attn), bf16),
            pltpu.VMEM((ndp, rows, width_ffn), bf16),
            dma,
            dma((ROLES,)),
            dma((ndp,)),
            dma((ndp, side - 1)),
            dma((ndp, side, side - 1)),
            dma((nf, ndp)),
            dma((2, size // tall)),
            dma((2, size // tall)),
            dma((ndp,)),
            dma((ROLES,)),
        ],
        compiler_params=pltpu.CompilerParams(
            collective_id=1, has_side_effects=True, vmem_limit_bytes=60 * 1024 * 1024
        ),
    )(attn_low, ffn_low)


def update_kernel(
    attn_w,
    ffn_w,
    vectors,
    attn_mom,
    ffn_mom,
    vec_mom,
    attn_ema,
    ffn_ema,
    vec_ema,
    attn_grad,
    up_grad,
    down_grad,
    vec_grad,
    attn_ortho,
    ffn_ortho,
    attn_new,
    ffn_new,
    vec_new,
    attn_mom_new,
    ffn_mom_new,
    vec_mom_new,
    attn_ema_new,
    ffn_ema_new,
    vec_ema_new,
    *,
    vector_rate,
):
    for index in range(4):
        rate = attn_rates[index]
        attn_mom_new[index] = matrix_decay * attn_mom[index] + attn_grad[index]
        new = attn_w[index] * (1.0 - weight_decay * rate) - rate * attn_ortho[index].astype(jnp.float32)
        attn_new[index] = new
        attn_ema_new[index] = average_decay * attn_ema[index] + (1.0 - average_decay) * new
    width = ffn_ortho.shape[-1]
    shape_factor = math.sqrt(FF / D)
    for index, grad in enumerate((up_grad, down_grad)):
        ffn_mom_new[index] = matrix_decay * ffn_mom[index] + grad[...]
        for half in range(2):
            at = slice(half * width, (half + 1) * width)
            ortho = ffn_ortho[index, half].astype(jnp.float32)
            new = ffn_w[index, :, at] * (1.0 - weight_decay) - shape_factor * ortho
            ffn_new[index, :, at] = new
            ffn_ema_new[index, :, at] = average_decay * ffn_ema[index, :, at] + (1.0 - average_decay) * new
    mom = vector_decay * vec_mom[...] + vec_grad[...]
    vec_mom_new[...] = mom
    new = vectors[...] - vector_rate * mom
    vec_new[...] = new
    vec_ema_new[...] = average_decay * vec_ema[...] + (1.0 - average_decay) * new


def update_all(vector_rate, *operands):
    states = operands[:9]
    return pl.pallas_call(
        functools.partial(update_kernel, vector_rate=vector_rate),
        name="update",
        out_shape=[jax.ShapeDtypeStruct(states[index % 3].shape, jnp.float32) for index in range(9)],
        in_specs=[pl.BlockSpec(memory_space=pltpu.VMEM)] * len(operands),
        out_specs=[pl.BlockSpec(memory_space=pltpu.VMEM)] * 9,
        compiler_params=pltpu.CompilerParams(vmem_limit_bytes=60 * 1024 * 1024),
    )(*operands)


ROOM = pltpu.CompilerParams(vmem_limit_bytes=56 * 1024 * 1024)
ROOT_HALF = math.sqrt(0.5)
BELL = 1.0 / math.sqrt(2.0 * math.pi)


def flat(block):
    return block.reshape(-1, block.shape[-1])


def head_lanes(values, head):
    if values.shape[1] == HDIM:
        return values
    lane = lax.broadcasted_iota(jnp.int32, values.shape, 1)
    return jnp.where(lax.div(lane, HDIM) == head, values, jnp.zeros_like(values))


def normalize(values):
    center = values - jnp.mean(values, axis=1, keepdims=True)
    inverse = lax.rsqrt(jnp.mean(center * center, axis=1, keepdims=True) + ln_epsilon)
    return center * inverse, inverse


def normalize_back(grad, scaled, inverse):
    return inverse * (
        grad
        - jnp.mean(grad, axis=1, keepdims=True)
        - scaled * jnp.mean(grad * scaled, axis=1, keepdims=True)
    )


def row_sum(values):
    return jnp.sum(values.astype(jnp.float32), axis=0, keepdims=True)


def forward_kernel(
    ndp,
    nf,
    tokens_ref,
    label_ref,
    cotangent_ref,
    attn_w,
    ffn_w,
    vectors_ref,
    attn_out,
    up_out,
    down_out,
    blocks_out,
    active_out,
    slope_out,
    vec_out,
    mixture_out,
    total_out,
    scaled_out,
    inverse_out,
    low_out,
    layer_out,
    d_second_out,
    sums_out,
    attn_shard,
    up_shard,
    down_shard,
    three_weight,
    out_weight,
    ffn_weight,
    vec_land,
    bias,
    bias_up,
    blocks,
    parts,
    active,
    slope,
    total,
    own_sem,
    own_recv,
    pair_recv,
    z_send,
    first_send,
    second_send,
    pair_send,
    load_sem,
    store_sem,
):
    chunks = 3
    shards, wholes = (attn_shard, up_shard, down_shard), (attn_out, up_out, down_out)
    z, core, y, x, nz, side = place(ndp, nf)
    dp, fs = z * 2 + core, y * side + x
    rows, width_attn = attn_w.shape[1:]
    width_ffn, share = ffn_w.shape[2], vectors_ref.shape[1]
    count = tokens_ref.shape[0]
    width = ffn_weight.shape[-1]
    per = width_ffn // width

    attn_shard[4 * rows :] = jnp.zeros((16, width_attn), jnp.bfloat16)
    attn_shard[4 * rows : 4 * rows + 12, :share] = vectors_ref[...].astype(jnp.bfloat16)
    for index in range(4):
        attn_shard[index * rows : (index + 1) * rows] = attn_w[index].astype(jnp.bfloat16)
    up_shard[...] = ffn_w[0].astype(jnp.bfloat16)
    down_shard[...] = ffn_w[1].astype(jnp.bfloat16)
    greet(line_partners(ndp, nf))

    def slot(chunk, plane_at, z_at):
        return wholes[chunk].at[plane_at, z_at * 2 + core]

    def source(chunk, plane_at, z_at, own):
        return shards[chunk] if own else slot(chunk, plane_at, z_at)

    def along(first, step):
        x_at = jnp.where(first, lax.rem(x + step, side), x)
        y_at = jnp.where(first, y, lax.rem(y + step, side))
        return y_at * side + x_at

    def first_copy(chunk, z_at, step, own):
        peer = along(lax.rem(z_at, 2) == 0, step)
        return remote(
            source(chunk, fs, z_at, own),
            slot(chunk, fs, z_at),
            first_send.at[chunk, z_at, step - 1],
            own_recv.at[chunk, fs, z_at],
            (dp, peer),
        )

    def second_copy(chunk, plane_at, z_at, step, own, line):
        peer = along(lax.rem(z_at, 2) != 0, step)
        return remote(
            source(chunk, plane_at, z_at, own),
            slot(chunk, plane_at, z_at),
            second_send.at[chunk, z_at, line, step - 1],
            own_recv.at[chunk, plane_at, z_at],
            (dp, peer),
        )

    def pair_copy(chunk, plane_at, z_at, own):
        return remote(
            source(chunk, plane_at, z_at, own),
            slot(chunk, plane_at, z_at),
            pair_send.at[chunk, plane_at, z_at],
            pair_recv.at[chunk, plane_at, z_at],
            (z * 2 + 1 - core, fs),
        )

    def z_copy(chunk, step):
        return remote(
            shards[chunk],
            slot(chunk, fs, z),
            z_send.at[chunk, step - 1],
            own_recv.at[chunk, fs, z],
            (lax.rem(z + step, nz) * 2 + core, fs),
        )

    def arrived(chunk, plane_at, z_at):
        here = slot(chunk, plane_at, z_at)
        remote(here, here, own_sem.at[chunk], own_recv.at[chunk, plane_at, z_at], (dp, fs)).wait_recv()

    def pass_on(chunk, z_at, own):
        for step in range(1, side):
            first_copy(chunk, z_at, step, own).start()
            second_copy(chunk, fs, z_at, step, own, 0).start()
        pair_copy(chunk, fs, z_at, own).start()

    def own_copy(chunk):
        return pltpu.make_async_copy(shards[chunk], slot(chunk, fs, z), own_sem.at[chunk])

    def near_first(body):
        def each(index):
            far = 1 + lax.div(index, 2)
            z_at = jnp.where(lax.rem(index, 2) == 0, z - far, z + far)

            @pl.when(jnp.logical_and(z_at >= 0, z_at < nz))
            def _():
                body(z_at)

        loop(2 * (nz - 1), each)

    def from_z(chunk):
        def each(z_at):
            arrived(chunk, fs, z_at)
            pass_on(chunk, z_at, False)

        near_first(each)

    def from_first(chunk):
        def each(z_at):
            for line in range(1, side):
                plane_at = along(lax.rem(z_at, 2) == 0, line)
                arrived(chunk, plane_at, z_at)
                for step in range(1, side):
                    second_copy(chunk, plane_at, z_at, step, False, line).start()
                pair_copy(chunk, plane_at, z_at, False).start()

        each(z)
        near_first(each)

    def last_places(z_at):
        x_first = lax.rem(z_at, 2) == 0
        for line in range(side):
            for step in range(1, side):
                near_x, far_y = lax.rem(x + line, side), lax.rem(y + step, side)
                far_x, near_y = lax.rem(x + step, side), lax.rem(y + line, side)
                yield jnp.where(x_first, far_y * side + near_x, near_y * side + far_x)

    def from_second(chunk):
        def each(z_at):
            for plane_at in last_places(z_at):
                arrived(chunk, plane_at, z_at)
                pair_copy(chunk, plane_at, z_at, False).start()

        each(z)
        near_first(each)

    def from_pair(chunk):
        own_copy(chunk).wait()

        def each(index):
            plane_at, z_at = lax.rem(index, nf), lax.div(index, nf)
            there = wholes[chunk].at[plane_at, z_at * 2 + 1 - core]
            remote(
                there, there, own_sem.at[chunk], pair_recv.at[chunk, plane_at, z_at], (dp, fs)
            ).wait_recv()

        loop(nf * nz, each)

    for chunk in range(chunks):
        own_copy(chunk).start(priority=1)
        for step in range(1, nz):
            z_copy(chunk, step).start()
        pass_on(chunk, z, True)

    from_z(0)
    from_first(0)
    from_z(1)
    from_second(0)
    from_pair(0)

    def load(index, source, target):
        return pltpu.make_async_copy(source, target, load_sem.at[index])

    def attn_load(index, block, at):
        per_block = ndp // nf
        if index == 0:
            return load(at, attn_out.at[block, :, pl.ds(0, 3 * rows)], three_weight.at[at])
        return load(
            2 + at,
            attn_out.at[:, pl.ds(block * per_block, per_block), pl.ds(3 * rows, rows)],
            out_weight.at[at],
        )

    vec_copy = load(4, attn_out.at[:, :, pl.ds(4 * rows, 16)], vec_land)
    vec_copy.start(priority=1)
    for index in range(2):
        attn_load(index, 0, 0).start(priority=1)
    vec_copy.wait()
    for row in range(ndp):
        for column in range(nf):
            left = (row * nf + column) * share
            vec_out[:, left : left + share] = vec_land[column, row, :, :share].astype(jnp.float32)
    for index in range(nf):
        at = slice(index * width_attn, (index + 1) * width_attn)
        bias[index, 0:1] = vec_out[0:1, at]
        bias[index, 1:2] = vec_out[1:2, at]
    for index in range(FF // width):
        left = index * width
        bias_up[index] = vec_out[5 + left // D : 6 + left // D, left % D : left % D + width]
    label_row = label_ref[...].astype(jnp.float32)
    label_col = jnp.transpose(jnp.broadcast_to(label_row, (128, count)))[:, 0:1]
    tokens = tokens_ref[...]
    lane = lax.broadcasted_iota(jnp.int32, (count, 128), 1)
    total[...] = jnp.broadcast_to(vec_out[2:3], (count, D))

    def attn_turn(block):
        at = lax.rem(block, 2)

        @pl.when(block < nf - 1)
        def _():
            for index in range(2):
                attn_load(index, block + 1, 1 - at).start(priority=1)

        attn_load(0, block, at).wait()
        attn_load(1, block, at).wait()
        weights = [flat(three_weight[at, :, index * rows : (index + 1) * rows]) for index in range(3)]
        queries = (product(tokens, weights[0]) + bias[block, 0:1]).astype(jnp.bfloat16)
        keys_all = product(tokens, weights[1]).astype(jnp.bfloat16)
        values_all = (product(tokens, weights[2]) + bias[block, 1:2]).astype(jnp.bfloat16)
        for index, values in enumerate((queries, keys_all, values_all)):
            blocks[block, index] = values
        pltpu.make_async_copy(blocks.at[block], blocks_out.at[block], store_sem.at[block]).start(priority=1)
        allowed = label_col == label_row
        totals = jnp.zeros((count, 128), jnp.float32)
        mixture = jnp.zeros((count, width_attn), jnp.float32)
        for head in range(width_attn // HDIM):
            scores = contract_cols(head_lanes(queries, head) * score_scale, keys_all)
            scores = jnp.where(allowed, scores, -1e30)
            top = jnp.max(scores, axis=1, keepdims=True)
            exponent = jnp.exp(scores - top)
            weight = jnp.sum(exponent, axis=1, keepdims=True)
            attention = (exponent * (1.0 / weight)).astype(jnp.bfloat16)
            totals = jnp.where(lane == head, top + jnp.log(weight), totals)
            mixture += product(attention, head_lanes(values_all, head))
        mixture = mixture.astype(jnp.bfloat16)
        parts[block] = mixture
        total_out[block] = jnp.transpose(totals)[:8]
        for index in range(nf):
            side_at = slice(index * width_attn, (index + 1) * width_attn)
            total[:, side_at] += product(mixture, flat(out_weight[at, index]))

        @pl.when(block == 0)
        def _():
            from_z(2)

        @pl.when(block == nf - 2)
        def _():
            from_first(1)

    loop(nf, attn_turn)

    def first_norm(index):
        at = pl.ds(pl.multiple_of(index * NORM_ROWS, NORM_ROWS), NORM_ROWS)
        scaled, inverse = normalize(tokens_ref[at].astype(jnp.float32) + total[at])
        scaled_out[at] = scaled
        inverse_out[at] = inverse
        normed = scaled * vec_out[3:4] + vec_out[4:5]
        low_out[at] = normed.astype(jnp.bfloat16)
        total[at] = normed + vec_out[9:10]

    loop(count // NORM_ROWS, first_norm)
    for index in range(nf):
        mixture_out[:, index * width_attn : (index + 1) * width_attn] = parts[index]

    def ffn_load(chunk, step, at):
        block, part = lax.div(step, per), lax.rem(step, per)
        left = pl.multiple_of(part * width, width)
        return load(5 + at, wholes[chunk].at[block, :, :, pl.ds(left, width)], ffn_weight.at[at])

    def ffn_steps(chunk, body, between):
        ffn_load(chunk, 0, 0).start(priority=1)

        def each(step):
            at = lax.rem(step, 2)

            @pl.when(step < FF // width - 1)
            def _():
                ffn_load(chunk, step + 1, 1 - at).start(priority=1)

            ffn_load(chunk, step, at).wait()
            body(step, at)
            between(step)

        loop(FF // width, each)

    def keep(step):
        column = pl.ds(pl.multiple_of(step * width, width), width)
        return (
            pltpu.make_async_copy(active.at[step], active_out.at[:, column], store_sem.at[nf]),
            pltpu.make_async_copy(slope.at[lax.rem(step, 2)], slope_out.at[:, column], store_sem.at[nf + 1]),
        )

    def up_step(step, at):
        up_proj = product(low_out[...], flat(ffn_weight[at])) + bias_up[step]
        half = 0.5 * (1.0 + lax.erf(up_proj * ROOT_HALF))

        @pl.when(step > 0)
        def _():
            for copy in keep(step - 1):
                copy.wait()

        active[step] = (up_proj * half).astype(jnp.bfloat16)
        slope[lax.rem(step, 2)] = (half + up_proj * (BELL * jnp.exp(-0.5 * up_proj * up_proj))).astype(
            jnp.bfloat16
        )
        for copy in keep(step):
            copy.start(priority=1)

    def down_step(step, at):
        total[...] += contract_cols(active[step], flat(ffn_weight[at]))

    def between_up(step):
        @pl.when(step == FF // width // 2)
        def _():
            from_first(2)

    from_second(1)
    from_pair(1)
    ffn_steps(1, up_step, between_up)
    for copy in keep(FF // width - 1):
        copy.wait()
    from_second(2)
    from_pair(2)
    ffn_steps(2, down_step, lambda step: None)
    sums_out[...] = jnp.zeros((8, D), jnp.float32)

    def second_norm(index):
        at = pl.ds(pl.multiple_of(index * NORM_ROWS, NORM_ROWS), NORM_ROWS)
        scaled, inverse = normalize(total[at])
        layer_out[at] = (scaled * vec_out[10:11] + vec_out[11:12]).astype(jnp.bfloat16)
        grad = cotangent_ref[at].astype(jnp.float32)
        d_second = normalize_back(grad * vec_out[10:11], scaled, inverse)
        d_second_out[at] = d_second
        sums_out[0:1] += row_sum(d_second.astype(jnp.bfloat16))
        sums_out[1:2] += row_sum(grad * scaled)
        sums_out[2:3] += row_sum(grad)

    loop(count // NORM_ROWS, second_norm)

    def stored(block):
        pltpu.make_async_copy(blocks.at[block], blocks_out.at[block], store_sem.at[block]).wait()

    loop(nf, stored)
    for chunk in range(chunks):
        for step in range(1, nz):
            z_copy(chunk, step).wait_send()

        def finish(z_at):
            for step in range(1, side):
                first_copy(chunk, z_at, step, False).wait_send()
                for line in range(side):
                    second_copy(chunk, fs, z_at, step, False, line).wait_send()

            def each(plane_at):
                pair_copy(chunk, plane_at, z_at, False).wait_send()

            loop(nf, each)

        loop(nz, finish)


def forward(ndp, nf, tokens, segments, cotangent, attn_w, ffn_w, vectors):
    nz, side, chunks = ndp // 2, math.isqrt(nf), 3
    count = tokens.shape[0]
    rows, width_attn = attn_w.shape[1:]
    width_ffn = ffn_w.shape[2]
    width = min(512, width_ffn)
    bf16, f32 = jnp.bfloat16, jnp.float32
    dma = pltpu.SemaphoreType.DMA
    anywhere, inside = pl.BlockSpec(memory_space=pl.ANY), pl.BlockSpec(memory_space=pltpu.VMEM)
    shape = jax.ShapeDtypeStruct
    return pl.pallas_call(
        functools.partial(forward_kernel, ndp, nf),
        name="forward",
        out_shape=[
            shape((nf, ndp, 4 * rows + 16, width_attn), bf16),
            shape((nf, ndp, rows, width_ffn), bf16),
            shape((nf, ndp, rows, width_ffn), bf16),
            shape((nf, 3, count, width_attn), bf16),
            shape((count, FF), bf16),
            shape((count, FF), bf16),
            shape((16, D), f32),
            shape((count, D), bf16),
            shape((nf, 8, count), f32),
            shape((count, D), f32),
            shape((count, 1), f32),
            shape((count, D), bf16),
            shape((count, D), bf16),
            shape((count, D), f32),
            shape((8, D), f32),
        ],
        in_specs=[inside] * 6,
        out_specs=[anywhere] * 6 + [inside] * 9,
        scratch_shapes=[
            pltpu.VMEM((4 * rows + 16, width_attn), bf16),
            pltpu.VMEM((rows, width_ffn), bf16),
            pltpu.VMEM((rows, width_ffn), bf16),
            pltpu.VMEM((2, ndp, 3 * rows, width_attn), bf16),
            pltpu.VMEM((2, nf, ndp // nf, rows, width_attn), bf16),
            pltpu.VMEM((2, ndp, rows, width), bf16),
            pltpu.VMEM((nf, ndp, 16, width_attn), bf16),
            pltpu.VMEM((nf, 8, width_attn), f32),
            pltpu.VMEM((FF // width, 1, width), f32),
            pltpu.VMEM((nf, 3, count, width_attn), bf16),
            pltpu.VMEM((nf, count, width_attn), bf16),
            pltpu.VMEM((FF // width, count, width), bf16),
            pltpu.VMEM((2, count, width), bf16),
            pltpu.VMEM((count, D), f32),
            dma((chunks,)),
            dma((chunks, nf, nz)),
            dma((chunks, nf, nz)),
            dma((chunks, nz - 1)),
            dma((chunks, nz, side - 1)),
            dma((chunks, nz, side, side - 1)),
            dma((chunks, nf, nz)),
            dma((7,)),
            dma((nf + 2,)),
        ],
        compiler_params=pltpu.CompilerParams(
            collective_id=2, has_side_effects=True, vmem_limit_bytes=60 * 1024 * 1024
        ),
    )(tokens, segments[None, :], cotangent, attn_w, ffn_w, vectors)


def backward_kernel(
    ndp,
    nf,
    d_second_ref,
    low_ref,
    scaled_ref,
    inverse_ref,
    vec_ref,
    active_ref,
    slope_ref,
    up_ref,
    down_ref,
    tokens_ref,
    label_ref,
    blocks_ref,
    mixture_ref,
    total_ref,
    attn_ref,
    tail_ref,
    attn_mom,
    ffn_mom,
    input_grad,
    up_out,
    down_out,
    attn_out,
    vec_out,
    attn_low,
    ffn_low,
    held_up,
    held_down,
    held_attn,
    first_up,
    first_down,
    first_attn,
    second_up,
    second_down,
    second_attn,
    z_up,
    z_down,
    z_attn,
    stages_out,
    land,
    ffn_weight,
    ffn_act,
    attn_weight,
    attn_block,
    wide_low,
    wide_two,
    turned_one,
    turned_two,
    branch,
    bias_up_sum,
    query_sum,
    value_sum,
    vec_land,
    load_sem,
    step_sem,
    pair_send,
    pair_recv,
    first_send,
    first_recv,
    second_send,
    second_recv,
    z_send,
    z_recv,
    vec_send,
    vec_recv,
):
    z, core, y, x, nz, side = place(ndp, nf)
    dp, fs = z * 2 + core, y * side + x
    other = (z * 2 + 1 - core, fs)
    held, outs = (held_up, held_down, held_attn), (up_out, down_out, attn_out)
    from_first, from_second = (first_up, first_down, first_attn), (second_up, second_down, second_attn)
    from_z = (z_up, z_down, z_attn)
    chunks = 3
    rows, width_ffn = held_up.shape[2:]
    width_attn = held_attn.shape[-1]
    width = ffn_weight.shape[-1]
    per = width_ffn // width
    greet(line_partners(ndp, nf))

    def place_of(turn):
        step = nf - 1 - turn
        return lax.rem(y + lax.div(step, side), side) * side + lax.rem(x + lax.rem(step, side), side)

    def first_copy(chunk, z_at, line, step):
        x_first = lax.rem(z_at, 2) == 0
        near, far = lax.rem(x + step, side), lax.rem(y + step, side)
        to = jnp.where(x_first, y * side + near, far * side + x)
        at = jnp.where(
            x_first,
            lax.rem(y + line, side) * side + near,
            far * side + lax.rem(x + line, side),
        )
        return remote(
            held[chunk].at[z_at, at],
            from_first[chunk].at[z_at, step - 1, line],
            first_send.at[chunk, z_at, step - 1, line],
            first_recv.at[chunk, z_at, step - 1, line],
            (dp, to),
        )

    lag = 2
    total_steps = nf * per + nf
    schedule = {}
    for sent, base, stride in (((0, 1), 0, per), ((2,), nf * per, 1)):
        for turns in ((0,), tuple(range(1, nf - 1))):
            ready = min(base + (turns[-1] + 1) * stride - 1 + lag, total_steps)
            for z_at in range(0, nz, 2):
                schedule.setdefault(ready, []).extend((chunk, turns, z_at) for chunk in sent)

    def send_first(chunk, turns, z_from):
        def each(z_at):
            x_first = lax.rem(z_at, 2) == 0
            for turn in turns:
                step_x, step_y = (nf - 1 - turn) % side, (nf - 1 - turn) // side
                step = jnp.where(x_first, step_x, step_y)
                line = jnp.where(x_first, step_y, step_x)

                @pl.when(step > 0)
                def _(line=line, step=step):
                    first_copy(chunk, z_at, line, step).start()

        loop(z_from + 2, each, z_from)

    def sends_at(step, steps):
        for when in steps:
            @pl.when(step == when)
            def _(when=when):
                for chunk, turns, z_at in schedule.get(when, ()):
                    send_first(chunk, turns, z_at)

    def line_place(z_at, line):
        x_first = lax.rem(z_at, 2) == 0
        return jnp.where(
            x_first, lax.rem(y + line, side) * side + x, y * side + lax.rem(x + line, side)
        )

    def second_copy(chunk, z_at, step):
        to = line_place(z_at, step)
        return remote(
            held[chunk].at[z_at, to],
            from_second[chunk].at[z_at, step - 1],
            second_send.at[chunk, z_at, step - 1],
            second_recv.at[chunk, z_at, step - 1],
            (dp, to),
        )

    def z_copy(chunk, step):
        z_at = lax.rem(z + step, nz)
        return remote(
            held[chunk].at[z_at, fs],
            from_z[chunk].at[step - 1],
            z_send.at[chunk, step - 1],
            z_recv.at[chunk, step - 1],
            (z_at * 2 + core, fs),
        )

    def take_first(chunk):
        def each(hop):
            z_at = lax.rem(z + 1 + hop, nz)
            for line in (*range(1, side), 0):
                at = line_place(z_at, line)
                for step in range(1, side):
                    first_copy(chunk, z_at, line, step).wait_recv()
                    held[chunk][z_at, at] += from_first[chunk][z_at, step - 1, line]
                if line:
                    second_copy(chunk, z_at, line).start()

        loop(nz, each)

    def take_second(chunk):
        def each(hop):
            z_at = lax.rem(z + 1 + hop, nz)
            for step in range(1, side):
                second_copy(chunk, z_at, step).wait_recv()
                held[chunk][z_at, fs] += from_second[chunk][z_at, step - 1]

            @pl.when(hop < nz - 1)
            def _():
                z_copy(chunk, hop + 1).start()

        loop(nz, each)

    def moments(chunk):
        source = ffn_mom.at[chunk] if chunk < 2 else attn_mom
        return pltpu.make_async_copy(source, outs[chunk], load_sem.at[3 + chunk])

    def take_z(chunk):
        total = held[chunk][z, fs].astype(jnp.float32)
        for step in range(1, nz):
            z_copy(chunk, step).wait_recv()
            total += from_z[chunk][step - 1].astype(jnp.float32)
        moments(chunk).wait()
        low = (matrix_decay * outs[chunk][...] + total).astype(jnp.bfloat16)
        outs[chunk][...] = total
        if chunk < 2:
            half = low.shape[1] // 2
            ffn_low[chunk, 0] = low[:, :half]
            ffn_low[chunk, 1] = low[:, half:]
        else:
            attn_low[...] = low

    vec_rounds = [[other]]
    vec_rounds.append([(dp, y * side + lax.rem(x + step, side)) for step in range(1, side)])
    vec_rounds.append([(dp, lax.rem(y + step, side) * side + x) for step in range(1, side)])
    vec_rounds.append([(lax.rem(z + step, nz) * 2 + core, fs) for step in range(1, nz)])
    starts = [sum(len(group) for group in vec_rounds[:index]) for index in range(4)]

    def vec_copy(index, step):
        at = starts[index] + step
        return remote(
            vec_land.at[index], vec_land.at[4 + at], vec_send.at[at], vec_recv.at[at], vec_rounds[index][step]
        )

    def vec_start(index):
        for step in range(len(vec_rounds[index])):
            vec_copy(index, step).start()

    def vec_take(index):
        total = vec_land[index]
        for step in range(len(vec_rounds[index])):
            vec_copy(index, step).wait_recv()
            total += vec_land[4 + starts[index] + step]
        if index < 3:
            vec_land[index + 1] = total
            vec_start(index + 1)
        else:
            vec_out[...] = total

    def split(values, keep, give):
        parts = values.astype(jnp.bfloat16).reshape(nz, 2, rows, values.shape[1])
        for which in range(2):
            @pl.when(core == which)
            def _(which=which):
                keep(parts[:, which])
                give(parts[:, 1 - which])

    def ffn_loads(slot, turn, part):
        block = place_of(turn)
        at = pl.ds(part * width, width)
        column = pl.ds(pl.multiple_of(block * width_ffn + part * width, width), width)
        pairs = (
            (up_ref.at[block, :, :, at], ffn_weight.at[slot, 0]),
            (down_ref.at[block, :, :, at], ffn_weight.at[slot, 1]),
            (active_ref.at[:, column], ffn_act.at[slot, 0]),
            (slope_ref.at[:, column], ffn_act.at[slot, 1]),
        )
        return [
            pltpu.make_async_copy(source, target, step_sem.at[slot, index])
            for index, (source, target) in enumerate(pairs)
        ]

    def load(index, source, target):
        return pltpu.make_async_copy(source, target, load_sem.at[index])

    load(0, low_ref, wide_low).start(priority=1)
    load(1, d_second_ref, input_grad).start(priority=1)
    for copy in ffn_loads(0, 0, 0):
        copy.start(priority=1)
    load(2, tokens_ref, wide_two).start(priority=1)
    for chunk in range(chunks):
        moments(chunk).start(priority=1)
    load(0, low_ref, wide_low).wait()
    turned_one[...] = jnp.transpose(wide_low[...])
    load(1, d_second_ref, input_grad).wait()
    wide_low[...] = input_grad[...].astype(jnp.bfloat16)
    turned_two[...] = jnp.transpose(wide_low[...])

    def pair_copy(step):
        stage, slot = lax.rem(step, lag), lax.rem(step, 2 * lag)
        return remote(stages_out.at[stage], land.at[slot], pair_send.at[stage], pair_recv.at[slot], other)

    def pair_take(step):
        pair_copy(step).wait()
        slot = lax.rem(step, 2 * lag)

        @pl.when(step < nf * per)
        def _():
            block, part = place_of(lax.div(step, per)), lax.rem(step, per)
            for index in range(2):
                for which in range(per):
                    @pl.when(part == which)
                    def _(index=index, which=which):
                        for half in range(2):
                            left = which * width + half * width_attn
                            at = slice(left, left + width_attn)
                            held[index][:, block, :, at] += land[slot, :, 2 * index + half]

        @pl.when(step >= nf * per)
        def _():
            held_attn[:, place_of(step - nf * per)] += land[slot]

    def ffn_turn(turn):
        block = place_of(turn)
        for part in range(per):
            now = turn * per + part
            slot = lax.rem(now, 2)
            if part < per - 1:
                for copy in ffn_loads(1 - slot, turn, part + 1):
                    copy.start(priority=1)
            else:
                @pl.when(turn < nf - 1)
                def _():
                    for copy in ffn_loads(1 - slot, turn + 1, 0):
                        copy.start(priority=1)

            for copy in ffn_loads(slot, turn, part):
                copy.wait()
            d_active = product(wide_low[...], flat(ffn_weight[slot, 1]))
            d_up = (d_active * ffn_act[slot, 1].astype(jnp.float32)).astype(jnp.bfloat16)
            bias_up_sum[block * per + part] = row_sum(d_up)
            input_grad[...] += contract_cols(d_up, flat(ffn_weight[slot, 0]))

            @pl.when(now >= lag)
            def _():
                pair_take(now - lag)

            sends_at(now, range(nf * per))
            at = slice(part * width, (part + 1) * width)
            for index in range(2):

                def keep(values, index=index):
                    held[index][:, block, :, at] = values

                def give(values, index=index):
                    for half in range(2):
                        side_at = slice(half * width_attn, (half + 1) * width_attn)
                        stages_out[lax.rem(now, lag), :, 2 * index + half] = values[:, :, side_at]

                if index == 0:
                    split(product(turned_one[...], d_up), keep, give)
                else:
                    split(product(turned_two[...], ffn_act[slot, 0]), keep, give)
            pair_copy(now).start()

    loop(nf, ffn_turn)

    load(2, tokens_ref, wide_two).wait()
    turned_one[...] = jnp.transpose(wide_two[...])
    load(0, mixture_ref, wide_two).start(priority=1)

    def attn_load(index, turn):
        block = place_of(turn)
        per_block = ndp // nf
        source, target = (
            (attn_ref.at[block, :, pl.ds(0, 3 * rows)], attn_weight[0]),
            (
                attn_ref.at[:, pl.ds(block * per_block, per_block), pl.ds(3 * rows, rows)],
                attn_weight[1],
            ),
            (blocks_ref.at[block], attn_block),
        )[index]
        return pltpu.make_async_copy(source, target, step_sem.at[0, index])

    for index in range(3):
        attn_load(index, 0).start(priority=1)
    vec_land[0] = jnp.zeros((16, D), jnp.float32)
    vec_land[0, 9:12] = tail_ref[0:3]

    def norm_back(index):
        at = pl.ds(pl.multiple_of(index * NORM_ROWS, NORM_ROWS), NORM_ROWS)
        grad = input_grad[at]
        scaled = scaled_ref[at]
        d_first = normalize_back(grad * vec_ref[3:4], scaled, inverse_ref[at])
        input_grad[at] = d_first
        low = d_first.astype(jnp.bfloat16)
        vec_land[0, 2:3] += row_sum(low)
        vec_land[0, 3:4] += row_sum(grad * scaled)
        vec_land[0, 4:5] += row_sum(grad)
        for column in range(nf):
            branch[column, at] = low[:, column * width_attn : (column + 1) * width_attn]

    loop(tokens_ref.shape[0] // NORM_ROWS, norm_back)
    label_row = label_ref[...].astype(jnp.float32)
    label_col = jnp.transpose(jnp.broadcast_to(label_row, (128, label_row.shape[1])))[:, 0:1]
    load(0, mixture_ref, wide_two).wait()
    turned_two[...] = jnp.transpose(wide_two[...])

    def attn_turn(turn):
        block = place_of(turn)
        now = nf * per + turn

        def load_next(index):
            @pl.when(turn < nf - 1)
            def _():
                attn_load(index, turn + 1).start(priority=1)

        for index in range(3):
            attn_load(index, turn).wait()
        count = tokens_ref.shape[0]
        zero = jnp.zeros((count, width_attn), jnp.float32)
        d_mixture = zero
        for index in range(nf):
            d_mixture += contract_cols(branch[index], flat(attn_weight[1][index]))
        load_next(1)
        d_mixture = d_mixture.astype(jnp.bfloat16)
        queries, keys_all, values_all = (attn_block[index] for index in range(3))
        allowed = label_col == label_row
        d_queries, d_keys, d_values = zero, zero, zero
        for head in range(width_attn // HDIM):
            my_queries = head_lanes(queries, head) * score_scale
            my_mixture = head_lanes(d_mixture, head)
            scores = contract_cols(keys_all, my_queries) - total_ref[block, head : head + 1, :]
            attention = jnp.where(allowed, jnp.exp(scores), 0.0)
            d_attention = contract_cols(values_all, my_mixture)
            inner = jnp.sum(d_attention * attention, axis=0, keepdims=True)
            d_scores = (attention * (d_attention - inner)).astype(jnp.bfloat16)
            d_keys += product(d_scores, my_queries)
            d_values += product(attention.astype(jnp.bfloat16), my_mixture)
            d_queries += contract_rows(d_scores, head_lanes(keys_all, head) * score_scale)
        load_next(2)
        grads = [values.astype(jnp.bfloat16) for values in (d_queries, d_keys, d_values)]
        query_sum[block] = row_sum(grads[0])
        value_sum[block] = row_sum(grads[2])
        moved = jnp.zeros((count, D), jnp.float32)
        for index in range(3):
            weight = attn_weight[0][:, index * rows : (index + 1) * rows]
            moved += contract_cols(grads[index], flat(weight))
        input_grad[...] += moved
        load_next(0)

        pair_take(now - lag)
        for index in range(4):
            turned, grad = (turned_one, grads[index]) if index < 3 else (turned_two, branch[block])

            def keep(values, index=index):
                held_attn[:, block, index] = values

            def give(values, index=index):
                stages_out[lax.rem(now, lag), :, index] = values

            split(product(turned[...], grad), keep, give)
        pair_copy(now).start()
        sends_at(now, range(nf * per, total_steps))

        @pl.when(turn == nf - 3)
        def _():
            take_first(0)
            take_first(1)

        @pl.when(turn == nf - 2)
        def _():
            take_second(0)
            take_second(1)

    loop(nf, attn_turn)
    for index in range(nf):
        at = slice(index * width_attn, (index + 1) * width_attn)
        vec_land[0, 0:1, at] = query_sum[index]
        vec_land[0, 1:2, at] = value_sum[index]
    for index in range(nf * per):
        left = index * width
        vec_land[0, 5 + left // D : 6 + left // D, left % D : left % D + width] = bias_up_sum[index]
    vec_start(0)
    for step in range(total_steps - lag, total_steps):
        pair_take(step)
    sends_at(total_steps, (total_steps,))

    vec_take(0)
    take_first(2)
    vec_take(1)
    take_z(0)
    take_second(2)
    vec_take(2)
    take_z(1)
    vec_take(3)
    take_z(2)

    for chunk in range(chunks):

        def finish(z_at):
            for step in range(1, side):
                second_copy(chunk, z_at, step).wait_send()
                for line in range(side):
                    first_copy(chunk, z_at, line, step).wait_send()

        loop(nz, finish)
        for step in range(1, nz):
            z_copy(chunk, step).wait_send()
    for index in range(4):
        for step in range(len(vec_rounds[index])):
            vec_copy(index, step).wait_send()


def backward_kernel_entry(ndp, nf, *refs):
    at = 18 + 7 + 12 + 2 + 2
    backward_kernel(ndp, nf, *refs[:at], refs[at : at + 2], *refs[at + 2 :])


def backward(
    ndp, nf, d_second, low, scaled, inverse, vectors, active, slope, up_all, down_all,
    tokens, segments, blocks, mixture, totals, attn_all, tail_sums, attn_mom, ffn_mom,
):
    nz, side = ndp // 2, math.isqrt(nf)
    count = tokens.shape[0]
    rows, width_ffn = up_all.shape[2:]
    width_attn = attn_all.shape[-1]
    width = 2 * width_attn
    bf16, f32 = jnp.bfloat16, jnp.float32
    dma = pltpu.SemaphoreType.DMA
    anywhere, inside = pl.BlockSpec(memory_space=pl.ANY), pl.BlockSpec(memory_space=pltpu.VMEM)
    shapes = [(rows, width_ffn), (rows, width_ffn), (4, rows, width_attn)]
    vec_copies = 1 + 2 * (side - 1) + nz - 1
    sums = []
    for lead in ((nz, nf), (nz, side - 1, side), (nz, side - 1), (nz - 1,)):
        sums += [pltpu.VMEM(lead + shape, bf16) for shape in shapes]
    return pl.pallas_call(
        functools.partial(backward_kernel_entry, ndp, nf),
        name="backward",
        out_shape=[jax.ShapeDtypeStruct((count, D), f32)]
        + [jax.ShapeDtypeStruct(shape, f32) for shape in shapes]
        + [
            jax.ShapeDtypeStruct((16, D), f32),
            jax.ShapeDtypeStruct(attn_mom.shape, bf16),
            jax.ShapeDtypeStruct((2, 2, rows, width_ffn // 2), bf16),
        ],
        in_specs=[
            anywhere,
            anywhere,
            inside,
            inside,
            inside,
            anywhere,
            anywhere,
            anywhere,
            anywhere,
            anywhere,
            inside,
            anywhere,
            anywhere,
            inside,
            anywhere,
            inside,
            anywhere,
            anywhere,
        ],
        out_specs=[inside] * 7,
        scratch_shapes=sums
        + [
            pltpu.VMEM((2, nz, 4, rows, width_attn), bf16),
            pltpu.VMEM((4, nz, 4, rows, width_attn), bf16),
            pltpu.VMEM((2, 2, ndp, rows, width), bf16),
            pltpu.VMEM((2, 2, count, width), bf16),
            pltpu.VMEM((ndp, 3 * rows, width_attn), bf16),
            pltpu.VMEM((nf, ndp // nf, rows, width_attn), bf16),
            pltpu.VMEM((3, count, width_attn), bf16),
            pltpu.VMEM((count, D), bf16),
            pltpu.VMEM((count, D), bf16),
            pltpu.VMEM((D, count), bf16),
            pltpu.VMEM((D, count), bf16),
            pltpu.VMEM((nf, count, width_attn), bf16),
            pltpu.VMEM((FF // width, 1, width), f32),
            pltpu.VMEM((nf, 1, width_attn), f32),
            pltpu.VMEM((nf, 1, width_attn), f32),
            pltpu.VMEM((4 + vec_copies, 16, D), f32),
            dma((6,)),
            dma((2, 4)),
            dma((2,)),
            dma((4,)),
            dma((3, nz, side - 1, side)),
            dma((3, nz, side - 1, side)),
            dma((3, nz, side - 1)),
            dma((3, nz, side - 1)),
            dma((3, nz - 1)),
            dma((3, nz - 1)),
            dma((vec_copies,)),
            dma((vec_copies,)),
        ],
        compiler_params=pltpu.CompilerParams(
            collective_id=3, has_side_effects=True, vmem_limit_bytes=63 * 1024 * 1024
        ),
    )(
        d_second, low, scaled, inverse, vectors, active, slope, up_all, down_all,
        tokens, segments[None, :], blocks, mixture, totals, attn_all, tail_sums, attn_mom, ffn_mom,
    )


def on_device(
    tokens,
    segments,
    cotangent,
    attn_w,
    ffn_w,
    vectors,
    attn_mom,
    ffn_mom,
    vec_mom,
    attn_ema,
    ffn_ema,
    vec_ema,
):
    ndp, nf = lax.axis_size("dp"), lax.axis_size("fsdp")
    share = vectors.shape[1]
    (
        attn_all, up_all, down_all, blocks, active, slope, vec_full, mixture, totals, scaled, inverse, low,
        layer_out, d_second, tail_sums,
    ) = forward(ndp, nf, tokens, segments, cotangent, attn_w, ffn_w, vectors)
    input_grad, up_grad, down_grad, attn_grad, vec_sum, attn_piece, ffn_piece = backward(
        ndp, nf, d_second, low, scaled, inverse, vec_full, active, slope, up_all, down_all,
        tokens, segments, blocks, mixture, totals, attn_all, tail_sums, attn_mom, ffn_mom,
    )
    mine = (lax.axis_index("dp") * nf + lax.axis_index("fsdp")) * share
    vec_grad = lax.dynamic_slice(vec_sum, (0, mine), (12, share))
    attn_ortho, ffn_ortho = orthogonalize(ndp, nf, attn_piece, ffn_piece)
    total_tokens = tokens.shape[0] * ndp * nf
    updated = update_all(
        vector_step / math.sqrt(total_tokens),
        attn_w,
        ffn_w,
        vectors,
        attn_mom,
        ffn_mom,
        vec_mom,
        attn_ema,
        ffn_ema,
        vec_ema,
        attn_grad,
        up_grad,
        down_grad,
        vec_grad,
        attn_ortho,
        ffn_ortho,
    )
    return (layer_out, input_grad, *updated, vec_grad[2])


def solution(mesh):
    in_specs = (
        P(("dp", "fsdp"), None),
        P(("dp", "fsdp")),
        P(("dp", "fsdp"), None),
        P(None, "dp", "fsdp"),
        P(None, "dp", "fsdp"),
        P(None, ("dp", "fsdp")),
        P(None, "dp", "fsdp"),
        P(None, "dp", "fsdp"),
        P(None, ("dp", "fsdp")),
        P(None, "dp", "fsdp"),
        P(None, "dp", "fsdp"),
        P(None, ("dp", "fsdp")),
    )
    out_specs = (
        P(("dp", "fsdp"), None),
        P(("dp", "fsdp"), None),
        P(None, "dp", "fsdp"),
        P(None, "dp", "fsdp"),
        P(None, ("dp", "fsdp")),
        P(None, "dp", "fsdp"),
        P(None, "dp", "fsdp"),
        P(None, ("dp", "fsdp")),
        P(None, "dp", "fsdp"),
        P(None, "dp", "fsdp"),
        P(None, ("dp", "fsdp")),
        P(("dp", "fsdp")),
    )
    return jax.shard_map(
        on_device, mesh=mesh, in_specs=in_specs, out_specs=out_specs, check_vma=False
    )
```

```python
import functools
import math

import jax
import jax.numpy as jnp
from jax import lax
from jax.experimental import pallas as pl
from jax.experimental.pallas import tpu as pltpu
from jax.sharding import PartitionSpec as P

D = 1024
FF = 4096
HEADS = 16
HDIM = 64
TILE = 512
ITERS = 5


score_scale = 0.125
ln_epsilon = 1e-05
norm_epsilon = 1e-06
ns_linear = 3.4445
ns_square = -4.775
ns_cubic = 2.0315
matrix_decay = 0.95
vector_decay = 0.9
average_decay = 0.7
weight_decay = 0.01
attn_rates = (1.0, 1.0, 1.0, 10.0)
vector_step = 0.3


def product(left, right):
    return jnp.dot(left, right, preferred_element_type=jnp.float32)


def contract_rows(left, right):
    return lax.dot_general(
        left, right, (((0,), (0,)), ((), ())), preferred_element_type=jnp.float32
    )


def contract_cols(left, right):
    return lax.dot_general(
        left, right, (((1,), (1,)), ((), ())), preferred_element_type=jnp.float32
    )


MESH = pl.DeviceIdType.MESH
ROLES = 8
STEP_ROWS = 512
NORM_ROWS = 128
TILE_ROWS = 128


def greet(partners):
    barrier = pltpu.get_barrier_semaphore()
    for partner in partners:
        pl.semaphore_signal(barrier, inc=1, device_id=partner, device_id_type=MESH)
    pl.semaphore_wait(barrier, len(partners))


def place(ndp, nf):
    dp, fs = lax.axis_index("dp"), lax.axis_index("fsdp")
    side = math.isqrt(nf)
    return lax.div(dp, 2), lax.rem(dp, 2), lax.div(fs, side), lax.rem(fs, side), ndp // 2, side


def line_partners(ndp, nf):
    z, core, y, x, nz, side = place(ndp, nf)
    mine = y * side + x
    return (
        [(z * 2 + 1 - core, mine)]
        + [(lax.rem(z + step, nz) * 2 + core, mine) for step in range(1, nz)]
        + [(z * 2 + core, y * side + lax.rem(x + step, side)) for step in range(1, side)]
        + [(z * 2 + core, lax.rem(y + step, side) * side + x) for step in range(1, side)]
    )


def remote(source, target, send_sem, recv_sem, device):
    return pltpu.make_async_remote_copy(
        src_ref=source,
        dst_ref=target,
        send_sem=send_sem,
        recv_sem=recv_sem,
        device_id=device,
        device_id_type=MESH,
    )


def loop(count, body, start=0):
    def step(index, carry):
        body(index)
        return carry

    lax.fori_loop(start, count, step, 0)


def ortho_kernel(
    ndp,
    nf,
    attn_ref,
    ffn_ref,
    attn_out,
    ffn_out,
    land_attn,
    land_ffn,
    iter_low,
    iter_full,
    gram,
    gram_send,
    gram_recv,
    off_low,
    poly_low,
    diag_row,
    diag_col,
    inverse_norm,
    own_low,
    own_full,
    own_attn,
    own_ffn,
    own_sem,
    piece_send,
    piece_recv,
    first_send,
    second_send,
    plane_recv,
    gram_send_sem,
    gram_recv_sem,
    back_send,
    back_recv,
):
    z, core, y, x, nz, side = place(ndp, nf)
    dp, fs = z * 2 + core, y * side + x
    rows = attn_ref.shape[1]
    size = rows * ndp
    is_attn = jnp.logical_or(dp < 2, jnp.logical_and(dp >= 6, dp < ROLES))
    is_ffn = jnp.logical_and(dp >= 2, dp < 6)
    partner = z * 2 + 1 - core

    greet(
        [(lax.rem(dp + step, ndp), fs) for step in range(1, ndp)]
        + [(dp, y * side + lax.rem(x + step, side)) for step in range(1, side)]
        + [(dp, lax.rem(y + step, side) * side + x) for step in range(1, side)]
    )

    def piece(role):
        if role < 2 or role >= 6:
            return attn_ref.at[role if role < 2 else role - 4], land_attn
        return ffn_ref.at[(role - 2) // 2, (role - 2) % 2], land_ffn

    def piece_copy(role):
        source, land = piece(role)
        return remote(source, land.at[fs, dp], piece_send.at[role], piece_recv.at[dp], (role, fs))

    for role in (2, 4, 3, 5, 0, 6, 1, 7):
        @pl.when(dp != role)
        def _(role=role):
            piece_copy(role).start()

        @pl.when(dp == role)
        def _(role=role):
            source, land = piece(role)
            pltpu.make_async_copy(source, land.at[fs, dp], own_sem).start()

    def along(first, step):
        x_at = jnp.where(first, lax.rem(x + step, side), x)
        y_at = jnp.where(first, y, lax.rem(y + step, side))
        return y_at * side + x_at

    def iterate(land, source, own_out, target, role, paired):
        width = land.shape[-1]
        columns = width * nf
        tall = min(STEP_ROWS, size)
        steps = size // tall
        wide = min(1024, columns)

        def row_of(index):
            return lax.rem(z + index // 2, nz) * 2 + lax.rem(core + index, 2)

        def x_first(row):
            return lax.rem(row // 2, 2) == 0

        def first_copy(row, step):
            here = land.at[fs, row]
            peer = along(x_first(row), step)
            return remote(here, here, first_send.at[row, step - 1], plane_recv.at[fs, row], (dp, peer))

        def second_copy(plane_at, row, line, step):
            here = land.at[plane_at, row]
            peer = along(jnp.logical_not(x_first(row)), step)
            return remote(
                here, here, second_send.at[row, line, step - 1], plane_recv.at[plane_at, row], (dp, peer)
            )

        def arrived(plane_at, row):
            here = land.at[plane_at, row]
            remote(here, here, own_sem, plane_recv.at[plane_at, row], (dp, fs)).wait_recv()

        def take_piece(index):
            row = row_of(index)

            @pl.when(index == 0)
            def _():
                pltpu.make_async_copy(source, land.at[fs, row], own_sem).wait()

            @pl.when(index > 0)
            def _():
                remote(source, land.at[fs, row], own_sem, piece_recv.at[row], (dp, fs)).wait_recv()

            for step in range(1, side):
                first_copy(row, step).start()
                second_copy(fs, row, 0, step).start()

        loop(ndp, take_piece)

        def pass_on(index):
            row = row_of(index)
            for line in range(1, side):
                plane_at = along(x_first(row), line)
                arrived(plane_at, row)
                for step in range(1, side):
                    second_copy(plane_at, row, line, step).start()

        def add_gram(plane_at, fresh):
            block = land[plane_at].reshape(size, width)
            for step in range(steps):
                at = slice(step * tall, (step + 1) * tall)
                part = contract_cols(block[at], block)
                if fresh:
                    gram[at] = part
                else:
                    gram[at] += part

        add_gram(fs, True)
        loop(ndp, pass_on)

        for line in range(side):
            for step in range(1, side):

                def last(index, line=line, step=step):
                    row = row_of(index)
                    near = jnp.where(
                        x_first(row),
                        lax.rem(y + step, side) * side + lax.rem(x + line, side),
                        lax.rem(y + line, side) * side + lax.rem(x + step, side),
                    )
                    arrived(near, row)

                loop(ndp, last)
            if line == 0:
                for step in range(1, side):
                    add_gram(along(True, step), False)
                    add_gram(along(False, step), False)
        for far_y in range(1, side):
            for far_x in range(1, side):
                add_gram(lax.rem(y + far_y, side) * side + lax.rem(x + far_x, side), False)

        def gram_copy(slot, step):
            at = pl.ds(step * tall, tall)
            return remote(
                gram_send.at[slot, at],
                gram_recv.at[slot, at],
                gram_send_sem.at[slot, step],
                gram_recv_sem.at[slot, step],
                (partner, fs),
            )

        if paired:
            for step in range(steps):
                at = slice(step * tall, (step + 1) * tall)
                gram_send[0, at] = gram[at].astype(jnp.bfloat16)
                gram_copy(0, step).start()
        for index in range(nf):
            block = land[index].reshape(size, width)
            at = slice(index * width, (index + 1) * width)
            iter_low[0, :, at] = block
            iter_full[:, at] = block.astype(jnp.float32)

        def back_copy(row):
            return remote(own_out.at[row], target, back_send.at[row], back_recv.at[role], (row, fs))

        def iteration(count):
            now = lax.rem(count, 2)
            later = 1 - now

            @pl.when(count > 0)
            def _():
                def gram_rows(step):
                    at = pl.ds(pl.multiple_of(step * tall, tall), tall)
                    part = contract_cols(iter_low[now, at, :columns], iter_low[now, :, :columns])
                    if paired:
                        gram_send[now, at] = part.astype(jnp.bfloat16)
                        gram_copy(now, step).start()
                    else:
                        gram[at] = part

                loop(steps, gram_rows)

            eye = lax.broadcasted_iota(jnp.int32, (TILE_ROWS, TILE_ROWS), 0) == lax.broadcasted_iota(
                jnp.int32, (TILE_ROWS, TILE_ROWS), 1
            )

            @pl.when(count == 0)
            def _():
                trace = jnp.zeros((TILE_ROWS, TILE_ROWS), jnp.float32)
                if paired:
                    for step in range(steps):
                        gram_copy(now, step).wait()
                for tile in range(size // TILE_ROWS):
                    at = slice(tile * TILE_ROWS, (tile + 1) * TILE_ROWS)
                    if paired:
                        square = gram_send[now, at, at].astype(jnp.float32)
                        trace += square + gram_recv[now, at, at].astype(jnp.float32)
                    else:
                        trace += gram[at, at]
                trace = jnp.sum(jnp.where(eye, trace, 0.0), axis=1, keepdims=True)
                trace = jnp.sum(trace, axis=0, keepdims=True)
                inverse_norm[...] = 1.0 / (jnp.sqrt(trace) + norm_epsilon)

            @pl.when(count > 0)
            def _():
                inverse_norm[...] = jnp.ones_like(inverse_norm)

            inverse = inverse_norm[...]
            shrink = inverse * inverse

            for step in range(steps):
                if paired:
                    @pl.when(count > 0)
                    def _(step=step):
                        gram_copy(now, step).wait()

                for tile in range(step * tall // TILE_ROWS, (step + 1) * tall // TILE_ROWS):
                    at = slice(tile * TILE_ROWS, (tile + 1) * TILE_ROWS)
                    if paired:
                        total = gram_send[now, at].astype(jnp.float32) + gram_recv[now, at].astype(jnp.float32)
                    else:
                        total = gram[at]
                    total = total * shrink
                    gram[at] = total
                    off_low[at] = total.astype(jnp.bfloat16)
                    square = total[:, at]
                    masked = jnp.where(eye, square, 0.0)
                    diag_col[at] = jnp.sum(masked, axis=1, keepdims=True)
                    diag_row[:, at] = jnp.sum(masked, axis=0, keepdims=True)
                    square = jnp.where(eye, 0.0, square)
                    gram[at, at] = square
                    off_low[at, at] = square.astype(jnp.bfloat16)

            linear, middle, cubic = ns_linear * inverse, ns_square * inverse, ns_cubic * inverse

            def poly_rows(step):
                at = pl.ds(step * tall, tall)
                again = product(off_low[at], off_low[...])
                mine = diag_col[at]
                poly = gram[at] * (middle + cubic * mine + cubic * diag_row[...]) + cubic * again
                poly_low[at] = poly.astype(jnp.bfloat16)
                again_diag = []
                for tile in range(tall // TILE_ROWS):
                    rows_at = slice(tile * TILE_ROWS, (tile + 1) * TILE_ROWS)
                    side_at = slice(step * tall + tile * TILE_ROWS, step * tall + (tile + 1) * TILE_ROWS)
                    again_diag.append(
                        jnp.sum(jnp.where(eye, again[rows_at, side_at], 0.0), axis=1, keepdims=True)
                    )
                    poly_low[side_at, side_at] = jnp.where(eye, 0.0, poly[rows_at, side_at]).astype(jnp.bfloat16)
                again_diag = jnp.concatenate(again_diag, axis=0)
                factor = linear + middle * mine + cubic * (mine * mine + again_diag)

                @pl.when(count < ITERS - 1)
                def _():
                    for left in range(0, columns, wide):
                        part = slice(left, left + wide)
                        moved = product(poly_low[at], iter_low[now, :, part])
                        fresh = factor * iter_full[at, part] + moved
                        iter_full[at, part] = fresh
                        iter_low[later, at, part] = fresh.astype(jnp.bfloat16)

                @pl.when(count == ITERS - 1)
                def _():
                    for index in range(nf):
                        @pl.when(fs == index)
                        def _(index=index):
                            part = slice(index * width, (index + 1) * width)
                            own_full[at, :width] = iter_full[at, part]

                            if step == 0:
                                own_low[:, :width] = iter_low[now, :, part]

                    moved = product(poly_low[at], own_low[:, :width])
                    fresh = factor * own_full[at, :width] + moved
                    blocks = tall // rows
                    own_out[pl.ds(step * blocks, blocks)] = fresh.astype(jnp.bfloat16).reshape(
                        blocks, rows, width
                    )

                    def give(index):
                        row = step * blocks + index

                        @pl.when(row != dp)
                        def _():
                            back_copy(row).start()

                        @pl.when(row == dp)
                        def _():
                            pltpu.make_async_copy(own_out.at[row], target, own_sem).start()

                    loop(blocks, give)

            for step in range(steps):
                poly_rows(step)

        loop(ITERS, iteration)

        def finish(row):
            for step in range(1, side):
                first_copy(row, step).wait_send()
                for line in range(side):
                    second_copy(fs, row, line, step).wait_send()

            @pl.when(row != dp)
            def _():
                back_copy(row).wait_send()

        loop(ndp, finish)
        pltpu.make_async_copy(own_out.at[dp], target, own_sem).wait()

    @pl.when(is_attn)
    def _():
        at = jnp.where(dp < 2, dp, dp - 4)
        iterate(land_attn, attn_ref.at[at], own_attn, attn_out.at[at], dp, False)

    @pl.when(is_ffn)
    def _():
        matrix, half = (dp - 2) // 2, lax.rem(dp - 2, 2)
        iterate(land_ffn, ffn_ref.at[matrix, half], own_ffn, ffn_out.at[matrix, half], dp, True)

    for role in range(ROLES):
        @pl.when(dp != role)
        def _(role=role):
            if role < 2 or role >= 6:
                target = attn_out.at[role if role < 2 else role - 4]
            else:
                target = ffn_out.at[(role - 2) // 2, (role - 2) % 2]
            piece_copy(role).wait_send()
            remote(target, target, own_sem, back_recv.at[role], (role, fs)).wait_recv()


def orthogonalize(ndp, nf, attn_low, ffn_low):
    rows, width_attn = attn_low.shape[1:]
    width_ffn = ffn_low.shape[3]
    side = math.isqrt(nf)
    size = rows * ndp
    columns = width_ffn * nf
    tall = min(STEP_ROWS, size)
    bf16, f32 = jnp.bfloat16, jnp.float32
    dma = pltpu.SemaphoreType.DMA
    return pl.pallas_call(
        functools.partial(ortho_kernel, ndp, nf),
        name="newton_schulz",
        out_shape=[
            jax.ShapeDtypeStruct(attn_low.shape, bf16),
            jax.ShapeDtypeStruct(ffn_low.shape, bf16),
        ],
        in_specs=[pl.BlockSpec(memory_space=pltpu.VMEM)] * 2,
        out_specs=[pl.BlockSpec(memory_space=pltpu.VMEM)] * 2,
        scratch_shapes=[
            pltpu.VMEM((nf, ndp, rows, width_attn), bf16),
            pltpu.VMEM((nf, ndp, rows, width_ffn), bf16),
            pltpu.VMEM((2, size, columns), bf16),
            pltpu.VMEM((size, columns), f32),
            pltpu.VMEM((size, size), f32),
            pltpu.VMEM((2, size, size), bf16),
            pltpu.VMEM((2, size, size), bf16),
            pltpu.VMEM((size, size), bf16),
            pltpu.VMEM((size, size), bf16),
            pltpu.VMEM((1, size), f32),
            pltpu.VMEM((size, 1), f32),
            pltpu.VMEM((1, 1), f32),
            pltpu.VMEM((size, width_ffn), bf16),
            pltpu.VMEM((size, width_ffn), f32),
            pltpu.VMEM((ndp, rows, width_attn), bf16),
            pltpu.VMEM((ndp, rows, width_ffn), bf16),
            dma,
            dma((ROLES,)),
            dma((ndp,)),
            dma((ndp, side - 1)),
            dma((ndp, side, side - 1)),
            dma((nf, ndp)),
            dma((2, size // tall)),
            dma((2, size // tall)),
            dma((ndp,)),
            dma((ROLES,)),
        ],
        compiler_params=pltpu.CompilerParams(
            collective_id=1, has_side_effects=True, vmem_limit_bytes=60 * 1024 * 1024
        ),
    )(attn_low, ffn_low)


def update_kernel(
    attn_w,
    ffn_w,
    vectors,
    attn_mom,
    ffn_mom,
    vec_mom,
    attn_ema,
    ffn_ema,
    vec_ema,
    attn_grad,
    up_grad,
    down_grad,
    vec_grad,
    attn_ortho,
    ffn_ortho,
    attn_new,
    ffn_new,
    vec_new,
    attn_mom_new,
    ffn_mom_new,
    vec_mom_new,
    attn_ema_new,
    ffn_ema_new,
    vec_ema_new,
    *,
    vector_rate,
):
    for index in range(4):
        rate = attn_rates[index]
        attn_mom_new[index] = matrix_decay * attn_mom[index] + attn_grad[index]
        new = attn_w[index] * (1.0 - weight_decay * rate) - rate * attn_ortho[index].astype(jnp.float32)
        attn_new[index] = new
        attn_ema_new[index] = average_decay * attn_ema[index] + (1.0 - average_decay) * new
    width = ffn_ortho.shape[-1]
    shape_factor = math.sqrt(FF / D)
    for index, grad in enumerate((up_grad, down_grad)):
        ffn_mom_new[index] = matrix_decay * ffn_mom[index] + grad[...]
        for half in range(2):
            at = slice(half * width, (half + 1) * width)
            ortho = ffn_ortho[index, half].astype(jnp.float32)
            new = ffn_w[index, :, at] * (1.0 - weight_decay) - shape_factor * ortho
            ffn_new[index, :, at] = new
            ffn_ema_new[index, :, at] = average_decay * ffn_ema[index, :, at] + (1.0 - average_decay) * new
    mom = vector_decay * vec_mom[...] + vec_grad[...]
    vec_mom_new[...] = mom
    new = vectors[...] - vector_rate * mom
    vec_new[...] = new
    vec_ema_new[...] = average_decay * vec_ema[...] + (1.0 - average_decay) * new


def update_all(vector_rate, *operands):
    states = operands[:9]
    return pl.pallas_call(
        functools.partial(update_kernel, vector_rate=vector_rate),
        name="update",
        out_shape=[jax.ShapeDtypeStruct(states[index % 3].shape, jnp.float32) for index in range(9)],
        in_specs=[pl.BlockSpec(memory_space=pltpu.VMEM)] * len(operands),
        out_specs=[pl.BlockSpec(memory_space=pltpu.VMEM)] * 9,
        compiler_params=pltpu.CompilerParams(vmem_limit_bytes=60 * 1024 * 1024),
    )(*operands)


ROOM = pltpu.CompilerParams(vmem_limit_bytes=56 * 1024 * 1024)
ROOT_HALF = math.sqrt(0.5)
BELL = 1.0 / math.sqrt(2.0 * math.pi)


def flat(block):
    return block.reshape(-1, block.shape[-1])


def head_lanes(values, head):
    if values.shape[1] == HDIM:
        return values
    lane = lax.broadcasted_iota(jnp.int32, values.shape, 1)
    return jnp.where(lax.div(lane, HDIM) == head, values, jnp.zeros_like(values))


def normalize(values):
    center = values - jnp.mean(values, axis=1, keepdims=True)
    inverse = lax.rsqrt(jnp.mean(center * center, axis=1, keepdims=True) + ln_epsilon)
    return center * inverse, inverse


def normalize_back(grad, scaled, inverse):
    return inverse * (
        grad
        - jnp.mean(grad, axis=1, keepdims=True)
        - scaled * jnp.mean(grad * scaled, axis=1, keepdims=True)
    )


def row_sum(values):
    return jnp.sum(values.astype(jnp.float32), axis=0, keepdims=True)


def forward_kernel(
    ndp,
    nf,
    tokens_ref,
    label_ref,
    cotangent_ref,
    attn_w,
    ffn_w,
    vectors_ref,
    attn_out,
    up_out,
    down_out,
    blocks_out,
    active_out,
    slope_out,
    vec_out,
    mixture_out,
    total_out,
    scaled_out,
    inverse_out,
    low_out,
    layer_out,
    d_second_out,
    sums_out,
    attn_shard,
    up_shard,
    down_shard,
    three_weight,
    out_weight,
    ffn_weight,
    vec_land,
    bias,
    bias_up,
    blocks,
    parts,
    active,
    slope,
    total,
    own_sem,
    own_recv,
    pair_recv,
    z_send,
    first_send,
    second_send,
    pair_send,
    load_sem,
    store_sem,
):
    chunks = 3
    shards, wholes = (attn_shard, up_shard, down_shard), (attn_out, up_out, down_out)
    z, core, y, x, nz, side = place(ndp, nf)
    dp, fs = z * 2 + core, y * side + x
    rows, width_attn = attn_w.shape[1:]
    width_ffn, share = ffn_w.shape[2], vectors_ref.shape[1]
    count = tokens_ref.shape[0]
    width = ffn_weight.shape[-1]
    per = width_ffn // width

    attn_shard[4 * rows :] = jnp.zeros((16, width_attn), jnp.bfloat16)
    attn_shard[4 * rows : 4 * rows + 12, :share] = vectors_ref[...].astype(jnp.bfloat16)
    for index in range(4):
        attn_shard[index * rows : (index + 1) * rows] = attn_w[index].astype(jnp.bfloat16)
    up_shard[...] = ffn_w[0].astype(jnp.bfloat16)
    down_shard[...] = ffn_w[1].astype(jnp.bfloat16)
    greet(line_partners(ndp, nf))

    def slot(chunk, plane_at, z_at):
        return wholes[chunk].at[plane_at, z_at * 2 + core]

    def source(chunk, plane_at, z_at, own):
        return shards[chunk] if own else slot(chunk, plane_at, z_at)

    def along(first, step):
        x_at = jnp.where(first, lax.rem(x + step, side), x)
        y_at = jnp.where(first, y, lax.rem(y + step, side))
        return y_at * side + x_at

    def first_copy(chunk, z_at, step, own):
        peer = along(lax.rem(z_at, 2) == 0, step)
        return remote(
            source(chunk, fs, z_at, own),
            slot(chunk, fs, z_at),
            first_send.at[chunk, z_at, step - 1],
            own_recv.at[chunk, fs, z_at],
            (dp, peer),
        )

    def second_copy(chunk, plane_at, z_at, step, own, line):
        peer = along(lax.rem(z_at, 2) != 0, step)
        return remote(
            source(chunk, plane_at, z_at, own),
            slot(chunk, plane_at, z_at),
            second_send.at[chunk, z_at, line, step - 1],
            own_recv.at[chunk, plane_at, z_at],
            (dp, peer),
        )

    def pair_copy(chunk, plane_at, z_at, own):
        return remote(
            source(chunk, plane_at, z_at, own),
            slot(chunk, plane_at, z_at),
            pair_send.at[chunk, plane_at, z_at],
            pair_recv.at[chunk, plane_at, z_at],
            (z * 2 + 1 - core, fs),
        )

    def z_copy(chunk, z_at, up, own):
        return remote(
            source(chunk, fs, z_at, own),
            slot(chunk, fs, z_at),
            z_send.at[chunk, z_at, up],
            own_recv.at[chunk, fs, z_at],
            ((z + (1 if up else -1)) * 2 + core, fs),
        )

    def along_z(chunk, z_at, own, act):
        @pl.when(jnp.logical_and(z_at <= z, z < nz - 1))
        def _():
            act(z_copy(chunk, z_at, 1, own))

        @pl.when(jnp.logical_and(z_at >= z, z > 0))
        def _():
            act(z_copy(chunk, z_at, 0, own))

    def arrived(chunk, plane_at, z_at):
        here = slot(chunk, plane_at, z_at)
        remote(here, here, own_sem.at[chunk], own_recv.at[chunk, plane_at, z_at], (dp, fs)).wait_recv()

    def pass_on(chunk, z_at, own):
        for step in range(1, side):
            first_copy(chunk, z_at, step, own).start()
            second_copy(chunk, fs, z_at, step, own, 0).start()
        pair_copy(chunk, fs, z_at, own).start()

    def own_copy(chunk):
        return pltpu.make_async_copy(shards[chunk], slot(chunk, fs, z), own_sem.at[chunk])

    def near_first(body):
        def each(index):
            far = 1 + lax.div(index, 2)
            z_at = jnp.where(lax.rem(index, 2) == 0, z - far, z + far)

            @pl.when(jnp.logical_and(z_at >= 0, z_at < nz))
            def _():
                body(z_at)

        loop(2 * (nz - 1), each)

    def from_z(chunk):
        def each(z_at):
            arrived(chunk, fs, z_at)
            along_z(chunk, z_at, False, lambda copy: copy.start())
            pass_on(chunk, z_at, False)

        near_first(each)

    def from_first(chunk):
        def each(z_at):
            for line in range(1, side):
                plane_at = along(lax.rem(z_at, 2) == 0, line)
                arrived(chunk, plane_at, z_at)
                for step in range(1, side):
                    second_copy(chunk, plane_at, z_at, step, False, line).start()
                pair_copy(chunk, plane_at, z_at, False).start()

        each(z)
        near_first(each)

    def last_places(z_at):
        x_first = lax.rem(z_at, 2) == 0
        for line in range(side):
            for step in range(1, side):
                near_x, far_y = lax.rem(x + line, side), lax.rem(y + step, side)
                far_x, near_y = lax.rem(x + step, side), lax.rem(y + line, side)
                yield jnp.where(x_first, far_y * side + near_x, near_y * side + far_x)

    def from_second(chunk):
        def each(z_at):
            for plane_at in last_places(z_at):
                arrived(chunk, plane_at, z_at)
                pair_copy(chunk, plane_at, z_at, False).start()

        each(z)
        near_first(each)

    def from_pair(chunk):
        own_copy(chunk).wait()

        def each(index):
            plane_at, z_at = lax.rem(index, nf), lax.div(index, nf)
            there = wholes[chunk].at[plane_at, z_at * 2 + 1 - core]
            remote(
                there, there, own_sem.at[chunk], pair_recv.at[chunk, plane_at, z_at], (dp, fs)
            ).wait_recv()

        loop(nf * nz, each)

    for chunk in range(chunks):
        own_copy(chunk).start(priority=1)
        along_z(chunk, z, True, lambda copy: copy.start())
        pass_on(chunk, z, True)

    from_z(0)
    from_first(0)
    from_z(1)
    from_second(0)
    from_pair(0)

    def load(index, source, target):
        return pltpu.make_async_copy(source, target, load_sem.at[index])

    def attn_load(index, block, at):
        per_block = ndp // nf
        if index == 0:
            return load(at, attn_out.at[block, :, pl.ds(0, 3 * rows)], three_weight.at[at])
        return load(
            2 + at,
            attn_out.at[:, pl.ds(block * per_block, per_block), pl.ds(3 * rows, rows)],
            out_weight.at[at],
        )

    vec_copy = load(4, attn_out.at[:, :, pl.ds(4 * rows, 16)], vec_land)
    vec_copy.start(priority=1)
    for index in range(2):
        attn_load(index, 0, 0).start(priority=1)
    vec_copy.wait()
    for row in range(ndp):
        for column in range(nf):
            left = (row * nf + column) * share
            vec_out[:, left : left + share] = vec_land[column, row, :, :share].astype(jnp.float32)
    for index in range(nf):
        at = slice(index * width_attn, (index + 1) * width_attn)
        bias[index, 0:1] = vec_out[0:1, at]
        bias[index, 1:2] = vec_out[1:2, at]
    for index in range(FF // width):
        left = index * width
        bias_up[index] = vec_out[5 + left // D : 6 + left // D, left % D : left % D + width]
    label_row = label_ref[...].astype(jnp.float32)
    label_col = jnp.transpose(jnp.broadcast_to(label_row, (128, count)))[:, 0:1]
    tokens = tokens_ref[...]
    lane = lax.broadcasted_iota(jnp.int32, (count, 128), 1)
    total[...] = jnp.broadcast_to(vec_out[2:3], (count, D))

    def attn_turn(block):
        at = lax.rem(block, 2)

        @pl.when(block < nf - 1)
        def _():
            for index in range(2):
                attn_load(index, block + 1, 1 - at).start(priority=1)

        attn_load(0, block, at).wait()
        attn_load(1, block, at).wait()
        weights = [flat(three_weight[at, :, index * rows : (index + 1) * rows]) for index in range(3)]
        queries = (product(tokens, weights[0]) + bias[block, 0:1]).astype(jnp.bfloat16)
        keys_all = product(tokens, weights[1]).astype(jnp.bfloat16)
        values_all = (product(tokens, weights[2]) + bias[block, 1:2]).astype(jnp.bfloat16)
        for index, values in enumerate((queries, keys_all, values_all)):
            blocks[block, index] = values
        pltpu.make_async_copy(blocks.at[block], blocks_out.at[block], store_sem.at[block]).start(priority=1)
        allowed = label_col == label_row
        totals = jnp.zeros((count, 128), jnp.float32)
        mixture = jnp.zeros((count, width_attn), jnp.float32)
        for head in range(width_attn // HDIM):
            scores = contract_cols(head_lanes(queries, head) * score_scale, keys_all)
            scores = jnp.where(allowed, scores, -1e30)
            top = jnp.max(scores, axis=1, keepdims=True)
            exponent = jnp.exp(scores - top)
            weight = jnp.sum(exponent, axis=1, keepdims=True)
            attention = (exponent * (1.0 / weight)).astype(jnp.bfloat16)
            totals = jnp.where(lane == head, top + jnp.log(weight), totals)
            mixture += product(attention, head_lanes(values_all, head))
        mixture = mixture.astype(jnp.bfloat16)
        parts[block] = mixture
        total_out[block] = jnp.transpose(totals)[:8]
        for index in range(nf):
            side_at = slice(index * width_attn, (index + 1) * width_attn)
            total[:, side_at] += product(mixture, flat(out_weight[at, index]))

        @pl.when(block == 0)
        def _():
            from_z(2)

        @pl.when(block == nf - 2)
        def _():
            from_first(1)

    loop(nf, attn_turn)

    def first_norm(index):
        at = pl.ds(pl.multiple_of(index * NORM_ROWS, NORM_ROWS), NORM_ROWS)
        scaled, inverse = normalize(tokens_ref[at].astype(jnp.float32) + total[at])
        scaled_out[at] = scaled
        inverse_out[at] = inverse
        normed = scaled * vec_out[3:4] + vec_out[4:5]
        low_out[at] = normed.astype(jnp.bfloat16)
        total[at] = normed + vec_out[9:10]

    loop(count // NORM_ROWS, first_norm)
    for index in range(nf):
        mixture_out[:, index * width_attn : (index + 1) * width_attn] = parts[index]

    def ffn_load(chunk, step, at):
        block, part = lax.div(step, per), lax.rem(step, per)
        left = pl.multiple_of(part * width, width)
        return load(5 + at, wholes[chunk].at[block, :, :, pl.ds(left, width)], ffn_weight.at[at])

    def ffn_steps(chunk, body, between):
        ffn_load(chunk, 0, 0).start(priority=1)

        def each(step):
            at = lax.rem(step, 2)

            @pl.when(step < FF // width - 1)
            def _():
                ffn_load(chunk, step + 1, 1 - at).start(priority=1)

            ffn_load(chunk, step, at).wait()
            body(step, at)
            between(step)

        loop(FF // width, each)

    def keep(step):
        column = pl.ds(pl.multiple_of(step * width, width), width)
        return (
            pltpu.make_async_copy(active.at[step], active_out.at[:, column], store_sem.at[nf]),
            pltpu.make_async_copy(slope.at[lax.rem(step, 2)], slope_out.at[:, column], store_sem.at[nf + 1]),
        )

    def up_step(step, at):
        up_proj = product(low_out[...], flat(ffn_weight[at])) + bias_up[step]
        half = 0.5 * (1.0 + lax.erf(up_proj * ROOT_HALF))

        @pl.when(step > 0)
        def _():
            for copy in keep(step - 1):
                copy.wait()

        active[step] = (up_proj * half).astype(jnp.bfloat16)
        slope[lax.rem(step, 2)] = (half + up_proj * (BELL * jnp.exp(-0.5 * up_proj * up_proj))).astype(
            jnp.bfloat16
        )
        for copy in keep(step):
            copy.start(priority=1)

    def down_step(step, at):
        total[...] += contract_cols(active[step], flat(ffn_weight[at]))

    def between_up(step):
        @pl.when(step == FF // width // 2)
        def _():
            from_first(2)

    from_second(1)
    from_pair(1)
    ffn_steps(1, up_step, between_up)
    for copy in keep(FF // width - 1):
        copy.wait()
    from_second(2)
    from_pair(2)
    ffn_steps(2, down_step, lambda step: None)
    sums_out[...] = jnp.zeros((8, D), jnp.float32)

    def second_norm(index):
        at = pl.ds(pl.multiple_of(index * NORM_ROWS, NORM_ROWS), NORM_ROWS)
        scaled, inverse = normalize(total[at])
        layer_out[at] = (scaled * vec_out[10:11] + vec_out[11:12]).astype(jnp.bfloat16)
        grad = cotangent_ref[at].astype(jnp.float32)
        d_second = normalize_back(grad * vec_out[10:11], scaled, inverse)
        d_second_out[at] = d_second
        sums_out[0:1] += row_sum(d_second.astype(jnp.bfloat16))
        sums_out[1:2] += row_sum(grad * scaled)
        sums_out[2:3] += row_sum(grad)

    loop(count // NORM_ROWS, second_norm)

    def stored(block):
        pltpu.make_async_copy(blocks.at[block], blocks_out.at[block], store_sem.at[block]).wait()

    loop(nf, stored)
    for chunk in range(chunks):
        def finish(z_at):
            along_z(chunk, z_at, False, lambda copy: copy.wait_send())
            for step in range(1, side):
                first_copy(chunk, z_at, step, False).wait_send()
                for line in range(side):
                    second_copy(chunk, fs, z_at, step, False, line).wait_send()

            def each(plane_at):
                pair_copy(chunk, plane_at, z_at, False).wait_send()

            loop(nf, each)

        loop(nz, finish)


def forward(ndp, nf, tokens, segments, cotangent, attn_w, ffn_w, vectors):
    nz, side, chunks = ndp // 2, math.isqrt(nf), 3
    count = tokens.shape[0]
    rows, width_attn = attn_w.shape[1:]
    width_ffn = ffn_w.shape[2]
    width = min(512, width_ffn)
    bf16, f32 = jnp.bfloat16, jnp.float32
    dma = pltpu.SemaphoreType.DMA
    anywhere, inside = pl.BlockSpec(memory_space=pl.ANY), pl.BlockSpec(memory_space=pltpu.VMEM)
    shape = jax.ShapeDtypeStruct
    return pl.pallas_call(
        functools.partial(forward_kernel, ndp, nf),
        name="forward",
        out_shape=[
            shape((nf, ndp, 4 * rows + 16, width_attn), bf16),
            shape((nf, ndp, rows, width_ffn), bf16),
            shape((nf, ndp, rows, width_ffn), bf16),
            shape((nf, 3, count, width_attn), bf16),
            shape((count, FF), bf16),
            shape((count, FF), bf16),
            shape((16, D), f32),
            shape((count, D), bf16),
            shape((nf, 8, count), f32),
            shape((count, D), f32),
            shape((count, 1), f32),
            shape((count, D), bf16),
            shape((count, D), bf16),
            shape((count, D), f32),
            shape((8, D), f32),
        ],
        in_specs=[inside] * 6,
        out_specs=[anywhere] * 6 + [inside] * 9,
        scratch_shapes=[
            pltpu.VMEM((4 * rows + 16, width_attn), bf16),
            pltpu.VMEM((rows, width_ffn), bf16),
            pltpu.VMEM((rows, width_ffn), bf16),
            pltpu.VMEM((2, ndp, 3 * rows, width_attn), bf16),
            pltpu.VMEM((2, nf, ndp // nf, rows, width_attn), bf16),
            pltpu.VMEM((2, ndp, rows, width), bf16),
            pltpu.VMEM((nf, ndp, 16, width_attn), bf16),
            pltpu.VMEM((nf, 8, width_attn), f32),
            pltpu.VMEM((FF // width, 1, width), f32),
            pltpu.VMEM((nf, 3, count, width_attn), bf16),
            pltpu.VMEM((nf, count, width_attn), bf16),
            pltpu.VMEM((FF // width, count, width), bf16),
            pltpu.VMEM((2, count, width), bf16),
            pltpu.VMEM((count, D), f32),
            dma((chunks,)),
            dma((chunks, nf, nz)),
            dma((chunks, nf, nz)),
            dma((chunks, nz, 2)),
            dma((chunks, nz, side - 1)),
            dma((chunks, nz, side, side - 1)),
            dma((chunks, nf, nz)),
            dma((7,)),
            dma((nf + 2,)),
        ],
        compiler_params=pltpu.CompilerParams(
            collective_id=2, has_side_effects=True, vmem_limit_bytes=60 * 1024 * 1024
        ),
    )(tokens, segments[None, :], cotangent, attn_w, ffn_w, vectors)


def backward_kernel(
    ndp,
    nf,
    d_second_ref,
    low_ref,
    scaled_ref,
    inverse_ref,
    vec_ref,
    active_ref,
    slope_ref,
    up_ref,
    down_ref,
    tokens_ref,
    label_ref,
    blocks_ref,
    mixture_ref,
    total_ref,
    attn_ref,
    tail_ref,
    attn_mom,
    ffn_mom,
    input_grad,
    up_out,
    down_out,
    attn_out,
    vec_out,
    attn_low,
    ffn_low,
    held_up,
    held_down,
    held_attn,
    first_up,
    first_down,
    first_attn,
    second_up,
    second_down,
    second_attn,
    z_up,
    z_down,
    z_attn,
    stages_out,
    land,
    ffn_weight,
    ffn_act,
    attn_weight,
    attn_block,
    wide_low,
    wide_two,
    turned_one,
    turned_two,
    branch,
    bias_up_sum,
    query_sum,
    value_sum,
    vec_land,
    load_sem,
    step_sem,
    pair_send,
    pair_recv,
    first_send,
    first_recv,
    second_send,
    second_recv,
    z_send,
    z_recv,
    vec_send,
    vec_recv,
):
    z, core, y, x, nz, side = place(ndp, nf)
    dp, fs = z * 2 + core, y * side + x
    other = (z * 2 + 1 - core, fs)
    held, outs = (held_up, held_down, held_attn), (up_out, down_out, attn_out)
    from_first, from_second = (first_up, first_down, first_attn), (second_up, second_down, second_attn)
    from_z = (z_up, z_down, z_attn)
    chunks = 3
    rows, width_ffn = held_up.shape[2:]
    width_attn = held_attn.shape[-1]
    width = ffn_weight.shape[-1]
    per = width_ffn // width
    greet(line_partners(ndp, nf))

    def place_of(turn):
        step = nf - 1 - turn
        return lax.rem(y + lax.div(step, side), side) * side + lax.rem(x + lax.rem(step, side), side)

    def first_copy(chunk, z_at, line, step):
        x_first = lax.rem(z_at, 2) == 0
        near, far = lax.rem(x + step, side), lax.rem(y + step, side)
        to = jnp.where(x_first, y * side + near, far * side + x)
        at = jnp.where(
            x_first,
            lax.rem(y + line, side) * side + near,
            far * side + lax.rem(x + line, side),
        )
        return remote(
            held[chunk].at[z_at, at],
            from_first[chunk].at[z_at, step - 1, line],
            first_send.at[chunk, z_at, step - 1, line],
            first_recv.at[chunk, z_at, step - 1, line],
            (dp, to),
        )

    lag = 2
    total_steps = nf * per + nf
    schedule = {}
    for sent, base, stride in (((0, 1), 0, per), ((2,), nf * per, 1)):
        for turns in ((0,), tuple(range(1, nf - 1))):
            ready = min(base + (turns[-1] + 1) * stride - 1 + lag, total_steps)
            for z_at in range(0, nz, 2):
                schedule.setdefault(ready, []).extend((chunk, turns, z_at) for chunk in sent)

    def send_first(chunk, turns, z_from):
        def each(z_at):
            x_first = lax.rem(z_at, 2) == 0
            for turn in turns:
                step_x, step_y = (nf - 1 - turn) % side, (nf - 1 - turn) // side
                step = jnp.where(x_first, step_x, step_y)
                line = jnp.where(x_first, step_y, step_x)

                @pl.when(step > 0)
                def _(line=line, step=step):
                    first_copy(chunk, z_at, line, step).start()

        loop(z_from + 2, each, z_from)

    def sends_at(step, steps):
        for when in steps:
            @pl.when(step == when)
            def _(when=when):
                for chunk, turns, z_at in schedule.get(when, ()):
                    send_first(chunk, turns, z_at)

    def line_place(z_at, line):
        x_first = lax.rem(z_at, 2) == 0
        return jnp.where(
            x_first, lax.rem(y + line, side) * side + x, y * side + lax.rem(x + line, side)
        )

    def second_copy(chunk, z_at, step):
        to = line_place(z_at, step)
        return remote(
            held[chunk].at[z_at, to],
            from_second[chunk].at[z_at, step - 1],
            second_send.at[chunk, z_at, step - 1],
            second_recv.at[chunk, z_at, step - 1],
            (dp, to),
        )

    def z_copy(chunk, step):
        z_at = lax.rem(z + step, nz)
        return remote(
            held[chunk].at[z_at, fs],
            from_z[chunk].at[step - 1],
            z_send.at[chunk, step - 1],
            z_recv.at[chunk, step - 1],
            (z_at * 2 + core, fs),
        )

    def take_first(chunk, lines):
        def each(hop):
            z_at = lax.rem(z + 1 + hop, nz)
            for line in lines:
                at = line_place(z_at, line)
                for step in range(1, side):
                    first_copy(chunk, z_at, line, step).wait_recv()
                    held[chunk][z_at, at] += from_first[chunk][z_at, step - 1, line]
                if line:
                    second_copy(chunk, z_at, line).start()

        loop(nz, each)

    def take_second(chunk):
        def each(hop):
            z_at = lax.rem(z + 1 + hop, nz)
            for step in range(1, side):
                second_copy(chunk, z_at, step).wait_recv()
                held[chunk][z_at, fs] += from_second[chunk][z_at, step - 1]

            @pl.when(hop < nz - 1)
            def _():
                z_copy(chunk, hop + 1).start()

        loop(nz, each)

    def moments(chunk):
        source = ffn_mom.at[chunk] if chunk < 2 else attn_mom
        return pltpu.make_async_copy(source, outs[chunk], load_sem.at[3 + chunk])

    def take_z(chunk):
        total = held[chunk][z, fs].astype(jnp.float32)
        for step in range(1, nz):
            z_copy(chunk, step).wait_recv()
            total += from_z[chunk][step - 1].astype(jnp.float32)
        moments(chunk).wait()
        low = (matrix_decay * outs[chunk][...] + total).astype(jnp.bfloat16)
        outs[chunk][...] = total
        if chunk < 2:
            half = low.shape[1] // 2
            ffn_low[chunk, 0] = low[:, :half]
            ffn_low[chunk, 1] = low[:, half:]
        else:
            attn_low[...] = low

    vec_rounds = [[other]]
    vec_rounds.append([(dp, y * side + lax.rem(x + step, side)) for step in range(1, side)])
    vec_rounds.append([(dp, lax.rem(y + step, side) * side + x) for step in range(1, side)])
    vec_rounds.append([(lax.rem(z + step, nz) * 2 + core, fs) for step in range(1, nz)])
    starts = [sum(len(group) for group in vec_rounds[:index]) for index in range(4)]

    def vec_copy(index, step):
        at = starts[index] + step
        return remote(
            vec_land.at[index], vec_land.at[4 + at], vec_send.at[at], vec_recv.at[at], vec_rounds[index][step]
        )

    def vec_start(index):
        for step in range(len(vec_rounds[index])):
            vec_copy(index, step).start()

    def vec_take(index):
        total = vec_land[index]
        for step in range(len(vec_rounds[index])):
            vec_copy(index, step).wait_recv()
            total += vec_land[4 + starts[index] + step]
        if index < 3:
            vec_land[index + 1] = total
            vec_start(index + 1)
        else:
            vec_out[...] = total

    def split(values, keep, give):
        parts = values.astype(jnp.bfloat16).reshape(nz, 2, rows, values.shape[1])
        for which in range(2):
            @pl.when(core == which)
            def _(which=which):
                keep(parts[:, which])
                give(parts[:, 1 - which])

    def ffn_loads(slot, turn, part):
        block = place_of(turn)
        at = pl.ds(part * width, width)
        column = pl.ds(pl.multiple_of(block * width_ffn + part * width, width), width)
        pairs = (
            (up_ref.at[block, :, :, at], ffn_weight.at[slot, 0]),
            (down_ref.at[block, :, :, at], ffn_weight.at[slot, 1]),
            (active_ref.at[:, column], ffn_act.at[slot, 0]),
            (slope_ref.at[:, column], ffn_act.at[slot, 1]),
        )
        return [
            pltpu.make_async_copy(source, target, step_sem.at[slot, index])
            for index, (source, target) in enumerate(pairs)
        ]

    def load(index, source, target):
        return pltpu.make_async_copy(source, target, load_sem.at[index])

    load(0, low_ref, wide_low).start(priority=1)
    load(1, d_second_ref, input_grad).start(priority=1)
    for copy in ffn_loads(0, 0, 0):
        copy.start(priority=1)
    load(2, tokens_ref, wide_two).start(priority=1)
    for chunk in range(chunks):
        moments(chunk).start(priority=1)
    load(0, low_ref, wide_low).wait()
    turned_one[...] = jnp.transpose(wide_low[...])
    load(1, d_second_ref, input_grad).wait()
    wide_low[...] = input_grad[...].astype(jnp.bfloat16)
    turned_two[...] = jnp.transpose(wide_low[...])

    def pair_copy(step):
        stage, slot = lax.rem(step, lag), lax.rem(step, 2 * lag)
        return remote(stages_out.at[stage], land.at[slot], pair_send.at[stage], pair_recv.at[slot], other)

    def pair_take(step):
        pair_copy(step).wait()
        slot = lax.rem(step, 2 * lag)

        @pl.when(step < nf * per)
        def _():
            block, part = place_of(lax.div(step, per)), lax.rem(step, per)
            for index in range(2):
                for which in range(per):
                    @pl.when(part == which)
                    def _(index=index, which=which):
                        for half in range(2):
                            left = which * width + half * width_attn
                            at = slice(left, left + width_attn)
                            held[index][:, block, :, at] += land[slot, :, 2 * index + half]

        @pl.when(step >= nf * per)
        def _():
            held_attn[:, place_of(step - nf * per)] += land[slot]

    def ffn_turn(turn):
        block = place_of(turn)
        for part in range(per):
            now = turn * per + part
            slot = lax.rem(now, 2)
            if part < per - 1:
                for copy in ffn_loads(1 - slot, turn, part + 1):
                    copy.start(priority=1)
            else:
                @pl.when(turn < nf - 1)
                def _():
                    for copy in ffn_loads(1 - slot, turn + 1, 0):
                        copy.start(priority=1)

            for copy in ffn_loads(slot, turn, part):
                copy.wait()
            d_active = product(wide_low[...], flat(ffn_weight[slot, 1]))
            d_up = (d_active * ffn_act[slot, 1].astype(jnp.float32)).astype(jnp.bfloat16)
            bias_up_sum[block * per + part] = row_sum(d_up)
            input_grad[...] += contract_cols(d_up, flat(ffn_weight[slot, 0]))

            @pl.when(now >= lag)
            def _():
                pair_take(now - lag)

            sends_at(now, range(nf * per))
            at = slice(part * width, (part + 1) * width)
            for index in range(2):

                def keep(values, index=index):
                    held[index][:, block, :, at] = values

                def give(values, index=index):
                    for half in range(2):
                        side_at = slice(half * width_attn, (half + 1) * width_attn)
                        stages_out[lax.rem(now, lag), :, 2 * index + half] = values[:, :, side_at]

                if index == 0:
                    split(product(turned_one[...], d_up), keep, give)
                else:
                    split(product(turned_two[...], ffn_act[slot, 0]), keep, give)
            pair_copy(now).start()

    loop(nf, ffn_turn)

    load(2, tokens_ref, wide_two).wait()
    turned_one[...] = jnp.transpose(wide_two[...])
    load(0, mixture_ref, wide_two).start(priority=1)

    def attn_load(index, turn):
        block = place_of(turn)
        per_block = ndp // nf
        source, target = (
            (attn_ref.at[block, :, pl.ds(0, 3 * rows)], attn_weight[0]),
            (
                attn_ref.at[:, pl.ds(block * per_block, per_block), pl.ds(3 * rows, rows)],
                attn_weight[1],
            ),
            (blocks_ref.at[block], attn_block),
        )[index]
        return pltpu.make_async_copy(source, target, step_sem.at[0, index])

    for index in range(3):
        attn_load(index, 0).start(priority=1)
    vec_land[0] = jnp.zeros((16, D), jnp.float32)
    vec_land[0, 9:12] = tail_ref[0:3]

    def norm_back(index):
        at = pl.ds(pl.multiple_of(index * NORM_ROWS, NORM_ROWS), NORM_ROWS)
        grad = input_grad[at]
        scaled = scaled_ref[at]
        d_first = normalize_back(grad * vec_ref[3:4], scaled, inverse_ref[at])
        input_grad[at] = d_first
        low = d_first.astype(jnp.bfloat16)
        vec_land[0, 2:3] += row_sum(low)
        vec_land[0, 3:4] += row_sum(grad * scaled)
        vec_land[0, 4:5] += row_sum(grad)
        for column in range(nf):
            branch[column, at] = low[:, column * width_attn : (column + 1) * width_attn]

    loop(tokens_ref.shape[0] // NORM_ROWS, norm_back)
    label_row = label_ref[...].astype(jnp.float32)
    label_col = jnp.transpose(jnp.broadcast_to(label_row, (128, label_row.shape[1])))[:, 0:1]
    load(0, mixture_ref, wide_two).wait()
    turned_two[...] = jnp.transpose(wide_two[...])

    def attn_turn(turn):
        block = place_of(turn)
        now = nf * per + turn

        def load_next(index):
            @pl.when(turn < nf - 1)
            def _():
                attn_load(index, turn + 1).start(priority=1)

        for index in range(3):
            attn_load(index, turn).wait()
        count = tokens_ref.shape[0]
        zero = jnp.zeros((count, width_attn), jnp.float32)
        d_mixture = zero
        for index in range(nf):
            d_mixture += contract_cols(branch[index], flat(attn_weight[1][index]))
        load_next(1)
        d_mixture = d_mixture.astype(jnp.bfloat16)
        queries, keys_all, values_all = (attn_block[index] for index in range(3))
        allowed = label_col == label_row
        d_queries, d_keys, d_values = zero, zero, zero
        for head in range(width_attn // HDIM):
            my_queries = head_lanes(queries, head) * score_scale
            my_mixture = head_lanes(d_mixture, head)
            scores = contract_cols(keys_all, my_queries) - total_ref[block, head : head + 1, :]
            attention = jnp.where(allowed, jnp.exp(scores), 0.0)
            d_attention = contract_cols(values_all, my_mixture)
            inner = jnp.sum(d_attention * attention, axis=0, keepdims=True)
            d_scores = (attention * (d_attention - inner)).astype(jnp.bfloat16)
            d_keys += product(d_scores, my_queries)
            d_values += product(attention.astype(jnp.bfloat16), my_mixture)
            d_queries += contract_rows(d_scores, head_lanes(keys_all, head) * score_scale)
        load_next(2)
        grads = [values.astype(jnp.bfloat16) for values in (d_queries, d_keys, d_values)]
        query_sum[block] = row_sum(grads[0])
        value_sum[block] = row_sum(grads[2])
        moved = jnp.zeros((count, D), jnp.float32)
        for index in range(3):
            weight = attn_weight[0][:, index * rows : (index + 1) * rows]
            moved += contract_cols(grads[index], flat(weight))
        input_grad[...] += moved
        load_next(0)

        pair_take(now - lag)
        for index in range(4):
            turned, grad = (turned_one, grads[index]) if index < 3 else (turned_two, branch[block])

            def keep(values, index=index):
                held_attn[:, block, index] = values

            def give(values, index=index):
                stages_out[lax.rem(now, lag), :, index] = values

            split(product(turned[...], grad), keep, give)
        pair_copy(now).start()
        sends_at(now, range(nf * per, total_steps))

        @pl.when(turn == nf - 4)
        def _():
            take_first(0, range(1, side))
            take_first(1, range(1, side))

        @pl.when(turn == nf - 3)
        def _():
            take_first(0, (0,))
            take_first(1, (0,))

        @pl.when(turn == nf - 2)
        def _():
            take_second(0)
            take_second(1)

    loop(nf, attn_turn)
    for index in range(nf):
        at = slice(index * width_attn, (index + 1) * width_attn)
        vec_land[0, 0:1, at] = query_sum[index]
        vec_land[0, 1:2, at] = value_sum[index]
    for index in range(nf * per):
        left = index * width
        vec_land[0, 5 + left // D : 6 + left // D, left % D : left % D + width] = bias_up_sum[index]
    vec_start(0)
    for step in range(total_steps - lag, total_steps):
        pair_take(step)
    sends_at(total_steps, (total_steps,))

    vec_take(0)
    take_first(2, range(1, side))
    take_first(2, (0,))
    vec_take(1)
    take_z(0)
    take_second(2)
    vec_take(2)
    take_z(1)
    vec_take(3)
    take_z(2)

    for chunk in range(chunks):

        def finish(z_at):
            for step in range(1, side):
                second_copy(chunk, z_at, step).wait_send()
                for line in range(side):
                    first_copy(chunk, z_at, line, step).wait_send()

        loop(nz, finish)
        for step in range(1, nz):
            z_copy(chunk, step).wait_send()
    for index in range(4):
        for step in range(len(vec_rounds[index])):
            vec_copy(index, step).wait_send()


def backward_kernel_entry(ndp, nf, *refs):
    at = 18 + 7 + 12 + 2 + 2
    backward_kernel(ndp, nf, *refs[:at], refs[at : at + 2], *refs[at + 2 :])


def backward(
    ndp, nf, d_second, low, scaled, inverse, vectors, active, slope, up_all, down_all,
    tokens, segments, blocks, mixture, totals, attn_all, tail_sums, attn_mom, ffn_mom,
):
    nz, side = ndp // 2, math.isqrt(nf)
    count = tokens.shape[0]
    rows, width_ffn = up_all.shape[2:]
    width_attn = attn_all.shape[-1]
    width = 2 * width_attn
    bf16, f32 = jnp.bfloat16, jnp.float32
    dma = pltpu.SemaphoreType.DMA
    anywhere, inside = pl.BlockSpec(memory_space=pl.ANY), pl.BlockSpec(memory_space=pltpu.VMEM)
    shapes = [(rows, width_ffn), (rows, width_ffn), (4, rows, width_attn)]
    vec_copies = 1 + 2 * (side - 1) + nz - 1
    sums = []
    for lead in ((nz, nf), (nz, side - 1, side), (nz, side - 1), (nz - 1,)):
        sums += [pltpu.VMEM(lead + shape, bf16) for shape in shapes]
    return pl.pallas_call(
        functools.partial(backward_kernel_entry, ndp, nf),
        name="backward",
        out_shape=[jax.ShapeDtypeStruct((count, D), f32)]
        + [jax.ShapeDtypeStruct(shape, f32) for shape in shapes]
        + [
            jax.ShapeDtypeStruct((16, D), f32),
            jax.ShapeDtypeStruct(attn_mom.shape, bf16),
            jax.ShapeDtypeStruct((2, 2, rows, width_ffn // 2), bf16),
        ],
        in_specs=[
            anywhere,
            anywhere,
            inside,
            inside,
            inside,
            anywhere,
            anywhere,
            anywhere,
            anywhere,
            anywhere,
            inside,
            anywhere,
            anywhere,
            inside,
            anywhere,
            inside,
            anywhere,
            anywhere,
        ],
        out_specs=[inside] * 7,
        scratch_shapes=sums
        + [
            pltpu.VMEM((2, nz, 4, rows, width_attn), bf16),
            pltpu.VMEM((4, nz, 4, rows, width_attn), bf16),
            pltpu.VMEM((2, 2, ndp, rows, width), bf16),
            pltpu.VMEM((2, 2, count, width), bf16),
            pltpu.VMEM((ndp, 3 * rows, width_attn), bf16),
            pltpu.VMEM((nf, ndp // nf, rows, width_attn), bf16),
            pltpu.VMEM((3, count, width_attn), bf16),
            pltpu.VMEM((count, D), bf16),
            pltpu.VMEM((count, D), bf16),
            pltpu.VMEM((D, count), bf16),
            pltpu.VMEM((D, count), bf16),
            pltpu.VMEM((nf, count, width_attn), bf16),
            pltpu.VMEM((FF // width, 1, width), f32),
            pltpu.VMEM((nf, 1, width_attn), f32),
            pltpu.VMEM((nf, 1, width_attn), f32),
            pltpu.VMEM((4 + vec_copies, 16, D), f32),
            dma((6,)),
            dma((2, 4)),
            dma((2,)),
            dma((4,)),
            dma((3, nz, side - 1, side)),
            dma((3, nz, side - 1, side)),
            dma((3, nz, side - 1)),
            dma((3, nz, side - 1)),
            dma((3, nz - 1)),
            dma((3, nz - 1)),
            dma((vec_copies,)),
            dma((vec_copies,)),
        ],
        compiler_params=pltpu.CompilerParams(
            collective_id=3, has_side_effects=True, vmem_limit_bytes=63 * 1024 * 1024
        ),
    )(
        d_second, low, scaled, inverse, vectors, active, slope, up_all, down_all,
        tokens, segments[None, :], blocks, mixture, totals, attn_all, tail_sums, attn_mom, ffn_mom,
    )


def on_device(
    tokens,
    segments,
    cotangent,
    attn_w,
    ffn_w,
    vectors,
    attn_mom,
    ffn_mom,
    vec_mom,
    attn_ema,
    ffn_ema,
    vec_ema,
):
    ndp, nf = lax.axis_size("dp"), lax.axis_size("fsdp")
    share = vectors.shape[1]
    (
        attn_all, up_all, down_all, blocks, active, slope, vec_full, mixture, totals, scaled, inverse, low,
        layer_out, d_second, tail_sums,
    ) = forward(ndp, nf, tokens, segments, cotangent, attn_w, ffn_w, vectors)
    input_grad, up_grad, down_grad, attn_grad, vec_sum, attn_piece, ffn_piece = backward(
        ndp, nf, d_second, low, scaled, inverse, vec_full, active, slope, up_all, down_all,
        tokens, segments, blocks, mixture, totals, attn_all, tail_sums, attn_mom, ffn_mom,
    )
    mine = (lax.axis_index("dp") * nf + lax.axis_index("fsdp")) * share
    vec_grad = lax.dynamic_slice(vec_sum, (0, mine), (12, share))
    attn_ortho, ffn_ortho = orthogonalize(ndp, nf, attn_piece, ffn_piece)
    total_tokens = tokens.shape[0] * ndp * nf
    updated = update_all(
        vector_step / math.sqrt(total_tokens),
        attn_w,
        ffn_w,
        vectors,
        attn_mom,
        ffn_mom,
        vec_mom,
        attn_ema,
        ffn_ema,
        vec_ema,
        attn_grad,
        up_grad,
        down_grad,
        vec_grad,
        attn_ortho,
        ffn_ortho,
    )
    return (layer_out, input_grad, *updated, vec_grad[2])


def solution(mesh):
    in_specs = (
        P(("dp", "fsdp"), None),
        P(("dp", "fsdp")),
        P(("dp", "fsdp"), None),
        P(None, "dp", "fsdp"),
        P(None, "dp", "fsdp"),
        P(None, ("dp", "fsdp")),
        P(None, "dp", "fsdp"),
        P(None, "dp", "fsdp"),
        P(None, ("dp", "fsdp")),
        P(None, "dp", "fsdp"),
        P(None, "dp", "fsdp"),
        P(None, ("dp", "fsdp")),
    )
    out_specs = (
        P(("dp", "fsdp"), None),
        P(("dp", "fsdp"), None),
        P(None, "dp", "fsdp"),
        P(None, "dp", "fsdp"),
        P(None, ("dp", "fsdp")),
        P(None, "dp", "fsdp"),
        P(None, "dp", "fsdp"),
        P(None, ("dp", "fsdp")),
        P(None, "dp", "fsdp"),
        P(None, "dp", "fsdp"),
        P(None, ("dp", "fsdp")),
        P(("dp", "fsdp")),
    )
    return jax.shard_map(
        on_device, mesh=mesh, in_specs=in_specs, out_specs=out_specs, check_vma=False
    )
```

```python
import functools
import math

import jax
import jax.numpy as jnp
from jax import lax
from jax.experimental import pallas as pl
from jax.experimental.pallas import tpu as pltpu
from jax.sharding import PartitionSpec as P

D = 1024
FF = 4096
HEADS = 16
HDIM = 64
TILE = 512
ITERS = 5


score_scale = 0.125
ln_epsilon = 1e-05
norm_epsilon = 1e-06
ns_linear = 3.4445
ns_square = -4.775
ns_cubic = 2.0315
matrix_decay = 0.95
vector_decay = 0.9
average_decay = 0.7
weight_decay = 0.01
attn_rates = (1.0, 1.0, 1.0, 10.0)
vector_step = 0.3


def product(left, right):
    return jnp.dot(left, right, preferred_element_type=jnp.float32)


def contract_rows(left, right):
    return lax.dot_general(
        left, right, (((0,), (0,)), ((), ())), preferred_element_type=jnp.float32
    )


def contract_cols(left, right):
    return lax.dot_general(
        left, right, (((1,), (1,)), ((), ())), preferred_element_type=jnp.float32
    )


MESH = pl.DeviceIdType.MESH
ROLES = 8
STEP_ROWS = 512
NORM_ROWS = 128
TILE_ROWS = 128


def greet(partners):
    barrier = pltpu.get_barrier_semaphore()
    for partner in partners:
        pl.semaphore_signal(barrier, inc=1, device_id=partner, device_id_type=MESH)
    pl.semaphore_wait(barrier, len(partners))


def place(ndp, nf):
    dp, fs = lax.axis_index("dp"), lax.axis_index("fsdp")
    side = math.isqrt(nf)
    return lax.div(dp, 2), lax.rem(dp, 2), lax.div(fs, side), lax.rem(fs, side), ndp // 2, side


def line_partners(ndp, nf):
    z, core, y, x, nz, side = place(ndp, nf)
    mine = y * side + x
    return (
        [(z * 2 + 1 - core, mine)]
        + [(lax.rem(z + step, nz) * 2 + core, mine) for step in range(1, nz)]
        + [(z * 2 + core, y * side + lax.rem(x + step, side)) for step in range(1, side)]
        + [(z * 2 + core, lax.rem(y + step, side) * side + x) for step in range(1, side)]
    )


def all_partners(ndp, nf):
    z, core, y, x, nz, side = place(ndp, nf)
    dp, fs = z * 2 + core, y * side + x
    return (
        [(lax.rem(dp + step, ndp), fs) for step in range(1, ndp)]
        + [(dp, y * side + lax.rem(x + step, side)) for step in range(1, side)]
        + [(dp, lax.rem(y + step, side) * side + x) for step in range(1, side)]
    )


def remote(source, target, send_sem, recv_sem, device):
    return pltpu.make_async_remote_copy(
        src_ref=source,
        dst_ref=target,
        send_sem=send_sem,
        recv_sem=recv_sem,
        device_id=device,
        device_id_type=MESH,
    )


def loop(count, body, start=0):
    def step(index, carry):
        body(index)
        return carry

    lax.fori_loop(start, count, step, 0)


class Crossing:
    def __init__(self, ndp, nf, land, own_sem, piece_recv, first_send, second_send, plane_recv, source):
        self.ndp, self.land, self.own_sem, self.piece_recv, self.source = ndp, land, own_sem, piece_recv, source
        self.first_send, self.second_send, self.plane_recv = first_send, second_send, plane_recv
        self.z, self.core, self.y, self.x, self.nz, self.side = place(ndp, nf)
        self.dp, self.fs = self.z * 2 + self.core, self.y * self.side + self.x

    def row_of(self, index):
        return lax.rem(self.z + index // 2, self.nz) * 2 + lax.rem(self.core + index, 2)

    def x_first(self, row):
        return lax.rem(row // 2, 2) == 0

    def along(self, first, step):
        x_at = jnp.where(first, lax.rem(self.x + step, self.side), self.x)
        y_at = jnp.where(first, self.y, lax.rem(self.y + step, self.side))
        return y_at * self.side + x_at

    def first_copy(self, row, step):
        here = self.land.at[self.fs, row]
        peer = self.along(self.x_first(row), step)
        sems = self.first_send.at[row, step - 1], self.plane_recv.at[self.fs, row]
        return remote(here, here, *sems, (self.dp, peer))

    def second_copy(self, plane_at, row, line, step):
        here = self.land.at[plane_at, row]
        peer = self.along(jnp.logical_not(self.x_first(row)), step)
        sems = self.second_send.at[row, line, step - 1], self.plane_recv.at[plane_at, row]
        return remote(here, here, *sems, (self.dp, peer))

    def arrived(self, plane_at, row):
        here = self.land.at[plane_at, row]
        remote(here, here, self.own_sem, self.plane_recv.at[plane_at, row], (self.dp, self.fs)).wait_recv()

    def take(self):
        def each(index):
            row = self.row_of(index)

            @pl.when(index == 0)
            def _():
                pltpu.make_async_copy(self.source, self.land.at[self.fs, row], self.own_sem).wait()

            @pl.when(index > 0)
            def _():
                here = self.land.at[self.fs, row]
                remote(self.source, here, self.own_sem, self.piece_recv.at[row], (self.dp, self.fs)).wait_recv()

            for step in range(1, self.side):
                self.first_copy(row, step).start()
                self.second_copy(self.fs, row, 0, step).start()

        loop(self.ndp, each)

    def pass_on(self):
        def each(index):
            row = self.row_of(index)
            for line in range(1, self.side):
                plane_at = self.along(self.x_first(row), line)
                self.arrived(plane_at, row)
                for step in range(1, self.side):
                    self.second_copy(plane_at, row, line, step).start()

        loop(self.ndp, each)

    def wait_line(self, line):
        for step in range(1, self.side):

            def each(index, step=step):
                row = self.row_of(index)
                x, y, side = self.x, self.y, self.side
                there = jnp.where(
                    self.x_first(row),
                    lax.rem(y + step, side) * side + lax.rem(x + line, side),
                    lax.rem(y + line, side) * side + lax.rem(x + step, side),
                )
                self.arrived(there, row)

            loop(self.ndp, each)

    def near(self):
        self.wait_line(0)

    def far(self):
        for line in range(1, self.side):
            self.wait_line(line)

    def finish(self):
        def each(row):
            for step in range(1, self.side):
                self.first_copy(row, step).wait_send()
                for line in range(self.side):
                    self.second_copy(self.fs, row, line, step).wait_send()

        loop(self.ndp, each)


def ortho_kernel(
    ndp,
    nf,
    attn_ref,
    ffn_whole,
    attn_out,
    ffn_out,
    land_attn,
    land_ffn,
    iter_low,
    iter_full,
    gram,
    gram_send,
    gram_recv,
    off_low,
    poly_low,
    diag_row,
    diag_col,
    inverse_norm,
    own_low,
    own_full,
    own_attn,
    own_ffn,
    own_sem,
    piece_send,
    piece_recv,
    first_send,
    second_send,
    plane_recv,
    gram_send_sem,
    gram_recv_sem,
    back_send,
    back_recv,
    load_sem,
):
    z, core, y, x, nz, side = place(ndp, nf)
    dp, fs = z * 2 + core, y * side + x
    rows = attn_ref.shape[1]
    size = rows * ndp
    is_attn = jnp.logical_or(dp < 2, jnp.logical_and(dp >= 6, dp < ROLES))
    is_ffn = jnp.logical_and(dp >= 2, dp < 6)
    partner = z * 2 + 1 - core

    greet(all_partners(ndp, nf))
    attn_roles = (0, 6, 1, 7)

    def piece(role):
        return attn_ref.at[role if role < 2 else role - 4]

    def piece_copy(role):
        return remote(piece(role), land_attn.at[fs, dp], piece_send.at[role], piece_recv.at[dp], (role, fs))

    for role in attn_roles:
        @pl.when(dp != role)
        def _(role=role):
            piece_copy(role).start()

        @pl.when(dp == role)
        def _(role=role):
            pltpu.make_async_copy(piece(role), land_attn.at[fs, dp], own_sem).start()

    def iterate(land, source, own_out, target, role, paired):
        width = land.shape[-1]
        columns = width * nf
        tall = min(STEP_ROWS, size)
        steps = size // tall
        wide = min(1024, columns)

        def add_gram(plane_at, fresh):
            block = land[plane_at].reshape(size, width)
            for step in range(steps):
                at = slice(step * tall, (step + 1) * tall)
                part = contract_cols(block[at], block)
                if fresh:
                    gram[at] = part
                else:
                    gram[at] += part

        if paired:

            def block_load(index):
                return pltpu.make_async_copy(ffn_whole.at[index], land.at[index], load_sem.at[index])

            for index in range(nf):
                block_load(index).start()
            for index in range(nf):
                block_load(index).wait()
                add_gram(index, index == 0)
        else:
            crossing = Crossing(ndp, nf, land, own_sem, piece_recv, first_send, second_send, plane_recv, source)
            crossing.take()
            add_gram(fs, True)
            crossing.pass_on()
            crossing.near()
            for step in range(1, side):
                add_gram(crossing.along(True, step), False)
                add_gram(crossing.along(False, step), False)
            crossing.far()
            for far_y in range(1, side):
                for far_x in range(1, side):
                    add_gram(lax.rem(y + far_y, side) * side + lax.rem(x + far_x, side), False)

        def gram_copy(slot, step):
            at = pl.ds(step * tall, tall)
            return remote(
                gram_send.at[slot, at],
                gram_recv.at[slot, at],
                gram_send_sem.at[slot, step],
                gram_recv_sem.at[slot, step],
                (partner, fs),
            )

        if paired:
            for step in range(steps):
                at = slice(step * tall, (step + 1) * tall)
                gram_send[0, at] = gram[at].astype(jnp.bfloat16)
                gram_copy(0, step).start()
        for index in range(nf):
            block = land[index].reshape(size, width)
            at = slice(index * width, (index + 1) * width)
            iter_low[0, :, at] = block
            iter_full[:, at] = block.astype(jnp.float32)

        def back_copy(row):
            return remote(own_out.at[row], target, back_send.at[row], back_recv.at[role], (row, fs))

        def iteration(count):
            now = lax.rem(count, 2)
            later = 1 - now

            @pl.when(count > 0)
            def _():
                def gram_rows(step):
                    at = pl.ds(pl.multiple_of(step * tall, tall), tall)
                    part = contract_cols(iter_low[now, at, :columns], iter_low[now, :, :columns])
                    if paired:
                        gram_send[now, at] = part.astype(jnp.bfloat16)
                        gram_copy(now, step).start()
                    else:
                        gram[at] = part

                loop(steps, gram_rows)

            eye = lax.broadcasted_iota(jnp.int32, (TILE_ROWS, TILE_ROWS), 0) == lax.broadcasted_iota(
                jnp.int32, (TILE_ROWS, TILE_ROWS), 1
            )

            @pl.when(count == 0)
            def _():
                trace = jnp.zeros((TILE_ROWS, TILE_ROWS), jnp.float32)
                if paired:
                    for step in range(steps):
                        gram_copy(now, step).wait()
                for tile in range(size // TILE_ROWS):
                    at = slice(tile * TILE_ROWS, (tile + 1) * TILE_ROWS)
                    if paired:
                        square = gram_send[now, at, at].astype(jnp.float32)
                        trace += square + gram_recv[now, at, at].astype(jnp.float32)
                    else:
                        trace += gram[at, at]
                trace = jnp.sum(jnp.where(eye, trace, 0.0), axis=1, keepdims=True)
                trace = jnp.sum(trace, axis=0, keepdims=True)
                inverse_norm[...] = 1.0 / (jnp.sqrt(trace) + norm_epsilon)

            @pl.when(count > 0)
            def _():
                inverse_norm[...] = jnp.ones_like(inverse_norm)

            inverse = inverse_norm[...]
            shrink = inverse * inverse

            for step in range(steps):
                if paired:
                    @pl.when(count > 0)
                    def _(step=step):
                        gram_copy(now, step).wait()

                for tile in range(step * tall // TILE_ROWS, (step + 1) * tall // TILE_ROWS):
                    at = slice(tile * TILE_ROWS, (tile + 1) * TILE_ROWS)
                    if paired:
                        total = gram_send[now, at].astype(jnp.float32) + gram_recv[now, at].astype(jnp.float32)
                    else:
                        total = gram[at]
                    total = total * shrink
                    gram[at] = total
                    off_low[at] = total.astype(jnp.bfloat16)
                    square = total[:, at]
                    masked = jnp.where(eye, square, 0.0)
                    diag_col[at] = jnp.sum(masked, axis=1, keepdims=True)
                    diag_row[:, at] = jnp.sum(masked, axis=0, keepdims=True)
                    square = jnp.where(eye, 0.0, square)
                    gram[at, at] = square
                    off_low[at, at] = square.astype(jnp.bfloat16)

            linear, middle, cubic = ns_linear * inverse, ns_square * inverse, ns_cubic * inverse

            def poly_rows(step):
                at = pl.ds(step * tall, tall)
                again = product(off_low[at], off_low[...])
                mine = diag_col[at]
                poly = gram[at] * (middle + cubic * mine + cubic * diag_row[...]) + cubic * again
                poly_low[at] = poly.astype(jnp.bfloat16)
                again_diag = []
                for tile in range(tall // TILE_ROWS):
                    rows_at = slice(tile * TILE_ROWS, (tile + 1) * TILE_ROWS)
                    side_at = slice(step * tall + tile * TILE_ROWS, step * tall + (tile + 1) * TILE_ROWS)
                    again_diag.append(
                        jnp.sum(jnp.where(eye, again[rows_at, side_at], 0.0), axis=1, keepdims=True)
                    )
                    poly_low[side_at, side_at] = jnp.where(eye, 0.0, poly[rows_at, side_at]).astype(jnp.bfloat16)
                again_diag = jnp.concatenate(again_diag, axis=0)
                factor = linear + middle * mine + cubic * (mine * mine + again_diag)

                @pl.when(count < ITERS - 1)
                def _():
                    for left in range(0, columns, wide):
                        part = slice(left, left + wide)
                        moved = product(poly_low[at], iter_low[now, :, part])
                        fresh = factor * iter_full[at, part] + moved
                        iter_full[at, part] = fresh
                        iter_low[later, at, part] = fresh.astype(jnp.bfloat16)

                @pl.when(count == ITERS - 1)
                def _():
                    for index in range(nf):
                        @pl.when(fs == index)
                        def _(index=index):
                            part = slice(index * width, (index + 1) * width)
                            own_full[at, :width] = iter_full[at, part]

                            if step == 0:
                                own_low[:, :width] = iter_low[now, :, part]

                    moved = product(poly_low[at], own_low[:, :width])
                    fresh = factor * own_full[at, :width] + moved
                    blocks = tall // rows
                    own_out[pl.ds(step * blocks, blocks)] = fresh.astype(jnp.bfloat16).reshape(
                        blocks, rows, width
                    )

                    def give(index):
                        row = step * blocks + index

                        @pl.when(row != dp)
                        def _():
                            back_copy(row).start()

                        @pl.when(row == dp)
                        def _():
                            pltpu.make_async_copy(own_out.at[row], target, own_sem).start()

                    loop(blocks, give)

            for step in range(steps):
                poly_rows(step)

        loop(ITERS, iteration)

        if not paired:
            crossing.finish()

        def finish(row):
            @pl.when(row != dp)
            def _():
                back_copy(row).wait_send()

        loop(ndp, finish)
        pltpu.make_async_copy(own_out.at[dp], target, own_sem).wait()

    @pl.when(is_attn)
    def _():
        at = jnp.where(dp < 2, dp, dp - 4)
        iterate(land_attn, attn_ref.at[at], own_attn, attn_out.at[at], dp, False)

    @pl.when(is_ffn)
    def _():
        matrix, half = (dp - 2) // 2, lax.rem(dp - 2, 2)
        iterate(land_ffn, None, own_ffn, ffn_out.at[matrix, half], dp, True)

    for role in range(ROLES):
        @pl.when(dp != role)
        def _(role=role):
            if role < 2 or role >= 6:
                target = attn_out.at[role if role < 2 else role - 4]
            else:
                target = ffn_out.at[(role - 2) // 2, (role - 2) % 2]
            if role in attn_roles:
                piece_copy(role).wait_send()
            remote(target, target, own_sem, back_recv.at[role], (role, fs)).wait_recv()


def orthogonalize(ndp, nf, attn_low, ffn_whole):
    rows, width_attn = attn_low.shape[1:]
    width_ffn = ffn_whole.shape[3]
    side = math.isqrt(nf)
    size = rows * ndp
    columns = width_ffn * nf
    tall = min(STEP_ROWS, size)
    bf16, f32 = jnp.bfloat16, jnp.float32
    dma = pltpu.SemaphoreType.DMA
    return pl.pallas_call(
        functools.partial(ortho_kernel, ndp, nf),
        name="newton_schulz",
        out_shape=[
            jax.ShapeDtypeStruct(attn_low.shape, bf16),
            jax.ShapeDtypeStruct((2, 2, rows, width_ffn), bf16),
        ],
        in_specs=[pl.BlockSpec(memory_space=pltpu.VMEM), pl.BlockSpec(memory_space=pl.ANY)],
        out_specs=[pl.BlockSpec(memory_space=pltpu.VMEM)] * 2,
        scratch_shapes=[
            pltpu.VMEM((nf, ndp, rows, width_attn), bf16),
            pltpu.VMEM((nf, ndp, rows, width_ffn), bf16),
            pltpu.VMEM((2, size, columns), bf16),
            pltpu.VMEM((size, columns), f32),
            pltpu.VMEM((size, size), f32),
            pltpu.VMEM((2, size, size), bf16),
            pltpu.VMEM((2, size, size), bf16),
            pltpu.VMEM((size, size), bf16),
            pltpu.VMEM((size, size), bf16),
            pltpu.VMEM((1, size), f32),
            pltpu.VMEM((size, 1), f32),
            pltpu.VMEM((1, 1), f32),
            pltpu.VMEM((size, width_ffn), bf16),
            pltpu.VMEM((size, width_ffn), f32),
            pltpu.VMEM((ndp, rows, width_attn), bf16),
            pltpu.VMEM((ndp, rows, width_ffn), bf16),
            dma,
            dma((ROLES,)),
            dma((ndp,)),
            dma((ndp, side - 1)),
            dma((ndp, side, side - 1)),
            dma((nf, ndp)),
            dma((2, size // tall)),
            dma((2, size // tall)),
            dma((ndp,)),
            dma((ROLES,)),
            dma((nf,)),
        ],
        compiler_params=pltpu.CompilerParams(
            collective_id=1, has_side_effects=True, vmem_limit_bytes=60 * 1024 * 1024
        ),
    )(attn_low, ffn_whole)


def update_kernel(
    attn_w,
    ffn_w,
    vectors,
    attn_mom,
    ffn_mom,
    vec_mom,
    attn_ema,
    ffn_ema,
    vec_ema,
    attn_grad,
    up_grad,
    down_grad,
    vec_grad,
    attn_ortho,
    ffn_ortho,
    attn_new,
    ffn_new,
    vec_new,
    attn_mom_new,
    ffn_mom_new,
    vec_mom_new,
    attn_ema_new,
    ffn_ema_new,
    vec_ema_new,
    *,
    vector_rate,
):
    for index in range(4):
        rate = attn_rates[index]
        attn_mom_new[index] = matrix_decay * attn_mom[index] + attn_grad[index]
        new = attn_w[index] * (1.0 - weight_decay * rate) - rate * attn_ortho[index].astype(jnp.float32)
        attn_new[index] = new
        attn_ema_new[index] = average_decay * attn_ema[index] + (1.0 - average_decay) * new
    width = ffn_ortho.shape[-1]
    shape_factor = math.sqrt(FF / D)
    for index, grad in enumerate((up_grad, down_grad)):
        ffn_mom_new[index] = matrix_decay * ffn_mom[index] + grad[...]
        for half in range(2):
            at = slice(half * width, (half + 1) * width)
            ortho = ffn_ortho[index, half].astype(jnp.float32)
            new = ffn_w[index, :, at] * (1.0 - weight_decay) - shape_factor * ortho
            ffn_new[index, :, at] = new
            ffn_ema_new[index, :, at] = average_decay * ffn_ema[index, :, at] + (1.0 - average_decay) * new
    mom = vector_decay * vec_mom[...] + vec_grad[...]
    vec_mom_new[...] = mom
    new = vectors[...] - vector_rate * mom
    vec_new[...] = new
    vec_ema_new[...] = average_decay * vec_ema[...] + (1.0 - average_decay) * new


def update_all(vector_rate, *operands):
    states = operands[:9]
    return pl.pallas_call(
        functools.partial(update_kernel, vector_rate=vector_rate),
        name="update",
        out_shape=[jax.ShapeDtypeStruct(states[index % 3].shape, jnp.float32) for index in range(9)],
        in_specs=[pl.BlockSpec(memory_space=pltpu.VMEM)] * len(operands),
        out_specs=[pl.BlockSpec(memory_space=pltpu.VMEM)] * 9,
        compiler_params=pltpu.CompilerParams(vmem_limit_bytes=60 * 1024 * 1024),
    )(*operands)


ROOM = pltpu.CompilerParams(vmem_limit_bytes=56 * 1024 * 1024)
ROOT_HALF = math.sqrt(0.5)
BELL = 1.0 / math.sqrt(2.0 * math.pi)


def flat(block):
    return block.reshape(-1, block.shape[-1])


def head_lanes(values, head):
    if values.shape[1] == HDIM:
        return values
    lane = lax.broadcasted_iota(jnp.int32, values.shape, 1)
    return jnp.where(lax.div(lane, HDIM) == head, values, jnp.zeros_like(values))


def normalize(values):
    center = values - jnp.mean(values, axis=1, keepdims=True)
    inverse = lax.rsqrt(jnp.mean(center * center, axis=1, keepdims=True) + ln_epsilon)
    return center * inverse, inverse


def normalize_back(grad, scaled, inverse):
    return inverse * (
        grad
        - jnp.mean(grad, axis=1, keepdims=True)
        - scaled * jnp.mean(grad * scaled, axis=1, keepdims=True)
    )


def row_sum(values):
    return jnp.sum(values.astype(jnp.float32), axis=0, keepdims=True)


def forward_kernel(
    ndp,
    nf,
    tokens_ref,
    label_ref,
    cotangent_ref,
    attn_w,
    ffn_w,
    vectors_ref,
    attn_out,
    up_out,
    down_out,
    blocks_out,
    active_out,
    slope_out,
    vec_out,
    mixture_out,
    total_out,
    scaled_out,
    inverse_out,
    low_out,
    layer_out,
    d_second_out,
    sums_out,
    attn_shard,
    up_shard,
    down_shard,
    three_weight,
    out_weight,
    ffn_weight,
    vec_land,
    bias,
    bias_up,
    blocks,
    parts,
    active,
    slope,
    total,
    own_sem,
    own_recv,
    pair_recv,
    z_send,
    first_send,
    second_send,
    pair_send,
    load_sem,
    store_sem,
):
    chunks = 3
    shards, wholes = (attn_shard, up_shard, down_shard), (attn_out, up_out, down_out)
    z, core, y, x, nz, side = place(ndp, nf)
    dp, fs = z * 2 + core, y * side + x
    rows, width_attn = attn_w.shape[1:]
    width_ffn, share = ffn_w.shape[2], vectors_ref.shape[1]
    count = tokens_ref.shape[0]
    width = ffn_weight.shape[-1]
    per = width_ffn // width

    attn_shard[4 * rows :] = jnp.zeros((16, width_attn), jnp.bfloat16)
    attn_shard[4 * rows : 4 * rows + 12, :share] = vectors_ref[...].astype(jnp.bfloat16)
    for index in range(4):
        attn_shard[index * rows : (index + 1) * rows] = attn_w[index].astype(jnp.bfloat16)
    up_shard[...] = ffn_w[0].astype(jnp.bfloat16)
    down_shard[...] = ffn_w[1].astype(jnp.bfloat16)
    greet(line_partners(ndp, nf))

    def slot(chunk, plane_at, z_at):
        return wholes[chunk].at[plane_at, z_at * 2 + core]

    def source(chunk, plane_at, z_at, own):
        return shards[chunk] if own else slot(chunk, plane_at, z_at)

    def along(first, step):
        x_at = jnp.where(first, lax.rem(x + step, side), x)
        y_at = jnp.where(first, y, lax.rem(y + step, side))
        return y_at * side + x_at

    def first_copy(chunk, z_at, step, own):
        peer = along(lax.rem(z_at, 2) == 0, step)
        return remote(
            source(chunk, fs, z_at, own),
            slot(chunk, fs, z_at),
            first_send.at[chunk, z_at, step - 1],
            own_recv.at[chunk, fs, z_at],
            (dp, peer),
        )

    def second_copy(chunk, plane_at, z_at, step, own, line):
        peer = along(lax.rem(z_at, 2) != 0, step)
        return remote(
            source(chunk, plane_at, z_at, own),
            slot(chunk, plane_at, z_at),
            second_send.at[chunk, z_at, line, step - 1],
            own_recv.at[chunk, plane_at, z_at],
            (dp, peer),
        )

    def pair_copy(chunk, plane_at, z_at, own):
        return remote(
            source(chunk, plane_at, z_at, own),
            slot(chunk, plane_at, z_at),
            pair_send.at[chunk, plane_at, z_at],
            pair_recv.at[chunk, plane_at, z_at],
            (z * 2 + 1 - core, fs),
        )

    def z_copy(chunk, z_at, up, own):
        return remote(
            source(chunk, fs, z_at, own),
            slot(chunk, fs, z_at),
            z_send.at[chunk, z_at, up],
            own_recv.at[chunk, fs, z_at],
            ((z + (1 if up else -1)) * 2 + core, fs),
        )

    def along_z(chunk, z_at, own, act):
        @pl.when(jnp.logical_and(z_at <= z, z < nz - 1))
        def _():
            act(z_copy(chunk, z_at, 1, own))

        @pl.when(jnp.logical_and(z_at >= z, z > 0))
        def _():
            act(z_copy(chunk, z_at, 0, own))

    def arrived(chunk, plane_at, z_at):
        here = slot(chunk, plane_at, z_at)
        remote(here, here, own_sem.at[chunk], own_recv.at[chunk, plane_at, z_at], (dp, fs)).wait_recv()

    def pass_on(chunk, z_at, own):
        for step in range(1, side):
            first_copy(chunk, z_at, step, own).start()
            second_copy(chunk, fs, z_at, step, own, 0).start()
        pair_copy(chunk, fs, z_at, own).start()

    def own_copy(chunk):
        return pltpu.make_async_copy(shards[chunk], slot(chunk, fs, z), own_sem.at[chunk])

    def near_first(body):
        def each(index):
            far = 1 + lax.div(index, 2)
            z_at = jnp.where(lax.rem(index, 2) == 0, z - far, z + far)

            @pl.when(jnp.logical_and(z_at >= 0, z_at < nz))
            def _():
                body(z_at)

        loop(2 * (nz - 1), each)

    def from_z(chunk):
        def each(z_at):
            arrived(chunk, fs, z_at)
            along_z(chunk, z_at, False, lambda copy: copy.start())
            pass_on(chunk, z_at, False)

        near_first(each)

    def from_first(chunk):
        def each(z_at):
            for line in range(1, side):
                plane_at = along(lax.rem(z_at, 2) == 0, line)
                arrived(chunk, plane_at, z_at)
                for step in range(1, side):
                    second_copy(chunk, plane_at, z_at, step, False, line).start()
                pair_copy(chunk, plane_at, z_at, False).start()

        each(z)
        near_first(each)

    def last_places(z_at):
        x_first = lax.rem(z_at, 2) == 0
        for line in range(side):
            for step in range(1, side):
                near_x, far_y = lax.rem(x + line, side), lax.rem(y + step, side)
                far_x, near_y = lax.rem(x + step, side), lax.rem(y + line, side)
                yield jnp.where(x_first, far_y * side + near_x, near_y * side + far_x)

    def from_second(chunk):
        def each(z_at):
            for plane_at in last_places(z_at):
                arrived(chunk, plane_at, z_at)
                pair_copy(chunk, plane_at, z_at, False).start()

        each(z)
        near_first(each)

    def from_pair(chunk):
        own_copy(chunk).wait()

        def each(index):
            plane_at, z_at = lax.rem(index, nf), lax.div(index, nf)
            there = wholes[chunk].at[plane_at, z_at * 2 + 1 - core]
            remote(
                there, there, own_sem.at[chunk], pair_recv.at[chunk, plane_at, z_at], (dp, fs)
            ).wait_recv()

        loop(nf * nz, each)

    for chunk in range(chunks):
        own_copy(chunk).start(priority=1)
        along_z(chunk, z, True, lambda copy: copy.start())
        pass_on(chunk, z, True)

    from_z(0)
    from_first(0)
    from_z(1)
    from_second(0)
    from_pair(0)

    def load(index, source, target):
        return pltpu.make_async_copy(source, target, load_sem.at[index])

    def attn_load(index, block, at):
        per_block = ndp // nf
        if index == 0:
            return load(at, attn_out.at[block, :, pl.ds(0, 3 * rows)], three_weight.at[at])
        return load(
            2 + at,
            attn_out.at[:, pl.ds(block * per_block, per_block), pl.ds(3 * rows, rows)],
            out_weight.at[at],
        )

    vec_copy = load(4, attn_out.at[:, :, pl.ds(4 * rows, 16)], vec_land)
    vec_copy.start(priority=1)
    for index in range(2):
        attn_load(index, 0, 0).start(priority=1)
    vec_copy.wait()
    for row in range(ndp):
        for column in range(nf):
            left = (row * nf + column) * share
            vec_out[:, left : left + share] = vec_land[column, row, :, :share].astype(jnp.float32)
    for index in range(nf):
        at = slice(index * width_attn, (index + 1) * width_attn)
        bias[index, 0:1] = vec_out[0:1, at]
        bias[index, 1:2] = vec_out[1:2, at]
    for index in range(FF // width):
        left = index * width
        bias_up[index] = vec_out[5 + left // D : 6 + left // D, left % D : left % D + width]
    label_row = label_ref[...].astype(jnp.float32)
    label_col = jnp.transpose(jnp.broadcast_to(label_row, (128, count)))[:, 0:1]
    tokens = tokens_ref[...]
    lane = lax.broadcasted_iota(jnp.int32, (count, 128), 1)
    total[...] = jnp.broadcast_to(vec_out[2:3], (count, D))

    def attn_turn(block):
        at = lax.rem(block, 2)

        @pl.when(block < nf - 1)
        def _():
            for index in range(2):
                attn_load(index, block + 1, 1 - at).start(priority=1)

        attn_load(0, block, at).wait()
        attn_load(1, block, at).wait()
        weights = [flat(three_weight[at, :, index * rows : (index + 1) * rows]) for index in range(3)]
        queries = (product(tokens, weights[0]) + bias[block, 0:1]).astype(jnp.bfloat16)
        keys_all = product(tokens, weights[1]).astype(jnp.bfloat16)
        values_all = (product(tokens, weights[2]) + bias[block, 1:2]).astype(jnp.bfloat16)
        for index, values in enumerate((queries, keys_all, values_all)):
            blocks[block, index] = values
        pltpu.make_async_copy(blocks.at[block], blocks_out.at[block], store_sem.at[block]).start(priority=1)
        allowed = label_col == label_row
        totals = jnp.zeros((count, 128), jnp.float32)
        mixture = jnp.zeros((count, width_attn), jnp.float32)
        for head in range(width_attn // HDIM):
            scores = contract_cols(head_lanes(queries, head) * score_scale, keys_all)
            scores = jnp.where(allowed, scores, -1e30)
            top = jnp.max(scores, axis=1, keepdims=True)
            exponent = jnp.exp(scores - top)
            weight = jnp.sum(exponent, axis=1, keepdims=True)
            attention = (exponent * (1.0 / weight)).astype(jnp.bfloat16)
            totals = jnp.where(lane == head, top + jnp.log(weight), totals)
            mixture += product(attention, head_lanes(values_all, head))
        mixture = mixture.astype(jnp.bfloat16)
        parts[block] = mixture
        total_out[block] = jnp.transpose(totals)[:8]
        for index in range(nf):
            side_at = slice(index * width_attn, (index + 1) * width_attn)
            total[:, side_at] += product(mixture, flat(out_weight[at, index]))

        @pl.when(block == 0)
        def _():
            from_z(2)

        @pl.when(block == nf - 2)
        def _():
            from_first(1)

    loop(nf, attn_turn)

    def first_norm(index):
        at = pl.ds(pl.multiple_of(index * NORM_ROWS, NORM_ROWS), NORM_ROWS)
        scaled, inverse = normalize(tokens_ref[at].astype(jnp.float32) + total[at])
        scaled_out[at] = scaled
        inverse_out[at] = inverse
        normed = scaled * vec_out[3:4] + vec_out[4:5]
        low_out[at] = normed.astype(jnp.bfloat16)
        total[at] = normed + vec_out[9:10]

    loop(count // NORM_ROWS, first_norm)
    for index in range(nf):
        mixture_out[:, index * width_attn : (index + 1) * width_attn] = parts[index]

    def ffn_load(chunk, step, at):
        block, part = lax.div(step, per), lax.rem(step, per)
        left = pl.multiple_of(part * width, width)
        return load(5 + at, wholes[chunk].at[block, :, :, pl.ds(left, width)], ffn_weight.at[at])

    def ffn_steps(chunk, body, between):
        ffn_load(chunk, 0, 0).start(priority=1)

        def each(step):
            at = lax.rem(step, 2)

            @pl.when(step < FF // width - 1)
            def _():
                ffn_load(chunk, step + 1, 1 - at).start(priority=1)

            ffn_load(chunk, step, at).wait()
            body(step, at)
            between(step)

        loop(FF // width, each)

    def keep(step):
        column = pl.ds(pl.multiple_of(step * width, width), width)
        return (
            pltpu.make_async_copy(active.at[step], active_out.at[:, column], store_sem.at[nf]),
            pltpu.make_async_copy(slope.at[lax.rem(step, 2)], slope_out.at[:, column], store_sem.at[nf + 1]),
        )

    def up_step(step, at):
        up_proj = product(low_out[...], flat(ffn_weight[at])) + bias_up[step]
        half = 0.5 * (1.0 + lax.erf(up_proj * ROOT_HALF))

        @pl.when(step > 0)
        def _():
            for copy in keep(step - 1):
                copy.wait()

        active[step] = (up_proj * half).astype(jnp.bfloat16)
        slope[lax.rem(step, 2)] = (half + up_proj * (BELL * jnp.exp(-0.5 * up_proj * up_proj))).astype(
            jnp.bfloat16
        )
        for copy in keep(step):
            copy.start(priority=1)

    def down_step(step, at):
        total[...] += contract_cols(active[step], flat(ffn_weight[at]))

    def between_up(step):
        @pl.when(step == FF // width // 2)
        def _():
            from_first(2)

    from_second(1)
    from_pair(1)
    ffn_steps(1, up_step, between_up)
    for copy in keep(FF // width - 1):
        copy.wait()
    from_second(2)
    from_pair(2)
    ffn_steps(2, down_step, lambda step: None)
    sums_out[...] = jnp.zeros((8, D), jnp.float32)

    def second_norm(index):
        at = pl.ds(pl.multiple_of(index * NORM_ROWS, NORM_ROWS), NORM_ROWS)
        scaled, inverse = normalize(total[at])
        layer_out[at] = (scaled * vec_out[10:11] + vec_out[11:12]).astype(jnp.bfloat16)
        grad = cotangent_ref[at].astype(jnp.float32)
        d_second = normalize_back(grad * vec_out[10:11], scaled, inverse)
        d_second_out[at] = d_second
        sums_out[0:1] += row_sum(d_second.astype(jnp.bfloat16))
        sums_out[1:2] += row_sum(grad * scaled)
        sums_out[2:3] += row_sum(grad)

    loop(count // NORM_ROWS, second_norm)

    def stored(block):
        pltpu.make_async_copy(blocks.at[block], blocks_out.at[block], store_sem.at[block]).wait()

    loop(nf, stored)
    for chunk in range(chunks):
        def finish(z_at):
            along_z(chunk, z_at, False, lambda copy: copy.wait_send())
            for step in range(1, side):
                first_copy(chunk, z_at, step, False).wait_send()
                for line in range(side):
                    second_copy(chunk, fs, z_at, step, False, line).wait_send()

            def each(plane_at):
                pair_copy(chunk, plane_at, z_at, False).wait_send()

            loop(nf, each)

        loop(nz, finish)


def forward(ndp, nf, tokens, segments, cotangent, attn_w, ffn_w, vectors):
    nz, side, chunks = ndp // 2, math.isqrt(nf), 3
    count = tokens.shape[0]
    rows, width_attn = attn_w.shape[1:]
    width_ffn = ffn_w.shape[2]
    width = min(512, width_ffn)
    bf16, f32 = jnp.bfloat16, jnp.float32
    dma = pltpu.SemaphoreType.DMA
    anywhere, inside = pl.BlockSpec(memory_space=pl.ANY), pl.BlockSpec(memory_space=pltpu.VMEM)
    shape = jax.ShapeDtypeStruct
    return pl.pallas_call(
        functools.partial(forward_kernel, ndp, nf),
        name="forward",
        out_shape=[
            shape((nf, ndp, 4 * rows + 16, width_attn), bf16),
            shape((nf, ndp, rows, width_ffn), bf16),
            shape((nf, ndp, rows, width_ffn), bf16),
            shape((nf, 3, count, width_attn), bf16),
            shape((count, FF), bf16),
            shape((count, FF), bf16),
            shape((16, D), f32),
            shape((count, D), bf16),
            shape((nf, 8, count), f32),
            shape((count, D), f32),
            shape((count, 1), f32),
            shape((count, D), bf16),
            shape((count, D), bf16),
            shape((count, D), f32),
            shape((8, D), f32),
        ],
        in_specs=[inside] * 6,
        out_specs=[anywhere] * 6 + [inside] * 9,
        scratch_shapes=[
            pltpu.VMEM((4 * rows + 16, width_attn), bf16),
            pltpu.VMEM((rows, width_ffn), bf16),
            pltpu.VMEM((rows, width_ffn), bf16),
            pltpu.VMEM((2, ndp, 3 * rows, width_attn), bf16),
            pltpu.VMEM((2, nf, ndp // nf, rows, width_attn), bf16),
            pltpu.VMEM((2, ndp, rows, width), bf16),
            pltpu.VMEM((nf, ndp, 16, width_attn), bf16),
            pltpu.VMEM((nf, 8, width_attn), f32),
            pltpu.VMEM((FF // width, 1, width), f32),
            pltpu.VMEM((nf, 3, count, width_attn), bf16),
            pltpu.VMEM((nf, count, width_attn), bf16),
            pltpu.VMEM((FF // width, count, width), bf16),
            pltpu.VMEM((2, count, width), bf16),
            pltpu.VMEM((count, D), f32),
            dma((chunks,)),
            dma((chunks, nf, nz)),
            dma((chunks, nf, nz)),
            dma((chunks, nz, 2)),
            dma((chunks, nz, side - 1)),
            dma((chunks, nz, side, side - 1)),
            dma((chunks, nf, nz)),
            dma((7,)),
            dma((nf + 2,)),
        ],
        compiler_params=pltpu.CompilerParams(
            collective_id=2, has_side_effects=True, vmem_limit_bytes=60 * 1024 * 1024
        ),
    )(tokens, segments[None, :], cotangent, attn_w, ffn_w, vectors)


def backward_kernel(
    ndp,
    nf,
    d_second_ref,
    low_ref,
    scaled_ref,
    inverse_ref,
    vec_ref,
    active_ref,
    slope_ref,
    up_ref,
    down_ref,
    tokens_ref,
    label_ref,
    blocks_ref,
    mixture_ref,
    total_ref,
    attn_ref,
    tail_ref,
    attn_mom,
    ffn_mom,
    input_grad,
    up_out,
    down_out,
    attn_out,
    vec_out,
    attn_low,
    ffn_low,
    ffn_whole,
    held_up,
    held_down,
    held_attn,
    first_up,
    first_down,
    first_attn,
    second_up,
    second_down,
    second_attn,
    z_up,
    z_down,
    z_attn,
    stages_out,
    land,
    ffn_weight,
    ffn_act,
    attn_weight,
    attn_block,
    wide_low,
    wide_two,
    turned_one,
    turned_two,
    branch,
    bias_up_sum,
    query_sum,
    value_sum,
    vec_land,
    load_sem,
    step_sem,
    pair_send,
    pair_recv,
    first_send,
    first_recv,
    second_send,
    second_recv,
    z_send,
    z_recv,
    vec_send,
    vec_recv,
    piece_own,
    piece_send,
    piece_recv,
    piece_first,
    piece_second,
    piece_plane,
):
    z, core, y, x, nz, side = place(ndp, nf)
    dp, fs = z * 2 + core, y * side + x
    other = (z * 2 + 1 - core, fs)
    held, outs = (held_up, held_down, held_attn), (up_out, down_out, attn_out)
    from_first, from_second = (first_up, first_down, first_attn), (second_up, second_down, second_attn)
    from_z = (z_up, z_down, z_attn)
    chunks = 3
    rows, width_ffn = held_up.shape[2:]
    width_attn = held_attn.shape[-1]
    width = ffn_weight.shape[-1]
    per = width_ffn // width
    greet(all_partners(ndp, nf))

    def place_of(turn):
        step = nf - 1 - turn
        return lax.rem(y + lax.div(step, side), side) * side + lax.rem(x + lax.rem(step, side), side)

    def first_copy(chunk, z_at, line, step):
        x_first = lax.rem(z_at, 2) == 0
        near, far = lax.rem(x + step, side), lax.rem(y + step, side)
        to = jnp.where(x_first, y * side + near, far * side + x)
        at = jnp.where(
            x_first,
            lax.rem(y + line, side) * side + near,
            far * side + lax.rem(x + line, side),
        )
        return remote(
            held[chunk].at[z_at, at],
            from_first[chunk].at[z_at, step - 1, line],
            first_send.at[chunk, z_at, step - 1, line],
            first_recv.at[chunk, z_at, step - 1, line],
            (dp, to),
        )

    lag = 2
    total_steps = nf * per + nf
    schedule = {}
    for sent, base, stride in (((0, 1), 0, per), ((2,), nf * per, 1)):
        for turns in ((0,), tuple(range(1, nf - 1))):
            ready = min(base + (turns[-1] + 1) * stride - 1 + lag, total_steps)
            for z_at in range(0, nz, 2):
                schedule.setdefault(ready, []).extend((chunk, turns, z_at) for chunk in sent)

    def send_first(chunk, turns, z_from):
        def each(z_at):
            x_first = lax.rem(z_at, 2) == 0
            for turn in turns:
                step_x, step_y = (nf - 1 - turn) % side, (nf - 1 - turn) // side
                step = jnp.where(x_first, step_x, step_y)
                line = jnp.where(x_first, step_y, step_x)

                @pl.when(step > 0)
                def _(line=line, step=step):
                    first_copy(chunk, z_at, line, step).start()

        loop(z_from + 2, each, z_from)

    def sends_at(step, steps):
        for when in steps:
            @pl.when(step == when)
            def _(when=when):
                for chunk, turns, z_at in schedule.get(when, ()):
                    send_first(chunk, turns, z_at)

    def line_place(z_at, line):
        x_first = lax.rem(z_at, 2) == 0
        return jnp.where(
            x_first, lax.rem(y + line, side) * side + x, y * side + lax.rem(x + line, side)
        )

    def second_copy(chunk, z_at, step):
        to = line_place(z_at, step)
        return remote(
            held[chunk].at[z_at, to],
            from_second[chunk].at[z_at, step - 1],
            second_send.at[chunk, z_at, step - 1],
            second_recv.at[chunk, z_at, step - 1],
            (dp, to),
        )

    def z_copy(chunk, step):
        z_at = lax.rem(z + step, nz)
        return remote(
            held[chunk].at[z_at, fs],
            from_z[chunk].at[step - 1],
            z_send.at[chunk, step - 1],
            z_recv.at[chunk, step - 1],
            (z_at * 2 + core, fs),
        )

    def take_first(chunk, lines):
        def each(hop):
            z_at = lax.rem(z + 1 + hop, nz)
            for line in lines:
                at = line_place(z_at, line)
                for step in range(1, side):
                    first_copy(chunk, z_at, line, step).wait_recv()
                    held[chunk][z_at, at] += from_first[chunk][z_at, step - 1, line]
                if line:
                    second_copy(chunk, z_at, line).start()

        loop(nz, each)

    def take_second(chunk):
        def each(hop):
            z_at = lax.rem(z + 1 + hop, nz)
            for step in range(1, side):
                second_copy(chunk, z_at, step).wait_recv()
                held[chunk][z_at, fs] += from_second[chunk][z_at, step - 1]

            @pl.when(hop < nz - 1)
            def _():
                z_copy(chunk, hop + 1).start()

        loop(nz, each)

    def moments(chunk):
        source = ffn_mom.at[chunk] if chunk < 2 else attn_mom
        return pltpu.make_async_copy(source, outs[chunk], load_sem.at[3 + chunk])

    def take_z(chunk):
        total = held[chunk][z, fs].astype(jnp.float32)
        for step in range(1, nz):
            z_copy(chunk, step).wait_recv()
            total += from_z[chunk][step - 1].astype(jnp.float32)
        moments(chunk).wait()
        low = (matrix_decay * outs[chunk][...] + total).astype(jnp.bfloat16)
        outs[chunk][...] = total
        if chunk < 2:
            half = low.shape[1] // 2
            ffn_low[chunk, 0] = low[:, :half]
            ffn_low[chunk, 1] = low[:, half:]
        else:
            attn_low[...] = low

    vec_rounds = [[other]]
    vec_rounds.append([(dp, y * side + lax.rem(x + step, side)) for step in range(1, side)])
    vec_rounds.append([(dp, lax.rem(y + step, side) * side + x) for step in range(1, side)])
    vec_rounds.append([(lax.rem(z + step, nz) * 2 + core, fs) for step in range(1, nz)])
    starts = [sum(len(group) for group in vec_rounds[:index]) for index in range(4)]

    def vec_copy(index, step):
        at = starts[index] + step
        return remote(
            vec_land.at[index], vec_land.at[4 + at], vec_send.at[at], vec_recv.at[at], vec_rounds[index][step]
        )

    def vec_start(index):
        for step in range(len(vec_rounds[index])):
            vec_copy(index, step).start()

    def vec_take(index):
        total = vec_land[index]
        for step in range(len(vec_rounds[index])):
            vec_copy(index, step).wait_recv()
            total += vec_land[4 + starts[index] + step]
        if index < 3:
            vec_land[index + 1] = total
            vec_start(index + 1)
        else:
            vec_out[...] = total

    def split(values, keep, give):
        parts = values.astype(jnp.bfloat16).reshape(nz, 2, rows, values.shape[1])
        for which in range(2):
            @pl.when(core == which)
            def _(which=which):
                keep(parts[:, which])
                give(parts[:, 1 - which])

    def piece_copy(matrix, half):
        return remote(
            ffn_low.at[matrix, half],
            ffn_whole.at[fs, dp],
            piece_send.at[2 * matrix + half],
            piece_recv.at[dp],
            (2 + 2 * matrix + half, fs),
        )

    def piece_local(matrix, half):
        return pltpu.make_async_copy(ffn_low.at[matrix, half], ffn_whole.at[fs, dp], piece_own)

    def start_pieces(matrix):
        for half in range(2):
            @pl.when(dp != 2 + 2 * matrix + half)
            def _(half=half):
                piece_copy(matrix, half).start()

            @pl.when(dp == 2 + 2 * matrix + half)
            def _(half=half):
                piece_local(matrix, half).start(priority=1)

    crossing = Crossing(
        ndp, nf, ffn_whole, piece_own, piece_recv, piece_first, piece_second, piece_plane, ffn_low.at[0, 0]
    )
    runs_ffn = jnp.logical_and(dp >= 2, dp < 6)

    def ffn_loads(slot, turn, part):
        block = place_of(turn)
        at = pl.ds(part * width, width)
        column = pl.ds(pl.multiple_of(block * width_ffn + part * width, width), width)
        pairs = (
            (up_ref.at[block, :, :, at], ffn_weight.at[slot, 0]),
            (down_ref.at[block, :, :, at], ffn_weight.at[slot, 1]),
            (active_ref.at[:, column], ffn_act.at[slot, 0]),
            (slope_ref.at[:, column], ffn_act.at[slot, 1]),
        )
        return [
            pltpu.make_async_copy(source, target, step_sem.at[slot, index])
            for index, (source, target) in enumerate(pairs)
        ]

    def load(index, source, target):
        return pltpu.make_async_copy(source, target, load_sem.at[index])

    load(0, low_ref, wide_low).start(priority=1)
    load(1, d_second_ref, input_grad).start(priority=1)
    for copy in ffn_loads(0, 0, 0):
        copy.start(priority=1)
    load(2, tokens_ref, wide_two).start(priority=1)
    for chunk in range(chunks):
        moments(chunk).start(priority=1)
    load(0, low_ref, wide_low).wait()
    turned_one[...] = jnp.transpose(wide_low[...])
    load(1, d_second_ref, input_grad).wait()
    wide_low[...] = input_grad[...].astype(jnp.bfloat16)
    turned_two[...] = jnp.transpose(wide_low[...])

    def pair_copy(step):
        stage, slot = lax.rem(step, lag), lax.rem(step, 2 * lag)
        return remote(stages_out.at[stage], land.at[slot], pair_send.at[stage], pair_recv.at[slot], other)

    def pair_take(step):
        pair_copy(step).wait()
        slot = lax.rem(step, 2 * lag)

        @pl.when(step < nf * per)
        def _():
            block, part = place_of(lax.div(step, per)), lax.rem(step, per)
            for index in range(2):
                for which in range(per):
                    @pl.when(part == which)
                    def _(index=index, which=which):
                        for half in range(2):
                            left = which * width + half * width_attn
                            at = slice(left, left + width_attn)
                            held[index][:, block, :, at] += land[slot, :, 2 * index + half]

        @pl.when(step >= nf * per)
        def _():
            held_attn[:, place_of(step - nf * per)] += land[slot]

    def ffn_turn(turn):
        block = place_of(turn)
        for part in range(per):
            now = turn * per + part
            slot = lax.rem(now, 2)
            if part < per - 1:
                for copy in ffn_loads(1 - slot, turn, part + 1):
                    copy.start(priority=1)
            else:
                @pl.when(turn < nf - 1)
                def _():
                    for copy in ffn_loads(1 - slot, turn + 1, 0):
                        copy.start(priority=1)

            for copy in ffn_loads(slot, turn, part):
                copy.wait()
            d_active = product(wide_low[...], flat(ffn_weight[slot, 1]))
            d_up = (d_active * ffn_act[slot, 1].astype(jnp.float32)).astype(jnp.bfloat16)
            bias_up_sum[block * per + part] = row_sum(d_up)
            input_grad[...] += contract_cols(d_up, flat(ffn_weight[slot, 0]))

            @pl.when(now >= lag)
            def _():
                pair_take(now - lag)

            sends_at(now, range(nf * per))
            at = slice(part * width, (part + 1) * width)
            for index in range(2):

                def keep(values, index=index):
                    held[index][:, block, :, at] = values

                def give(values, index=index):
                    for half in range(2):
                        side_at = slice(half * width_attn, (half + 1) * width_attn)
                        stages_out[lax.rem(now, lag), :, 2 * index + half] = values[:, :, side_at]

                if index == 0:
                    split(product(turned_one[...], d_up), keep, give)
                else:
                    split(product(turned_two[...], ffn_act[slot, 0]), keep, give)
            pair_copy(now).start()

    loop(nf, ffn_turn)

    load(2, tokens_ref, wide_two).wait()
    turned_one[...] = jnp.transpose(wide_two[...])
    load(0, mixture_ref, wide_two).start(priority=1)

    def attn_load(index, turn):
        block = place_of(turn)
        per_block = ndp // nf
        source, target = (
            (attn_ref.at[block, :, pl.ds(0, 3 * rows)], attn_weight[0]),
            (
                attn_ref.at[:, pl.ds(block * per_block, per_block), pl.ds(3 * rows, rows)],
                attn_weight[1],
            ),
            (blocks_ref.at[block], attn_block),
        )[index]
        return pltpu.make_async_copy(source, target, step_sem.at[0, index])

    for index in range(3):
        attn_load(index, 0).start(priority=1)
    vec_land[0] = jnp.zeros((16, D), jnp.float32)
    vec_land[0, 9:12] = tail_ref[0:3]

    def norm_back(index):
        at = pl.ds(pl.multiple_of(index * NORM_ROWS, NORM_ROWS), NORM_ROWS)
        grad = input_grad[at]
        scaled = scaled_ref[at]
        d_first = normalize_back(grad * vec_ref[3:4], scaled, inverse_ref[at])
        input_grad[at] = d_first
        low = d_first.astype(jnp.bfloat16)
        vec_land[0, 2:3] += row_sum(low)
        vec_land[0, 3:4] += row_sum(grad * scaled)
        vec_land[0, 4:5] += row_sum(grad)
        for column in range(nf):
            branch[column, at] = low[:, column * width_attn : (column + 1) * width_attn]

    loop(tokens_ref.shape[0] // NORM_ROWS, norm_back)
    label_row = label_ref[...].astype(jnp.float32)
    label_col = jnp.transpose(jnp.broadcast_to(label_row, (128, label_row.shape[1])))[:, 0:1]
    load(0, mixture_ref, wide_two).wait()
    turned_two[...] = jnp.transpose(wide_two[...])

    def attn_turn(turn):
        block = place_of(turn)
        now = nf * per + turn

        def load_next(index):
            @pl.when(turn < nf - 1)
            def _():
                attn_load(index, turn + 1).start(priority=1)

        for index in range(3):
            attn_load(index, turn).wait()
        count = tokens_ref.shape[0]
        zero = jnp.zeros((count, width_attn), jnp.float32)
        d_mixture = zero
        for index in range(nf):
            d_mixture += contract_cols(branch[index], flat(attn_weight[1][index]))
        load_next(1)
        d_mixture = d_mixture.astype(jnp.bfloat16)
        queries, keys_all, values_all = (attn_block[index] for index in range(3))
        allowed = label_col == label_row
        d_queries, d_keys, d_values = zero, zero, zero
        for head in range(width_attn // HDIM):
            my_queries = head_lanes(queries, head) * score_scale
            my_mixture = head_lanes(d_mixture, head)
            scores = contract_cols(keys_all, my_queries) - total_ref[block, head : head + 1, :]
            attention = jnp.where(allowed, jnp.exp(scores), 0.0)
            d_attention = contract_cols(values_all, my_mixture)
            inner = jnp.sum(d_attention * attention, axis=0, keepdims=True)
            d_scores = (attention * (d_attention - inner)).astype(jnp.bfloat16)
            d_keys += product(d_scores, my_queries)
            d_values += product(attention.astype(jnp.bfloat16), my_mixture)
            d_queries += contract_rows(d_scores, head_lanes(keys_all, head) * score_scale)
        load_next(2)
        grads = [values.astype(jnp.bfloat16) for values in (d_queries, d_keys, d_values)]
        query_sum[block] = row_sum(grads[0])
        value_sum[block] = row_sum(grads[2])
        moved = jnp.zeros((count, D), jnp.float32)
        for index in range(3):
            weight = attn_weight[0][:, index * rows : (index + 1) * rows]
            moved += contract_cols(grads[index], flat(weight))
        input_grad[...] += moved
        load_next(0)

        pair_take(now - lag)
        for index in range(4):
            turned, grad = (turned_one, grads[index]) if index < 3 else (turned_two, branch[block])

            def keep(values, index=index):
                held_attn[:, block, index] = values

            def give(values, index=index):
                stages_out[lax.rem(now, lag), :, index] = values

            split(product(turned[...], grad), keep, give)
        pair_copy(now).start()
        sends_at(now, range(nf * per, total_steps))

        @pl.when(turn == nf - 4)
        def _():
            take_first(0, range(1, side))
            take_first(1, range(1, side))

        @pl.when(turn == nf - 3)
        def _():
            take_first(0, (0,))
            take_first(1, (0,))

        @pl.when(turn == nf - 2)
        def _():
            take_second(0)
            take_second(1)

    loop(nf, attn_turn)
    for index in range(nf):
        at = slice(index * width_attn, (index + 1) * width_attn)
        vec_land[0, 0:1, at] = query_sum[index]
        vec_land[0, 1:2, at] = value_sum[index]
    for index in range(nf * per):
        left = index * width
        vec_land[0, 5 + left // D : 6 + left // D, left % D : left % D + width] = bias_up_sum[index]
    vec_start(0)
    for step in range(total_steps - lag, total_steps):
        pair_take(step)
    sends_at(total_steps, (total_steps,))

    take_first(2, range(1, side))
    take_z(0)
    start_pieces(0)
    take_z(1)
    start_pieces(1)
    vec_take(0)
    take_first(2, (0,))
    take_second(2)
    vec_take(1)

    @pl.when(runs_ffn)
    def _():
        crossing.take()

    vec_take(2)
    take_z(2)
    vec_take(3)

    @pl.when(runs_ffn)
    def _():
        crossing.pass_on()
        crossing.near()
        crossing.far()
        crossing.finish()

    for matrix in range(2):
        for half in range(2):
            @pl.when(dp != 2 + 2 * matrix + half)
            def _(matrix=matrix, half=half):
                piece_copy(matrix, half).wait_send()

    for chunk in range(chunks):

        def finish(z_at):
            for step in range(1, side):
                second_copy(chunk, z_at, step).wait_send()
                for line in range(side):
                    first_copy(chunk, z_at, line, step).wait_send()

        loop(nz, finish)
        for step in range(1, nz):
            z_copy(chunk, step).wait_send()
    for index in range(4):
        for step in range(len(vec_rounds[index])):
            vec_copy(index, step).wait_send()


def backward_kernel_entry(ndp, nf, *refs):
    at = 18 + 8 + 12 + 2 + 2
    backward_kernel(ndp, nf, *refs[:at], refs[at : at + 2], *refs[at + 2 :])


def backward(
    ndp, nf, d_second, low, scaled, inverse, vectors, active, slope, up_all, down_all,
    tokens, segments, blocks, mixture, totals, attn_all, tail_sums, attn_mom, ffn_mom,
):
    nz, side = ndp // 2, math.isqrt(nf)
    count = tokens.shape[0]
    rows, width_ffn = up_all.shape[2:]
    width_attn = attn_all.shape[-1]
    width = 2 * width_attn
    bf16, f32 = jnp.bfloat16, jnp.float32
    dma = pltpu.SemaphoreType.DMA
    anywhere, inside = pl.BlockSpec(memory_space=pl.ANY), pl.BlockSpec(memory_space=pltpu.VMEM)
    shapes = [(rows, width_ffn), (rows, width_ffn), (4, rows, width_attn)]
    vec_copies = 1 + 2 * (side - 1) + nz - 1
    sums = []
    for lead in ((nz, nf), (nz, side - 1, side), (nz, side - 1), (nz - 1,)):
        sums += [pltpu.VMEM(lead + shape, bf16) for shape in shapes]
    return pl.pallas_call(
        functools.partial(backward_kernel_entry, ndp, nf),
        name="backward",
        out_shape=[jax.ShapeDtypeStruct((count, D), f32)]
        + [jax.ShapeDtypeStruct(shape, f32) for shape in shapes]
        + [
            jax.ShapeDtypeStruct((16, D), f32),
            jax.ShapeDtypeStruct(attn_mom.shape, bf16),
            jax.ShapeDtypeStruct((2, 2, rows, width_ffn // 2), bf16),
            jax.ShapeDtypeStruct((nf, ndp, rows, width_ffn // 2), bf16),
        ],
        in_specs=[
            anywhere,
            anywhere,
            inside,
            inside,
            inside,
            anywhere,
            anywhere,
            anywhere,
            anywhere,
            anywhere,
            inside,
            anywhere,
            anywhere,
            inside,
            anywhere,
            inside,
            anywhere,
            anywhere,
        ],
        out_specs=[inside] * 7 + [anywhere],
        scratch_shapes=sums
        + [
            pltpu.VMEM((2, nz, 4, rows, width_attn), bf16),
            pltpu.VMEM((4, nz, 4, rows, width_attn), bf16),
            pltpu.VMEM((2, 2, ndp, rows, width), bf16),
            pltpu.VMEM((2, 2, count, width), bf16),
            pltpu.VMEM((ndp, 3 * rows, width_attn), bf16),
            pltpu.VMEM((nf, ndp // nf, rows, width_attn), bf16),
            pltpu.VMEM((3, count, width_attn), bf16),
            pltpu.VMEM((count, D), bf16),
            pltpu.VMEM((count, D), bf16),
            pltpu.VMEM((D, count), bf16),
            pltpu.VMEM((D, count), bf16),
            pltpu.VMEM((nf, count, width_attn), bf16),
            pltpu.VMEM((FF // width, 1, width), f32),
            pltpu.VMEM((nf, 1, width_attn), f32),
            pltpu.VMEM((nf, 1, width_attn), f32),
            pltpu.VMEM((4 + vec_copies, 16, D), f32),
            dma((6,)),
            dma((2, 4)),
            dma((2,)),
            dma((4,)),
            dma((3, nz, side - 1, side)),
            dma((3, nz, side - 1, side)),
            dma((3, nz, side - 1)),
            dma((3, nz, side - 1)),
            dma((3, nz - 1)),
            dma((3, nz - 1)),
            dma((vec_copies,)),
            dma((vec_copies,)),
            dma,
            dma((4,)),
            dma((ndp,)),
            dma((ndp, side - 1)),
            dma((ndp, side, side - 1)),
            dma((nf, ndp)),
        ],
        compiler_params=pltpu.CompilerParams(
            collective_id=3, has_side_effects=True, vmem_limit_bytes=63 * 1024 * 1024
        ),
    )(
        d_second, low, scaled, inverse, vectors, active, slope, up_all, down_all,
        tokens, segments[None, :], blocks, mixture, totals, attn_all, tail_sums, attn_mom, ffn_mom,
    )


def on_device(
    tokens,
    segments,
    cotangent,
    attn_w,
    ffn_w,
    vectors,
    attn_mom,
    ffn_mom,
    vec_mom,
    attn_ema,
    ffn_ema,
    vec_ema,
):
    ndp, nf = lax.axis_size("dp"), lax.axis_size("fsdp")
    share = vectors.shape[1]
    (
        attn_all, up_all, down_all, blocks, active, slope, vec_full, mixture, totals, scaled, inverse, low,
        layer_out, d_second, tail_sums,
    ) = forward(ndp, nf, tokens, segments, cotangent, attn_w, ffn_w, vectors)
    input_grad, up_grad, down_grad, attn_grad, vec_sum, attn_piece, _, ffn_whole = backward(
        ndp, nf, d_second, low, scaled, inverse, vec_full, active, slope, up_all, down_all,
        tokens, segments, blocks, mixture, totals, attn_all, tail_sums, attn_mom, ffn_mom,
    )
    mine = (lax.axis_index("dp") * nf + lax.axis_index("fsdp")) * share
    vec_grad = lax.dynamic_slice(vec_sum, (0, mine), (12, share))
    attn_ortho, ffn_ortho = orthogonalize(ndp, nf, attn_piece, ffn_whole)
    total_tokens = tokens.shape[0] * ndp * nf
    updated = update_all(
        vector_step / math.sqrt(total_tokens),
        attn_w,
        ffn_w,
        vectors,
        attn_mom,
        ffn_mom,
        vec_mom,
        attn_ema,
        ffn_ema,
        vec_ema,
        attn_grad,
        up_grad,
        down_grad,
        vec_grad,
        attn_ortho,
        ffn_ortho,
    )
    return (layer_out, input_grad, *updated, vec_grad[2])


def solution(mesh):
    in_specs = (
        P(("dp", "fsdp"), None),
        P(("dp", "fsdp")),
        P(("dp", "fsdp"), None),
        P(None, "dp", "fsdp"),
        P(None, "dp", "fsdp"),
        P(None, ("dp", "fsdp")),
        P(None, "dp", "fsdp"),
        P(None, "dp", "fsdp"),
        P(None, ("dp", "fsdp")),
        P(None, "dp", "fsdp"),
        P(None, "dp", "fsdp"),
        P(None, ("dp", "fsdp")),
    )
    out_specs = (
        P(("dp", "fsdp"), None),
        P(("dp", "fsdp"), None),
        P(None, "dp", "fsdp"),
        P(None, "dp", "fsdp"),
        P(None, ("dp", "fsdp")),
        P(None, "dp", "fsdp"),
        P(None, "dp", "fsdp"),
        P(None, ("dp", "fsdp")),
        P(None, "dp", "fsdp"),
        P(None, "dp", "fsdp"),
        P(None, ("dp", "fsdp")),
        P(("dp", "fsdp")),
    )
    return jax.shard_map(
        on_device, mesh=mesh, in_specs=in_specs, out_specs=out_specs, check_vma=False
    )
```

```python
import functools
import math

import jax
import jax.numpy as jnp
from jax import lax
from jax.experimental import pallas as pl
from jax.experimental.pallas import tpu as pltpu
from jax.sharding import PartitionSpec as P

D = 1024
FF = 4096
HEADS = 16
HDIM = 64
TILE = 512
ITERS = 5


score_scale = 0.125
ln_epsilon = 1e-05
norm_epsilon = 1e-06
ns_linear = 3.4445
ns_square = -4.775
ns_cubic = 2.0315
matrix_decay = 0.95
vector_decay = 0.9
average_decay = 0.7
weight_decay = 0.01
attn_rates = (1.0, 1.0, 1.0, 10.0)
vector_step = 0.3


def product(left, right):
    return jnp.dot(left, right, preferred_element_type=jnp.float32)


def contract_rows(left, right):
    return lax.dot_general(
        left, right, (((0,), (0,)), ((), ())), preferred_element_type=jnp.float32
    )


def contract_cols(left, right):
    return lax.dot_general(
        left, right, (((1,), (1,)), ((), ())), preferred_element_type=jnp.float32
    )


MESH = pl.DeviceIdType.MESH
ROLES = 8
STEP_ROWS = 512
NORM_ROWS = 128
TILE_ROWS = 128


def greet(partners):
    barrier = pltpu.get_barrier_semaphore()
    for partner in partners:
        pl.semaphore_signal(barrier, inc=1, device_id=partner, device_id_type=MESH)
    pl.semaphore_wait(barrier, len(partners))


def place(ndp, nf):
    dp, fs = lax.axis_index("dp"), lax.axis_index("fsdp")
    side = math.isqrt(nf)
    return lax.div(dp, 2), lax.rem(dp, 2), lax.div(fs, side), lax.rem(fs, side), ndp // 2, side


def line_partners(ndp, nf):
    z, core, y, x, nz, side = place(ndp, nf)
    mine = y * side + x
    return (
        [(z * 2 + 1 - core, mine)]
        + [(lax.rem(z + step, nz) * 2 + core, mine) for step in range(1, nz)]
        + [(z * 2 + core, y * side + lax.rem(x + step, side)) for step in range(1, side)]
        + [(z * 2 + core, lax.rem(y + step, side) * side + x) for step in range(1, side)]
    )


def all_partners(ndp, nf):
    z, core, y, x, nz, side = place(ndp, nf)
    dp, fs = z * 2 + core, y * side + x
    return (
        [(lax.rem(dp + step, ndp), fs) for step in range(1, ndp)]
        + [(dp, y * side + lax.rem(x + step, side)) for step in range(1, side)]
        + [(dp, lax.rem(y + step, side) * side + x) for step in range(1, side)]
    )


def remote(source, target, send_sem, recv_sem, device):
    return pltpu.make_async_remote_copy(
        src_ref=source,
        dst_ref=target,
        send_sem=send_sem,
        recv_sem=recv_sem,
        device_id=device,
        device_id_type=MESH,
    )


def loop(count, body, start=0):
    def step(index, carry):
        body(index)
        return carry

    lax.fori_loop(start, count, step, 0)


class Crossing:
    def __init__(self, ndp, nf, land, own_sem, piece_recv, first_send, second_send, plane_recv, source):
        self.ndp, self.land, self.own_sem, self.piece_recv, self.source = ndp, land, own_sem, piece_recv, source
        self.first_send, self.second_send, self.plane_recv = first_send, second_send, plane_recv
        self.z, self.core, self.y, self.x, self.nz, self.side = place(ndp, nf)
        self.dp, self.fs = self.z * 2 + self.core, self.y * self.side + self.x

    def row_of(self, index):
        return lax.rem(self.z + index // 2, self.nz) * 2 + lax.rem(self.core + index, 2)

    def x_first(self, row):
        return lax.rem(row // 2, 2) == 0

    def along(self, first, step):
        x_at = jnp.where(first, lax.rem(self.x + step, self.side), self.x)
        y_at = jnp.where(first, self.y, lax.rem(self.y + step, self.side))
        return y_at * self.side + x_at

    def first_copy(self, row, step):
        here = self.land.at[self.fs, row]
        peer = self.along(self.x_first(row), step)
        sems = self.first_send.at[row, step - 1], self.plane_recv.at[self.fs, row]
        return remote(here, here, *sems, (self.dp, peer))

    def second_copy(self, plane_at, row, line, step):
        here = self.land.at[plane_at, row]
        peer = self.along(jnp.logical_not(self.x_first(row)), step)
        sems = self.second_send.at[row, line, step - 1], self.plane_recv.at[plane_at, row]
        return remote(here, here, *sems, (self.dp, peer))

    def arrived(self, plane_at, row):
        here = self.land.at[plane_at, row]
        remote(here, here, self.own_sem, self.plane_recv.at[plane_at, row], (self.dp, self.fs)).wait_recv()

    def take(self):
        def each(index):
            row = self.row_of(index)

            @pl.when(index == 0)
            def _():
                pltpu.make_async_copy(self.source, self.land.at[self.fs, row], self.own_sem).wait()

            @pl.when(index > 0)
            def _():
                here = self.land.at[self.fs, row]
                remote(self.source, here, self.own_sem, self.piece_recv.at[row], (self.dp, self.fs)).wait_recv()

            for step in range(1, self.side):
                self.first_copy(row, step).start()
                self.second_copy(self.fs, row, 0, step).start()

        loop(self.ndp, each)

    def pass_on(self):
        def each(index):
            row = self.row_of(index)
            for line in range(1, self.side):
                plane_at = self.along(self.x_first(row), line)
                self.arrived(plane_at, row)
                for step in range(1, self.side):
                    self.second_copy(plane_at, row, line, step).start()

        loop(self.ndp, each)

    def wait_line(self, line):
        for step in range(1, self.side):

            def each(index, step=step):
                row = self.row_of(index)
                x, y, side = self.x, self.y, self.side
                there = jnp.where(
                    self.x_first(row),
                    lax.rem(y + step, side) * side + lax.rem(x + line, side),
                    lax.rem(y + line, side) * side + lax.rem(x + step, side),
                )
                self.arrived(there, row)

            loop(self.ndp, each)

    def near(self):
        self.wait_line(0)

    def far(self):
        for line in range(1, self.side):
            self.wait_line(line)

    def finish(self):
        def each(row):
            for step in range(1, self.side):
                self.first_copy(row, step).wait_send()
                for line in range(self.side):
                    self.second_copy(self.fs, row, line, step).wait_send()

        loop(self.ndp, each)


def ortho_kernel(
    ndp,
    nf,
    attn_ref,
    ffn_whole,
    attn_out,
    ffn_out,
    land_attn,
    land_ffn,
    iter_low,
    iter_full,
    gram,
    gram_send,
    gram_recv,
    off_low,
    poly_low,
    diag_row,
    diag_col,
    inverse_norm,
    own_low,
    own_full,
    own_attn,
    own_ffn,
    own_sem,
    piece_send,
    piece_recv,
    first_send,
    second_send,
    plane_recv,
    gram_send_sem,
    gram_recv_sem,
    back_send,
    back_recv,
    load_sem,
):
    z, core, y, x, nz, side = place(ndp, nf)
    dp, fs = z * 2 + core, y * side + x
    rows = attn_ref.shape[1]
    size = rows * ndp
    is_attn = jnp.logical_or(dp < 2, jnp.logical_and(dp >= 6, dp < ROLES))
    is_ffn = jnp.logical_and(dp >= 2, dp < 6)
    partner = z * 2 + 1 - core

    greet(all_partners(ndp, nf))
    attn_roles = (0, 6, 1, 7)

    def piece(role):
        return attn_ref.at[role if role < 2 else role - 4]

    def piece_copy(role):
        return remote(piece(role), land_attn.at[fs, dp], piece_send.at[role], piece_recv.at[dp], (role, fs))

    for role in attn_roles:
        @pl.when(dp != role)
        def _(role=role):
            piece_copy(role).start()

        @pl.when(dp == role)
        def _(role=role):
            pltpu.make_async_copy(piece(role), land_attn.at[fs, dp], own_sem).start()

    def iterate(land, source, own_out, target, role, paired):
        width = land.shape[-1]
        columns = width * nf
        tall = min(STEP_ROWS, size)
        steps = size // tall
        wide = min(1024, columns)

        def add_gram(plane_at, fresh):
            block = land[plane_at].reshape(size, width)
            for step in range(steps):
                at = slice(step * tall, (step + 1) * tall)
                part = contract_cols(block[at], block)
                if fresh:
                    gram[at] = part
                else:
                    gram[at] += part

        if paired:

            def block_load(index):
                return pltpu.make_async_copy(ffn_whole.at[index], land.at[index], load_sem.at[index])

            for index in range(nf):
                block_load(index).start()
            for index in range(nf):
                block_load(index).wait()
                add_gram(index, index == 0)
        else:
            crossing = Crossing(ndp, nf, land, own_sem, piece_recv, first_send, second_send, plane_recv, source)
            crossing.take()
            add_gram(fs, True)
            crossing.pass_on()
            crossing.near()
            for step in range(1, side):
                add_gram(crossing.along(True, step), False)
                add_gram(crossing.along(False, step), False)
            crossing.far()
            for far_y in range(1, side):
                for far_x in range(1, side):
                    add_gram(lax.rem(y + far_y, side) * side + lax.rem(x + far_x, side), False)

        def gram_copy(slot, step):
            at = pl.ds(step * tall, tall)
            return remote(
                gram_send.at[slot, at],
                gram_recv.at[slot, at],
                gram_send_sem.at[slot, step],
                gram_recv_sem.at[slot, step],
                (partner, fs),
            )

        if paired:
            for step in range(steps):
                at = slice(step * tall, (step + 1) * tall)
                gram_send[0, at] = gram[at].astype(jnp.bfloat16)
                gram_copy(0, step).start()
        for index in range(nf):
            block = land[index].reshape(size, width)
            at = slice(index * width, (index + 1) * width)
            iter_low[0, :, at] = block
            iter_full[:, at] = block.astype(jnp.float32)

        def back_copy(row):
            return remote(own_out.at[row], target, back_send.at[row], back_recv.at[role], (row, fs))

        def iteration(count):
            now = lax.rem(count, 2)
            later = 1 - now

            @pl.when(count > 0)
            def _():
                def gram_rows(step):
                    at = pl.ds(pl.multiple_of(step * tall, tall), tall)
                    part = contract_cols(iter_low[now, at, :columns], iter_low[now, :, :columns])
                    if paired:
                        gram_send[now, at] = part.astype(jnp.bfloat16)
                        gram_copy(now, step).start()
                    else:
                        gram[at] = part

                loop(steps, gram_rows)

            eye = lax.broadcasted_iota(jnp.int32, (TILE_ROWS, TILE_ROWS), 0) == lax.broadcasted_iota(
                jnp.int32, (TILE_ROWS, TILE_ROWS), 1
            )

            @pl.when(count == 0)
            def _():
                trace = jnp.zeros((TILE_ROWS, TILE_ROWS), jnp.float32)
                if paired:
                    for step in range(steps):
                        gram_copy(now, step).wait()
                for tile in range(size // TILE_ROWS):
                    at = slice(tile * TILE_ROWS, (tile + 1) * TILE_ROWS)
                    if paired:
                        square = gram_send[now, at, at].astype(jnp.float32)
                        trace += square + gram_recv[now, at, at].astype(jnp.float32)
                    else:
                        trace += gram[at, at]
                trace = jnp.sum(jnp.where(eye, trace, 0.0), axis=1, keepdims=True)
                trace = jnp.sum(trace, axis=0, keepdims=True)
                inverse_norm[...] = 1.0 / (jnp.sqrt(trace) + norm_epsilon)

            @pl.when(count > 0)
            def _():
                inverse_norm[...] = jnp.ones_like(inverse_norm)

            inverse = inverse_norm[...]
            shrink = inverse * inverse

            for step in range(steps):
                if paired:
                    @pl.when(count > 0)
                    def _(step=step):
                        gram_copy(now, step).wait()

                for tile in range(step * tall // TILE_ROWS, (step + 1) * tall // TILE_ROWS):
                    at = slice(tile * TILE_ROWS, (tile + 1) * TILE_ROWS)
                    if paired:
                        total = gram_send[now, at].astype(jnp.float32) + gram_recv[now, at].astype(jnp.float32)
                    else:
                        total = gram[at]
                    total = total * shrink
                    gram[at] = total
                    off_low[at] = total.astype(jnp.bfloat16)
                    square = total[:, at]
                    masked = jnp.where(eye, square, 0.0)
                    diag_col[at] = jnp.sum(masked, axis=1, keepdims=True)
                    diag_row[:, at] = jnp.sum(masked, axis=0, keepdims=True)
                    square = jnp.where(eye, 0.0, square)
                    gram[at, at] = square
                    off_low[at, at] = square.astype(jnp.bfloat16)

            linear, middle, cubic = ns_linear * inverse, ns_square * inverse, ns_cubic * inverse

            def poly_rows(step):
                at = pl.ds(step * tall, tall)
                again = product(off_low[at], off_low[...])
                mine = diag_col[at]
                poly = gram[at] * (middle + cubic * mine + cubic * diag_row[...]) + cubic * again
                poly_low[at] = poly.astype(jnp.bfloat16)
                again_diag = []
                for tile in range(tall // TILE_ROWS):
                    rows_at = slice(tile * TILE_ROWS, (tile + 1) * TILE_ROWS)
                    side_at = slice(step * tall + tile * TILE_ROWS, step * tall + (tile + 1) * TILE_ROWS)
                    again_diag.append(
                        jnp.sum(jnp.where(eye, again[rows_at, side_at], 0.0), axis=1, keepdims=True)
                    )
                    poly_low[side_at, side_at] = jnp.where(eye, 0.0, poly[rows_at, side_at]).astype(jnp.bfloat16)
                again_diag = jnp.concatenate(again_diag, axis=0)
                factor = linear + middle * mine + cubic * (mine * mine + again_diag)

                @pl.when(count < ITERS - 1)
                def _():
                    for left in range(0, columns, wide):
                        part = slice(left, left + wide)
                        moved = product(poly_low[at], iter_low[now, :, part])
                        fresh = factor * iter_full[at, part] + moved
                        iter_full[at, part] = fresh
                        iter_low[later, at, part] = fresh.astype(jnp.bfloat16)

                @pl.when(count == ITERS - 1)
                def _():
                    for index in range(nf):
                        @pl.when(fs == index)
                        def _(index=index):
                            part = slice(index * width, (index + 1) * width)
                            own_full[at, :width] = iter_full[at, part]

                            if step == 0:
                                own_low[:, :width] = iter_low[now, :, part]

                    moved = product(poly_low[at], own_low[:, :width])
                    fresh = factor * own_full[at, :width] + moved
                    blocks = tall // rows
                    own_out[pl.ds(step * blocks, blocks)] = fresh.astype(jnp.bfloat16).reshape(
                        blocks, rows, width
                    )

                    def give(index):
                        row = step * blocks + index

                        @pl.when(row != dp)
                        def _():
                            back_copy(row).start()

                        @pl.when(row == dp)
                        def _():
                            pltpu.make_async_copy(own_out.at[row], target, own_sem).start()

                    loop(blocks, give)

            for step in range(steps):
                poly_rows(step)

        loop(ITERS, iteration)

        if not paired:
            crossing.finish()

        def finish(row):
            @pl.when(row != dp)
            def _():
                back_copy(row).wait_send()

        loop(ndp, finish)
        pltpu.make_async_copy(own_out.at[dp], target, own_sem).wait()

    @pl.when(is_attn)
    def _():
        at = jnp.where(dp < 2, dp, dp - 4)
        iterate(land_attn, attn_ref.at[at], own_attn, attn_out.at[at], dp, False)

    @pl.when(is_ffn)
    def _():
        matrix, half = (dp - 2) // 2, lax.rem(dp - 2, 2)
        iterate(land_ffn, None, own_ffn, ffn_out.at[matrix, half], dp, True)

    for role in range(ROLES):
        @pl.when(dp != role)
        def _(role=role):
            if role < 2 or role >= 6:
                target = attn_out.at[role if role < 2 else role - 4]
            else:
                target = ffn_out.at[(role - 2) // 2, (role - 2) % 2]
            if role in attn_roles:
                piece_copy(role).wait_send()
            remote(target, target, own_sem, back_recv.at[role], (role, fs)).wait_recv()


def orthogonalize(ndp, nf, attn_low, ffn_whole):
    rows, width_attn = attn_low.shape[1:]
    width_ffn = ffn_whole.shape[3]
    side = math.isqrt(nf)
    size = rows * ndp
    columns = width_ffn * nf
    tall = min(STEP_ROWS, size)
    bf16, f32 = jnp.bfloat16, jnp.float32
    dma = pltpu.SemaphoreType.DMA
    return pl.pallas_call(
        functools.partial(ortho_kernel, ndp, nf),
        name="newton_schulz",
        out_shape=[
            jax.ShapeDtypeStruct(attn_low.shape, bf16),
            jax.ShapeDtypeStruct((2, 2, rows, width_ffn), bf16),
        ],
        in_specs=[pl.BlockSpec(memory_space=pltpu.VMEM), pl.BlockSpec(memory_space=pl.ANY)],
        out_specs=[pl.BlockSpec(memory_space=pltpu.VMEM)] * 2,
        scratch_shapes=[
            pltpu.VMEM((nf, ndp, rows, width_attn), bf16),
            pltpu.VMEM((nf, ndp, rows, width_ffn), bf16),
            pltpu.VMEM((2, size, columns), bf16),
            pltpu.VMEM((size, columns), f32),
            pltpu.VMEM((size, size), f32),
            pltpu.VMEM((2, size, size), bf16),
            pltpu.VMEM((2, size, size), bf16),
            pltpu.VMEM((size, size), bf16),
            pltpu.VMEM((size, size), bf16),
            pltpu.VMEM((1, size), f32),
            pltpu.VMEM((size, 1), f32),
            pltpu.VMEM((1, 1), f32),
            pltpu.VMEM((size, width_ffn), bf16),
            pltpu.VMEM((size, width_ffn), f32),
            pltpu.VMEM((ndp, rows, width_attn), bf16),
            pltpu.VMEM((ndp, rows, width_ffn), bf16),
            dma,
            dma((ROLES,)),
            dma((ndp,)),
            dma((ndp, side - 1)),
            dma((ndp, side, side - 1)),
            dma((nf, ndp)),
            dma((2, size // tall)),
            dma((2, size // tall)),
            dma((ndp,)),
            dma((ROLES,)),
            dma((nf,)),
        ],
        compiler_params=pltpu.CompilerParams(
            collective_id=1, has_side_effects=True, vmem_limit_bytes=60 * 1024 * 1024
        ),
    )(attn_low, ffn_whole)


def update_kernel(
    attn_w,
    ffn_w,
    vectors,
    attn_mom,
    ffn_mom,
    vec_mom,
    attn_ema,
    ffn_ema,
    vec_ema,
    attn_grad,
    up_grad,
    down_grad,
    vec_grad,
    attn_ortho,
    ffn_ortho,
    attn_new,
    ffn_new,
    vec_new,
    attn_mom_new,
    ffn_mom_new,
    vec_mom_new,
    attn_ema_new,
    ffn_ema_new,
    vec_ema_new,
    *,
    vector_rate,
):
    for index in range(4):
        rate = attn_rates[index]
        attn_mom_new[index] = matrix_decay * attn_mom[index] + attn_grad[index]
        new = attn_w[index] * (1.0 - weight_decay * rate) - rate * attn_ortho[index].astype(jnp.float32)
        attn_new[index] = new
        attn_ema_new[index] = average_decay * attn_ema[index] + (1.0 - average_decay) * new
    width = ffn_ortho.shape[-1]
    shape_factor = math.sqrt(FF / D)
    for index, grad in enumerate((up_grad, down_grad)):
        ffn_mom_new[index] = matrix_decay * ffn_mom[index] + grad[...]
        for half in range(2):
            at = slice(half * width, (half + 1) * width)
            ortho = ffn_ortho[index, half].astype(jnp.float32)
            new = ffn_w[index, :, at] * (1.0 - weight_decay) - shape_factor * ortho
            ffn_new[index, :, at] = new
            ffn_ema_new[index, :, at] = average_decay * ffn_ema[index, :, at] + (1.0 - average_decay) * new
    mom = vector_decay * vec_mom[...] + vec_grad[...]
    vec_mom_new[...] = mom
    new = vectors[...] - vector_rate * mom
    vec_new[...] = new
    vec_ema_new[...] = average_decay * vec_ema[...] + (1.0 - average_decay) * new


def update_all(vector_rate, *operands):
    states = operands[:9]
    return pl.pallas_call(
        functools.partial(update_kernel, vector_rate=vector_rate),
        name="update",
        out_shape=[jax.ShapeDtypeStruct(states[index % 3].shape, jnp.float32) for index in range(9)],
        in_specs=[pl.BlockSpec(memory_space=pltpu.VMEM)] * len(operands),
        out_specs=[pl.BlockSpec(memory_space=pltpu.VMEM)] * 9,
        compiler_params=pltpu.CompilerParams(vmem_limit_bytes=60 * 1024 * 1024),
    )(*operands)


ROOM = pltpu.CompilerParams(vmem_limit_bytes=56 * 1024 * 1024)
ROOT_HALF = math.sqrt(0.5)
BELL = 1.0 / math.sqrt(2.0 * math.pi)


def flat(block):
    return block.reshape(-1, block.shape[-1])


def head_lanes(values, head):
    if values.shape[1] == HDIM:
        return values
    lane = lax.broadcasted_iota(jnp.int32, values.shape, 1)
    return jnp.where(lax.div(lane, HDIM) == head, values, jnp.zeros_like(values))


def normalize(values):
    center = values - jnp.mean(values, axis=1, keepdims=True)
    inverse = lax.rsqrt(jnp.mean(center * center, axis=1, keepdims=True) + ln_epsilon)
    return center * inverse, inverse


def normalize_back(grad, scaled, inverse):
    return inverse * (
        grad
        - jnp.mean(grad, axis=1, keepdims=True)
        - scaled * jnp.mean(grad * scaled, axis=1, keepdims=True)
    )


def row_sum(values):
    return jnp.sum(values.astype(jnp.float32), axis=0, keepdims=True)


def forward_kernel(
    ndp,
    nf,
    tokens_ref,
    label_ref,
    cotangent_ref,
    attn_w,
    ffn_w,
    vectors_ref,
    attn_out,
    up_out,
    down_out,
    blocks_out,
    active_out,
    slope_out,
    vec_out,
    mixture_out,
    total_out,
    scaled_out,
    inverse_out,
    low_out,
    layer_out,
    d_second_out,
    sums_out,
    attn_shard,
    up_shard,
    down_shard,
    three_weight,
    out_weight,
    ffn_weight,
    vec_land,
    bias,
    bias_up,
    blocks,
    parts,
    active,
    slope,
    total,
    own_sem,
    own_recv,
    pair_recv,
    z_send,
    first_send,
    second_send,
    pair_send,
    load_sem,
    store_sem,
):
    chunks, turned = 4, 3
    wholes = (attn_out, up_out, down_out)
    z, core, y, x, nz, side = place(ndp, nf)
    dp, fs = z * 2 + core, y * side + x
    rows, width_attn = attn_w.shape[1:]
    width_ffn, share = ffn_w.shape[2], vectors_ref.shape[1]
    count = tokens_ref.shape[0]
    width = ffn_weight.shape[-1]
    per = width_ffn // width

    attn_shard[4 * rows :] = jnp.zeros((16, width_attn), jnp.bfloat16)
    attn_shard[4 * rows : 4 * rows + 12, :share] = vectors_ref[...].astype(jnp.bfloat16)
    for index in range(4):
        attn_shard[index * rows : (index + 1) * rows] = attn_w[index].astype(jnp.bfloat16)
    up_shard[...] = ffn_w[0].astype(jnp.bfloat16)
    down_shard[...] = ffn_w[1].astype(jnp.bfloat16)
    greet(line_partners(ndp, nf))

    halves = slice(0, width_ffn // 2), slice(width_ffn // 2, width_ffn)
    shards = (attn_shard, up_shard, down_shard.at[:, halves[0]], down_shard.at[:, halves[1]])

    def row_slot(chunk, plane_at, row):
        if chunk < 2:
            return wholes[chunk].at[plane_at, row]
        return down_out.at[plane_at, row, :, halves[chunk - 2]]

    def slot(chunk, plane_at, z_at):
        return row_slot(chunk, plane_at, z_at * 2 + core)

    def source(chunk, plane_at, z_at, own):
        return shards[chunk] if own else slot(chunk, plane_at, z_at)

    def along(first, step):
        x_at = jnp.where(first, lax.rem(x + step, side), x)
        y_at = jnp.where(first, y, lax.rem(y + step, side))
        return y_at * side + x_at

    def first_copy(chunk, z_at, step, own):
        peer = along(lax.rem(z_at, 2) == 0, step)
        return remote(
            source(chunk, fs, z_at, own),
            slot(chunk, fs, z_at),
            first_send.at[chunk, z_at, step - 1],
            own_recv.at[chunk, fs, z_at],
            (dp, peer),
        )

    def second_copy(chunk, plane_at, z_at, step, own, line):
        peer = along(lax.rem(z_at, 2) != 0, step)
        return remote(
            source(chunk, plane_at, z_at, own),
            slot(chunk, plane_at, z_at),
            second_send.at[chunk, z_at, line, step - 1],
            own_recv.at[chunk, plane_at, z_at],
            (dp, peer),
        )

    def pair_copy(chunk, plane_at, z_at, own):
        return remote(
            source(chunk, plane_at, z_at, own),
            slot(chunk, plane_at, z_at),
            pair_send.at[chunk, plane_at, z_at],
            pair_recv.at[chunk, plane_at, z_at],
            (z * 2 + 1 - core, fs),
        )

    def z_copy(chunk, plane_at, z_at, up, own):
        return remote(
            source(chunk, plane_at, z_at, own),
            slot(chunk, plane_at, z_at),
            z_send.at[chunk, plane_at, z_at, up],
            own_recv.at[chunk, plane_at, z_at],
            ((z + (1 if up else -1)) * 2 + core, fs),
        )

    def along_z(chunk, plane_at, z_at, own, act):
        @pl.when(jnp.logical_and(z_at <= z, z < nz - 1))
        def _():
            act(z_copy(chunk, plane_at, z_at, 1, own))

        @pl.when(jnp.logical_and(z_at >= z, z > 0))
        def _():
            act(z_copy(chunk, plane_at, z_at, 0, own))

    def begin(copy):
        copy.start()

    def arrived(chunk, plane_at, z_at):
        here = slot(chunk, plane_at, z_at)
        remote(here, here, own_sem.at[chunk], own_recv.at[chunk, plane_at, z_at], (dp, fs)).wait_recv()

    def pass_on(chunk, z_at, own):
        for step in range(1, side):
            first_copy(chunk, z_at, step, own).start()
            second_copy(chunk, fs, z_at, step, own, 0).start()
        pair_copy(chunk, fs, z_at, own).start()

    def own_copy(chunk):
        return pltpu.make_async_copy(shards[chunk], slot(chunk, fs, z), own_sem.at[chunk])

    def near_first(body):
        def each(index):
            far = 1 + lax.div(index, 2)
            z_at = jnp.where(lax.rem(index, 2) == 0, z - far, z + far)

            @pl.when(jnp.logical_and(z_at >= 0, z_at < nz))
            def _():
                body(z_at)

        loop(2 * (nz - 1), each)

    def from_z(chunk):
        def each(z_at):
            arrived(chunk, fs, z_at)
            along_z(chunk, fs, z_at, False, begin)
            pass_on(chunk, z_at, False)

        near_first(each)

    def from_first(chunk):
        def each(z_at):
            for line in range(1, side):
                plane_at = along(lax.rem(z_at, 2) == 0, line)
                arrived(chunk, plane_at, z_at)
                for step in range(1, side):
                    second_copy(chunk, plane_at, z_at, step, False, line).start()
                pair_copy(chunk, plane_at, z_at, False).start()

        each(z)
        near_first(each)

    def last_places(z_at):
        x_first = lax.rem(z_at, 2) == 0
        for line in range(side):
            for step in range(1, side):
                near_x, far_y = lax.rem(x + line, side), lax.rem(y + step, side)
                far_x, near_y = lax.rem(x + step, side), lax.rem(y + line, side)
                yield jnp.where(x_first, far_y * side + near_x, near_y * side + far_x)

    def from_second(chunk):
        def each(z_at):
            for plane_at in last_places(z_at):
                arrived(chunk, plane_at, z_at)
                pair_copy(chunk, plane_at, z_at, False).start()

        each(z)
        near_first(each)

    def turned_first():
        for line in range(1, side):
            plane_at = along(lax.rem(z, 2) == 0, line)
            arrived(turned, plane_at, z)
            for step in range(1, side):
                second_copy(turned, plane_at, z, step, False, line).start()
            along_z(turned, plane_at, z, False, begin)
            pair_copy(turned, plane_at, z, False).start()

    def turned_second():
        for plane_at in last_places(z):
            arrived(turned, plane_at, z)
            along_z(turned, plane_at, z, False, begin)
            pair_copy(turned, plane_at, z, False).start()

    def turned_z(far):
        for z_at in (z - far, z + far):
            @pl.when(jnp.logical_and(z_at >= 0, z_at < nz))
            def _(z_at=z_at):
                def each(step):
                    plane_at = lax.rem(fs + step, nf)
                    arrived(turned, plane_at, z_at)
                    along_z(turned, plane_at, z_at, False, begin)
                    pair_copy(turned, plane_at, z_at, False).start()

                loop(nf, each)

    def from_pair(chunk):
        own_copy(chunk).wait()

        def each(index):
            plane_at, z_at = lax.rem(index, nf), lax.div(index, nf)
            there = row_slot(chunk, plane_at, z_at * 2 + 1 - core)
            remote(
                there, there, own_sem.at[chunk], pair_recv.at[chunk, plane_at, z_at], (dp, fs)
            ).wait_recv()

        loop(nf * nz, each)

    for chunk in (0, turned, 1, 2):
        own_copy(chunk).start(priority=1)
        along_z(chunk, fs, z, True, begin)
        pass_on(chunk, z, True)

    from_z(0)
    from_first(0)
    turned_first()
    from_z(1)
    from_second(0)
    turned_second()
    from_pair(0)

    def load(index, source, target):
        return pltpu.make_async_copy(source, target, load_sem.at[index])

    def attn_load(index, block, at):
        per_block = ndp // nf
        if index == 0:
            return load(at, attn_out.at[block, :, pl.ds(0, 3 * rows)], three_weight.at[at])
        return load(
            2 + at,
            attn_out.at[:, pl.ds(block * per_block, per_block), pl.ds(3 * rows, rows)],
            out_weight.at[at],
        )

    vec_copy = load(4, attn_out.at[:, :, pl.ds(4 * rows, 16)], vec_land)
    vec_copy.start(priority=1)
    for index in range(2):
        attn_load(index, 0, 0).start(priority=1)
    vec_copy.wait()
    for row in range(ndp):
        for column in range(nf):
            left = (row * nf + column) * share
            vec_out[:, left : left + share] = vec_land[column, row, :, :share].astype(jnp.float32)
    for index in range(nf):
        at = slice(index * width_attn, (index + 1) * width_attn)
        bias[index, 0:1] = vec_out[0:1, at]
        bias[index, 1:2] = vec_out[1:2, at]
    for index in range(FF // width):
        left = index * width
        bias_up[index] = vec_out[5 + left // D : 6 + left // D, left % D : left % D + width]
    label_row = label_ref[...].astype(jnp.float32)
    label_col = jnp.transpose(jnp.broadcast_to(label_row, (128, count)))[:, 0:1]
    tokens = tokens_ref[...]
    lane = lax.broadcasted_iota(jnp.int32, (count, 128), 1)
    total[...] = jnp.broadcast_to(vec_out[2:3], (count, D))

    def attn_turn(block):
        at = lax.rem(block, 2)

        @pl.when(block < nf - 1)
        def _():
            for index in range(2):
                attn_load(index, block + 1, 1 - at).start(priority=1)

        attn_load(0, block, at).wait()
        attn_load(1, block, at).wait()
        weights = [flat(three_weight[at, :, index * rows : (index + 1) * rows]) for index in range(3)]
        queries = (product(tokens, weights[0]) + bias[block, 0:1]).astype(jnp.bfloat16)
        keys_all = product(tokens, weights[1]).astype(jnp.bfloat16)
        values_all = (product(tokens, weights[2]) + bias[block, 1:2]).astype(jnp.bfloat16)
        for index, values in enumerate((queries, keys_all, values_all)):
            blocks[block, index] = values
        pltpu.make_async_copy(blocks.at[block], blocks_out.at[block], store_sem.at[block]).start(priority=1)
        allowed = label_col == label_row
        totals = jnp.zeros((count, 128), jnp.float32)
        mixture = jnp.zeros((count, width_attn), jnp.float32)
        for head in range(width_attn // HDIM):
            scores = contract_cols(head_lanes(queries, head) * score_scale, keys_all)
            scores = jnp.where(allowed, scores, -1e30)
            top = jnp.max(scores, axis=1, keepdims=True)
            exponent = jnp.exp(scores - top)
            weight = jnp.sum(exponent, axis=1, keepdims=True)
            attention = (exponent * (1.0 / weight)).astype(jnp.bfloat16)
            totals = jnp.where(lane == head, top + jnp.log(weight), totals)
            mixture += product(attention, head_lanes(values_all, head))
        mixture = mixture.astype(jnp.bfloat16)
        parts[block] = mixture
        total_out[block] = jnp.transpose(totals)[:8]
        for index in range(nf):
            side_at = slice(index * width_attn, (index + 1) * width_attn)
            total[:, side_at] += product(mixture, flat(out_weight[at, index]))

        @pl.when(block == 0)
        def _():
            from_z(2)
            turned_z(1)

        @pl.when(block == nf - 2)
        def _():
            from_first(1)
            turned_z(2)

    loop(nf, attn_turn)

    def first_norm(index):
        at = pl.ds(pl.multiple_of(index * NORM_ROWS, NORM_ROWS), NORM_ROWS)
        scaled, inverse = normalize(tokens_ref[at].astype(jnp.float32) + total[at])
        scaled_out[at] = scaled
        inverse_out[at] = inverse
        normed = scaled * vec_out[3:4] + vec_out[4:5]
        low_out[at] = normed.astype(jnp.bfloat16)
        total[at] = normed + vec_out[9:10]

    loop(count // NORM_ROWS, first_norm)
    for index in range(nf):
        mixture_out[:, index * width_attn : (index + 1) * width_attn] = parts[index]

    def ffn_load(chunk, step, at):
        block, part = lax.div(step, per), lax.rem(step, per)
        left = pl.multiple_of(part * width, width)
        return load(5 + at, wholes[chunk].at[block, :, :, pl.ds(left, width)], ffn_weight.at[at])

    def ffn_steps(chunk, body, between):
        ffn_load(chunk, 0, 0).start(priority=1)

        def each(step):
            at = lax.rem(step, 2)

            @pl.when(step < FF // width - 1)
            def _():
                ffn_load(chunk, step + 1, 1 - at).start(priority=1)

            ffn_load(chunk, step, at).wait()
            body(step, at)
            between(step)

        loop(FF // width, each)

    def keep(step):
        column = pl.ds(pl.multiple_of(step * width, width), width)
        return (
            pltpu.make_async_copy(active.at[step], active_out.at[:, column], store_sem.at[nf]),
            pltpu.make_async_copy(slope.at[lax.rem(step, 2)], slope_out.at[:, column], store_sem.at[nf + 1]),
        )

    def up_step(step, at):
        up_proj = product(low_out[...], flat(ffn_weight[at])) + bias_up[step]
        half = 0.5 * (1.0 + lax.erf(up_proj * ROOT_HALF))

        @pl.when(step > 0)
        def _():
            for copy in keep(step - 1):
                copy.wait()

        active[step] = (up_proj * half).astype(jnp.bfloat16)
        slope[lax.rem(step, 2)] = (half + up_proj * (BELL * jnp.exp(-0.5 * up_proj * up_proj))).astype(
            jnp.bfloat16
        )
        for copy in keep(step):
            copy.start(priority=1)

    def down_step(step, at):
        total[...] += contract_cols(active[step], flat(ffn_weight[at]))

    def between_up(step):
        @pl.when(step == 0)
        def _():
            for far in range(3, nz):
                turned_z(far)

        @pl.when(step == FF // width // 2)
        def _():
            from_first(2)

    from_second(1)
    from_pair(1)
    ffn_steps(1, up_step, between_up)
    for copy in keep(FF // width - 1):
        copy.wait()
    from_second(2)
    from_pair(2)
    from_pair(turned)
    ffn_steps(2, down_step, lambda step: None)
    sums_out[...] = jnp.zeros((8, D), jnp.float32)

    def second_norm(index):
        at = pl.ds(pl.multiple_of(index * NORM_ROWS, NORM_ROWS), NORM_ROWS)
        scaled, inverse = normalize(total[at])
        layer_out[at] = (scaled * vec_out[10:11] + vec_out[11:12]).astype(jnp.bfloat16)
        grad = cotangent_ref[at].astype(jnp.float32)
        d_second = normalize_back(grad * vec_out[10:11], scaled, inverse)
        d_second_out[at] = d_second
        sums_out[0:1] += row_sum(d_second.astype(jnp.bfloat16))
        sums_out[1:2] += row_sum(grad * scaled)
        sums_out[2:3] += row_sum(grad)

    loop(count // NORM_ROWS, second_norm)

    def stored(block):
        pltpu.make_async_copy(blocks.at[block], blocks_out.at[block], store_sem.at[block]).wait()

    loop(nf, stored)
    for chunk in range(chunks):
        def finish(z_at):
            def sent():
                for step in range(1, side):
                    first_copy(chunk, z_at, step, False).wait_send()
                    for line in range(side):
                        second_copy(chunk, fs, z_at, step, False, line).wait_send()

            if chunk == turned:
                pl.when(z_at == z)(sent)
            else:
                sent()
                along_z(chunk, fs, z_at, False, lambda copy: copy.wait_send())

            def each(plane_at):
                pair_copy(chunk, plane_at, z_at, False).wait_send()
                if chunk == turned:
                    along_z(chunk, plane_at, z_at, False, lambda copy: copy.wait_send())

            loop(nf, each)

        loop(nz, finish)


def forward(ndp, nf, tokens, segments, cotangent, attn_w, ffn_w, vectors):
    nz, side, chunks = ndp // 2, math.isqrt(nf), 4
    count = tokens.shape[0]
    rows, width_attn = attn_w.shape[1:]
    width_ffn = ffn_w.shape[2]
    width = min(512, width_ffn)
    bf16, f32 = jnp.bfloat16, jnp.float32
    dma = pltpu.SemaphoreType.DMA
    anywhere, inside = pl.BlockSpec(memory_space=pl.ANY), pl.BlockSpec(memory_space=pltpu.VMEM)
    shape = jax.ShapeDtypeStruct
    return pl.pallas_call(
        functools.partial(forward_kernel, ndp, nf),
        name="forward",
        out_shape=[
            shape((nf, ndp, 4 * rows + 16, width_attn), bf16),
            shape((nf, ndp, rows, width_ffn), bf16),
            shape((nf, ndp, rows, width_ffn), bf16),
            shape((nf, 3, count, width_attn), bf16),
            shape((count, FF), bf16),
            shape((count, FF), bf16),
            shape((16, D), f32),
            shape((count, D), bf16),
            shape((nf, 8, count), f32),
            shape((count, D), f32),
            shape((count, 1), f32),
            shape((count, D), bf16),
            shape((count, D), bf16),
            shape((count, D), f32),
            shape((8, D), f32),
        ],
        in_specs=[inside] * 6,
        out_specs=[anywhere] * 6 + [inside] * 9,
        scratch_shapes=[
            pltpu.VMEM((4 * rows + 16, width_attn), bf16),
            pltpu.VMEM((rows, width_ffn), bf16),
            pltpu.VMEM((rows, width_ffn), bf16),
            pltpu.VMEM((2, ndp, 3 * rows, width_attn), bf16),
            pltpu.VMEM((2, nf, ndp // nf, rows, width_attn), bf16),
            pltpu.VMEM((2, ndp, rows, width), bf16),
            pltpu.VMEM((nf, ndp, 16, width_attn), bf16),
            pltpu.VMEM((nf, 8, width_attn), f32),
            pltpu.VMEM((FF // width, 1, width), f32),
            pltpu.VMEM((nf, 3, count, width_attn), bf16),
            pltpu.VMEM((nf, count, width_attn), bf16),
            pltpu.VMEM((FF // width, count, width), bf16),
            pltpu.VMEM((2, count, width), bf16),
            pltpu.VMEM((count, D), f32),
            dma((chunks,)),
            dma((chunks, nf, nz)),
            dma((chunks, nf, nz)),
            dma((chunks, nf, nz, 2)),
            dma((chunks, nz, side - 1)),
            dma((chunks, nz, side, side - 1)),
            dma((chunks, nf, nz)),
            dma((7,)),
            dma((nf + 2,)),
        ],
        compiler_params=pltpu.CompilerParams(
            collective_id=2, has_side_effects=True, vmem_limit_bytes=60 * 1024 * 1024
        ),
    )(tokens, segments[None, :], cotangent, attn_w, ffn_w, vectors)


def backward_kernel(
    ndp,
    nf,
    d_second_ref,
    low_ref,
    scaled_ref,
    inverse_ref,
    vec_ref,
    active_ref,
    slope_ref,
    up_ref,
    down_ref,
    tokens_ref,
    label_ref,
    blocks_ref,
    mixture_ref,
    total_ref,
    attn_ref,
    tail_ref,
    attn_mom,
    ffn_mom,
    input_grad,
    up_out,
    down_out,
    attn_out,
    vec_out,
    attn_low,
    ffn_low,
    ffn_whole,
    held_up,
    held_down,
    held_attn,
    first_up,
    first_down,
    first_attn,
    second_up,
    second_down,
    second_attn,
    z_up,
    z_down,
    z_attn,
    stages_out,
    land,
    ffn_weight,
    ffn_act,
    attn_weight,
    attn_block,
    wide_low,
    wide_two,
    turned_one,
    turned_two,
    branch,
    bias_up_sum,
    query_sum,
    value_sum,
    vec_land,
    load_sem,
    step_sem,
    pair_send,
    pair_recv,
    first_send,
    first_recv,
    second_send,
    second_recv,
    z_send,
    z_recv,
    vec_send,
    vec_recv,
    piece_own,
    piece_send,
    piece_recv,
    piece_first,
    piece_second,
    piece_plane,
):
    z, core, y, x, nz, side = place(ndp, nf)
    dp, fs = z * 2 + core, y * side + x
    other = (z * 2 + 1 - core, fs)
    held, outs = (held_up, held_down, held_attn), (up_out, down_out, attn_out)
    from_first, from_second = (first_up, first_down, first_attn), (second_up, second_down, second_attn)
    from_z = (z_up, z_down, z_attn)
    chunks = 3
    rows, width_ffn = held_up.shape[2:]
    width_attn = held_attn.shape[-1]
    width = ffn_weight.shape[-1]
    per = width_ffn // width
    greet(all_partners(ndp, nf))

    def place_of(turn):
        step = nf - 1 - turn
        return lax.rem(y + lax.div(step, side), side) * side + lax.rem(x + lax.rem(step, side), side)

    def first_copy(chunk, z_at, line, step):
        x_first = lax.rem(z_at, 2) == 0
        near, far = lax.rem(x + step, side), lax.rem(y + step, side)
        to = jnp.where(x_first, y * side + near, far * side + x)
        at = jnp.where(
            x_first,
            lax.rem(y + line, side) * side + near,
            far * side + lax.rem(x + line, side),
        )
        return remote(
            held[chunk].at[z_at, at],
            from_first[chunk].at[z_at, step - 1, line],
            first_send.at[chunk, z_at, step - 1, line],
            first_recv.at[chunk, z_at, step - 1, line],
            (dp, to),
        )

    lag = 2
    total_steps = nf * per + nf
    schedule = {}
    for sent, base, stride in (((0, 1), 0, per), ((2,), nf * per, 1)):
        for turns in ((0,), tuple(range(1, nf - 1))):
            ready = min(base + (turns[-1] + 1) * stride - 1 + lag, total_steps)
            for z_at in range(0, nz, 2):
                schedule.setdefault(ready, []).extend((chunk, turns, z_at) for chunk in sent)

    def send_first(chunk, turns, z_from):
        def each(z_at):
            x_first = lax.rem(z_at, 2) == 0
            for turn in turns:
                step_x, step_y = (nf - 1 - turn) % side, (nf - 1 - turn) // side
                step = jnp.where(x_first, step_x, step_y)
                line = jnp.where(x_first, step_y, step_x)

                @pl.when(step > 0)
                def _(line=line, step=step):
                    first_copy(chunk, z_at, line, step).start()

        loop(z_from + 2, each, z_from)

    def sends_at(step, steps):
        for when in steps:
            @pl.when(step == when)
            def _(when=when):
                for chunk, turns, z_at in schedule.get(when, ()):
                    send_first(chunk, turns, z_at)

    def line_place(z_at, line):
        x_first = lax.rem(z_at, 2) == 0
        return jnp.where(
            x_first, lax.rem(y + line, side) * side + x, y * side + lax.rem(x + line, side)
        )

    def second_copy(chunk, z_at, step):
        to = line_place(z_at, step)
        return remote(
            held[chunk].at[z_at, to],
            from_second[chunk].at[z_at, step - 1],
            second_send.at[chunk, z_at, step - 1],
            second_recv.at[chunk, z_at, step - 1],
            (dp, to),
        )

    def z_copy(chunk, step):
        z_at = lax.rem(z + step, nz)
        return remote(
            held[chunk].at[z_at, fs],
            from_z[chunk].at[step - 1],
            z_send.at[chunk, step - 1],
            z_recv.at[chunk, step - 1],
            (z_at * 2 + core, fs),
        )

    def take_first(chunk, lines):
        def each(hop):
            z_at = lax.rem(z + 1 + hop, nz)
            for line in lines:
                at = line_place(z_at, line)
                for step in range(1, side):
                    first_copy(chunk, z_at, line, step).wait_recv()
                    held[chunk][z_at, at] += from_first[chunk][z_at, step - 1, line]
                if line:
                    second_copy(chunk, z_at, line).start()

        loop(nz, each)

    def take_second(chunk):
        def each(hop):
            z_at = lax.rem(z + 1 + hop, nz)
            for step in range(1, side):
                second_copy(chunk, z_at, step).wait_recv()
                held[chunk][z_at, fs] += from_second[chunk][z_at, step - 1]

            @pl.when(hop < nz - 1)
            def _():
                z_copy(chunk, hop + 1).start()

        loop(nz, each)

    def moments(chunk):
        source = ffn_mom.at[chunk] if chunk < 2 else attn_mom
        return pltpu.make_async_copy(source, outs[chunk], load_sem.at[3 + chunk])

    def take_z(chunk):
        total = held[chunk][z, fs].astype(jnp.float32)
        for step in range(1, nz):
            z_copy(chunk, step).wait_recv()
            total += from_z[chunk][step - 1].astype(jnp.float32)
        moments(chunk).wait()
        low = (matrix_decay * outs[chunk][...] + total).astype(jnp.bfloat16)
        outs[chunk][...] = total
        if chunk < 2:
            half = low.shape[1] // 2
            ffn_low[chunk, 0] = low[:, :half]
            ffn_low[chunk, 1] = low[:, half:]
        else:
            attn_low[...] = low

    vec_rounds = [[other]]
    vec_rounds.append([(dp, y * side + lax.rem(x + step, side)) for step in range(1, side)])
    vec_rounds.append([(dp, lax.rem(y + step, side) * side + x) for step in range(1, side)])
    vec_rounds.append([(lax.rem(z + step, nz) * 2 + core, fs) for step in range(1, nz)])
    starts = [sum(len(group) for group in vec_rounds[:index]) for index in range(4)]

    def vec_copy(index, step):
        at = starts[index] + step
        return remote(
            vec_land.at[index], vec_land.at[4 + at], vec_send.at[at], vec_recv.at[at], vec_rounds[index][step]
        )

    def vec_start(index):
        for step in range(len(vec_rounds[index])):
            vec_copy(index, step).start()

    def vec_take(index):
        total = vec_land[index]
        for step in range(len(vec_rounds[index])):
            vec_copy(index, step).wait_recv()
            total += vec_land[4 + starts[index] + step]
        if index < 3:
            vec_land[index + 1] = total
            vec_start(index + 1)
        else:
            vec_out[...] = total

    def split(values, keep, give):
        parts = values.astype(jnp.bfloat16).reshape(nz, 2, rows, values.shape[1])
        for which in range(2):
            @pl.when(core == which)
            def _(which=which):
                keep(parts[:, which])
                give(parts[:, 1 - which])

    def piece_copy(matrix, half):
        return remote(
            ffn_low.at[matrix, half],
            ffn_whole.at[fs, dp],
            piece_send.at[2 * matrix + half],
            piece_recv.at[dp],
            (2 + 2 * matrix + half, fs),
        )

    def piece_local(matrix, half):
        return pltpu.make_async_copy(ffn_low.at[matrix, half], ffn_whole.at[fs, dp], piece_own)

    def start_pieces(matrix):
        for half in range(2):
            @pl.when(dp != 2 + 2 * matrix + half)
            def _(half=half):
                piece_copy(matrix, half).start()

            @pl.when(dp == 2 + 2 * matrix + half)
            def _(half=half):
                piece_local(matrix, half).start(priority=1)

    crossing = Crossing(
        ndp, nf, ffn_whole, piece_own, piece_recv, piece_first, piece_second, piece_plane, ffn_low.at[0, 0]
    )
    runs_ffn = jnp.logical_and(dp >= 2, dp < 6)

    def ffn_loads(slot, turn, part):
        block = place_of(turn)
        at = pl.ds(part * width, width)
        column = pl.ds(pl.multiple_of(block * width_ffn + part * width, width), width)
        pairs = (
            (up_ref.at[block, :, :, at], ffn_weight.at[slot, 0]),
            (down_ref.at[block, :, :, at], ffn_weight.at[slot, 1]),
            (active_ref.at[:, column], ffn_act.at[slot, 0]),
            (slope_ref.at[:, column], ffn_act.at[slot, 1]),
        )
        return [
            pltpu.make_async_copy(source, target, step_sem.at[slot, index])
            for index, (source, target) in enumerate(pairs)
        ]

    def load(index, source, target):
        return pltpu.make_async_copy(source, target, load_sem.at[index])

    load(0, low_ref, wide_low).start(priority=1)
    load(1, d_second_ref, input_grad).start(priority=1)
    for copy in ffn_loads(0, 0, 0):
        copy.start(priority=1)
    load(2, tokens_ref, wide_two).start(priority=1)
    for chunk in range(chunks):
        moments(chunk).start(priority=1)
    load(0, low_ref, wide_low).wait()
    turned_one[...] = jnp.transpose(wide_low[...])
    load(1, d_second_ref, input_grad).wait()
    wide_low[...] = input_grad[...].astype(jnp.bfloat16)
    turned_two[...] = jnp.transpose(wide_low[...])

    def pair_copy(step):
        stage, slot = lax.rem(step, lag), lax.rem(step, 2 * lag)
        return remote(stages_out.at[stage], land.at[slot], pair_send.at[stage], pair_recv.at[slot], other)

    def pair_take(step):
        pair_copy(step).wait()
        slot = lax.rem(step, 2 * lag)

        @pl.when(step < nf * per)
        def _():
            block, part = place_of(lax.div(step, per)), lax.rem(step, per)
            for index in range(2):
                for which in range(per):
                    @pl.when(part == which)
                    def _(index=index, which=which):
                        for half in range(2):
                            left = which * width + half * width_attn
                            at = slice(left, left + width_attn)
                            held[index][:, block, :, at] += land[slot, :, 2 * index + half]

        @pl.when(step >= nf * per)
        def _():
            held_attn[:, place_of(step - nf * per)] += land[slot]

    def ffn_turn(turn):
        block = place_of(turn)
        for part in range(per):
            now = turn * per + part
            slot = lax.rem(now, 2)
            if part < per - 1:
                for copy in ffn_loads(1 - slot, turn, part + 1):
                    copy.start(priority=1)
            else:
                @pl.when(turn < nf - 1)
                def _():
                    for copy in ffn_loads(1 - slot, turn + 1, 0):
                        copy.start(priority=1)

            for copy in ffn_loads(slot, turn, part):
                copy.wait()
            d_active = product(wide_low[...], flat(ffn_weight[slot, 1]))
            d_up = (d_active * ffn_act[slot, 1].astype(jnp.float32)).astype(jnp.bfloat16)
            bias_up_sum[block * per + part] = row_sum(d_up)
            input_grad[...] += contract_cols(d_up, flat(ffn_weight[slot, 0]))

            @pl.when(now >= lag)
            def _():
                pair_take(now - lag)

            sends_at(now, range(nf * per))
            at = slice(part * width, (part + 1) * width)
            for index in range(2):

                def keep(values, index=index):
                    held[index][:, block, :, at] = values

                def give(values, index=index):
                    for half in range(2):
                        side_at = slice(half * width_attn, (half + 1) * width_attn)
                        stages_out[lax.rem(now, lag), :, 2 * index + half] = values[:, :, side_at]

                if index == 0:
                    split(product(turned_one[...], d_up), keep, give)
                else:
                    split(product(turned_two[...], ffn_act[slot, 0]), keep, give)
            pair_copy(now).start()

    loop(nf, ffn_turn)

    load(2, tokens_ref, wide_two).wait()
    turned_one[...] = jnp.transpose(wide_two[...])
    load(0, mixture_ref, wide_two).start(priority=1)

    def attn_load(index, turn):
        block = place_of(turn)
        per_block = ndp // nf
        source, target = (
            (attn_ref.at[block, :, pl.ds(0, 3 * rows)], attn_weight[0]),
            (
                attn_ref.at[:, pl.ds(block * per_block, per_block), pl.ds(3 * rows, rows)],
                attn_weight[1],
            ),
            (blocks_ref.at[block], attn_block),
        )[index]
        return pltpu.make_async_copy(source, target, step_sem.at[0, index])

    for index in range(3):
        attn_load(index, 0).start(priority=1)
    vec_land[0] = jnp.zeros((16, D), jnp.float32)
    vec_land[0, 9:12] = tail_ref[0:3]

    def norm_back(index):
        at = pl.ds(pl.multiple_of(index * NORM_ROWS, NORM_ROWS), NORM_ROWS)
        grad = input_grad[at]
        scaled = scaled_ref[at]
        d_first = normalize_back(grad * vec_ref[3:4], scaled, inverse_ref[at])
        input_grad[at] = d_first
        low = d_first.astype(jnp.bfloat16)
        vec_land[0, 2:3] += row_sum(low)
        vec_land[0, 3:4] += row_sum(grad * scaled)
        vec_land[0, 4:5] += row_sum(grad)
        for column in range(nf):
            branch[column, at] = low[:, column * width_attn : (column + 1) * width_attn]

    loop(tokens_ref.shape[0] // NORM_ROWS, norm_back)
    label_row = label_ref[...].astype(jnp.float32)
    label_col = jnp.transpose(jnp.broadcast_to(label_row, (128, label_row.shape[1])))[:, 0:1]
    load(0, mixture_ref, wide_two).wait()
    turned_two[...] = jnp.transpose(wide_two[...])

    def attn_turn(turn):
        block = place_of(turn)
        now = nf * per + turn

        def load_next(index):
            @pl.when(turn < nf - 1)
            def _():
                attn_load(index, turn + 1).start(priority=1)

        for index in range(3):
            attn_load(index, turn).wait()
        count = tokens_ref.shape[0]
        zero = jnp.zeros((count, width_attn), jnp.float32)
        d_mixture = zero
        for index in range(nf):
            d_mixture += contract_cols(branch[index], flat(attn_weight[1][index]))
        load_next(1)
        d_mixture = d_mixture.astype(jnp.bfloat16)
        queries, keys_all, values_all = (attn_block[index] for index in range(3))
        allowed = label_col == label_row
        d_queries, d_keys, d_values = zero, zero, zero
        for head in range(width_attn // HDIM):
            my_queries = head_lanes(queries, head) * score_scale
            my_mixture = head_lanes(d_mixture, head)
            scores = contract_cols(keys_all, my_queries) - total_ref[block, head : head + 1, :]
            attention = jnp.where(allowed, jnp.exp(scores), 0.0)
            d_attention = contract_cols(values_all, my_mixture)
            inner = jnp.sum(d_attention * attention, axis=0, keepdims=True)
            d_scores = (attention * (d_attention - inner)).astype(jnp.bfloat16)
            d_keys += product(d_scores, my_queries)
            d_values += product(attention.astype(jnp.bfloat16), my_mixture)
            d_queries += contract_rows(d_scores, head_lanes(keys_all, head) * score_scale)
        load_next(2)
        grads = [values.astype(jnp.bfloat16) for values in (d_queries, d_keys, d_values)]
        query_sum[block] = row_sum(grads[0])
        value_sum[block] = row_sum(grads[2])
        moved = jnp.zeros((count, D), jnp.float32)
        for index in range(3):
            weight = attn_weight[0][:, index * rows : (index + 1) * rows]
            moved += contract_cols(grads[index], flat(weight))
        input_grad[...] += moved
        load_next(0)

        pair_take(now - lag)
        for index in range(4):
            turned, grad = (turned_one, grads[index]) if index < 3 else (turned_two, branch[block])

            def keep(values, index=index):
                held_attn[:, block, index] = values

            def give(values, index=index):
                stages_out[lax.rem(now, lag), :, index] = values

            split(product(turned[...], grad), keep, give)
        pair_copy(now).start()
        sends_at(now, range(nf * per, total_steps))

        @pl.when(turn == nf - 4)
        def _():
            take_first(0, range(1, side))
            take_first(1, range(1, side))

        @pl.when(turn == nf - 3)
        def _():
            take_first(0, (0,))
            take_first(1, (0,))

        @pl.when(turn == nf - 2)
        def _():
            take_second(0)
            take_second(1)

    loop(nf, attn_turn)
    for index in range(nf):
        at = slice(index * width_attn, (index + 1) * width_attn)
        vec_land[0, 0:1, at] = query_sum[index]
        vec_land[0, 1:2, at] = value_sum[index]
    for index in range(nf * per):
        left = index * width
        vec_land[0, 5 + left // D : 6 + left // D, left % D : left % D + width] = bias_up_sum[index]
    vec_start(0)
    for step in range(total_steps - lag, total_steps):
        pair_take(step)
    sends_at(total_steps, (total_steps,))

    take_first(2, range(1, side))
    take_z(0)
    start_pieces(0)
    take_z(1)
    start_pieces(1)
    vec_take(0)
    take_first(2, (0,))
    take_second(2)
    vec_take(1)

    @pl.when(runs_ffn)
    def _():
        crossing.take()

    vec_take(2)
    take_z(2)
    vec_take(3)

    @pl.when(runs_ffn)
    def _():
        crossing.pass_on()
        crossing.near()
        crossing.far()
        crossing.finish()

    for matrix in range(2):
        for half in range(2):
            @pl.when(dp != 2 + 2 * matrix + half)
            def _(matrix=matrix, half=half):
                piece_copy(matrix, half).wait_send()

    for chunk in range(chunks):

        def finish(z_at):
            for step in range(1, side):
                second_copy(chunk, z_at, step).wait_send()
                for line in range(side):
                    first_copy(chunk, z_at, line, step).wait_send()

        loop(nz, finish)
        for step in range(1, nz):
            z_copy(chunk, step).wait_send()
    for index in range(4):
        for step in range(len(vec_rounds[index])):
            vec_copy(index, step).wait_send()


def backward_kernel_entry(ndp, nf, *refs):
    at = 18 + 8 + 12 + 2 + 2
    backward_kernel(ndp, nf, *refs[:at], refs[at : at + 2], *refs[at + 2 :])


def backward(
    ndp, nf, d_second, low, scaled, inverse, vectors, active, slope, up_all, down_all,
    tokens, segments, blocks, mixture, totals, attn_all, tail_sums, attn_mom, ffn_mom,
):
    nz, side = ndp // 2, math.isqrt(nf)
    count = tokens.shape[0]
    rows, width_ffn = up_all.shape[2:]
    width_attn = attn_all.shape[-1]
    width = 2 * width_attn
    bf16, f32 = jnp.bfloat16, jnp.float32
    dma = pltpu.SemaphoreType.DMA
    anywhere, inside = pl.BlockSpec(memory_space=pl.ANY), pl.BlockSpec(memory_space=pltpu.VMEM)
    shapes = [(rows, width_ffn), (rows, width_ffn), (4, rows, width_attn)]
    vec_copies = 1 + 2 * (side - 1) + nz - 1
    sums = []
    for lead in ((nz, nf), (nz, side - 1, side), (nz, side - 1), (nz - 1,)):
        sums += [pltpu.VMEM(lead + shape, bf16) for shape in shapes]
    return pl.pallas_call(
        functools.partial(backward_kernel_entry, ndp, nf),
        name="backward",
        out_shape=[jax.ShapeDtypeStruct((count, D), f32)]
        + [jax.ShapeDtypeStruct(shape, f32) for shape in shapes]
        + [
            jax.ShapeDtypeStruct((16, D), f32),
            jax.ShapeDtypeStruct(attn_mom.shape, bf16),
            jax.ShapeDtypeStruct((2, 2, rows, width_ffn // 2), bf16),
            jax.ShapeDtypeStruct((nf, ndp, rows, width_ffn // 2), bf16),
        ],
        in_specs=[
            anywhere,
            anywhere,
            inside,
            inside,
            inside,
            anywhere,
            anywhere,
            anywhere,
            anywhere,
            anywhere,
            inside,
            anywhere,
            anywhere,
            inside,
            anywhere,
            inside,
            anywhere,
            anywhere,
        ],
        out_specs=[inside] * 7 + [anywhere],
        scratch_shapes=sums
        + [
            pltpu.VMEM((2, nz, 4, rows, width_attn), bf16),
            pltpu.VMEM((4, nz, 4, rows, width_attn), bf16),
            pltpu.VMEM((2, 2, ndp, rows, width), bf16),
            pltpu.VMEM((2, 2, count, width), bf16),
            pltpu.VMEM((ndp, 3 * rows, width_attn), bf16),
            pltpu.VMEM((nf, ndp // nf, rows, width_attn), bf16),
            pltpu.VMEM((3, count, width_attn), bf16),
            pltpu.VMEM((count, D), bf16),
            pltpu.VMEM((count, D), bf16),
            pltpu.VMEM((D, count), bf16),
            pltpu.VMEM((D, count), bf16),
            pltpu.VMEM((nf, count, width_attn), bf16),
            pltpu.VMEM((FF // width, 1, width), f32),
            pltpu.VMEM((nf, 1, width_attn), f32),
            pltpu.VMEM((nf, 1, width_attn), f32),
            pltpu.VMEM((4 + vec_copies, 16, D), f32),
            dma((6,)),
            dma((2, 4)),
            dma((2,)),
            dma((4,)),
            dma((3, nz, side - 1, side)),
            dma((3, nz, side - 1, side)),
            dma((3, nz, side - 1)),
            dma((3, nz, side - 1)),
            dma((3, nz - 1)),
            dma((3, nz - 1)),
            dma((vec_copies,)),
            dma((vec_copies,)),
            dma,
            dma((4,)),
            dma((ndp,)),
            dma((ndp, side - 1)),
            dma((ndp, side, side - 1)),
            dma((nf, ndp)),
        ],
        compiler_params=pltpu.CompilerParams(
            collective_id=3, has_side_effects=True, vmem_limit_bytes=63 * 1024 * 1024
        ),
    )(
        d_second, low, scaled, inverse, vectors, active, slope, up_all, down_all,
        tokens, segments[None, :], blocks, mixture, totals, attn_all, tail_sums, attn_mom, ffn_mom,
    )


def on_device(
    tokens,
    segments,
    cotangent,
    attn_w,
    ffn_w,
    vectors,
    attn_mom,
    ffn_mom,
    vec_mom,
    attn_ema,
    ffn_ema,
    vec_ema,
):
    ndp, nf = lax.axis_size("dp"), lax.axis_size("fsdp")
    share = vectors.shape[1]
    (
        attn_all, up_all, down_all, blocks, active, slope, vec_full, mixture, totals, scaled, inverse, low,
        layer_out, d_second, tail_sums,
    ) = forward(ndp, nf, tokens, segments, cotangent, attn_w, ffn_w, vectors)
    input_grad, up_grad, down_grad, attn_grad, vec_sum, attn_piece, _, ffn_whole = backward(
        ndp, nf, d_second, low, scaled, inverse, vec_full, active, slope, up_all, down_all,
        tokens, segments, blocks, mixture, totals, attn_all, tail_sums, attn_mom, ffn_mom,
    )
    mine = (lax.axis_index("dp") * nf + lax.axis_index("fsdp")) * share
    vec_grad = lax.dynamic_slice(vec_sum, (0, mine), (12, share))
    attn_ortho, ffn_ortho = orthogonalize(ndp, nf, attn_piece, ffn_whole)
    total_tokens = tokens.shape[0] * ndp * nf
    updated = update_all(
        vector_step / math.sqrt(total_tokens),
        attn_w,
        ffn_w,
        vectors,
        attn_mom,
        ffn_mom,
        vec_mom,
        attn_ema,
        ffn_ema,
        vec_ema,
        attn_grad,
        up_grad,
        down_grad,
        vec_grad,
        attn_ortho,
        ffn_ortho,
    )
    return (layer_out, input_grad, *updated, vec_grad[2])


def solution(mesh):
    in_specs = (
        P(("dp", "fsdp"), None),
        P(("dp", "fsdp")),
        P(("dp", "fsdp"), None),
        P(None, "dp", "fsdp"),
        P(None, "dp", "fsdp"),
        P(None, ("dp", "fsdp")),
        P(None, "dp", "fsdp"),
        P(None, "dp", "fsdp"),
        P(None, ("dp", "fsdp")),
        P(None, "dp", "fsdp"),
        P(None, "dp", "fsdp"),
        P(None, ("dp", "fsdp")),
    )
    out_specs = (
        P(("dp", "fsdp"), None),
        P(("dp", "fsdp"), None),
        P(None, "dp", "fsdp"),
        P(None, "dp", "fsdp"),
        P(None, ("dp", "fsdp")),
        P(None, "dp", "fsdp"),
        P(None, "dp", "fsdp"),
        P(None, ("dp", "fsdp")),
        P(None, "dp", "fsdp"),
        P(None, "dp", "fsdp"),
        P(None, ("dp", "fsdp")),
        P(("dp", "fsdp")),
    )
    return jax.shard_map(
        on_device, mesh=mesh, in_specs=in_specs, out_specs=out_specs, check_vma=False
    )
```

```python
import functools
import math

import jax
import jax.numpy as jnp
from jax import lax
from jax.experimental import pallas as pl
from jax.experimental.pallas import tpu as pltpu
from jax.sharding import PartitionSpec as P

D = 1024
FF = 4096
HEADS = 16
HDIM = 64
TILE = 512
ITERS = 5


score_scale = 0.125
ln_epsilon = 1e-05
norm_epsilon = 1e-06
ns_linear = 3.4445
ns_square = -4.775
ns_cubic = 2.0315
matrix_decay = 0.95
vector_decay = 0.9
average_decay = 0.7
weight_decay = 0.01
attn_rates = (1.0, 1.0, 1.0, 10.0)
vector_step = 0.3


def product(left, right):
    return jnp.dot(left, right, preferred_element_type=jnp.float32)


def contract_rows(left, right):
    return lax.dot_general(
        left, right, (((0,), (0,)), ((), ())), preferred_element_type=jnp.float32
    )


def contract_cols(left, right):
    return lax.dot_general(
        left, right, (((1,), (1,)), ((), ())), preferred_element_type=jnp.float32
    )


MESH = pl.DeviceIdType.MESH
ROLES = 8
STEP_ROWS = 512
NORM_ROWS = 128
TILE_ROWS = 128


def greet(partners):
    barrier = pltpu.get_barrier_semaphore()
    for partner in partners:
        pl.semaphore_signal(barrier, inc=1, device_id=partner, device_id_type=MESH)
    pl.semaphore_wait(barrier, len(partners))


def place(ndp, nf):
    dp, fs = lax.axis_index("dp"), lax.axis_index("fsdp")
    side = math.isqrt(nf)
    return lax.div(dp, 2), lax.rem(dp, 2), lax.div(fs, side), lax.rem(fs, side), ndp // 2, side


def line_partners(ndp, nf):
    z, core, y, x, nz, side = place(ndp, nf)
    mine = y * side + x
    return (
        [(z * 2 + 1 - core, mine)]
        + [(lax.rem(z + step, nz) * 2 + core, mine) for step in range(1, nz)]
        + [(z * 2 + core, y * side + lax.rem(x + step, side)) for step in range(1, side)]
        + [(z * 2 + core, lax.rem(y + step, side) * side + x) for step in range(1, side)]
    )


def all_partners(ndp, nf):
    z, core, y, x, nz, side = place(ndp, nf)
    dp, fs = z * 2 + core, y * side + x
    return (
        [(lax.rem(dp + step, ndp), fs) for step in range(1, ndp)]
        + [(dp, y * side + lax.rem(x + step, side)) for step in range(1, side)]
        + [(dp, lax.rem(y + step, side) * side + x) for step in range(1, side)]
    )


def remote(source, target, send_sem, recv_sem, device):
    return pltpu.make_async_remote_copy(
        src_ref=source,
        dst_ref=target,
        send_sem=send_sem,
        recv_sem=recv_sem,
        device_id=device,
        device_id_type=MESH,
    )


def loop(count, body, start=0):
    def step(index, carry):
        body(index)
        return carry

    lax.fori_loop(start, count, step, 0)


class Crossing:
    def __init__(self, ndp, nf, land, own_sem, piece_recv, first_send, second_send, plane_recv, source):
        self.ndp, self.land, self.own_sem, self.piece_recv, self.source = ndp, land, own_sem, piece_recv, source
        self.first_send, self.second_send, self.plane_recv = first_send, second_send, plane_recv
        self.z, self.core, self.y, self.x, self.nz, self.side = place(ndp, nf)
        self.dp, self.fs = self.z * 2 + self.core, self.y * self.side + self.x

    def row_of(self, index):
        return lax.rem(self.z + index // 2, self.nz) * 2 + lax.rem(self.core + index, 2)

    def x_first(self, row):
        return lax.rem(row // 2, 2) == 0

    def along(self, first, step):
        x_at = jnp.where(first, lax.rem(self.x + step, self.side), self.x)
        y_at = jnp.where(first, self.y, lax.rem(self.y + step, self.side))
        return y_at * self.side + x_at

    def first_copy(self, row, step):
        here = self.land.at[self.fs, row]
        peer = self.along(self.x_first(row), step)
        sems = self.first_send.at[row, step - 1], self.plane_recv.at[self.fs, row]
        return remote(here, here, *sems, (self.dp, peer))

    def second_copy(self, plane_at, row, line, step):
        here = self.land.at[plane_at, row]
        peer = self.along(jnp.logical_not(self.x_first(row)), step)
        sems = self.second_send.at[row, line, step - 1], self.plane_recv.at[plane_at, row]
        return remote(here, here, *sems, (self.dp, peer))

    def arrived(self, plane_at, row):
        here = self.land.at[plane_at, row]
        remote(here, here, self.own_sem, self.plane_recv.at[plane_at, row], (self.dp, self.fs)).wait_recv()

    def take(self):
        def each(index):
            row = self.row_of(index)

            @pl.when(index == 0)
            def _():
                pltpu.make_async_copy(self.source, self.land.at[self.fs, row], self.own_sem).wait()

            @pl.when(index > 0)
            def _():
                here = self.land.at[self.fs, row]
                remote(self.source, here, self.own_sem, self.piece_recv.at[row], (self.dp, self.fs)).wait_recv()

            for step in range(1, self.side):
                self.first_copy(row, step).start()
                self.second_copy(self.fs, row, 0, step).start()

        loop(self.ndp, each)

    def pass_on(self):
        def each(index):
            row = self.row_of(index)
            for line in range(1, self.side):
                plane_at = self.along(self.x_first(row), line)
                self.arrived(plane_at, row)
                for step in range(1, self.side):
                    self.second_copy(plane_at, row, line, step).start()

        loop(self.ndp, each)

    def wait_line(self, line):
        for step in range(1, self.side):

            def each(index, step=step):
                row = self.row_of(index)
                x, y, side = self.x, self.y, self.side
                there = jnp.where(
                    self.x_first(row),
                    lax.rem(y + step, side) * side + lax.rem(x + line, side),
                    lax.rem(y + line, side) * side + lax.rem(x + step, side),
                )
                self.arrived(there, row)

            loop(self.ndp, each)

    def near(self):
        self.wait_line(0)

    def far(self):
        for line in range(1, self.side):
            self.wait_line(line)

    def finish(self):
        def each(row):
            for step in range(1, self.side):
                self.first_copy(row, step).wait_send()
                for line in range(self.side):
                    self.second_copy(self.fs, row, line, step).wait_send()

        loop(self.ndp, each)


def ortho_kernel(
    ndp,
    nf,
    attn_ref,
    ffn_whole,
    attn_out,
    ffn_out,
    land_attn,
    land_ffn,
    iter_low,
    iter_full,
    gram,
    gram_send,
    gram_recv,
    off_low,
    poly_low,
    diag_row,
    diag_col,
    inverse_norm,
    own_low,
    own_full,
    own_attn,
    own_ffn,
    own_sem,
    piece_send,
    piece_recv,
    first_send,
    second_send,
    plane_recv,
    gram_send_sem,
    gram_recv_sem,
    back_send,
    back_recv,
    load_sem,
):
    z, core, y, x, nz, side = place(ndp, nf)
    dp, fs = z * 2 + core, y * side + x
    rows = attn_ref.shape[1]
    size = rows * ndp
    is_attn = jnp.logical_or(dp < 2, jnp.logical_and(dp >= 6, dp < ROLES))
    is_ffn = jnp.logical_and(dp >= 2, dp < 6)
    partner = z * 2 + 1 - core

    greet(all_partners(ndp, nf))
    attn_roles = (0, 6, 1, 7)

    def piece(role):
        return attn_ref.at[role if role < 2 else role - 4]

    def piece_copy(role):
        return remote(piece(role), land_attn.at[fs, dp], piece_send.at[role], piece_recv.at[dp], (role, fs))

    for role in attn_roles:
        @pl.when(dp != role)
        def _(role=role):
            piece_copy(role).start()

        @pl.when(dp == role)
        def _(role=role):
            pltpu.make_async_copy(piece(role), land_attn.at[fs, dp], own_sem).start()

    def iterate(land, source, own_out, target, role, paired):
        width = land.shape[-1]
        columns = width * nf
        tall = min(STEP_ROWS, size)
        steps = size // tall
        wide = min(1024, columns)

        def add_gram(plane_at, fresh):
            block = land[plane_at].reshape(size, width)
            for step in range(steps):
                at = slice(step * tall, (step + 1) * tall)
                part = contract_cols(block[at], block)
                if fresh:
                    gram[at] = part
                else:
                    gram[at] += part

        if paired:

            def block_load(index):
                return pltpu.make_async_copy(ffn_whole.at[index], land.at[index], load_sem.at[index])

            for index in range(nf):
                block_load(index).start()
            for index in range(nf):
                block_load(index).wait()
                add_gram(index, index == 0)
        else:
            crossing = Crossing(ndp, nf, land, own_sem, piece_recv, first_send, second_send, plane_recv, source)
            crossing.take()
            add_gram(fs, True)
            crossing.pass_on()
            crossing.near()
            for step in range(1, side):
                add_gram(crossing.along(True, step), False)
                add_gram(crossing.along(False, step), False)
            crossing.far()
            for far_y in range(1, side):
                for far_x in range(1, side):
                    add_gram(lax.rem(y + far_y, side) * side + lax.rem(x + far_x, side), False)

        def gram_copy(slot, step):
            at = pl.ds(step * tall, tall)
            return remote(
                gram_send.at[slot, at],
                gram_recv.at[slot, at],
                gram_send_sem.at[slot, step],
                gram_recv_sem.at[slot, step],
                (partner, fs),
            )

        if paired:
            for step in range(steps):
                at = slice(step * tall, (step + 1) * tall)
                gram_send[0, at] = gram[at].astype(jnp.bfloat16)
                gram_copy(0, step).start()
        for index in range(nf):
            block = land[index].reshape(size, width)
            at = slice(index * width, (index + 1) * width)
            iter_low[0, :, at] = block
            iter_full[:, at] = block.astype(jnp.float32)

        def back_copy(row):
            return remote(own_out.at[row], target, back_send.at[row], back_recv.at[role], (row, fs))

        def iteration(count):
            now = lax.rem(count, 2)
            later = 1 - now

            @pl.when(count > 0)
            def _():
                def gram_rows(step):
                    at = pl.ds(pl.multiple_of(step * tall, tall), tall)
                    part = contract_cols(iter_low[now, at, :columns], iter_low[now, :, :columns])
                    if paired:
                        gram_send[now, at] = part.astype(jnp.bfloat16)
                        gram_copy(now, step).start()
                    else:
                        gram[at] = part

                loop(steps, gram_rows)

            eye = lax.broadcasted_iota(jnp.int32, (TILE_ROWS, TILE_ROWS), 0) == lax.broadcasted_iota(
                jnp.int32, (TILE_ROWS, TILE_ROWS), 1
            )

            @pl.when(count == 0)
            def _():
                trace = jnp.zeros((TILE_ROWS, TILE_ROWS), jnp.float32)
                if paired:
                    for step in range(steps):
                        gram_copy(now, step).wait()
                for tile in range(size // TILE_ROWS):
                    at = slice(tile * TILE_ROWS, (tile + 1) * TILE_ROWS)
                    if paired:
                        square = gram_send[now, at, at].astype(jnp.float32)
                        trace += square + gram_recv[now, at, at].astype(jnp.float32)
                    else:
                        trace += gram[at, at]
                trace = jnp.sum(jnp.where(eye, trace, 0.0), axis=1, keepdims=True)
                trace = jnp.sum(trace, axis=0, keepdims=True)
                inverse_norm[...] = 1.0 / (jnp.sqrt(trace) + norm_epsilon)

            @pl.when(count > 0)
            def _():
                inverse_norm[...] = jnp.ones_like(inverse_norm)

            inverse = inverse_norm[...]
            shrink = inverse * inverse

            for step in range(steps):
                if paired:
                    @pl.when(count > 0)
                    def _(step=step):
                        gram_copy(now, step).wait()

                for tile in range(step * tall // TILE_ROWS, (step + 1) * tall // TILE_ROWS):
                    at = slice(tile * TILE_ROWS, (tile + 1) * TILE_ROWS)
                    if paired:
                        total = gram_send[now, at].astype(jnp.float32) + gram_recv[now, at].astype(jnp.float32)
                    else:
                        total = gram[at]
                    total = total * shrink
                    gram[at] = total
                    off_low[at] = total.astype(jnp.bfloat16)
                    square = total[:, at]
                    masked = jnp.where(eye, square, 0.0)
                    diag_col[at] = jnp.sum(masked, axis=1, keepdims=True)
                    diag_row[:, at] = jnp.sum(masked, axis=0, keepdims=True)
                    square = jnp.where(eye, 0.0, square)
                    gram[at, at] = square
                    off_low[at, at] = square.astype(jnp.bfloat16)

            linear, middle, cubic = ns_linear * inverse, ns_square * inverse, ns_cubic * inverse

            def poly_rows(step):
                at = pl.ds(step * tall, tall)
                again = product(off_low[at], off_low[...])
                mine = diag_col[at]
                poly = gram[at] * (middle + cubic * mine + cubic * diag_row[...]) + cubic * again
                poly_low[at] = poly.astype(jnp.bfloat16)
                again_diag = []
                for tile in range(tall // TILE_ROWS):
                    rows_at = slice(tile * TILE_ROWS, (tile + 1) * TILE_ROWS)
                    side_at = slice(step * tall + tile * TILE_ROWS, step * tall + (tile + 1) * TILE_ROWS)
                    again_diag.append(
                        jnp.sum(jnp.where(eye, again[rows_at, side_at], 0.0), axis=1, keepdims=True)
                    )
                    poly_low[side_at, side_at] = jnp.where(eye, 0.0, poly[rows_at, side_at]).astype(jnp.bfloat16)
                again_diag = jnp.concatenate(again_diag, axis=0)
                factor = linear + middle * mine + cubic * (mine * mine + again_diag)

                @pl.when(count < ITERS - 1)
                def _():
                    for left in range(0, columns, wide):
                        part = slice(left, left + wide)
                        moved = product(poly_low[at], iter_low[now, :, part])
                        fresh = factor * iter_full[at, part] + moved
                        iter_full[at, part] = fresh
                        iter_low[later, at, part] = fresh.astype(jnp.bfloat16)

                @pl.when(count == ITERS - 1)
                def _():
                    for index in range(nf):
                        @pl.when(fs == index)
                        def _(index=index):
                            part = slice(index * width, (index + 1) * width)
                            own_full[at, :width] = iter_full[at, part]

                            if step == 0:
                                own_low[:, :width] = iter_low[now, :, part]

                    moved = product(poly_low[at], own_low[:, :width])
                    fresh = factor * own_full[at, :width] + moved
                    blocks = tall // rows
                    own_out[pl.ds(step * blocks, blocks)] = fresh.astype(jnp.bfloat16).reshape(
                        blocks, rows, width
                    )

                    def give(index):
                        row = step * blocks + index

                        @pl.when(row != dp)
                        def _():
                            back_copy(row).start()

                        @pl.when(row == dp)
                        def _():
                            pltpu.make_async_copy(own_out.at[row], target, own_sem).start()

                    loop(blocks, give)

            for step in range(steps):
                poly_rows(step)

        loop(ITERS, iteration)

        if not paired:
            crossing.finish()

        def finish(row):
            @pl.when(row != dp)
            def _():
                back_copy(row).wait_send()

        loop(ndp, finish)
        pltpu.make_async_copy(own_out.at[dp], target, own_sem).wait()

    @pl.when(is_attn)
    def _():
        at = jnp.where(dp < 2, dp, dp - 4)
        iterate(land_attn, attn_ref.at[at], own_attn, attn_out.at[at], dp, False)

    @pl.when(is_ffn)
    def _():
        matrix, half = (dp - 2) // 2, lax.rem(dp - 2, 2)
        iterate(land_ffn, None, own_ffn, ffn_out.at[matrix, half], dp, True)

    for role in range(ROLES):
        @pl.when(dp != role)
        def _(role=role):
            if role < 2 or role >= 6:
                target = attn_out.at[role if role < 2 else role - 4]
            else:
                target = ffn_out.at[(role - 2) // 2, (role - 2) % 2]
            if role in attn_roles:
                piece_copy(role).wait_send()
            remote(target, target, own_sem, back_recv.at[role], (role, fs)).wait_recv()


def orthogonalize(ndp, nf, attn_low, ffn_whole):
    rows, width_attn = attn_low.shape[1:]
    width_ffn = ffn_whole.shape[3]
    side = math.isqrt(nf)
    size = rows * ndp
    columns = width_ffn * nf
    tall = min(STEP_ROWS, size)
    bf16, f32 = jnp.bfloat16, jnp.float32
    dma = pltpu.SemaphoreType.DMA
    return pl.pallas_call(
        functools.partial(ortho_kernel, ndp, nf),
        name="newton_schulz",
        out_shape=[
            jax.ShapeDtypeStruct(attn_low.shape, bf16),
            jax.ShapeDtypeStruct((2, 2, rows, width_ffn), bf16),
        ],
        in_specs=[pl.BlockSpec(memory_space=pltpu.VMEM), pl.BlockSpec(memory_space=pl.ANY)],
        out_specs=[pl.BlockSpec(memory_space=pltpu.VMEM)] * 2,
        scratch_shapes=[
            pltpu.VMEM((nf, ndp, rows, width_attn), bf16),
            pltpu.VMEM((nf, ndp, rows, width_ffn), bf16),
            pltpu.VMEM((2, size, columns), bf16),
            pltpu.VMEM((size, columns), f32),
            pltpu.VMEM((size, size), f32),
            pltpu.VMEM((2, size, size), bf16),
            pltpu.VMEM((2, size, size), bf16),
            pltpu.VMEM((size, size), bf16),
            pltpu.VMEM((size, size), bf16),
            pltpu.VMEM((1, size), f32),
            pltpu.VMEM((size, 1), f32),
            pltpu.VMEM((1, 1), f32),
            pltpu.VMEM((size, width_ffn), bf16),
            pltpu.VMEM((size, width_ffn), f32),
            pltpu.VMEM((ndp, rows, width_attn), bf16),
            pltpu.VMEM((ndp, rows, width_ffn), bf16),
            dma,
            dma((ROLES,)),
            dma((ndp,)),
            dma((ndp, side - 1)),
            dma((ndp, side, side - 1)),
            dma((nf, ndp)),
            dma((2, size // tall)),
            dma((2, size // tall)),
            dma((ndp,)),
            dma((ROLES,)),
            dma((nf,)),
        ],
        compiler_params=pltpu.CompilerParams(
            collective_id=1, has_side_effects=True, vmem_limit_bytes=60 * 1024 * 1024
        ),
    )(attn_low, ffn_whole)


def update_kernel(
    attn_w,
    ffn_w,
    vectors,
    attn_mom,
    ffn_mom,
    vec_mom,
    attn_ema,
    ffn_ema,
    vec_ema,
    attn_grad,
    up_grad,
    down_grad,
    vec_grad,
    attn_ortho,
    ffn_ortho,
    attn_new,
    ffn_new,
    vec_new,
    attn_mom_new,
    ffn_mom_new,
    vec_mom_new,
    attn_ema_new,
    ffn_ema_new,
    vec_ema_new,
    *,
    vector_rate,
):
    for index in range(4):
        rate = attn_rates[index]
        attn_mom_new[index] = matrix_decay * attn_mom[index] + attn_grad[index]
        new = attn_w[index] * (1.0 - weight_decay * rate) - rate * attn_ortho[index].astype(jnp.float32)
        attn_new[index] = new
        attn_ema_new[index] = average_decay * attn_ema[index] + (1.0 - average_decay) * new
    width = ffn_ortho.shape[-1]
    shape_factor = math.sqrt(FF / D)
    for index, grad in enumerate((up_grad, down_grad)):
        ffn_mom_new[index] = matrix_decay * ffn_mom[index] + grad[...]
        for half in range(2):
            at = slice(half * width, (half + 1) * width)
            ortho = ffn_ortho[index, half].astype(jnp.float32)
            new = ffn_w[index, :, at] * (1.0 - weight_decay) - shape_factor * ortho
            ffn_new[index, :, at] = new
            ffn_ema_new[index, :, at] = average_decay * ffn_ema[index, :, at] + (1.0 - average_decay) * new
    mom = vector_decay * vec_mom[...] + vec_grad[...]
    vec_mom_new[...] = mom
    new = vectors[...] - vector_rate * mom
    vec_new[...] = new
    vec_ema_new[...] = average_decay * vec_ema[...] + (1.0 - average_decay) * new


def update_all(vector_rate, *operands):
    states = operands[:9]
    return pl.pallas_call(
        functools.partial(update_kernel, vector_rate=vector_rate),
        name="update",
        out_shape=[jax.ShapeDtypeStruct(states[index % 3].shape, jnp.float32) for index in range(9)],
        in_specs=[pl.BlockSpec(memory_space=pltpu.VMEM)] * len(operands),
        out_specs=[pl.BlockSpec(memory_space=pltpu.VMEM)] * 9,
        compiler_params=pltpu.CompilerParams(vmem_limit_bytes=60 * 1024 * 1024),
    )(*operands)


ROOM = pltpu.CompilerParams(vmem_limit_bytes=56 * 1024 * 1024)
ROOT_HALF = math.sqrt(0.5)
BELL = 1.0 / math.sqrt(2.0 * math.pi)


def flat(block):
    return block.reshape(-1, block.shape[-1])


def head_lanes(values, head):
    if values.shape[1] == HDIM:
        return values
    lane = lax.broadcasted_iota(jnp.int32, values.shape, 1)
    return jnp.where(lax.div(lane, HDIM) == head, values, jnp.zeros_like(values))


def normalize(values):
    center = values - jnp.mean(values, axis=1, keepdims=True)
    inverse = lax.rsqrt(jnp.mean(center * center, axis=1, keepdims=True) + ln_epsilon)
    return center * inverse, inverse


def normalize_back(grad, scaled, inverse):
    return inverse * (
        grad
        - jnp.mean(grad, axis=1, keepdims=True)
        - scaled * jnp.mean(grad * scaled, axis=1, keepdims=True)
    )


def row_sum(values):
    return jnp.sum(values.astype(jnp.float32), axis=0, keepdims=True)


def forward_kernel(
    ndp,
    nf,
    tokens_ref,
    label_ref,
    cotangent_ref,
    attn_w,
    ffn_w,
    vectors_ref,
    attn_out,
    up_out,
    down_out,
    blocks_out,
    active_out,
    slope_out,
    vec_out,
    mixture_out,
    total_out,
    scaled_out,
    inverse_out,
    low_out,
    layer_out,
    d_second_out,
    sums_out,
    attn_shard,
    up_shard,
    down_shard,
    three_weight,
    out_weight,
    ffn_weight,
    vec_land,
    bias,
    bias_up,
    blocks,
    parts,
    active,
    slope,
    total,
    own_sem,
    own_recv,
    pair_recv,
    z_send,
    first_send,
    second_send,
    pair_send,
    load_sem,
    store_sem,
):
    chunks, turned = 4, 3
    wholes = (attn_out, up_out, down_out)
    z, core, y, x, nz, side = place(ndp, nf)
    dp, fs = z * 2 + core, y * side + x
    rows, width_attn = attn_w.shape[1:]
    width_ffn, share = ffn_w.shape[2], vectors_ref.shape[1]
    count = tokens_ref.shape[0]
    width = ffn_weight.shape[-1]
    per = width_ffn // width

    attn_shard[4 * rows :] = jnp.zeros((16, width_attn), jnp.bfloat16)
    attn_shard[4 * rows : 4 * rows + 12, :share] = vectors_ref[...].astype(jnp.bfloat16)
    for index in range(4):
        attn_shard[index * rows : (index + 1) * rows] = attn_w[index].astype(jnp.bfloat16)
    up_shard[...] = ffn_w[0].astype(jnp.bfloat16)
    down_shard[...] = ffn_w[1].astype(jnp.bfloat16)
    greet(line_partners(ndp, nf))

    halves = slice(0, width_ffn // 2), slice(width_ffn // 2, width_ffn)
    shards = (attn_shard, up_shard, down_shard.at[:, halves[0]], down_shard.at[:, halves[1]])

    def row_slot(chunk, plane_at, row):
        if chunk < 2:
            return wholes[chunk].at[plane_at, row]
        return down_out.at[plane_at, row, :, halves[chunk - 2]]

    def slot(chunk, plane_at, z_at):
        return row_slot(chunk, plane_at, z_at * 2 + core)

    def source(chunk, plane_at, z_at, own):
        return shards[chunk] if own else slot(chunk, plane_at, z_at)

    def along(first, step):
        x_at = jnp.where(first, lax.rem(x + step, side), x)
        y_at = jnp.where(first, y, lax.rem(y + step, side))
        return y_at * side + x_at

    def first_copy(chunk, z_at, step, own):
        peer = along(lax.rem(z_at, 2) == 0, step)
        return remote(
            source(chunk, fs, z_at, own),
            slot(chunk, fs, z_at),
            first_send.at[chunk, z_at, step - 1],
            own_recv.at[chunk, fs, z_at],
            (dp, peer),
        )

    def second_copy(chunk, plane_at, z_at, step, own, line):
        peer = along(lax.rem(z_at, 2) != 0, step)
        return remote(
            source(chunk, plane_at, z_at, own),
            slot(chunk, plane_at, z_at),
            second_send.at[chunk, z_at, line, step - 1],
            own_recv.at[chunk, plane_at, z_at],
            (dp, peer),
        )

    def pair_copy(chunk, plane_at, z_at, own):
        return remote(
            source(chunk, plane_at, z_at, own),
            slot(chunk, plane_at, z_at),
            pair_send.at[chunk, plane_at, z_at],
            pair_recv.at[chunk, plane_at, z_at],
            (z * 2 + 1 - core, fs),
        )

    def z_copy(chunk, plane_at, z_at, up, own):
        return remote(
            source(chunk, plane_at, z_at, own),
            slot(chunk, plane_at, z_at),
            z_send.at[chunk, plane_at, z_at, up],
            own_recv.at[chunk, plane_at, z_at],
            ((z + (1 if up else -1)) * 2 + core, fs),
        )

    def along_z(chunk, plane_at, z_at, own, act):
        @pl.when(jnp.logical_and(z_at <= z, z < nz - 1))
        def _():
            act(z_copy(chunk, plane_at, z_at, 1, own))

        @pl.when(jnp.logical_and(z_at >= z, z > 0))
        def _():
            act(z_copy(chunk, plane_at, z_at, 0, own))

    def begin(copy):
        copy.start()

    def arrived(chunk, plane_at, z_at):
        here = slot(chunk, plane_at, z_at)
        remote(here, here, own_sem.at[chunk], own_recv.at[chunk, plane_at, z_at], (dp, fs)).wait_recv()

    def pass_on(chunk, z_at, own):
        for step in range(1, side):
            first_copy(chunk, z_at, step, own).start()
            second_copy(chunk, fs, z_at, step, own, 0).start()
        pair_copy(chunk, fs, z_at, own).start()

    def own_copy(chunk):
        return pltpu.make_async_copy(shards[chunk], slot(chunk, fs, z), own_sem.at[chunk])

    def near_first(body):
        def each(index):
            far = 1 + lax.div(index, 2)
            z_at = jnp.where(lax.rem(index, 2) == 0, z - far, z + far)

            @pl.when(jnp.logical_and(z_at >= 0, z_at < nz))
            def _():
                body(z_at)

        loop(2 * (nz - 1), each)

    def from_z(chunk):
        def each(z_at):
            arrived(chunk, fs, z_at)
            along_z(chunk, fs, z_at, False, begin)
            pass_on(chunk, z_at, False)

        near_first(each)

    def from_first(chunk):
        def each(z_at):
            for line in range(1, side):
                plane_at = along(lax.rem(z_at, 2) == 0, line)
                arrived(chunk, plane_at, z_at)
                for step in range(1, side):
                    second_copy(chunk, plane_at, z_at, step, False, line).start()
                pair_copy(chunk, plane_at, z_at, False).start()

        each(z)
        near_first(each)

    def last_places(z_at):
        x_first = lax.rem(z_at, 2) == 0
        for line in range(side):
            for step in range(1, side):
                near_x, far_y = lax.rem(x + line, side), lax.rem(y + step, side)
                far_x, near_y = lax.rem(x + step, side), lax.rem(y + line, side)
                yield jnp.where(x_first, far_y * side + near_x, near_y * side + far_x)

    def from_second(chunk):
        def each(z_at):
            for plane_at in last_places(z_at):
                arrived(chunk, plane_at, z_at)
                pair_copy(chunk, plane_at, z_at, False).start()

        each(z)
        near_first(each)

    def turned_first():
        for line in range(1, side):
            plane_at = along(lax.rem(z, 2) == 0, line)
            arrived(turned, plane_at, z)
            for step in range(1, side):
                second_copy(turned, plane_at, z, step, False, line).start()
            along_z(turned, plane_at, z, False, begin)
            pair_copy(turned, plane_at, z, False).start()

    def turned_second():
        for plane_at in last_places(z):
            arrived(turned, plane_at, z)
            along_z(turned, plane_at, z, False, begin)
            pair_copy(turned, plane_at, z, False).start()

    def turned_z(far):
        for z_at in (z - far, z + far):
            @pl.when(jnp.logical_and(z_at >= 0, z_at < nz))
            def _(z_at=z_at):
                def each(step):
                    plane_at = lax.rem(fs + step, nf)
                    arrived(turned, plane_at, z_at)
                    along_z(turned, plane_at, z_at, False, begin)
                    pair_copy(turned, plane_at, z_at, False).start()

                loop(nf, each)

    def from_pair(chunk):
        own_copy(chunk).wait()

        def each(index):
            plane_at, z_at = lax.rem(index, nf), lax.div(index, nf)
            there = row_slot(chunk, plane_at, z_at * 2 + 1 - core)
            remote(
                there, there, own_sem.at[chunk], pair_recv.at[chunk, plane_at, z_at], (dp, fs)
            ).wait_recv()

        loop(nf * nz, each)

    for chunk in (0, turned, 1, 2):
        own_copy(chunk).start(priority=1)
        along_z(chunk, fs, z, True, begin)
        pass_on(chunk, z, True)

    from_z(0)
    from_first(0)
    turned_first()
    from_z(1)
    from_second(0)
    turned_second()
    from_pair(0)

    def load(index, source, target):
        return pltpu.make_async_copy(source, target, load_sem.at[index])

    def attn_load(index, block, at):
        per_block = ndp // nf
        if index == 0:
            return load(at, attn_out.at[block, :, pl.ds(0, 3 * rows)], three_weight.at[at])
        return load(
            2 + at,
            attn_out.at[:, pl.ds(block * per_block, per_block), pl.ds(3 * rows, rows)],
            out_weight.at[at],
        )

    vec_copy = load(4, attn_out.at[:, :, pl.ds(4 * rows, 16)], vec_land)
    vec_copy.start(priority=1)
    for index in range(2):
        attn_load(index, 0, 0).start(priority=1)
    vec_copy.wait()
    for row in range(ndp):
        for column in range(nf):
            left = (row * nf + column) * share
            vec_out[:, left : left + share] = vec_land[column, row, :, :share].astype(jnp.float32)
    for index in range(nf):
        at = slice(index * width_attn, (index + 1) * width_attn)
        bias[index, 0:1] = vec_out[0:1, at]
        bias[index, 1:2] = vec_out[1:2, at]
    for index in range(FF // width):
        left = index * width
        bias_up[index] = vec_out[5 + left // D : 6 + left // D, left % D : left % D + width]
    label_row = label_ref[...].astype(jnp.float32)
    label_col = jnp.transpose(jnp.broadcast_to(label_row, (128, count)))[:, 0:1]
    tokens = tokens_ref[...]
    lane = lax.broadcasted_iota(jnp.int32, (count, 128), 1)
    total[...] = jnp.broadcast_to(vec_out[2:3], (count, D))

    def attn_turn(block):
        at = lax.rem(block, 2)

        @pl.when(block < nf - 1)
        def _():
            for index in range(2):
                attn_load(index, block + 1, 1 - at).start(priority=1)

        attn_load(0, block, at).wait()
        attn_load(1, block, at).wait()
        weights = [flat(three_weight[at, :, index * rows : (index + 1) * rows]) for index in range(3)]
        queries = (product(tokens, weights[0]) + bias[block, 0:1]).astype(jnp.bfloat16)
        keys_all = product(tokens, weights[1]).astype(jnp.bfloat16)
        values_all = (product(tokens, weights[2]) + bias[block, 1:2]).astype(jnp.bfloat16)
        for index, values in enumerate((queries, keys_all, values_all)):
            blocks[block, index] = values
        pltpu.make_async_copy(blocks.at[block], blocks_out.at[block], store_sem.at[block]).start(priority=1)
        allowed = label_col == label_row
        totals = jnp.zeros((count, 128), jnp.float32)
        mixture = jnp.zeros((count, width_attn), jnp.float32)
        for head in range(width_attn // HDIM):
            scores = contract_cols(head_lanes(queries, head) * score_scale, keys_all)
            scores = jnp.where(allowed, scores, -1e30)
            top = jnp.max(scores, axis=1, keepdims=True)
            exponent = jnp.exp(scores - top)
            weight = jnp.sum(exponent, axis=1, keepdims=True)
            attention = (exponent * (1.0 / weight)).astype(jnp.bfloat16)
            totals = jnp.where(lane == head, top + jnp.log(weight), totals)
            mixture += product(attention, head_lanes(values_all, head))
        mixture = mixture.astype(jnp.bfloat16)
        parts[block] = mixture
        total_out[block] = jnp.transpose(totals)[:8]
        for index in range(nf):
            side_at = slice(index * width_attn, (index + 1) * width_attn)
            total[:, side_at] += product(mixture, flat(out_weight[at, index]))

        @pl.when(block == 0)
        def _():
            from_z(2)
            turned_z(1)

        @pl.when(block == nf - 2)
        def _():
            from_first(1)
            turned_z(2)

    loop(nf, attn_turn)

    def first_norm(index):
        at = pl.ds(pl.multiple_of(index * NORM_ROWS, NORM_ROWS), NORM_ROWS)
        scaled, inverse = normalize(tokens_ref[at].astype(jnp.float32) + total[at])
        scaled_out[at] = scaled
        inverse_out[at] = inverse
        normed = scaled * vec_out[3:4] + vec_out[4:5]
        low_out[at] = normed.astype(jnp.bfloat16)
        total[at] = normed + vec_out[9:10]

    loop(count // NORM_ROWS, first_norm)
    for index in range(nf):
        mixture_out[:, index * width_attn : (index + 1) * width_attn] = parts[index]

    def ffn_load(chunk, step, at):
        block, part = lax.div(step, per), lax.rem(step, per)
        left = pl.multiple_of(part * width, width)
        return load(5 + at, wholes[chunk].at[block, :, :, pl.ds(left, width)], ffn_weight.at[at])

    def ffn_steps(chunk, body, between):
        ffn_load(chunk, 0, 0).start(priority=1)

        def each(step):
            at = lax.rem(step, 2)

            @pl.when(step < FF // width - 1)
            def _():
                ffn_load(chunk, step + 1, 1 - at).start(priority=1)

            ffn_load(chunk, step, at).wait()
            body(step, at)
            between(step)

        loop(FF // width, each)

    def keep(step):
        column = pl.ds(pl.multiple_of(step * width, width), width)
        return (
            pltpu.make_async_copy(active.at[step], active_out.at[:, column], store_sem.at[nf]),
            pltpu.make_async_copy(slope.at[lax.rem(step, 2)], slope_out.at[:, column], store_sem.at[nf + 1]),
        )

    def up_step(step, at):
        up_proj = product(low_out[...], flat(ffn_weight[at])) + bias_up[step]
        half = 0.5 * (1.0 + lax.erf(up_proj * ROOT_HALF))

        @pl.when(step > 0)
        def _():
            for copy in keep(step - 1):
                copy.wait()

        active[step] = (up_proj * half).astype(jnp.bfloat16)
        slope[lax.rem(step, 2)] = (half + up_proj * (BELL * jnp.exp(-0.5 * up_proj * up_proj))).astype(
            jnp.bfloat16
        )
        for copy in keep(step):
            copy.start(priority=1)

    def down_step(step, at):
        total[...] += contract_cols(active[step], flat(ffn_weight[at]))

    def between_up(step):
        @pl.when(step == 0)
        def _():
            for far in range(3, nz):
                turned_z(far)

        @pl.when(step == FF // width // 2)
        def _():
            from_first(2)

    from_second(1)
    from_pair(1)
    ffn_steps(1, up_step, between_up)
    for copy in keep(FF // width - 1):
        copy.wait()
    from_second(2)
    from_pair(2)
    from_pair(turned)
    ffn_steps(2, down_step, lambda step: None)
    sums_out[...] = jnp.zeros((8, D), jnp.float32)

    def second_norm(index):
        at = pl.ds(pl.multiple_of(index * NORM_ROWS, NORM_ROWS), NORM_ROWS)
        scaled, inverse = normalize(total[at])
        layer_out[at] = (scaled * vec_out[10:11] + vec_out[11:12]).astype(jnp.bfloat16)
        grad = cotangent_ref[at].astype(jnp.float32)
        d_second = normalize_back(grad * vec_out[10:11], scaled, inverse)
        d_second_out[at] = d_second
        sums_out[0:1] += row_sum(d_second.astype(jnp.bfloat16))
        sums_out[1:2] += row_sum(grad * scaled)
        sums_out[2:3] += row_sum(grad)

    loop(count // NORM_ROWS, second_norm)

    def stored(block):
        pltpu.make_async_copy(blocks.at[block], blocks_out.at[block], store_sem.at[block]).wait()

    loop(nf, stored)
    for chunk in range(chunks):
        def finish(z_at):
            def sent():
                for step in range(1, side):
                    first_copy(chunk, z_at, step, False).wait_send()
                    for line in range(side):
                        second_copy(chunk, fs, z_at, step, False, line).wait_send()

            if chunk == turned:
                pl.when(z_at == z)(sent)
            else:
                sent()
                along_z(chunk, fs, z_at, False, lambda copy: copy.wait_send())

            def each(plane_at):
                pair_copy(chunk, plane_at, z_at, False).wait_send()
                if chunk == turned:
                    along_z(chunk, plane_at, z_at, False, lambda copy: copy.wait_send())

            loop(nf, each)

        loop(nz, finish)


def forward(ndp, nf, tokens, segments, cotangent, attn_w, ffn_w, vectors):
    nz, side, chunks = ndp // 2, math.isqrt(nf), 4
    count = tokens.shape[0]
    rows, width_attn = attn_w.shape[1:]
    width_ffn = ffn_w.shape[2]
    width = min(512, width_ffn)
    bf16, f32 = jnp.bfloat16, jnp.float32
    dma = pltpu.SemaphoreType.DMA
    anywhere, inside = pl.BlockSpec(memory_space=pl.ANY), pl.BlockSpec(memory_space=pltpu.VMEM)
    shape = jax.ShapeDtypeStruct
    return pl.pallas_call(
        functools.partial(forward_kernel, ndp, nf),
        name="forward",
        out_shape=[
            shape((nf, ndp, 4 * rows + 16, width_attn), bf16),
            shape((nf, ndp, rows, width_ffn), bf16),
            shape((nf, ndp, rows, width_ffn), bf16),
            shape((nf, 3, count, width_attn), bf16),
            shape((count, FF), bf16),
            shape((count, FF), bf16),
            shape((16, D), f32),
            shape((count, D), bf16),
            shape((nf, 8, count), f32),
            shape((count, D), f32),
            shape((count, 1), f32),
            shape((count, D), bf16),
            shape((count, D), bf16),
            shape((count, D), f32),
            shape((8, D), f32),
        ],
        in_specs=[inside] * 6,
        out_specs=[anywhere] * 6 + [inside] * 9,
        scratch_shapes=[
            pltpu.VMEM((4 * rows + 16, width_attn), bf16),
            pltpu.VMEM((rows, width_ffn), bf16),
            pltpu.VMEM((rows, width_ffn), bf16),
            pltpu.VMEM((2, ndp, 3 * rows, width_attn), bf16),
            pltpu.VMEM((2, nf, ndp // nf, rows, width_attn), bf16),
            pltpu.VMEM((2, ndp, rows, width), bf16),
            pltpu.VMEM((nf, ndp, 16, width_attn), bf16),
            pltpu.VMEM((nf, 8, width_attn), f32),
            pltpu.VMEM((FF // width, 1, width), f32),
            pltpu.VMEM((nf, 3, count, width_attn), bf16),
            pltpu.VMEM((nf, count, width_attn), bf16),
            pltpu.VMEM((FF // width, count, width), bf16),
            pltpu.VMEM((2, count, width), bf16),
            pltpu.VMEM((count, D), f32),
            dma((chunks,)),
            dma((chunks, nf, nz)),
            dma((chunks, nf, nz)),
            dma((chunks, nf, nz, 2)),
            dma((chunks, nz, side - 1)),
            dma((chunks, nz, side, side - 1)),
            dma((chunks, nf, nz)),
            dma((7,)),
            dma((nf + 2,)),
        ],
        compiler_params=pltpu.CompilerParams(
            collective_id=2, has_side_effects=True, vmem_limit_bytes=60 * 1024 * 1024
        ),
    )(tokens, segments[None, :], cotangent, attn_w, ffn_w, vectors)


def backward_kernel(
    ndp,
    nf,
    d_second_ref,
    low_ref,
    scaled_ref,
    inverse_ref,
    vec_ref,
    active_ref,
    slope_ref,
    up_ref,
    down_ref,
    tokens_ref,
    label_ref,
    blocks_ref,
    mixture_ref,
    total_ref,
    attn_ref,
    tail_ref,
    attn_mom,
    ffn_mom,
    input_grad,
    up_out,
    down_out,
    attn_out,
    vec_out,
    attn_low,
    ffn_low,
    ffn_whole,
    held_up,
    held_down,
    held_attn,
    first_up,
    first_down,
    first_attn,
    second_up,
    second_down,
    second_attn,
    z_up,
    z_down,
    z_attn,
    first_turned,
    second_turned,
    z_turned,
    stages_out,
    land,
    ffn_weight,
    ffn_act,
    attn_weight,
    attn_block,
    wide_low,
    wide_two,
    turned_one,
    turned_two,
    branch,
    bias_up_sum,
    query_sum,
    value_sum,
    vec_land,
    load_sem,
    step_sem,
    pair_send,
    pair_recv,
    first_send,
    first_recv,
    second_send,
    second_recv,
    z_send,
    z_recv,
    vec_send,
    vec_recv,
    piece_own,
    piece_send,
    piece_recv,
    piece_first,
    piece_second,
    piece_plane,
    turned_send,
    turned_recv,
):
    z, core, y, x, nz, side = place(ndp, nf)
    dp, fs = z * 2 + core, y * side + x
    other = (z * 2 + 1 - core, fs)
    chunks, turned = 3, 3
    rows, width_ffn = held_up.shape[2:]
    half_width = width_ffn // 2
    held, outs = (held_up, held_down, held_attn), (up_out, down_out, attn_out)
    from_first = (first_up, first_down, first_attn, first_turned)
    from_second = (second_up, second_down, second_attn, second_turned)
    from_z = (z_up, z_down, z_attn)
    width_attn = held_attn.shape[-1]
    width = ffn_weight.shape[-1]
    per = width_ffn // width
    greet(all_partners(ndp, nf))

    def place_of(turn):
        step = nf - 1 - turn
        return lax.rem(y + lax.div(step, side), side) * side + lax.rem(x + lax.rem(step, side), side)

    def sums(chunk, z_at, plane_at):
        if chunk == 1:
            return held_down.at[z_at, plane_at, :, pl.ds(0, half_width)]
        if chunk == turned:
            return held_down.at[z_at, plane_at, :, pl.ds(half_width, half_width)]
        return held[chunk].at[z_at, plane_at]

    def add(target, source):
        target[...] = target[...] + source[...]

    def first_land(chunk, z_at, step, line):
        return from_first[chunk].at[0 if chunk == turned else z_at, step - 1, line]

    def second_land(chunk, z_at, step):
        return from_second[chunk].at[0 if chunk == turned else z_at, step - 1]

    def first_copy(chunk, z_at, line, step):
        x_first = lax.rem(z_at, 2) == 0
        near, far = lax.rem(x + step, side), lax.rem(y + step, side)
        to = jnp.where(x_first, y * side + near, far * side + x)
        at = jnp.where(
            x_first,
            lax.rem(y + line, side) * side + near,
            far * side + lax.rem(x + line, side),
        )
        return remote(
            sums(chunk, z_at, at),
            first_land(chunk, z_at, step, line),
            first_send.at[chunk, z_at, step - 1, line],
            first_recv.at[chunk, z_at, step - 1, line],
            (dp, to),
        )

    lag = 2
    total_steps = nf * per + nf
    schedule = {}
    for sent, base, stride in (((0, 1), 0, per), ((2,), nf * per, 1)):
        for turns in ((0,), tuple(range(1, nf - 1))):
            ready = min(base + (turns[-1] + 1) * stride - 1 + lag, total_steps)
            for z_at in range(0, nz, 2):
                schedule.setdefault(ready, []).extend((chunk, turns, z_at) for chunk in sent)

    def send_first(chunk, turns, z_from, z_count=2):
        def each(z_at):
            x_first = lax.rem(z_at, 2) == 0
            for turn in turns:
                step_x, step_y = (nf - 1 - turn) % side, (nf - 1 - turn) // side
                step = jnp.where(x_first, step_x, step_y)
                line = jnp.where(x_first, step_y, step_x)

                @pl.when(step > 0)
                def _(line=line, step=step):
                    first_copy(chunk, z_at, line, step).start()

        loop(z_from + z_count, each, z_from)

    def sends_at(step, steps):
        for when in steps:
            @pl.when(step == when)
            def _(when=when):
                for chunk, turns, z_at in schedule.get(when, ()):
                    send_first(chunk, turns, z_at)

    def line_place(z_at, line):
        x_first = lax.rem(z_at, 2) == 0
        return jnp.where(
            x_first, lax.rem(y + line, side) * side + x, y * side + lax.rem(x + line, side)
        )

    def second_copy(chunk, z_at, step):
        to = line_place(z_at, step)
        return remote(
            sums(chunk, z_at, to),
            second_land(chunk, z_at, step),
            second_send.at[chunk, z_at, step - 1],
            second_recv.at[chunk, z_at, step - 1],
            (dp, to),
        )

    def z_copy(chunk, step):
        z_at = lax.rem(z + step, nz)
        return remote(
            sums(chunk, z_at, fs),
            from_z[chunk].at[step - 1],
            z_send.at[chunk, step - 1],
            z_recv.at[chunk, step - 1],
            (z_at * 2 + core, fs),
        )

    def take_first(chunk, lines):
        def each(hop):
            z_at = lax.rem(z + 1 + hop, nz)
            for line in lines:
                at = line_place(z_at, line)
                for step in range(1, side):
                    first_copy(chunk, z_at, line, step).wait_recv()
                    add(sums(chunk, z_at, at), first_land(chunk, z_at, step, line))
                if line:
                    second_copy(chunk, z_at, line).start()

        if chunk == turned:
            each(nz - 1)
        else:
            loop(nz, each)

    def turned_copy(plane_at, step):
        z_at = lax.rem(z + step, nz)
        return remote(
            sums(turned, z_at, plane_at),
            z_turned.at[step - 1, plane_at],
            turned_send.at[step - 1, plane_at],
            turned_recv.at[step - 1, plane_at],
            (z_at * 2 + core, fs),
        )

    def turned_start(turns):
        for turn in turns:
            for step in range(1, nz):
                turned_copy(place_of(turn), step).start()

    def turned_take(turns):
        for turn in turns:
            plane_at = place_of(turn)
            for step in range(1, nz):
                turned_copy(plane_at, step).wait_recv()
                add(sums(turned, z, plane_at), z_turned.at[step - 1, plane_at])
        send_first(turned, turns, z, 1)

    def take_second(chunk):
        def each(hop):
            z_at = lax.rem(z + 1 + hop, nz)
            for step in range(1, side):
                second_copy(chunk, z_at, step).wait_recv()
                add(sums(chunk, z_at, fs), second_land(chunk, z_at, step))

            @pl.when(hop < nz - 1)
            def _():
                z_copy(chunk, hop + 1).start()

        loop(nz, each)

    def moments(chunk):
        source = ffn_mom.at[chunk] if chunk < 2 else attn_mom
        return pltpu.make_async_copy(source, outs[chunk], load_sem.at[3 + chunk])

    def take_z(chunk):
        moments(chunk).wait()
        total = sums(chunk, z, fs)[...].astype(jnp.float32)
        for step in range(1, nz):
            z_copy(chunk, step).wait_recv()
            total += from_z[chunk][step - 1].astype(jnp.float32)
        if chunk == 0:
            low = (matrix_decay * up_out[...] + total).astype(jnp.bfloat16)
            up_out[...] = total
            ffn_low[0, 0] = low[:, :half_width]
            ffn_low[0, 1] = low[:, half_width:]
        elif chunk == 1:
            for step in range(1, side):
                second_copy(turned, z, step).wait_recv()
                add(sums(turned, z, fs), second_land(turned, z, step))
            for index, value in enumerate((total, sums(turned, z, fs)[...].astype(jnp.float32))):
                at = slice(index * half_width, (index + 1) * half_width)
                ffn_low[1, index] = (matrix_decay * down_out[:, at] + value).astype(jnp.bfloat16)
                down_out[:, at] = value
        else:
            attn_low[...] = (matrix_decay * attn_out[...] + total).astype(jnp.bfloat16)
            attn_out[...] = total

    vec_rounds = [[other]]
    vec_rounds.append([(dp, y * side + lax.rem(x + step, side)) for step in range(1, side)])
    vec_rounds.append([(dp, lax.rem(y + step, side) * side + x) for step in range(1, side)])
    vec_rounds.append([(lax.rem(z + step, nz) * 2 + core, fs) for step in range(1, nz)])
    starts = [sum(len(group) for group in vec_rounds[:index]) for index in range(4)]

    def vec_copy(index, step):
        at = starts[index] + step
        return remote(
            vec_land.at[index], vec_land.at[4 + at], vec_send.at[at], vec_recv.at[at], vec_rounds[index][step]
        )

    def vec_start(index):
        for step in range(len(vec_rounds[index])):
            vec_copy(index, step).start()

    def vec_take(index):
        total = vec_land[index]
        for step in range(len(vec_rounds[index])):
            vec_copy(index, step).wait_recv()
            total += vec_land[4 + starts[index] + step]
        if index < 3:
            vec_land[index + 1] = total
            vec_start(index + 1)
        else:
            vec_out[...] = total

    def split(values, keep, give):
        parts = values.astype(jnp.bfloat16).reshape(nz, 2, rows, values.shape[1])
        for which in range(2):
            @pl.when(core == which)
            def _(which=which):
                keep(parts[:, which])
                give(parts[:, 1 - which])

    def piece_copy(matrix, half):
        return remote(
            ffn_low.at[matrix, half],
            ffn_whole.at[fs, dp],
            piece_send.at[2 * matrix + half],
            piece_recv.at[dp],
            (2 + 2 * matrix + half, fs),
        )

    def piece_local(matrix, half):
        return pltpu.make_async_copy(ffn_low.at[matrix, half], ffn_whole.at[fs, dp], piece_own)

    def start_pieces(matrix):
        for half in range(2):
            @pl.when(dp != 2 + 2 * matrix + half)
            def _(half=half):
                piece_copy(matrix, half).start()

            @pl.when(dp == 2 + 2 * matrix + half)
            def _(half=half):
                piece_local(matrix, half).start(priority=1)

    crossing = Crossing(
        ndp, nf, ffn_whole, piece_own, piece_recv, piece_first, piece_second, piece_plane, ffn_low.at[0, 0]
    )
    runs_ffn = jnp.logical_and(dp >= 2, dp < 6)

    def ffn_loads(slot, turn, part):
        block = place_of(turn)
        at = pl.ds(part * width, width)
        column = pl.ds(pl.multiple_of(block * width_ffn + part * width, width), width)
        pairs = (
            (up_ref.at[block, :, :, at], ffn_weight.at[slot, 0]),
            (down_ref.at[block, :, :, at], ffn_weight.at[slot, 1]),
            (active_ref.at[:, column], ffn_act.at[slot, 0]),
            (slope_ref.at[:, column], ffn_act.at[slot, 1]),
        )
        return [
            pltpu.make_async_copy(source, target, step_sem.at[slot, index])
            for index, (source, target) in enumerate(pairs)
        ]

    def load(index, source, target):
        return pltpu.make_async_copy(source, target, load_sem.at[index])

    load(0, low_ref, wide_low).start(priority=1)
    load(1, d_second_ref, input_grad).start(priority=1)
    for copy in ffn_loads(0, 0, 0):
        copy.start(priority=1)
    load(2, tokens_ref, wide_two).start(priority=1)
    for chunk in range(chunks):
        moments(chunk).start(priority=1)
    load(0, low_ref, wide_low).wait()
    turned_one[...] = jnp.transpose(wide_low[...])
    load(1, d_second_ref, input_grad).wait()
    wide_low[...] = input_grad[...].astype(jnp.bfloat16)
    turned_two[...] = jnp.transpose(wide_low[...])

    def pair_copy(step):
        stage, slot = lax.rem(step, lag), lax.rem(step, 2 * lag)
        return remote(stages_out.at[stage], land.at[slot], pair_send.at[stage], pair_recv.at[slot], other)

    def pair_take(step):
        pair_copy(step).wait()
        slot = lax.rem(step, 2 * lag)

        @pl.when(step < nf * per)
        def _():
            block, part = place_of(lax.div(step, per)), lax.rem(step, per)
            for index in range(2):
                for which in range(per):
                    @pl.when(part == which)
                    def _(index=index, which=which):
                        for half in range(2):
                            left = which * width + half * width_attn
                            at = slice(left, left + width_attn)
                            held[index][:, block, :, at] += land[slot, :, 2 * index + half]

        @pl.when(step >= nf * per)
        def _():
            held_attn[:, place_of(step - nf * per)] += land[slot]

    def ffn_turn(turn):
        block = place_of(turn)
        for part in range(per):
            now = turn * per + part
            slot = lax.rem(now, 2)
            if part < per - 1:
                for copy in ffn_loads(1 - slot, turn, part + 1):
                    copy.start(priority=1)
            else:
                @pl.when(turn < nf - 1)
                def _():
                    for copy in ffn_loads(1 - slot, turn + 1, 0):
                        copy.start(priority=1)

            for copy in ffn_loads(slot, turn, part):
                copy.wait()
            d_active = product(wide_low[...], flat(ffn_weight[slot, 1]))
            d_up = (d_active * ffn_act[slot, 1].astype(jnp.float32)).astype(jnp.bfloat16)
            bias_up_sum[block * per + part] = row_sum(d_up)
            input_grad[...] += contract_cols(d_up, flat(ffn_weight[slot, 0]))

            @pl.when(now >= lag)
            def _():
                pair_take(now - lag)

            sends_at(now, range(nf * per))

            @pl.when(now == per - 1 + lag)
            def _():
                turned_start((0,))

            @pl.when(now == (nf - 1) * per - 1 + lag)
            def _():
                turned_start(range(1, nf - 1))
            at = slice(part * width, (part + 1) * width)
            for index in range(2):

                def keep(values, index=index):
                    held[index][:, block, :, at] = values

                def give(values, index=index):
                    for half in range(2):
                        side_at = slice(half * width_attn, (half + 1) * width_attn)
                        stages_out[lax.rem(now, lag), :, 2 * index + half] = values[:, :, side_at]

                if index == 0:
                    split(product(turned_one[...], d_up), keep, give)
                else:
                    split(product(turned_two[...], ffn_act[slot, 0]), keep, give)
            pair_copy(now).start()

    loop(nf, ffn_turn)

    load(2, tokens_ref, wide_two).wait()
    turned_one[...] = jnp.transpose(wide_two[...])
    load(0, mixture_ref, wide_two).start(priority=1)

    def attn_load(index, turn):
        block = place_of(turn)
        per_block = ndp // nf
        source, target = (
            (attn_ref.at[block, :, pl.ds(0, 3 * rows)], attn_weight[0]),
            (
                attn_ref.at[:, pl.ds(block * per_block, per_block), pl.ds(3 * rows, rows)],
                attn_weight[1],
            ),
            (blocks_ref.at[block], attn_block),
        )[index]
        return pltpu.make_async_copy(source, target, step_sem.at[0, index])

    for index in range(3):
        attn_load(index, 0).start(priority=1)
    vec_land[0] = jnp.zeros((16, D), jnp.float32)
    vec_land[0, 9:12] = tail_ref[0:3]

    def norm_back(index):
        at = pl.ds(pl.multiple_of(index * NORM_ROWS, NORM_ROWS), NORM_ROWS)
        grad = input_grad[at]
        scaled = scaled_ref[at]
        d_first = normalize_back(grad * vec_ref[3:4], scaled, inverse_ref[at])
        input_grad[at] = d_first
        low = d_first.astype(jnp.bfloat16)
        vec_land[0, 2:3] += row_sum(low)
        vec_land[0, 3:4] += row_sum(grad * scaled)
        vec_land[0, 4:5] += row_sum(grad)
        for column in range(nf):
            branch[column, at] = low[:, column * width_attn : (column + 1) * width_attn]

    loop(tokens_ref.shape[0] // NORM_ROWS, norm_back)
    label_row = label_ref[...].astype(jnp.float32)
    label_col = jnp.transpose(jnp.broadcast_to(label_row, (128, label_row.shape[1])))[:, 0:1]
    load(0, mixture_ref, wide_two).wait()
    turned_two[...] = jnp.transpose(wide_two[...])

    def attn_turn(turn):
        block = place_of(turn)
        now = nf * per + turn

        def load_next(index):
            @pl.when(turn < nf - 1)
            def _():
                attn_load(index, turn + 1).start(priority=1)

        for index in range(3):
            attn_load(index, turn).wait()
        count = tokens_ref.shape[0]
        zero = jnp.zeros((count, width_attn), jnp.float32)
        d_mixture = zero
        for index in range(nf):
            d_mixture += contract_cols(branch[index], flat(attn_weight[1][index]))
        load_next(1)
        d_mixture = d_mixture.astype(jnp.bfloat16)
        queries, keys_all, values_all = (attn_block[index] for index in range(3))
        allowed = label_col == label_row
        d_queries, d_keys, d_values = zero, zero, zero
        for head in range(width_attn // HDIM):
            my_queries = head_lanes(queries, head) * score_scale
            my_mixture = head_lanes(d_mixture, head)
            scores = contract_cols(keys_all, my_queries) - total_ref[block, head : head + 1, :]
            attention = jnp.where(allowed, jnp.exp(scores), 0.0)
            d_attention = contract_cols(values_all, my_mixture)
            inner = jnp.sum(d_attention * attention, axis=0, keepdims=True)
            d_scores = (attention * (d_attention - inner)).astype(jnp.bfloat16)
            d_keys += product(d_scores, my_queries)
            d_values += product(attention.astype(jnp.bfloat16), my_mixture)
            d_queries += contract_rows(d_scores, head_lanes(keys_all, head) * score_scale)
        load_next(2)
        grads = [values.astype(jnp.bfloat16) for values in (d_queries, d_keys, d_values)]
        query_sum[block] = row_sum(grads[0])
        value_sum[block] = row_sum(grads[2])
        moved = jnp.zeros((count, D), jnp.float32)
        for index in range(3):
            weight = attn_weight[0][:, index * rows : (index + 1) * rows]
            moved += contract_cols(grads[index], flat(weight))
        input_grad[...] += moved
        load_next(0)

        pair_take(now - lag)
        for index in range(4):
            flipped, grad = (turned_one, grads[index]) if index < 3 else (turned_two, branch[block])

            def keep(values, index=index):
                held_attn[:, block, index] = values

            def give(values, index=index):
                stages_out[lax.rem(now, lag), :, index] = values

            split(product(flipped[...], grad), keep, give)
        pair_copy(now).start()
        sends_at(now, range(nf * per, total_steps))

        @pl.when(turn == nf - 4)
        def _():
            turned_take((0,))
            take_first(0, range(1, side))
            take_first(1, range(1, side))

        @pl.when(turn == lag - 1)
        def _():
            turned_start((nf - 1,))

        @pl.when(turn == nf - 3)
        def _():
            turned_take(range(1, nf - 1))
            take_first(0, (0,))
            take_first(1, (0,))

        @pl.when(turn == nf - 2)
        def _():
            take_first(turned, range(1, side))

        @pl.when(turn == nf - 1)
        def _():
            turned_take((nf - 1,))
            take_first(turned, (0,))

        @pl.when(turn == nf - 2)
        def _():
            take_second(0)
            take_second(1)

    loop(nf, attn_turn)
    for index in range(nf):
        at = slice(index * width_attn, (index + 1) * width_attn)
        vec_land[0, 0:1, at] = query_sum[index]
        vec_land[0, 1:2, at] = value_sum[index]
    for index in range(nf * per):
        left = index * width
        vec_land[0, 5 + left // D : 6 + left // D, left % D : left % D + width] = bias_up_sum[index]
    vec_start(0)
    for step in range(total_steps - lag, total_steps):
        pair_take(step)
    sends_at(total_steps, (total_steps,))

    take_first(2, range(1, side))
    take_z(0)
    start_pieces(0)
    take_z(1)
    start_pieces(1)
    vec_take(0)
    take_first(2, (0,))
    take_second(2)
    vec_take(1)

    @pl.when(runs_ffn)
    def _():
        crossing.take()

    vec_take(2)
    take_z(2)
    vec_take(3)

    @pl.when(runs_ffn)
    def _():
        crossing.pass_on()
        crossing.near()
        crossing.far()
        crossing.finish()

    for matrix in range(2):
        for half in range(2):
            @pl.when(dp != 2 + 2 * matrix + half)
            def _(matrix=matrix, half=half):
                piece_copy(matrix, half).wait_send()

    def turned_sent(plane_at):
        for step in range(1, nz):
            turned_copy(plane_at, step).wait_send()

    loop(nf, turned_sent)
    for step in range(1, side):
        second_copy(turned, z, step).wait_send()
        for line in range(side):
            first_copy(turned, z, line, step).wait_send()
    for chunk in range(chunks):

        def finish(z_at):
            for step in range(1, side):
                second_copy(chunk, z_at, step).wait_send()
                for line in range(side):
                    first_copy(chunk, z_at, line, step).wait_send()

        loop(nz, finish)
        for step in range(1, nz):
            z_copy(chunk, step).wait_send()
    for index in range(4):
        for step in range(len(vec_rounds[index])):
            vec_copy(index, step).wait_send()


def backward_kernel_entry(ndp, nf, *refs):
    at = 18 + 8 + 15 + 2 + 2
    backward_kernel(ndp, nf, *refs[:at], refs[at : at + 2], *refs[at + 2 :])


def backward(
    ndp, nf, d_second, low, scaled, inverse, vectors, active, slope, up_all, down_all,
    tokens, segments, blocks, mixture, totals, attn_all, tail_sums, attn_mom, ffn_mom,
):
    nz, side = ndp // 2, math.isqrt(nf)
    count = tokens.shape[0]
    rows, width_ffn = up_all.shape[2:]
    width_attn = attn_all.shape[-1]
    width = 2 * width_attn
    bf16, f32 = jnp.bfloat16, jnp.float32
    dma = pltpu.SemaphoreType.DMA
    anywhere, inside = pl.BlockSpec(memory_space=pl.ANY), pl.BlockSpec(memory_space=pltpu.VMEM)
    shapes = [(rows, width_ffn), (rows, width_ffn), (4, rows, width_attn)]
    vec_copies = 1 + 2 * (side - 1) + nz - 1
    half = (rows, width_ffn // 2)
    sums = [pltpu.VMEM((nz, nf) + shape, bf16) for shape in shapes]
    for lead in ((nz, side - 1, side), (nz, side - 1), (nz - 1,)):
        sums += [pltpu.VMEM(lead + shape, bf16) for shape in (shapes[0], half, shapes[2])]
    sums += [pltpu.VMEM(lead + half, bf16) for lead in ((1, side - 1, side), (1, side - 1), (nz - 1, nf))]
    return pl.pallas_call(
        functools.partial(backward_kernel_entry, ndp, nf),
        name="backward",
        out_shape=[jax.ShapeDtypeStruct((count, D), f32)]
        + [jax.ShapeDtypeStruct(shape, f32) for shape in shapes]
        + [
            jax.ShapeDtypeStruct((16, D), f32),
            jax.ShapeDtypeStruct(attn_mom.shape, bf16),
            jax.ShapeDtypeStruct((2, 2, rows, width_ffn // 2), bf16),
            jax.ShapeDtypeStruct((nf, ndp, rows, width_ffn // 2), bf16),
        ],
        in_specs=[
            anywhere,
            anywhere,
            inside,
            inside,
            inside,
            anywhere,
            anywhere,
            anywhere,
            anywhere,
            anywhere,
            inside,
            anywhere,
            anywhere,
            inside,
            anywhere,
            inside,
            anywhere,
            anywhere,
        ],
        out_specs=[inside] * 7 + [anywhere],
        scratch_shapes=sums
        + [
            pltpu.VMEM((2, nz, 4, rows, width_attn), bf16),
            pltpu.VMEM((4, nz, 4, rows, width_attn), bf16),
            pltpu.VMEM((2, 2, ndp, rows, width), bf16),
            pltpu.VMEM((2, 2, count, width), bf16),
            pltpu.VMEM((ndp, 3 * rows, width_attn), bf16),
            pltpu.VMEM((nf, ndp // nf, rows, width_attn), bf16),
            pltpu.VMEM((3, count, width_attn), bf16),
            pltpu.VMEM((count, D), bf16),
            pltpu.VMEM((count, D), bf16),
            pltpu.VMEM((D, count), bf16),
            pltpu.VMEM((D, count), bf16),
            pltpu.VMEM((nf, count, width_attn), bf16),
            pltpu.VMEM((FF // width, 1, width), f32),
            pltpu.VMEM((nf, 1, width_attn), f32),
            pltpu.VMEM((nf, 1, width_attn), f32),
            pltpu.VMEM((4 + vec_copies, 16, D), f32),
            dma((6,)),
            dma((2, 4)),
            dma((2,)),
            dma((4,)),
            dma((4, nz, side - 1, side)),
            dma((4, nz, side - 1, side)),
            dma((4, nz, side - 1)),
            dma((4, nz, side - 1)),
            dma((3, nz - 1)),
            dma((3, nz - 1)),
            dma((vec_copies,)),
            dma((vec_copies,)),
            dma,
            dma((4,)),
            dma((ndp,)),
            dma((ndp, side - 1)),
            dma((ndp, side, side - 1)),
            dma((nf, ndp)),
            dma((nz - 1, nf)),
            dma((nz - 1, nf)),
        ],
        compiler_params=pltpu.CompilerParams(
            collective_id=3, has_side_effects=True, vmem_limit_bytes=63 * 1024 * 1024
        ),
    )(
        d_second, low, scaled, inverse, vectors, active, slope, up_all, down_all,
        tokens, segments[None, :], blocks, mixture, totals, attn_all, tail_sums, attn_mom, ffn_mom,
    )


def on_device(
    tokens,
    segments,
    cotangent,
    attn_w,
    ffn_w,
    vectors,
    attn_mom,
    ffn_mom,
    vec_mom,
    attn_ema,
    ffn_ema,
    vec_ema,
):
    ndp, nf = lax.axis_size("dp"), lax.axis_size("fsdp")
    share = vectors.shape[1]
    (
        attn_all, up_all, down_all, blocks, active, slope, vec_full, mixture, totals, scaled, inverse, low,
        layer_out, d_second, tail_sums,
    ) = forward(ndp, nf, tokens, segments, cotangent, attn_w, ffn_w, vectors)
    input_grad, up_grad, down_grad, attn_grad, vec_sum, attn_piece, _, ffn_whole = backward(
        ndp, nf, d_second, low, scaled, inverse, vec_full, active, slope, up_all, down_all,
        tokens, segments, blocks, mixture, totals, attn_all, tail_sums, attn_mom, ffn_mom,
    )
    mine = (lax.axis_index("dp") * nf + lax.axis_index("fsdp")) * share
    vec_grad = lax.dynamic_slice(vec_sum, (0, mine), (12, share))
    attn_ortho, ffn_ortho = orthogonalize(ndp, nf, attn_piece, ffn_whole)
    total_tokens = tokens.shape[0] * ndp * nf
    updated = update_all(
        vector_step / math.sqrt(total_tokens),
        attn_w,
        ffn_w,
        vectors,
        attn_mom,
        ffn_mom,
        vec_mom,
        attn_ema,
        ffn_ema,
        vec_ema,
        attn_grad,
        up_grad,
        down_grad,
        vec_grad,
        attn_ortho,
        ffn_ortho,
    )
    return (layer_out, input_grad, *updated, vec_grad[2])


def solution(mesh):
    in_specs = (
        P(("dp", "fsdp"), None),
        P(("dp", "fsdp")),
        P(("dp", "fsdp"), None),
        P(None, "dp", "fsdp"),
        P(None, "dp", "fsdp"),
        P(None, ("dp", "fsdp")),
        P(None, "dp", "fsdp"),
        P(None, "dp", "fsdp"),
        P(None, ("dp", "fsdp")),
        P(None, "dp", "fsdp"),
        P(None, "dp", "fsdp"),
        P(None, ("dp", "fsdp")),
    )
    out_specs = (
        P(("dp", "fsdp"), None),
        P(("dp", "fsdp"), None),
        P(None, "dp", "fsdp"),
        P(None, "dp", "fsdp"),
        P(None, ("dp", "fsdp")),
        P(None, "dp", "fsdp"),
        P(None, "dp", "fsdp"),
        P(None, ("dp", "fsdp")),
        P(None, "dp", "fsdp"),
        P(None, "dp", "fsdp"),
        P(None, ("dp", "fsdp")),
        P(("dp", "fsdp")),
    )
    return jax.shard_map(
        on_device, mesh=mesh, in_specs=in_specs, out_specs=out_specs, check_vma=False
    )
```

```python
import functools
import math

import jax
import jax.numpy as jnp
from jax import lax
from jax.experimental import pallas as pl
from jax.experimental.pallas import tpu as pltpu
from jax.sharding import PartitionSpec as P

D = 1024
FF = 4096
HEADS = 16
HDIM = 64
TILE = 512
ITERS = 5


score_scale = 0.125
ln_epsilon = 1e-05
norm_epsilon = 1e-06
ns_linear = 3.4445
ns_square = -4.775
ns_cubic = 2.0315
matrix_decay = 0.95
vector_decay = 0.9
average_decay = 0.7
weight_decay = 0.01
attn_rates = (1.0, 1.0, 1.0, 10.0)
vector_step = 0.3


def product(left, right):
    return jnp.dot(left, right, preferred_element_type=jnp.float32)


def contract_rows(left, right):
    return lax.dot_general(
        left, right, (((0,), (0,)), ((), ())), preferred_element_type=jnp.float32
    )


def contract_cols(left, right):
    return lax.dot_general(
        left, right, (((1,), (1,)), ((), ())), preferred_element_type=jnp.float32
    )


MESH = pl.DeviceIdType.MESH
ROLES = 8
STEP_ROWS = 512
NORM_ROWS = 128
TILE_ROWS = 128


def greet(partners):
    barrier = pltpu.get_barrier_semaphore()
    for partner in partners:
        pl.semaphore_signal(barrier, inc=1, device_id=partner, device_id_type=MESH)
    pl.semaphore_wait(barrier, len(partners))


def place(ndp, nf):
    dp, fs = lax.axis_index("dp"), lax.axis_index("fsdp")
    side = math.isqrt(nf)
    return lax.div(dp, 2), lax.rem(dp, 2), lax.div(fs, side), lax.rem(fs, side), ndp // 2, side


def line_partners(ndp, nf):
    z, core, y, x, nz, side = place(ndp, nf)
    mine = y * side + x
    return (
        [(z * 2 + 1 - core, mine)]
        + [(lax.rem(z + step, nz) * 2 + core, mine) for step in range(1, nz)]
        + [(z * 2 + core, y * side + lax.rem(x + step, side)) for step in range(1, side)]
        + [(z * 2 + core, lax.rem(y + step, side) * side + x) for step in range(1, side)]
    )


def all_partners(ndp, nf):
    z, core, y, x, nz, side = place(ndp, nf)
    dp, fs = z * 2 + core, y * side + x
    return (
        [(lax.rem(dp + step, ndp), fs) for step in range(1, ndp)]
        + [(dp, y * side + lax.rem(x + step, side)) for step in range(1, side)]
        + [(dp, lax.rem(y + step, side) * side + x) for step in range(1, side)]
    )


def remote(source, target, send_sem, recv_sem, device):
    return pltpu.make_async_remote_copy(
        src_ref=source,
        dst_ref=target,
        send_sem=send_sem,
        recv_sem=recv_sem,
        device_id=device,
        device_id_type=MESH,
    )


def loop(count, body, start=0):
    def step(index, carry):
        body(index)
        return carry

    lax.fori_loop(start, count, step, 0)


class Crossing:
    def __init__(self, ndp, nf, land, own_sem, piece_recv, first_send, second_send, plane_recv, source):
        self.ndp, self.land, self.own_sem, self.piece_recv, self.source = ndp, land, own_sem, piece_recv, source
        self.first_send, self.second_send, self.plane_recv = first_send, second_send, plane_recv
        self.z, self.core, self.y, self.x, self.nz, self.side = place(ndp, nf)
        self.dp, self.fs = self.z * 2 + self.core, self.y * self.side + self.x

    def row_of(self, index):
        return lax.rem(self.z + index // 2, self.nz) * 2 + lax.rem(self.core + index, 2)

    def x_first(self, row):
        return lax.rem(row // 2, 2) == 0

    def along(self, first, step):
        x_at = jnp.where(first, lax.rem(self.x + step, self.side), self.x)
        y_at = jnp.where(first, self.y, lax.rem(self.y + step, self.side))
        return y_at * self.side + x_at

    def first_copy(self, row, step):
        here = self.land.at[self.fs, row]
        peer = self.along(self.x_first(row), step)
        sems = self.first_send.at[row, step - 1], self.plane_recv.at[self.fs, row]
        return remote(here, here, *sems, (self.dp, peer))

    def second_copy(self, plane_at, row, line, step):
        here = self.land.at[plane_at, row]
        peer = self.along(jnp.logical_not(self.x_first(row)), step)
        sems = self.second_send.at[row, line, step - 1], self.plane_recv.at[plane_at, row]
        return remote(here, here, *sems, (self.dp, peer))

    def arrived(self, plane_at, row):
        here = self.land.at[plane_at, row]
        remote(here, here, self.own_sem, self.plane_recv.at[plane_at, row], (self.dp, self.fs)).wait_recv()

    def take(self):
        def each(index):
            row = self.row_of(index)

            @pl.when(index == 0)
            def _():
                pltpu.make_async_copy(self.source, self.land.at[self.fs, row], self.own_sem).wait()

            @pl.when(index > 0)
            def _():
                here = self.land.at[self.fs, row]
                remote(self.source, here, self.own_sem, self.piece_recv.at[row], (self.dp, self.fs)).wait_recv()

            for step in range(1, self.side):
                self.first_copy(row, step).start()
                self.second_copy(self.fs, row, 0, step).start()

        loop(self.ndp, each)

    def pass_on(self):
        def each(index):
            row = self.row_of(index)
            for line in range(1, self.side):
                plane_at = self.along(self.x_first(row), line)
                self.arrived(plane_at, row)
                for step in range(1, self.side):
                    self.second_copy(plane_at, row, line, step).start()

        loop(self.ndp, each)

    def wait_line(self, line):
        for step in range(1, self.side):

            def each(index, step=step):
                row = self.row_of(index)
                x, y, side = self.x, self.y, self.side
                there = jnp.where(
                    self.x_first(row),
                    lax.rem(y + step, side) * side + lax.rem(x + line, side),
                    lax.rem(y + line, side) * side + lax.rem(x + step, side),
                )
                self.arrived(there, row)

            loop(self.ndp, each)

    def near(self):
        self.wait_line(0)

    def far(self):
        for line in range(1, self.side):
            self.wait_line(line)

    def finish(self):
        def each(row):
            for step in range(1, self.side):
                self.first_copy(row, step).wait_send()
                for line in range(self.side):
                    self.second_copy(self.fs, row, line, step).wait_send()

        loop(self.ndp, each)


def ortho_kernel(
    ndp,
    nf,
    attn_ref,
    ffn_whole,
    attn_out,
    ffn_out,
    land_attn,
    land_ffn,
    iter_low,
    iter_full,
    gram,
    gram_send,
    gram_recv,
    off_low,
    poly_low,
    diag_row,
    diag_col,
    inverse_norm,
    own_low,
    own_full,
    own_attn,
    own_ffn,
    own_sem,
    piece_send,
    piece_recv,
    first_send,
    second_send,
    plane_recv,
    gram_send_sem,
    gram_recv_sem,
    back_send,
    back_recv,
    load_sem,
):
    z, core, y, x, nz, side = place(ndp, nf)
    dp, fs = z * 2 + core, y * side + x
    rows = attn_ref.shape[1]
    size = rows * ndp
    is_attn = jnp.logical_or(dp < 2, jnp.logical_and(dp >= 6, dp < ROLES))
    is_ffn = jnp.logical_and(dp >= 2, dp < 6)
    partner = z * 2 + 1 - core

    greet(all_partners(ndp, nf))
    attn_roles = (0, 6, 1, 7)

    def piece(role):
        return attn_ref.at[role if role < 2 else role - 4]

    def piece_copy(role):
        return remote(piece(role), land_attn.at[fs, dp], piece_send.at[role], piece_recv.at[dp], (role, fs))

    for role in attn_roles:
        @pl.when(dp != role)
        def _(role=role):
            piece_copy(role).start()

        @pl.when(dp == role)
        def _(role=role):
            pltpu.make_async_copy(piece(role), land_attn.at[fs, dp], own_sem).start()

    def iterate(land, source, own_out, target, role, paired):
        width = land.shape[-1]
        columns = width * nf
        tall = min(STEP_ROWS, size)
        steps = size // tall
        wide = min(1024, columns)

        def add_gram(plane_at, fresh):
            block = land[plane_at].reshape(size, width)
            for step in range(steps):
                at = slice(step * tall, (step + 1) * tall)
                part = contract_cols(block[at], block)
                if fresh:
                    gram[at] = part
                else:
                    gram[at] += part

        if paired:

            def block_load(index):
                return pltpu.make_async_copy(ffn_whole.at[index], land.at[index], load_sem.at[index])

            for index in range(nf):
                block_load(index).start()
            for index in range(nf):
                block_load(index).wait()
                add_gram(index, index == 0)
        else:
            crossing = Crossing(ndp, nf, land, own_sem, piece_recv, first_send, second_send, plane_recv, source)
            crossing.take()
            add_gram(fs, True)
            crossing.pass_on()
            crossing.near()
            for step in range(1, side):
                add_gram(crossing.along(True, step), False)
                add_gram(crossing.along(False, step), False)
            crossing.far()
            for far_y in range(1, side):
                for far_x in range(1, side):
                    add_gram(lax.rem(y + far_y, side) * side + lax.rem(x + far_x, side), False)

        def gram_copy(slot, step):
            at = pl.ds(step * tall, tall)
            return remote(
                gram_send.at[slot, at],
                gram_recv.at[slot, at],
                gram_send_sem.at[slot, step],
                gram_recv_sem.at[slot, step],
                (partner, fs),
            )

        if paired:
            for step in range(steps):
                at = slice(step * tall, (step + 1) * tall)
                gram_send[0, at] = gram[at].astype(jnp.bfloat16)
                gram_copy(0, step).start()
        for index in range(nf):
            block = land[index].reshape(size, width)
            at = slice(index * width, (index + 1) * width)
            iter_low[0, :, at] = block
            iter_full[:, at] = block.astype(jnp.float32)

        def back_copy(row):
            return remote(own_out.at[row], target, back_send.at[row], back_recv.at[role], (row, fs))

        def iteration(count):
            now = lax.rem(count, 2)
            later = 1 - now

            @pl.when(count > 0)
            def _():
                def gram_rows(step):
                    at = pl.ds(pl.multiple_of(step * tall, tall), tall)
                    part = contract_cols(iter_low[now, at, :columns], iter_low[now, :, :columns])
                    if paired:
                        gram_send[now, at] = part.astype(jnp.bfloat16)
                        gram_copy(now, step).start()
                    else:
                        gram[at] = part

                loop(steps, gram_rows)

            eye = lax.broadcasted_iota(jnp.int32, (TILE_ROWS, TILE_ROWS), 0) == lax.broadcasted_iota(
                jnp.int32, (TILE_ROWS, TILE_ROWS), 1
            )

            @pl.when(count == 0)
            def _():
                trace = jnp.zeros((TILE_ROWS, TILE_ROWS), jnp.float32)
                if paired:
                    for step in range(steps):
                        gram_copy(now, step).wait()
                for tile in range(size // TILE_ROWS):
                    at = slice(tile * TILE_ROWS, (tile + 1) * TILE_ROWS)
                    if paired:
                        square = gram_send[now, at, at].astype(jnp.float32)
                        trace += square + gram_recv[now, at, at].astype(jnp.float32)
                    else:
                        trace += gram[at, at]
                trace = jnp.sum(jnp.where(eye, trace, 0.0), axis=1, keepdims=True)
                trace = jnp.sum(trace, axis=0, keepdims=True)
                inverse_norm[...] = 1.0 / (jnp.sqrt(trace) + norm_epsilon)

            @pl.when(count > 0)
            def _():
                inverse_norm[...] = jnp.ones_like(inverse_norm)

            inverse = inverse_norm[...]
            shrink = inverse * inverse

            for step in range(steps):
                if paired:
                    @pl.when(count > 0)
                    def _(step=step):
                        gram_copy(now, step).wait()

                for tile in range(step * tall // TILE_ROWS, (step + 1) * tall // TILE_ROWS):
                    at = slice(tile * TILE_ROWS, (tile + 1) * TILE_ROWS)
                    if paired:
                        total = gram_send[now, at].astype(jnp.float32) + gram_recv[now, at].astype(jnp.float32)
                    else:
                        total = gram[at]
                    total = total * shrink
                    gram[at] = total
                    off_low[at] = total.astype(jnp.bfloat16)
                    square = total[:, at]
                    masked = jnp.where(eye, square, 0.0)
                    diag_col[at] = jnp.sum(masked, axis=1, keepdims=True)
                    diag_row[:, at] = jnp.sum(masked, axis=0, keepdims=True)
                    square = jnp.where(eye, 0.0, square)
                    gram[at, at] = square
                    off_low[at, at] = square.astype(jnp.bfloat16)

            linear, middle, cubic = ns_linear * inverse, ns_square * inverse, ns_cubic * inverse

            def poly_rows(step):
                at = pl.ds(step * tall, tall)
                again = product(off_low[at], off_low[...])
                mine = diag_col[at]
                poly = gram[at] * (middle + cubic * mine + cubic * diag_row[...]) + cubic * again
                poly_low[at] = poly.astype(jnp.bfloat16)
                again_diag = []
                for tile in range(tall // TILE_ROWS):
                    rows_at = slice(tile * TILE_ROWS, (tile + 1) * TILE_ROWS)
                    side_at = slice(step * tall + tile * TILE_ROWS, step * tall + (tile + 1) * TILE_ROWS)
                    again_diag.append(
                        jnp.sum(jnp.where(eye, again[rows_at, side_at], 0.0), axis=1, keepdims=True)
                    )
                    poly_low[side_at, side_at] = jnp.where(eye, 0.0, poly[rows_at, side_at]).astype(jnp.bfloat16)
                again_diag = jnp.concatenate(again_diag, axis=0)
                factor = linear + middle * mine + cubic * (mine * mine + again_diag)

                @pl.when(count < ITERS - 1)
                def _():
                    for left in range(0, columns, wide):
                        part = slice(left, left + wide)
                        moved = product(poly_low[at], iter_low[now, :, part])
                        fresh = factor * iter_full[at, part] + moved
                        iter_full[at, part] = fresh
                        iter_low[later, at, part] = fresh.astype(jnp.bfloat16)

                @pl.when(count == ITERS - 1)
                def _():
                    for index in range(nf):
                        @pl.when(fs == index)
                        def _(index=index):
                            part = slice(index * width, (index + 1) * width)
                            own_full[at, :width] = iter_full[at, part]

                            if step == 0:
                                own_low[:, :width] = iter_low[now, :, part]

                    moved = product(poly_low[at], own_low[:, :width])
                    fresh = factor * own_full[at, :width] + moved
                    blocks = tall // rows
                    own_out[pl.ds(step * blocks, blocks)] = fresh.astype(jnp.bfloat16).reshape(
                        blocks, rows, width
                    )

                    def give(index):
                        row = step * blocks + index

                        @pl.when(row != dp)
                        def _():
                            back_copy(row).start()

                        @pl.when(row == dp)
                        def _():
                            pltpu.make_async_copy(own_out.at[row], target, own_sem).start()

                    loop(blocks, give)

            for step in range(steps):
                poly_rows(step)

        loop(ITERS, iteration)

        if not paired:
            crossing.finish()

        def finish(row):
            @pl.when(row != dp)
            def _():
                back_copy(row).wait_send()

        loop(ndp, finish)
        pltpu.make_async_copy(own_out.at[dp], target, own_sem).wait()

    @pl.when(is_attn)
    def _():
        at = jnp.where(dp < 2, dp, dp - 4)
        iterate(land_attn, attn_ref.at[at], own_attn, attn_out.at[at], dp, False)

    @pl.when(is_ffn)
    def _():
        matrix, half = (dp - 2) // 2, lax.rem(dp - 2, 2)
        iterate(land_ffn, None, own_ffn, ffn_out.at[matrix, half], dp, True)

    for role in range(ROLES):
        @pl.when(dp != role)
        def _(role=role):
            if role < 2 or role >= 6:
                target = attn_out.at[role if role < 2 else role - 4]
            else:
                target = ffn_out.at[(role - 2) // 2, (role - 2) % 2]
            if role in attn_roles:
                piece_copy(role).wait_send()
            remote(target, target, own_sem, back_recv.at[role], (role, fs)).wait_recv()


def orthogonalize(ndp, nf, attn_low, ffn_whole):
    rows, width_attn = attn_low.shape[1:]
    width_ffn = ffn_whole.shape[3]
    side = math.isqrt(nf)
    size = rows * ndp
    columns = width_ffn * nf
    tall = min(STEP_ROWS, size)
    bf16, f32 = jnp.bfloat16, jnp.float32
    dma = pltpu.SemaphoreType.DMA
    return pl.pallas_call(
        functools.partial(ortho_kernel, ndp, nf),
        name="newton_schulz",
        out_shape=[
            jax.ShapeDtypeStruct(attn_low.shape, bf16),
            jax.ShapeDtypeStruct((2, 2, rows, width_ffn), bf16),
        ],
        in_specs=[pl.BlockSpec(memory_space=pltpu.VMEM), pl.BlockSpec(memory_space=pl.ANY)],
        out_specs=[pl.BlockSpec(memory_space=pltpu.VMEM)] * 2,
        scratch_shapes=[
            pltpu.VMEM((nf, ndp, rows, width_attn), bf16),
            pltpu.VMEM((nf, ndp, rows, width_ffn), bf16),
            pltpu.VMEM((2, size, columns), bf16),
            pltpu.VMEM((size, columns), f32),
            pltpu.VMEM((size, size), f32),
            pltpu.VMEM((2, size, size), bf16),
            pltpu.VMEM((2, size, size), bf16),
            pltpu.VMEM((size, size), bf16),
            pltpu.VMEM((size, size), bf16),
            pltpu.VMEM((1, size), f32),
            pltpu.VMEM((size, 1), f32),
            pltpu.VMEM((1, 1), f32),
            pltpu.VMEM((size, width_ffn), bf16),
            pltpu.VMEM((size, width_ffn), f32),
            pltpu.VMEM((ndp, rows, width_attn), bf16),
            pltpu.VMEM((ndp, rows, width_ffn), bf16),
            dma,
            dma((ROLES,)),
            dma((ndp,)),
            dma((ndp, side - 1)),
            dma((ndp, side, side - 1)),
            dma((nf, ndp)),
            dma((2, size // tall)),
            dma((2, size // tall)),
            dma((ndp,)),
            dma((ROLES,)),
            dma((nf,)),
        ],
        compiler_params=pltpu.CompilerParams(
            collective_id=1, has_side_effects=True, vmem_limit_bytes=60 * 1024 * 1024
        ),
    )(attn_low, ffn_whole)


def update_kernel(
    attn_w,
    ffn_w,
    vectors,
    attn_mom,
    ffn_mom,
    vec_mom,
    attn_ema,
    ffn_ema,
    vec_ema,
    attn_grad,
    up_grad,
    down_grad,
    vec_grad,
    attn_ortho,
    ffn_ortho,
    attn_new,
    ffn_new,
    vec_new,
    attn_mom_new,
    ffn_mom_new,
    vec_mom_new,
    attn_ema_new,
    ffn_ema_new,
    vec_ema_new,
    *,
    vector_rate,
):
    for index in range(4):
        rate = attn_rates[index]
        attn_mom_new[index] = matrix_decay * attn_mom[index] + attn_grad[index]
        new = attn_w[index] * (1.0 - weight_decay * rate) - rate * attn_ortho[index].astype(jnp.float32)
        attn_new[index] = new
        attn_ema_new[index] = average_decay * attn_ema[index] + (1.0 - average_decay) * new
    width = ffn_ortho.shape[-1]
    shape_factor = math.sqrt(FF / D)
    for index, grad in enumerate((up_grad, down_grad)):
        ffn_mom_new[index] = matrix_decay * ffn_mom[index] + grad[...]
        for half in range(2):
            at = slice(half * width, (half + 1) * width)
            ortho = ffn_ortho[index, half].astype(jnp.float32)
            new = ffn_w[index, :, at] * (1.0 - weight_decay) - shape_factor * ortho
            ffn_new[index, :, at] = new
            ffn_ema_new[index, :, at] = average_decay * ffn_ema[index, :, at] + (1.0 - average_decay) * new
    mom = vector_decay * vec_mom[...] + vec_grad[...]
    vec_mom_new[...] = mom
    new = vectors[...] - vector_rate * mom
    vec_new[...] = new
    vec_ema_new[...] = average_decay * vec_ema[...] + (1.0 - average_decay) * new


def update_all(vector_rate, *operands):
    states = operands[:9]
    return pl.pallas_call(
        functools.partial(update_kernel, vector_rate=vector_rate),
        name="update",
        out_shape=[jax.ShapeDtypeStruct(states[index % 3].shape, jnp.float32) for index in range(9)],
        in_specs=[pl.BlockSpec(memory_space=pltpu.VMEM)] * len(operands),
        out_specs=[pl.BlockSpec(memory_space=pltpu.VMEM)] * 9,
        compiler_params=pltpu.CompilerParams(vmem_limit_bytes=60 * 1024 * 1024),
    )(*operands)


ROOM = pltpu.CompilerParams(vmem_limit_bytes=56 * 1024 * 1024)
ROOT_HALF = math.sqrt(0.5)
BELL = 1.0 / math.sqrt(2.0 * math.pi)


def flat(block):
    return block.reshape(-1, block.shape[-1])


def head_lanes(values, head):
    if values.shape[1] == HDIM:
        return values
    lane = lax.broadcasted_iota(jnp.int32, values.shape, 1)
    return jnp.where(lax.div(lane, HDIM) == head, values, jnp.zeros_like(values))


def normalize(values):
    center = values - jnp.mean(values, axis=1, keepdims=True)
    inverse = lax.rsqrt(jnp.mean(center * center, axis=1, keepdims=True) + ln_epsilon)
    return center * inverse, inverse


def normalize_back(grad, scaled, inverse):
    return inverse * (
        grad
        - jnp.mean(grad, axis=1, keepdims=True)
        - scaled * jnp.mean(grad * scaled, axis=1, keepdims=True)
    )


def row_sum(values):
    return jnp.sum(values.astype(jnp.float32), axis=0, keepdims=True)


def forward_kernel(
    ndp,
    nf,
    tokens_ref,
    label_ref,
    cotangent_ref,
    attn_w,
    ffn_w,
    vectors_ref,
    attn_out,
    up_out,
    down_out,
    blocks_out,
    active_out,
    slope_out,
    vec_out,
    mixture_out,
    total_out,
    scaled_out,
    inverse_out,
    low_out,
    layer_out,
    d_second_out,
    sums_out,
    attn_shard,
    up_shard,
    down_shard,
    three_weight,
    out_weight,
    ffn_weight,
    vec_land,
    bias,
    bias_up,
    blocks,
    parts,
    active,
    slope,
    total,
    own_sem,
    own_recv,
    pair_recv,
    z_send,
    first_send,
    second_send,
    pair_send,
    load_sem,
    store_sem,
):
    chunks, turned = 4, 3
    wholes = (attn_out, up_out, down_out)
    z, core, y, x, nz, side = place(ndp, nf)
    dp, fs = z * 2 + core, y * side + x
    rows, width_attn = attn_w.shape[1:]
    width_ffn, share = ffn_w.shape[2], vectors_ref.shape[1]
    count = tokens_ref.shape[0]
    width = ffn_weight.shape[-1]
    per = width_ffn // width

    attn_shard[4 * rows :] = jnp.zeros((16, width_attn), jnp.bfloat16)
    attn_shard[4 * rows : 4 * rows + 12, :share] = vectors_ref[...].astype(jnp.bfloat16)
    for index in range(4):
        attn_shard[index * rows : (index + 1) * rows] = attn_w[index].astype(jnp.bfloat16)
    up_shard[...] = ffn_w[0].astype(jnp.bfloat16)
    down_shard[...] = ffn_w[1].astype(jnp.bfloat16)
    greet(line_partners(ndp, nf))

    halves = slice(0, width_ffn // 2), slice(width_ffn // 2, width_ffn)
    shards = (attn_shard, up_shard, down_shard.at[:, halves[0]], down_shard.at[:, halves[1]])

    def row_slot(chunk, plane_at, row):
        if chunk < 2:
            return wholes[chunk].at[plane_at, row]
        return down_out.at[plane_at, row, :, halves[chunk - 2]]

    def slot(chunk, plane_at, z_at):
        return row_slot(chunk, plane_at, z_at * 2 + core)

    def source(chunk, plane_at, z_at, own):
        return shards[chunk] if own else slot(chunk, plane_at, z_at)

    def along(first, step):
        x_at = jnp.where(first, lax.rem(x + step, side), x)
        y_at = jnp.where(first, y, lax.rem(y + step, side))
        return y_at * side + x_at

    def first_copy(chunk, z_at, step, own):
        peer = along(lax.rem(z_at, 2) == 0, step)
        return remote(
            source(chunk, fs, z_at, own),
            slot(chunk, fs, z_at),
            first_send.at[chunk, z_at, step - 1],
            own_recv.at[chunk, fs, z_at],
            (dp, peer),
        )

    def second_copy(chunk, plane_at, z_at, step, own, line):
        peer = along(lax.rem(z_at, 2) != 0, step)
        return remote(
            source(chunk, plane_at, z_at, own),
            slot(chunk, plane_at, z_at),
            second_send.at[chunk, z_at, line, step - 1],
            own_recv.at[chunk, plane_at, z_at],
            (dp, peer),
        )

    def pair_copy(chunk, plane_at, z_at, own):
        return remote(
            source(chunk, plane_at, z_at, own),
            slot(chunk, plane_at, z_at),
            pair_send.at[chunk, plane_at, z_at],
            pair_recv.at[chunk, plane_at, z_at],
            (z * 2 + 1 - core, fs),
        )

    def z_copy(chunk, plane_at, z_at, up, own):
        return remote(
            source(chunk, plane_at, z_at, own),
            slot(chunk, plane_at, z_at),
            z_send.at[chunk, plane_at, z_at, up],
            own_recv.at[chunk, plane_at, z_at],
            ((z + (1 if up else -1)) * 2 + core, fs),
        )

    def along_z(chunk, plane_at, z_at, own, act):
        @pl.when(jnp.logical_and(z_at <= z, z < nz - 1))
        def _():
            act(z_copy(chunk, plane_at, z_at, 1, own))

        @pl.when(jnp.logical_and(z_at >= z, z > 0))
        def _():
            act(z_copy(chunk, plane_at, z_at, 0, own))

    def begin(copy):
        copy.start()

    def arrived(chunk, plane_at, z_at):
        here = slot(chunk, plane_at, z_at)
        remote(here, here, own_sem.at[chunk], own_recv.at[chunk, plane_at, z_at], (dp, fs)).wait_recv()

    def pass_on(chunk, z_at, own):
        for step in range(1, side):
            first_copy(chunk, z_at, step, own).start()
            second_copy(chunk, fs, z_at, step, own, 0).start()
        pair_copy(chunk, fs, z_at, own).start()

    def own_copy(chunk):
        return pltpu.make_async_copy(shards[chunk], slot(chunk, fs, z), own_sem.at[chunk])

    def near_first(body):
        def each(index):
            far = 1 + lax.div(index, 2)
            z_at = jnp.where(lax.rem(index, 2) == 0, z - far, z + far)

            @pl.when(jnp.logical_and(z_at >= 0, z_at < nz))
            def _():
                body(z_at)

        loop(2 * (nz - 1), each)

    def from_z(chunk):
        def each(z_at):
            arrived(chunk, fs, z_at)
            along_z(chunk, fs, z_at, False, begin)
            pass_on(chunk, z_at, False)

        near_first(each)

    def from_first(chunk):
        def each(z_at):
            for line in range(1, side):
                plane_at = along(lax.rem(z_at, 2) == 0, line)
                arrived(chunk, plane_at, z_at)
                for step in range(1, side):
                    second_copy(chunk, plane_at, z_at, step, False, line).start()
                pair_copy(chunk, plane_at, z_at, False).start()

        each(z)
        near_first(each)

    def last_places(z_at):
        x_first = lax.rem(z_at, 2) == 0
        for line in range(side):
            for step in range(1, side):
                near_x, far_y = lax.rem(x + line, side), lax.rem(y + step, side)
                far_x, near_y = lax.rem(x + step, side), lax.rem(y + line, side)
                yield jnp.where(x_first, far_y * side + near_x, near_y * side + far_x)

    def from_second(chunk):
        def each(z_at):
            for plane_at in last_places(z_at):
                arrived(chunk, plane_at, z_at)
                pair_copy(chunk, plane_at, z_at, False).start()

        each(z)
        near_first(each)

    def turned_first():
        for line in range(1, side):
            plane_at = along(lax.rem(z, 2) == 0, line)
            arrived(turned, plane_at, z)
            for step in range(1, side):
                second_copy(turned, plane_at, z, step, False, line).start()
            along_z(turned, plane_at, z, False, begin)
            pair_copy(turned, plane_at, z, False).start()

    def turned_second():
        for plane_at in last_places(z):
            arrived(turned, plane_at, z)
            along_z(turned, plane_at, z, False, begin)
            pair_copy(turned, plane_at, z, False).start()

    def turned_z(far):
        for z_at in (z - far, z + far):
            @pl.when(jnp.logical_and(z_at >= 0, z_at < nz))
            def _(z_at=z_at):
                def each(step):
                    plane_at = lax.rem(fs + step, nf)
                    arrived(turned, plane_at, z_at)
                    along_z(turned, plane_at, z_at, False, begin)
                    pair_copy(turned, plane_at, z_at, False).start()

                loop(nf, each)

    def from_pair(chunk):
        own_copy(chunk).wait()

        def each(index):
            plane_at, z_at = lax.rem(index, nf), lax.div(index, nf)
            there = row_slot(chunk, plane_at, z_at * 2 + 1 - core)
            remote(
                there, there, own_sem.at[chunk], pair_recv.at[chunk, plane_at, z_at], (dp, fs)
            ).wait_recv()

        loop(nf * nz, each)

    for chunk in (0, turned, 1, 2):
        own_copy(chunk).start(priority=1)
        along_z(chunk, fs, z, True, begin)
        pass_on(chunk, z, True)

    from_z(0)
    from_first(0)
    turned_first()
    from_z(1)
    from_second(0)
    turned_second()
    from_pair(0)

    def load(index, source, target):
        return pltpu.make_async_copy(source, target, load_sem.at[index])

    def attn_load(index, block, at):
        per_block = ndp // nf
        if index == 0:
            return load(at, attn_out.at[block, :, pl.ds(0, 3 * rows)], three_weight.at[at])
        return load(
            2 + at,
            attn_out.at[:, pl.ds(block * per_block, per_block), pl.ds(3 * rows, rows)],
            out_weight.at[at],
        )

    vec_copy = load(4, attn_out.at[:, :, pl.ds(4 * rows, 16)], vec_land)
    vec_copy.start(priority=1)
    for index in range(2):
        attn_load(index, 0, 0).start(priority=1)
    vec_copy.wait()
    for row in range(ndp):
        for column in range(nf):
            left = (row * nf + column) * share
            vec_out[:, left : left + share] = vec_land[column, row, :, :share].astype(jnp.float32)
    for index in range(nf):
        at = slice(index * width_attn, (index + 1) * width_attn)
        bias[index, 0:1] = vec_out[0:1, at]
        bias[index, 1:2] = vec_out[1:2, at]
    for index in range(FF // width):
        left = index * width
        bias_up[index] = vec_out[5 + left // D : 6 + left // D, left % D : left % D + width]
    label_row = label_ref[...].astype(jnp.float32)
    label_col = jnp.transpose(jnp.broadcast_to(label_row, (128, count)))[:, 0:1]
    tokens = tokens_ref[...]
    lane = lax.broadcasted_iota(jnp.int32, (count, 128), 1)
    total[...] = jnp.broadcast_to(vec_out[2:3], (count, D))

    def attn_turn(block):
        at = lax.rem(block, 2)

        @pl.when(block < nf - 1)
        def _():
            for index in range(2):
                attn_load(index, block + 1, 1 - at).start(priority=1)

        attn_load(0, block, at).wait()
        attn_load(1, block, at).wait()
        weights = [flat(three_weight[at, :, index * rows : (index + 1) * rows]) for index in range(3)]
        queries = (product(tokens, weights[0]) + bias[block, 0:1]).astype(jnp.bfloat16)
        keys_all = product(tokens, weights[1]).astype(jnp.bfloat16)
        values_all = (product(tokens, weights[2]) + bias[block, 1:2]).astype(jnp.bfloat16)
        for index, values in enumerate((queries, keys_all, values_all)):
            blocks[block, index] = values
        pltpu.make_async_copy(blocks.at[block], blocks_out.at[block], store_sem.at[block]).start(priority=1)
        allowed = label_col == label_row
        totals = jnp.zeros((count, 128), jnp.float32)
        mixture = jnp.zeros((count, width_attn), jnp.float32)
        for head in range(width_attn // HDIM):
            scores = contract_cols(head_lanes(queries, head) * score_scale, keys_all)
            scores = jnp.where(allowed, scores, -1e30)
            top = jnp.max(scores, axis=1, keepdims=True)
            exponent = jnp.exp(scores - top)
            weight = jnp.sum(exponent, axis=1, keepdims=True)
            attention = (exponent * (1.0 / weight)).astype(jnp.bfloat16)
            totals = jnp.where(lane == head, top + jnp.log(weight), totals)
            mixture += product(attention, head_lanes(values_all, head))
        mixture = mixture.astype(jnp.bfloat16)
        parts[block] = mixture
        total_out[block] = jnp.transpose(totals)[:8]
        for index in range(nf):
            side_at = slice(index * width_attn, (index + 1) * width_attn)
            total[:, side_at] += product(mixture, flat(out_weight[at, index]))

        @pl.when(block == 0)
        def _():
            from_z(2)
            turned_z(1)

        @pl.when(block == nf - 2)
        def _():
            from_first(1)
            turned_z(2)

    loop(nf, attn_turn)

    def first_norm(index):
        at = pl.ds(pl.multiple_of(index * NORM_ROWS, NORM_ROWS), NORM_ROWS)
        scaled, inverse = normalize(tokens_ref[at].astype(jnp.float32) + total[at])
        scaled_out[at] = scaled
        inverse_out[at] = inverse
        normed = scaled * vec_out[3:4] + vec_out[4:5]
        low_out[at] = normed.astype(jnp.bfloat16)
        total[at] = normed + vec_out[9:10]

    loop(count // NORM_ROWS, first_norm)
    for index in range(nf):
        mixture_out[:, index * width_attn : (index + 1) * width_attn] = parts[index]

    def ffn_load(chunk, step, at):
        block, part = lax.div(step, per), lax.rem(step, per)
        left = pl.multiple_of(part * width, width)
        return load(5 + at, wholes[chunk].at[block, :, :, pl.ds(left, width)], ffn_weight.at[at])

    def ffn_steps(chunk, body, between, first=0, stride=1):
        ffn_load(chunk, first, 0).start(priority=1)
        count_steps = FF // width // stride

        def each(index):
            at, step = lax.rem(index, 2), first + index * stride

            @pl.when(index < count_steps - 1)
            def _():
                ffn_load(chunk, step + stride, 1 - at).start(priority=1)

            ffn_load(chunk, step, at).wait()
            body(step, at)
            between(step)

        loop(count_steps, each)

    def keep(step):
        column = pl.ds(pl.multiple_of(step * width, width), width)
        return (
            pltpu.make_async_copy(active.at[step], active_out.at[:, column], store_sem.at[nf]),
            pltpu.make_async_copy(slope.at[lax.rem(step, 2)], slope_out.at[:, column], store_sem.at[nf + 1]),
        )

    def up_step(step, at):
        up_proj = product(low_out[...], flat(ffn_weight[at])) + bias_up[step]
        half = 0.5 * (1.0 + lax.erf(up_proj * ROOT_HALF))

        @pl.when(step > 0)
        def _():
            for copy in keep(step - 1):
                copy.wait()

        active[step] = (up_proj * half).astype(jnp.bfloat16)
        slope[lax.rem(step, 2)] = (half + up_proj * (BELL * jnp.exp(-0.5 * up_proj * up_proj))).astype(
            jnp.bfloat16
        )
        for copy in keep(step):
            copy.start(priority=1)

    def down_step(step, at):
        total[...] += contract_cols(active[step], flat(ffn_weight[at]))

    def between_up(step):
        @pl.when(step == 0)
        def _():
            for far in range(3, nz):
                turned_z(far)

        @pl.when(step == FF // width // 2)
        def _():
            from_first(2)

    from_second(1)
    from_pair(1)
    ffn_steps(1, up_step, between_up)
    for copy in keep(FF // width - 1):
        copy.wait()
    from_second(2)
    from_pair(turned)
    ffn_steps(2, down_step, lambda step: None, 1, 2)
    from_pair(2)
    ffn_steps(2, down_step, lambda step: None, 0, 2)
    sums_out[...] = jnp.zeros((8, D), jnp.float32)

    def second_norm(index):
        at = pl.ds(pl.multiple_of(index * NORM_ROWS, NORM_ROWS), NORM_ROWS)
        scaled, inverse = normalize(total[at])
        layer_out[at] = (scaled * vec_out[10:11] + vec_out[11:12]).astype(jnp.bfloat16)
        grad = cotangent_ref[at].astype(jnp.float32)
        d_second = normalize_back(grad * vec_out[10:11], scaled, inverse)
        d_second_out[at] = d_second
        sums_out[0:1] += row_sum(d_second.astype(jnp.bfloat16))
        sums_out[1:2] += row_sum(grad * scaled)
        sums_out[2:3] += row_sum(grad)

    loop(count // NORM_ROWS, second_norm)

    def stored(block):
        pltpu.make_async_copy(blocks.at[block], blocks_out.at[block], store_sem.at[block]).wait()

    loop(nf, stored)
    for chunk in range(chunks):
        def finish(z_at):
            def sent():
                for step in range(1, side):
                    first_copy(chunk, z_at, step, False).wait_send()
                    for line in range(side):
                        second_copy(chunk, fs, z_at, step, False, line).wait_send()

            if chunk == turned:
                pl.when(z_at == z)(sent)
            else:
                sent()
                along_z(chunk, fs, z_at, False, lambda copy: copy.wait_send())

            def each(plane_at):
                pair_copy(chunk, plane_at, z_at, False).wait_send()
                if chunk == turned:
                    along_z(chunk, plane_at, z_at, False, lambda copy: copy.wait_send())

            loop(nf, each)

        loop(nz, finish)


def forward(ndp, nf, tokens, segments, cotangent, attn_w, ffn_w, vectors):
    nz, side, chunks = ndp // 2, math.isqrt(nf), 4
    count = tokens.shape[0]
    rows, width_attn = attn_w.shape[1:]
    width_ffn = ffn_w.shape[2]
    width = width_ffn // 2
    bf16, f32 = jnp.bfloat16, jnp.float32
    dma = pltpu.SemaphoreType.DMA
    anywhere, inside = pl.BlockSpec(memory_space=pl.ANY), pl.BlockSpec(memory_space=pltpu.VMEM)
    shape = jax.ShapeDtypeStruct
    return pl.pallas_call(
        functools.partial(forward_kernel, ndp, nf),
        name="forward",
        out_shape=[
            shape((nf, ndp, 4 * rows + 16, width_attn), bf16),
            shape((nf, ndp, rows, width_ffn), bf16),
            shape((nf, ndp, rows, width_ffn), bf16),
            shape((nf, 3, count, width_attn), bf16),
            shape((count, FF), bf16),
            shape((count, FF), bf16),
            shape((16, D), f32),
            shape((count, D), bf16),
            shape((nf, 8, count), f32),
            shape((count, D), f32),
            shape((count, 1), f32),
            shape((count, D), bf16),
            shape((count, D), bf16),
            shape((count, D), f32),
            shape((8, D), f32),
        ],
        in_specs=[inside] * 6,
        out_specs=[anywhere] * 6 + [inside] * 9,
        scratch_shapes=[
            pltpu.VMEM((4 * rows + 16, width_attn), bf16),
            pltpu.VMEM((rows, width_ffn), bf16),
            pltpu.VMEM((rows, width_ffn), bf16),
            pltpu.VMEM((2, ndp, 3 * rows, width_attn), bf16),
            pltpu.VMEM((2, nf, ndp // nf, rows, width_attn), bf16),
            pltpu.VMEM((2, ndp, rows, width), bf16),
            pltpu.VMEM((nf, ndp, 16, width_attn), bf16),
            pltpu.VMEM((nf, 8, width_attn), f32),
            pltpu.VMEM((FF // width, 1, width), f32),
            pltpu.VMEM((nf, 3, count, width_attn), bf16),
            pltpu.VMEM((nf, count, width_attn), bf16),
            pltpu.VMEM((FF // width, count, width), bf16),
            pltpu.VMEM((2, count, width), bf16),
            pltpu.VMEM((count, D), f32),
            dma((chunks,)),
            dma((chunks, nf, nz)),
            dma((chunks, nf, nz)),
            dma((chunks, nf, nz, 2)),
            dma((chunks, nz, side - 1)),
            dma((chunks, nz, side, side - 1)),
            dma((chunks, nf, nz)),
            dma((7,)),
            dma((nf + 2,)),
        ],
        compiler_params=pltpu.CompilerParams(
            collective_id=2, has_side_effects=True, vmem_limit_bytes=60 * 1024 * 1024
        ),
    )(tokens, segments[None, :], cotangent, attn_w, ffn_w, vectors)


def backward_kernel(
    ndp,
    nf,
    d_second_ref,
    low_ref,
    scaled_ref,
    inverse_ref,
    vec_ref,
    active_ref,
    slope_ref,
    up_ref,
    down_ref,
    tokens_ref,
    label_ref,
    blocks_ref,
    mixture_ref,
    total_ref,
    attn_ref,
    tail_ref,
    attn_mom,
    ffn_mom,
    input_grad,
    up_out,
    down_out,
    attn_out,
    vec_out,
    attn_low,
    ffn_low,
    ffn_whole,
    held_up,
    held_down,
    held_attn,
    first_up,
    first_down,
    first_attn,
    second_up,
    second_down,
    second_attn,
    z_up,
    z_down,
    z_attn,
    first_turned,
    second_turned,
    z_turned,
    stages_out,
    land,
    ffn_weight,
    ffn_act,
    attn_weight,
    attn_block,
    wide_low,
    wide_two,
    turned_one,
    turned_two,
    branch,
    bias_up_sum,
    query_sum,
    value_sum,
    vec_land,
    load_sem,
    step_sem,
    pair_send,
    pair_recv,
    first_send,
    first_recv,
    second_send,
    second_recv,
    z_send,
    z_recv,
    vec_send,
    vec_recv,
    piece_own,
    piece_send,
    piece_recv,
    piece_first,
    piece_second,
    piece_plane,
    turned_send,
    turned_recv,
):
    z, core, y, x, nz, side = place(ndp, nf)
    dp, fs = z * 2 + core, y * side + x
    other = (z * 2 + 1 - core, fs)
    chunks, turned = 3, 3
    rows, width_ffn = held_up.shape[2:]
    half_width = width_ffn // 2
    held, outs = (held_up, held_down, held_attn), (up_out, down_out, attn_out)
    from_first = (first_up, first_down, first_attn, first_turned)
    from_second = (second_up, second_down, second_attn, second_turned)
    from_z = (z_up, z_down, z_attn)
    width_attn = held_attn.shape[-1]
    width = ffn_weight.shape[-1]
    per = width_ffn // width
    greet(all_partners(ndp, nf))

    def place_of(turn):
        step = nf - 1 - turn
        return lax.rem(y + lax.div(step, side), side) * side + lax.rem(x + lax.rem(step, side), side)

    def sums(chunk, z_at, plane_at):
        if chunk == 1:
            return held_down.at[z_at, plane_at, :, pl.ds(0, half_width)]
        if chunk == turned:
            return held_down.at[z_at, plane_at, :, pl.ds(half_width, half_width)]
        return held[chunk].at[z_at, plane_at]

    def add(target, source):
        target[...] = target[...] + source[...]

    def first_land(chunk, z_at, step, line):
        return from_first[chunk].at[0 if chunk == turned else z_at, step - 1, line]

    def second_land(chunk, z_at, step):
        return from_second[chunk].at[0 if chunk == turned else z_at, step - 1]

    def first_copy(chunk, z_at, line, step):
        x_first = lax.rem(z_at, 2) == 0
        near, far = lax.rem(x + step, side), lax.rem(y + step, side)
        to = jnp.where(x_first, y * side + near, far * side + x)
        at = jnp.where(
            x_first,
            lax.rem(y + line, side) * side + near,
            far * side + lax.rem(x + line, side),
        )
        return remote(
            sums(chunk, z_at, at),
            first_land(chunk, z_at, step, line),
            first_send.at[chunk, z_at, step - 1, line],
            first_recv.at[chunk, z_at, step - 1, line],
            (dp, to),
        )

    lag = 1
    total_steps = nf * per + nf
    schedule = {}
    for sent, base, stride in (((0, 1), 0, per), ((2,), nf * per, 1)):
        for turns in ((0,), tuple(range(1, nf - 1))):
            ready = min(base + (turns[-1] + 1) * stride - 1 + lag, total_steps)
            for z_at in range(0, nz, 2):
                schedule.setdefault(ready, []).extend((chunk, turns, z_at) for chunk in sent)

    def send_first(chunk, turns, z_from, z_count=2):
        def each(z_at):
            x_first = lax.rem(z_at, 2) == 0
            for turn in turns:
                step_x, step_y = (nf - 1 - turn) % side, (nf - 1 - turn) // side
                step = jnp.where(x_first, step_x, step_y)
                line = jnp.where(x_first, step_y, step_x)

                @pl.when(step > 0)
                def _(line=line, step=step):
                    first_copy(chunk, z_at, line, step).start()

        loop(z_from + z_count, each, z_from)

    def sends_at(step, steps):
        for when in steps:
            @pl.when(step == when)
            def _(when=when):
                for chunk, turns, z_at in schedule.get(when, ()):
                    send_first(chunk, turns, z_at)

    def line_place(z_at, line):
        x_first = lax.rem(z_at, 2) == 0
        return jnp.where(
            x_first, lax.rem(y + line, side) * side + x, y * side + lax.rem(x + line, side)
        )

    def second_copy(chunk, z_at, step):
        to = line_place(z_at, step)
        return remote(
            sums(chunk, z_at, to),
            second_land(chunk, z_at, step),
            second_send.at[chunk, z_at, step - 1],
            second_recv.at[chunk, z_at, step - 1],
            (dp, to),
        )

    def z_copy(chunk, step):
        z_at = lax.rem(z + step, nz)
        return remote(
            sums(chunk, z_at, fs),
            from_z[chunk].at[step - 1],
            z_send.at[chunk, step - 1],
            z_recv.at[chunk, step - 1],
            (z_at * 2 + core, fs),
        )

    def take_first(chunk, lines):
        def each(hop):
            z_at = lax.rem(z + 1 + hop, nz)
            for line in lines:
                at = line_place(z_at, line)
                for step in range(1, side):
                    first_copy(chunk, z_at, line, step).wait_recv()
                    add(sums(chunk, z_at, at), first_land(chunk, z_at, step, line))
                if line:
                    second_copy(chunk, z_at, line).start()

        if chunk == turned:
            each(nz - 1)
        else:
            loop(nz, each)

    def turned_copy(plane_at, step):
        z_at = lax.rem(z + step, nz)
        return remote(
            sums(turned, z_at, plane_at),
            z_turned.at[step - 1, plane_at],
            turned_send.at[step - 1, plane_at],
            turned_recv.at[step - 1, plane_at],
            (z_at * 2 + core, fs),
        )

    def turned_start(turns):
        for turn in turns:
            for step in range(1, nz):
                turned_copy(place_of(turn), step).start()

    def turned_take(turns):
        for turn in turns:
            plane_at = place_of(turn)
            for step in range(1, nz):
                turned_copy(plane_at, step).wait_recv()
                add(sums(turned, z, plane_at), z_turned.at[step - 1, plane_at])
        send_first(turned, turns, z, 1)

    def take_second(chunk):
        def each(hop):
            z_at = lax.rem(z + 1 + hop, nz)
            for step in range(1, side):
                second_copy(chunk, z_at, step).wait_recv()
                add(sums(chunk, z_at, fs), second_land(chunk, z_at, step))

            @pl.when(hop < nz - 1)
            def _():
                z_copy(chunk, hop + 1).start()

        loop(nz, each)

    def moments(chunk):
        source = ffn_mom.at[chunk] if chunk < 2 else attn_mom
        return pltpu.make_async_copy(source, outs[chunk], load_sem.at[3 + chunk])

    def take_z(chunk):
        moments(chunk).wait()
        total = sums(chunk, z, fs)[...].astype(jnp.float32)
        for step in range(1, nz):
            z_copy(chunk, step).wait_recv()
            total += from_z[chunk][step - 1].astype(jnp.float32)
        if chunk == 0:
            low = (matrix_decay * up_out[...] + total).astype(jnp.bfloat16)
            up_out[...] = total
            ffn_low[0, 0] = low[:, :half_width]
            ffn_low[0, 1] = low[:, half_width:]
        elif chunk == 1:
            for step in range(1, side):
                second_copy(turned, z, step).wait_recv()
                add(sums(turned, z, fs), second_land(turned, z, step))
            for index, value in enumerate((total, sums(turned, z, fs)[...].astype(jnp.float32))):
                at = slice(index * half_width, (index + 1) * half_width)
                ffn_low[1, index] = (matrix_decay * down_out[:, at] + value).astype(jnp.bfloat16)
                down_out[:, at] = value
        else:
            attn_low[...] = (matrix_decay * attn_out[...] + total).astype(jnp.bfloat16)
            attn_out[...] = total

    vec_rounds = [[other]]
    vec_rounds.append([(dp, y * side + lax.rem(x + step, side)) for step in range(1, side)])
    vec_rounds.append([(dp, lax.rem(y + step, side) * side + x) for step in range(1, side)])
    vec_rounds.append([(lax.rem(z + step, nz) * 2 + core, fs) for step in range(1, nz)])
    starts = [sum(len(group) for group in vec_rounds[:index]) for index in range(4)]

    def vec_copy(index, step):
        at = starts[index] + step
        return remote(
            vec_land.at[index], vec_land.at[4 + at], vec_send.at[at], vec_recv.at[at], vec_rounds[index][step]
        )

    def vec_start(index):
        for step in range(len(vec_rounds[index])):
            vec_copy(index, step).start()

    def vec_take(index):
        total = vec_land[index]
        for step in range(len(vec_rounds[index])):
            vec_copy(index, step).wait_recv()
            total += vec_land[4 + starts[index] + step]
        if index < 3:
            vec_land[index + 1] = total
            vec_start(index + 1)
        else:
            vec_out[...] = total

    def split(values, keep, give):
        parts = values.astype(jnp.bfloat16).reshape(nz, 2, rows, values.shape[1])
        for which in range(2):
            @pl.when(core == which)
            def _(which=which):
                keep(parts[:, which])
                give(parts[:, 1 - which])

    def piece_copy(matrix, half):
        return remote(
            ffn_low.at[matrix, half],
            ffn_whole.at[fs, dp],
            piece_send.at[2 * matrix + half],
            piece_recv.at[dp],
            (2 + 2 * matrix + half, fs),
        )

    def piece_local(matrix, half):
        return pltpu.make_async_copy(ffn_low.at[matrix, half], ffn_whole.at[fs, dp], piece_own)

    def start_pieces(matrix):
        for half in range(2):
            @pl.when(dp != 2 + 2 * matrix + half)
            def _(half=half):
                piece_copy(matrix, half).start()

            @pl.when(dp == 2 + 2 * matrix + half)
            def _(half=half):
                piece_local(matrix, half).start(priority=1)

    crossing = Crossing(
        ndp, nf, ffn_whole, piece_own, piece_recv, piece_first, piece_second, piece_plane, ffn_low.at[0, 0]
    )
    runs_ffn = jnp.logical_and(dp >= 2, dp < 6)

    def ffn_loads(slot, turn, part):
        block = place_of(turn)
        at = pl.ds(part * width, width)
        column = pl.ds(pl.multiple_of(block * width_ffn + part * width, width), width)
        pairs = (
            (up_ref.at[block, :, :, at], ffn_weight.at[slot, 0]),
            (down_ref.at[block, :, :, at], ffn_weight.at[slot, 1]),
            (active_ref.at[:, column], ffn_act.at[slot, 0]),
            (slope_ref.at[:, column], ffn_act.at[slot, 1]),
        )
        return [
            pltpu.make_async_copy(source, target, step_sem.at[slot, index])
            for index, (source, target) in enumerate(pairs)
        ]

    def load(index, source, target):
        return pltpu.make_async_copy(source, target, load_sem.at[index])

    load(0, low_ref, wide_low).start(priority=1)
    load(1, d_second_ref, input_grad).start(priority=1)
    for copy in ffn_loads(0, 0, 0):
        copy.start(priority=1)
    load(2, tokens_ref, wide_two).start(priority=1)
    for chunk in range(chunks):
        moments(chunk).start(priority=1)
    load(0, low_ref, wide_low).wait()
    turned_one[...] = jnp.transpose(wide_low[...])
    load(1, d_second_ref, input_grad).wait()
    wide_low[...] = input_grad[...].astype(jnp.bfloat16)
    turned_two[...] = jnp.transpose(wide_low[...])

    def pair_copy(step):
        stage, slot = lax.rem(step, lag), lax.rem(step, 2 * lag)
        return remote(stages_out.at[stage], land.at[slot], pair_send.at[stage], pair_recv.at[slot], other)

    def pair_take(step):
        pair_copy(step).wait()
        slot = lax.rem(step, 2 * lag)

        @pl.when(step < nf * per)
        def _():
            block, part = place_of(lax.div(step, per)), lax.rem(step, per)
            for index in range(2):
                for which in range(per):
                    @pl.when(part == which)
                    def _(index=index, which=which):
                        for half in range(2):
                            left = which * width + half * width_attn
                            at = slice(left, left + width_attn)
                            held[index][:, block, :, at] += land[slot, :, 2 * index + half]

        @pl.when(step >= nf * per)
        def _():
            held_attn[:, place_of(step - nf * per)] += land[slot]

    def ffn_turn(turn):
        block = place_of(turn)
        for part in range(per):
            now = turn * per + part
            slot = lax.rem(now, 2)
            if part < per - 1:
                for copy in ffn_loads(1 - slot, turn, part + 1):
                    copy.start(priority=1)
            else:
                @pl.when(turn < nf - 1)
                def _():
                    for copy in ffn_loads(1 - slot, turn + 1, 0):
                        copy.start(priority=1)

            for copy in ffn_loads(slot, turn, part):
                copy.wait()
            d_active = product(wide_low[...], flat(ffn_weight[slot, 1]))
            d_up = (d_active * ffn_act[slot, 1].astype(jnp.float32)).astype(jnp.bfloat16)
            bias_up_sum[block * per + part] = row_sum(d_up)
            input_grad[...] += contract_cols(d_up, flat(ffn_weight[slot, 0]))

            @pl.when(now >= lag)
            def _():
                pair_take(now - lag)

            sends_at(now, range(nf * per))

            @pl.when(now == per - 1 + lag)
            def _():
                turned_start((0,))

            @pl.when(now == (nf - 1) * per - 1 + lag)
            def _():
                turned_start(range(1, nf - 1))
            at = slice(part * width, (part + 1) * width)
            for index in range(2):

                def keep(values, index=index):
                    held[index][:, block, :, at] = values

                def give(values, index=index):
                    for half in range(2):
                        side_at = slice(half * width_attn, (half + 1) * width_attn)
                        stages_out[lax.rem(now, lag), :, 2 * index + half] = values[:, :, side_at]

                if index == 0:
                    split(product(turned_one[...], d_up), keep, give)
                else:
                    split(product(turned_two[...], ffn_act[slot, 0]), keep, give)
            pair_copy(now).start()

    loop(nf, ffn_turn)

    load(2, tokens_ref, wide_two).wait()
    turned_one[...] = jnp.transpose(wide_two[...])
    load(0, mixture_ref, wide_two).start(priority=1)

    def attn_load(index, turn):
        block = place_of(turn)
        per_block = ndp // nf
        source, target = (
            (attn_ref.at[block, :, pl.ds(0, 3 * rows)], attn_weight[0]),
            (
                attn_ref.at[:, pl.ds(block * per_block, per_block), pl.ds(3 * rows, rows)],
                attn_weight[1],
            ),
            (blocks_ref.at[block], attn_block),
        )[index]
        return pltpu.make_async_copy(source, target, step_sem.at[0, index])

    for index in range(3):
        attn_load(index, 0).start(priority=1)
    vec_land[0] = jnp.zeros((16, D), jnp.float32)
    vec_land[0, 9:12] = tail_ref[0:3]

    def norm_back(index):
        at = pl.ds(pl.multiple_of(index * NORM_ROWS, NORM_ROWS), NORM_ROWS)
        grad = input_grad[at]
        scaled = scaled_ref[at]
        d_first = normalize_back(grad * vec_ref[3:4], scaled, inverse_ref[at])
        input_grad[at] = d_first
        low = d_first.astype(jnp.bfloat16)
        vec_land[0, 2:3] += row_sum(low)
        vec_land[0, 3:4] += row_sum(grad * scaled)
        vec_land[0, 4:5] += row_sum(grad)
        for column in range(nf):
            branch[column, at] = low[:, column * width_attn : (column + 1) * width_attn]

    loop(tokens_ref.shape[0] // NORM_ROWS, norm_back)
    label_row = label_ref[...].astype(jnp.float32)
    label_col = jnp.transpose(jnp.broadcast_to(label_row, (128, label_row.shape[1])))[:, 0:1]
    load(0, mixture_ref, wide_two).wait()
    turned_two[...] = jnp.transpose(wide_two[...])

    def attn_turn(turn):
        block = place_of(turn)
        now = nf * per + turn

        def load_next(index):
            @pl.when(turn < nf - 1)
            def _():
                attn_load(index, turn + 1).start(priority=1)

        for index in range(3):
            attn_load(index, turn).wait()
        count = tokens_ref.shape[0]
        zero = jnp.zeros((count, width_attn), jnp.float32)
        d_mixture = zero
        for index in range(nf):
            d_mixture += contract_cols(branch[index], flat(attn_weight[1][index]))
        load_next(1)
        d_mixture = d_mixture.astype(jnp.bfloat16)
        queries, keys_all, values_all = (attn_block[index] for index in range(3))
        allowed = label_col == label_row
        d_queries, d_keys, d_values = zero, zero, zero
        for head in range(width_attn // HDIM):
            my_queries = head_lanes(queries, head) * score_scale
            my_mixture = head_lanes(d_mixture, head)
            scores = contract_cols(keys_all, my_queries) - total_ref[block, head : head + 1, :]
            attention = jnp.where(allowed, jnp.exp(scores), 0.0)
            d_attention = contract_cols(values_all, my_mixture)
            inner = jnp.sum(d_attention * attention, axis=0, keepdims=True)
            d_scores = (attention * (d_attention - inner)).astype(jnp.bfloat16)
            d_keys += product(d_scores, my_queries)
            d_values += product(attention.astype(jnp.bfloat16), my_mixture)
            d_queries += contract_rows(d_scores, head_lanes(keys_all, head) * score_scale)
        load_next(2)
        grads = [values.astype(jnp.bfloat16) for values in (d_queries, d_keys, d_values)]
        query_sum[block] = row_sum(grads[0])
        value_sum[block] = row_sum(grads[2])
        moved = jnp.zeros((count, D), jnp.float32)
        for index in range(3):
            weight = attn_weight[0][:, index * rows : (index + 1) * rows]
            moved += contract_cols(grads[index], flat(weight))
        input_grad[...] += moved
        load_next(0)

        pair_take(now - lag)
        for index in range(4):
            flipped, grad = (turned_one, grads[index]) if index < 3 else (turned_two, branch[block])

            def keep(values, index=index):
                held_attn[:, block, index] = values

            def give(values, index=index):
                stages_out[lax.rem(now, lag), :, index] = values

            split(product(flipped[...], grad), keep, give)
        pair_copy(now).start()
        sends_at(now, range(nf * per, total_steps))

        @pl.when(turn == lag - 1)
        def _():
            turned_start((nf - 1,))

        @pl.when(turn == nf - 4)
        def _():
            turned_take((0,))
            take_first(0, range(1, side))
            take_first(1, range(1, side))

        @pl.when(turn == nf - 3)
        def _():
            turned_take(range(1, nf - 1))
            take_first(0, (0,))
            take_first(1, (0,))

        @pl.when(turn == nf - 2)
        def _():
            take_first(turned, range(1, side))

        @pl.when(turn == nf - 1)
        def _():
            turned_take((nf - 1,))
            take_first(turned, (0,))

        @pl.when(turn == nf - 2)
        def _():
            take_second(0)
            take_second(1)

    loop(nf, attn_turn)
    for index in range(nf):
        at = slice(index * width_attn, (index + 1) * width_attn)
        vec_land[0, 0:1, at] = query_sum[index]
        vec_land[0, 1:2, at] = value_sum[index]
    for index in range(nf * per):
        left = index * width
        vec_land[0, 5 + left // D : 6 + left // D, left % D : left % D + width] = bias_up_sum[index]
    vec_start(0)
    for step in range(total_steps - lag, total_steps):
        pair_take(step)
    sends_at(total_steps, (total_steps,))

    take_first(2, range(1, side))
    take_z(0)
    start_pieces(0)
    take_z(1)
    start_pieces(1)
    vec_take(0)
    take_first(2, (0,))
    take_second(2)
    vec_take(1)

    @pl.when(runs_ffn)
    def _():
        crossing.take()

    vec_take(2)
    take_z(2)
    vec_take(3)

    @pl.when(runs_ffn)
    def _():
        crossing.pass_on()
        crossing.near()
        crossing.far()
        crossing.finish()

    for matrix in range(2):
        for half in range(2):
            @pl.when(dp != 2 + 2 * matrix + half)
            def _(matrix=matrix, half=half):
                piece_copy(matrix, half).wait_send()

    def turned_sent(plane_at):
        for step in range(1, nz):
            turned_copy(plane_at, step).wait_send()

    loop(nf, turned_sent)
    for step in range(1, side):
        second_copy(turned, z, step).wait_send()
        for line in range(side):
            first_copy(turned, z, line, step).wait_send()
    for chunk in range(chunks):

        def finish(z_at):
            for step in range(1, side):
                second_copy(chunk, z_at, step).wait_send()
                for line in range(side):
                    first_copy(chunk, z_at, line, step).wait_send()

        loop(nz, finish)
        for step in range(1, nz):
            z_copy(chunk, step).wait_send()
    for index in range(4):
        for step in range(len(vec_rounds[index])):
            vec_copy(index, step).wait_send()


def backward_kernel_entry(ndp, nf, *refs):
    at = 18 + 8 + 15 + 2 + 2
    backward_kernel(ndp, nf, *refs[:at], refs[at : at + 2], *refs[at + 2 :])


def backward(
    ndp, nf, d_second, low, scaled, inverse, vectors, active, slope, up_all, down_all,
    tokens, segments, blocks, mixture, totals, attn_all, tail_sums, attn_mom, ffn_mom,
):
    nz, side = ndp // 2, math.isqrt(nf)
    count = tokens.shape[0]
    rows, width_ffn = up_all.shape[2:]
    width_attn = attn_all.shape[-1]
    width = 2 * width_attn
    bf16, f32 = jnp.bfloat16, jnp.float32
    dma = pltpu.SemaphoreType.DMA
    anywhere, inside = pl.BlockSpec(memory_space=pl.ANY), pl.BlockSpec(memory_space=pltpu.VMEM)
    shapes = [(rows, width_ffn), (rows, width_ffn), (4, rows, width_attn)]
    vec_copies = 1 + 2 * (side - 1) + nz - 1
    half = (rows, width_ffn // 2)
    sums = [pltpu.VMEM((nz, nf) + shape, bf16) for shape in shapes]
    for lead in ((nz, side - 1, side), (nz, side - 1), (nz - 1,)):
        sums += [pltpu.VMEM(lead + shape, bf16) for shape in (shapes[0], half, shapes[2])]
    sums += [pltpu.VMEM(lead + half, bf16) for lead in ((1, side - 1, side), (1, side - 1), (nz - 1, nf))]
    return pl.pallas_call(
        functools.partial(backward_kernel_entry, ndp, nf),
        name="backward",
        out_shape=[jax.ShapeDtypeStruct((count, D), f32)]
        + [jax.ShapeDtypeStruct(shape, f32) for shape in shapes]
        + [
            jax.ShapeDtypeStruct((16, D), f32),
            jax.ShapeDtypeStruct(attn_mom.shape, bf16),
            jax.ShapeDtypeStruct((2, 2, rows, width_ffn // 2), bf16),
            jax.ShapeDtypeStruct((nf, ndp, rows, width_ffn // 2), bf16),
        ],
        in_specs=[
            anywhere,
            anywhere,
            inside,
            inside,
            inside,
            anywhere,
            anywhere,
            anywhere,
            anywhere,
            anywhere,
            inside,
            anywhere,
            anywhere,
            inside,
            anywhere,
            inside,
            anywhere,
            anywhere,
        ],
        out_specs=[inside] * 7 + [anywhere],
        scratch_shapes=sums
        + [
            pltpu.VMEM((1, nz, 4, rows, width_attn), bf16),
            pltpu.VMEM((2, nz, 4, rows, width_attn), bf16),
            pltpu.VMEM((2, 2, ndp, rows, width), bf16),
            pltpu.VMEM((2, 2, count, width), bf16),
            pltpu.VMEM((ndp, 3 * rows, width_attn), bf16),
            pltpu.VMEM((nf, ndp // nf, rows, width_attn), bf16),
            pltpu.VMEM((3, count, width_attn), bf16),
            pltpu.VMEM((count, D), bf16),
            pltpu.VMEM((count, D), bf16),
            pltpu.VMEM((D, count), bf16),
            pltpu.VMEM((D, count), bf16),
            pltpu.VMEM((nf, count, width_attn), bf16),
            pltpu.VMEM((FF // width, 1, width), f32),
            pltpu.VMEM((nf, 1, width_attn), f32),
            pltpu.VMEM((nf, 1, width_attn), f32),
            pltpu.VMEM((4 + vec_copies, 16, D), f32),
            dma((6,)),
            dma((2, 4)),
            dma((1,)),
            dma((2,)),
            dma((4, nz, side - 1, side)),
            dma((4, nz, side - 1, side)),
            dma((4, nz, side - 1)),
            dma((4, nz, side - 1)),
            dma((3, nz - 1)),
            dma((3, nz - 1)),
            dma((vec_copies,)),
            dma((vec_copies,)),
            dma,
            dma((4,)),
            dma((ndp,)),
            dma((ndp, side - 1)),
            dma((ndp, side, side - 1)),
            dma((nf, ndp)),
            dma((nz - 1, nf)),
            dma((nz - 1, nf)),
        ],
        compiler_params=pltpu.CompilerParams(
            collective_id=3, has_side_effects=True, vmem_limit_bytes=63 * 1024 * 1024
        ),
    )(
        d_second, low, scaled, inverse, vectors, active, slope, up_all, down_all,
        tokens, segments[None, :], blocks, mixture, totals, attn_all, tail_sums, attn_mom, ffn_mom,
    )


def on_device(
    tokens,
    segments,
    cotangent,
    attn_w,
    ffn_w,
    vectors,
    attn_mom,
    ffn_mom,
    vec_mom,
    attn_ema,
    ffn_ema,
    vec_ema,
):
    ndp, nf = lax.axis_size("dp"), lax.axis_size("fsdp")
    share = vectors.shape[1]
    (
        attn_all, up_all, down_all, blocks, active, slope, vec_full, mixture, totals, scaled, inverse, low,
        layer_out, d_second, tail_sums,
    ) = forward(ndp, nf, tokens, segments, cotangent, attn_w, ffn_w, vectors)
    input_grad, up_grad, down_grad, attn_grad, vec_sum, attn_piece, _, ffn_whole = backward(
        ndp, nf, d_second, low, scaled, inverse, vec_full, active, slope, up_all, down_all,
        tokens, segments, blocks, mixture, totals, attn_all, tail_sums, attn_mom, ffn_mom,
    )
    mine = (lax.axis_index("dp") * nf + lax.axis_index("fsdp")) * share
    vec_grad = lax.dynamic_slice(vec_sum, (0, mine), (12, share))
    attn_ortho, ffn_ortho = orthogonalize(ndp, nf, attn_piece, ffn_whole)
    total_tokens = tokens.shape[0] * ndp * nf
    updated = update_all(
        vector_step / math.sqrt(total_tokens),
        attn_w,
        ffn_w,
        vectors,
        attn_mom,
        ffn_mom,
        vec_mom,
        attn_ema,
        ffn_ema,
        vec_ema,
        attn_grad,
        up_grad,
        down_grad,
        vec_grad,
        attn_ortho,
        ffn_ortho,
    )
    return (layer_out, input_grad, *updated, vec_grad[2])


def solution(mesh):
    in_specs = (
        P(("dp", "fsdp"), None),
        P(("dp", "fsdp")),
        P(("dp", "fsdp"), None),
        P(None, "dp", "fsdp"),
        P(None, "dp", "fsdp"),
        P(None, ("dp", "fsdp")),
        P(None, "dp", "fsdp"),
        P(None, "dp", "fsdp"),
        P(None, ("dp", "fsdp")),
        P(None, "dp", "fsdp"),
        P(None, "dp", "fsdp"),
        P(None, ("dp", "fsdp")),
    )
    out_specs = (
        P(("dp", "fsdp"), None),
        P(("dp", "fsdp"), None),
        P(None, "dp", "fsdp"),
        P(None, "dp", "fsdp"),
        P(None, ("dp", "fsdp")),
        P(None, "dp", "fsdp"),
        P(None, "dp", "fsdp"),
        P(None, ("dp", "fsdp")),
        P(None, "dp", "fsdp"),
        P(None, "dp", "fsdp"),
        P(None, ("dp", "fsdp")),
        P(("dp", "fsdp")),
    )
    return jax.shard_map(
        on_device, mesh=mesh, in_specs=in_specs, out_specs=out_specs, check_vma=False
    )
```

```python
import functools
import math

import jax
import jax.numpy as jnp
from jax import lax
from jax.experimental import pallas as pl
from jax.experimental.pallas import tpu as pltpu
from jax.sharding import PartitionSpec as P

D = 1024
FF = 4096
HEADS = 16
HDIM = 64
TILE = 512
ITERS = 5


score_scale = 0.125
ln_epsilon = 1e-05
norm_epsilon = 1e-06
ns_linear = 3.4445
ns_square = -4.775
ns_cubic = 2.0315
matrix_decay = 0.95
vector_decay = 0.9
average_decay = 0.7
weight_decay = 0.01
attn_rates = (1.0, 1.0, 1.0, 10.0)
vector_step = 0.3


def product(left, right):
    return jnp.dot(left, right, preferred_element_type=jnp.float32)


def contract_rows(left, right):
    return lax.dot_general(
        left, right, (((0,), (0,)), ((), ())), preferred_element_type=jnp.float32
    )


def contract_cols(left, right):
    return lax.dot_general(
        left, right, (((1,), (1,)), ((), ())), preferred_element_type=jnp.float32
    )


MESH = pl.DeviceIdType.MESH
ROLES = 8
STEP_ROWS = 512
NORM_ROWS = 128
TILE_ROWS = 128


def greet(partners):
    barrier = pltpu.get_barrier_semaphore()
    for partner in partners:
        pl.semaphore_signal(barrier, inc=1, device_id=partner, device_id_type=MESH)
    pl.semaphore_wait(barrier, len(partners))


def place(ndp, nf):
    dp, fs = lax.axis_index("dp"), lax.axis_index("fsdp")
    side = math.isqrt(nf)
    return lax.div(dp, 2), lax.rem(dp, 2), lax.div(fs, side), lax.rem(fs, side), ndp // 2, side


def line_partners(ndp, nf):
    z, core, y, x, nz, side = place(ndp, nf)
    mine = y * side + x
    return (
        [(z * 2 + 1 - core, mine)]
        + [(lax.rem(z + step, nz) * 2 + core, mine) for step in range(1, nz)]
        + [(z * 2 + core, y * side + lax.rem(x + step, side)) for step in range(1, side)]
        + [(z * 2 + core, lax.rem(y + step, side) * side + x) for step in range(1, side)]
    )


def all_partners(ndp, nf):
    z, core, y, x, nz, side = place(ndp, nf)
    dp, fs = z * 2 + core, y * side + x
    return (
        [(lax.rem(dp + step, ndp), fs) for step in range(1, ndp)]
        + [(dp, y * side + lax.rem(x + step, side)) for step in range(1, side)]
        + [(dp, lax.rem(y + step, side) * side + x) for step in range(1, side)]
    )


def remote(source, target, send_sem, recv_sem, device):
    return pltpu.make_async_remote_copy(
        src_ref=source,
        dst_ref=target,
        send_sem=send_sem,
        recv_sem=recv_sem,
        device_id=device,
        device_id_type=MESH,
    )


def loop(count, body, start=0):
    def step(index, carry):
        body(index)
        return carry

    lax.fori_loop(start, count, step, 0)


class Crossing:
    def __init__(self, ndp, nf, land, own_sem, piece_recv, first_send, second_send, plane_recv, source):
        self.ndp, self.land, self.own_sem, self.piece_recv, self.source = ndp, land, own_sem, piece_recv, source
        self.first_send, self.second_send, self.plane_recv = first_send, second_send, plane_recv
        self.z, self.core, self.y, self.x, self.nz, self.side = place(ndp, nf)
        self.dp, self.fs = self.z * 2 + self.core, self.y * self.side + self.x

    def row_of(self, index):
        return lax.rem(self.z + index // 2, self.nz) * 2 + lax.rem(self.core + index, 2)

    def x_first(self, row):
        return lax.rem(row // 2, 2) == 0

    def along(self, first, step):
        x_at = jnp.where(first, lax.rem(self.x + step, self.side), self.x)
        y_at = jnp.where(first, self.y, lax.rem(self.y + step, self.side))
        return y_at * self.side + x_at

    def first_copy(self, row, step):
        here = self.land.at[self.fs, row]
        peer = self.along(self.x_first(row), step)
        sems = self.first_send.at[row, step - 1], self.plane_recv.at[self.fs, row]
        return remote(here, here, *sems, (self.dp, peer))

    def second_copy(self, plane_at, row, line, step):
        here = self.land.at[plane_at, row]
        peer = self.along(jnp.logical_not(self.x_first(row)), step)
        sems = self.second_send.at[row, line, step - 1], self.plane_recv.at[plane_at, row]
        return remote(here, here, *sems, (self.dp, peer))

    def arrived(self, plane_at, row):
        here = self.land.at[plane_at, row]
        remote(here, here, self.own_sem, self.plane_recv.at[plane_at, row], (self.dp, self.fs)).wait_recv()

    def take(self):
        def each(index):
            row = self.row_of(index)

            @pl.when(index == 0)
            def _():
                pltpu.make_async_copy(self.source, self.land.at[self.fs, row], self.own_sem).wait()

            @pl.when(index > 0)
            def _():
                here = self.land.at[self.fs, row]
                remote(self.source, here, self.own_sem, self.piece_recv.at[row], (self.dp, self.fs)).wait_recv()

            for step in range(1, self.side):
                self.first_copy(row, step).start()
                self.second_copy(self.fs, row, 0, step).start()

        loop(self.ndp, each)

    def pass_on(self):
        def each(index):
            row = self.row_of(index)
            for line in range(1, self.side):
                plane_at = self.along(self.x_first(row), line)
                self.arrived(plane_at, row)
                for step in range(1, self.side):
                    self.second_copy(plane_at, row, line, step).start()

        loop(self.ndp, each)

    def wait_line(self, line):
        for step in range(1, self.side):

            def each(index, step=step):
                row = self.row_of(index)
                x, y, side = self.x, self.y, self.side
                there = jnp.where(
                    self.x_first(row),
                    lax.rem(y + step, side) * side + lax.rem(x + line, side),
                    lax.rem(y + line, side) * side + lax.rem(x + step, side),
                )
                self.arrived(there, row)

            loop(self.ndp, each)

    def near(self):
        self.wait_line(0)

    def far(self):
        for line in range(1, self.side):
            self.wait_line(line)

    def finish(self):
        def each(row):
            for step in range(1, self.side):
                self.first_copy(row, step).wait_send()
                for line in range(self.side):
                    self.second_copy(self.fs, row, line, step).wait_send()

        loop(self.ndp, each)


def ortho_kernel(
    ndp,
    nf,
    attn_ref,
    ffn_whole,
    attn_out,
    ffn_out,
    land_attn,
    land_ffn,
    iter_low,
    iter_full,
    gram,
    gram_send,
    gram_recv,
    off_low,
    poly_low,
    diag_row,
    diag_col,
    inverse_norm,
    own_low,
    own_full,
    own_attn,
    own_ffn,
    own_sem,
    piece_send,
    piece_recv,
    first_send,
    second_send,
    plane_recv,
    gram_send_sem,
    gram_recv_sem,
    back_send,
    back_recv,
    load_sem,
):
    z, core, y, x, nz, side = place(ndp, nf)
    dp, fs = z * 2 + core, y * side + x
    rows = attn_ref.shape[1]
    size = rows * ndp
    is_attn = jnp.logical_or(dp < 2, jnp.logical_and(dp >= 6, dp < ROLES))
    is_ffn = jnp.logical_and(dp >= 2, dp < 6)
    partner = z * 2 + 1 - core

    greet(all_partners(ndp, nf))
    attn_roles = (0, 6, 1, 7)

    def piece(role):
        return attn_ref.at[role if role < 2 else role - 4]

    def piece_copy(role):
        return remote(piece(role), land_attn.at[fs, dp], piece_send.at[role], piece_recv.at[dp], (role, fs))

    for role in attn_roles:
        @pl.when(dp != role)
        def _(role=role):
            piece_copy(role).start()

        @pl.when(dp == role)
        def _(role=role):
            pltpu.make_async_copy(piece(role), land_attn.at[fs, dp], own_sem).start()

    def iterate(land, source, own_out, target, role, paired):
        width = land.shape[-1]
        columns = width * nf
        tall = min(STEP_ROWS, size)
        steps = size // tall
        wide = min(1024, columns)

        def add_gram(plane_at, fresh):
            block = land[plane_at].reshape(size, width)
            for step in range(steps):
                at = slice(step * tall, (step + 1) * tall)
                part = contract_cols(block[at], block)
                if fresh:
                    gram[at] = part
                else:
                    gram[at] += part

        if paired:

            def block_load(index):
                return pltpu.make_async_copy(ffn_whole.at[index], land.at[index], load_sem.at[index])

            for index in range(nf):
                block_load(index).start()
            for index in range(nf):
                block_load(index).wait()
                add_gram(index, index == 0)
        else:
            crossing = Crossing(ndp, nf, land, own_sem, piece_recv, first_send, second_send, plane_recv, source)
            crossing.take()
            add_gram(fs, True)
            crossing.pass_on()
            crossing.near()
            for step in range(1, side):
                add_gram(crossing.along(True, step), False)
                add_gram(crossing.along(False, step), False)
            crossing.far()
            for far_y in range(1, side):
                for far_x in range(1, side):
                    add_gram(lax.rem(y + far_y, side) * side + lax.rem(x + far_x, side), False)

        def gram_copy(slot, step):
            at = pl.ds(step * tall, tall)
            return remote(
                gram_send.at[slot, at],
                gram_recv.at[slot, at],
                gram_send_sem.at[slot, step],
                gram_recv_sem.at[slot, step],
                (partner, fs),
            )

        if paired:
            for step in range(steps):
                at = slice(step * tall, (step + 1) * tall)
                gram_send[0, at] = gram[at].astype(jnp.bfloat16)
                gram_copy(0, step).start()
        for index in range(nf):
            block = land[index].reshape(size, width)
            at = slice(index * width, (index + 1) * width)
            iter_low[0, :, at] = block
            iter_full[:, at] = block.astype(jnp.float32)

        def back_copy(row):
            return remote(own_out.at[row], target, back_send.at[row], back_recv.at[role], (row, fs))

        def iteration(count):
            now = lax.rem(count, 2)
            later = 1 - now

            @pl.when(count > 0)
            def _():
                def gram_rows(step):
                    at = pl.ds(pl.multiple_of(step * tall, tall), tall)
                    part = contract_cols(iter_low[now, at, :columns], iter_low[now, :, :columns])
                    if paired:
                        gram_send[now, at] = part.astype(jnp.bfloat16)
                        gram_copy(now, step).start()
                    else:
                        gram[at] = part

                loop(steps, gram_rows)

            eye = lax.broadcasted_iota(jnp.int32, (TILE_ROWS, TILE_ROWS), 0) == lax.broadcasted_iota(
                jnp.int32, (TILE_ROWS, TILE_ROWS), 1
            )

            @pl.when(count == 0)
            def _():
                trace = jnp.zeros((TILE_ROWS, TILE_ROWS), jnp.float32)
                if paired:
                    for step in range(steps):
                        gram_copy(now, step).wait()
                for tile in range(size // TILE_ROWS):
                    at = slice(tile * TILE_ROWS, (tile + 1) * TILE_ROWS)
                    if paired:
                        square = gram_send[now, at, at].astype(jnp.float32)
                        trace += square + gram_recv[now, at, at].astype(jnp.float32)
                    else:
                        trace += gram[at, at]
                trace = jnp.sum(jnp.where(eye, trace, 0.0), axis=1, keepdims=True)
                trace = jnp.sum(trace, axis=0, keepdims=True)
                inverse_norm[...] = 1.0 / (jnp.sqrt(trace) + norm_epsilon)

            @pl.when(count > 0)
            def _():
                inverse_norm[...] = jnp.ones_like(inverse_norm)

            inverse = inverse_norm[...]
            shrink = inverse * inverse

            for step in range(steps):
                if paired:
                    @pl.when(count > 0)
                    def _(step=step):
                        gram_copy(now, step).wait()

                for tile in range(step * tall // TILE_ROWS, (step + 1) * tall // TILE_ROWS):
                    at = slice(tile * TILE_ROWS, (tile + 1) * TILE_ROWS)
                    if paired:
                        total = gram_send[now, at].astype(jnp.float32) + gram_recv[now, at].astype(jnp.float32)
                    else:
                        total = gram[at]
                    total = total * shrink
                    gram[at] = total
                    off_low[at] = total.astype(jnp.bfloat16)
                    square = total[:, at]
                    masked = jnp.where(eye, square, 0.0)
                    diag_col[at] = jnp.sum(masked, axis=1, keepdims=True)
                    diag_row[:, at] = jnp.sum(masked, axis=0, keepdims=True)
                    square = jnp.where(eye, 0.0, square)
                    gram[at, at] = square
                    off_low[at, at] = square.astype(jnp.bfloat16)

            linear, middle, cubic = ns_linear * inverse, ns_square * inverse, ns_cubic * inverse

            def poly_rows(step):
                at = pl.ds(step * tall, tall)
                again = product(off_low[at], off_low[...])
                mine = diag_col[at]
                poly = gram[at] * (middle + cubic * mine + cubic * diag_row[...]) + cubic * again
                poly_low[at] = poly.astype(jnp.bfloat16)
                again_diag = []
                for tile in range(tall // TILE_ROWS):
                    rows_at = slice(tile * TILE_ROWS, (tile + 1) * TILE_ROWS)
                    side_at = slice(step * tall + tile * TILE_ROWS, step * tall + (tile + 1) * TILE_ROWS)
                    again_diag.append(
                        jnp.sum(jnp.where(eye, again[rows_at, side_at], 0.0), axis=1, keepdims=True)
                    )
                    poly_low[side_at, side_at] = jnp.where(eye, 0.0, poly[rows_at, side_at]).astype(jnp.bfloat16)
                again_diag = jnp.concatenate(again_diag, axis=0)
                factor = linear + middle * mine + cubic * (mine * mine + again_diag)

                @pl.when(count < ITERS - 1)
                def _():
                    for left in range(0, columns, wide):
                        part = slice(left, left + wide)
                        moved = product(poly_low[at], iter_low[now, :, part])
                        fresh = factor * iter_full[at, part] + moved
                        iter_full[at, part] = fresh
                        iter_low[later, at, part] = fresh.astype(jnp.bfloat16)

                @pl.when(count == ITERS - 1)
                def _():
                    for index in range(nf):
                        @pl.when(fs == index)
                        def _(index=index):
                            part = slice(index * width, (index + 1) * width)
                            own_full[at, :width] = iter_full[at, part]

                            if step == 0:
                                own_low[:, :width] = iter_low[now, :, part]

                    moved = product(poly_low[at], own_low[:, :width])
                    fresh = factor * own_full[at, :width] + moved
                    blocks = tall // rows
                    own_out[pl.ds(step * blocks, blocks)] = fresh.astype(jnp.bfloat16).reshape(
                        blocks, rows, width
                    )

                    def give(index):
                        row = step * blocks + index

                        @pl.when(row != dp)
                        def _():
                            back_copy(row).start()

                        @pl.when(row == dp)
                        def _():
                            pltpu.make_async_copy(own_out.at[row], target, own_sem).start()

                    loop(blocks, give)

            for step in range(steps):
                poly_rows(step)

        loop(ITERS, iteration)

        if not paired:
            crossing.finish()

        def finish(row):
            @pl.when(row != dp)
            def _():
                back_copy(row).wait_send()

        loop(ndp, finish)
        pltpu.make_async_copy(own_out.at[dp], target, own_sem).wait()

    @pl.when(is_attn)
    def _():
        at = jnp.where(dp < 2, dp, dp - 4)
        iterate(land_attn, attn_ref.at[at], own_attn, attn_out.at[at], dp, False)

    @pl.when(is_ffn)
    def _():
        matrix, half = (dp - 2) // 2, lax.rem(dp - 2, 2)
        iterate(land_ffn, None, own_ffn, ffn_out.at[matrix, half], dp, True)

    for role in range(ROLES):
        @pl.when(dp != role)
        def _(role=role):
            if role < 2 or role >= 6:
                target = attn_out.at[role if role < 2 else role - 4]
            else:
                target = ffn_out.at[(role - 2) // 2, (role - 2) % 2]
            if role in attn_roles:
                piece_copy(role).wait_send()
            remote(target, target, own_sem, back_recv.at[role], (role, fs)).wait_recv()


def orthogonalize(ndp, nf, attn_low, ffn_whole):
    rows, width_attn = attn_low.shape[1:]
    width_ffn = ffn_whole.shape[3]
    side = math.isqrt(nf)
    size = rows * ndp
    columns = width_ffn * nf
    tall = min(STEP_ROWS, size)
    bf16, f32 = jnp.bfloat16, jnp.float32
    dma = pltpu.SemaphoreType.DMA
    return pl.pallas_call(
        functools.partial(ortho_kernel, ndp, nf),
        name="newton_schulz",
        out_shape=[
            jax.ShapeDtypeStruct(attn_low.shape, bf16),
            jax.ShapeDtypeStruct((2, 2, rows, width_ffn), bf16),
        ],
        in_specs=[pl.BlockSpec(memory_space=pltpu.VMEM), pl.BlockSpec(memory_space=pl.ANY)],
        out_specs=[pl.BlockSpec(memory_space=pltpu.VMEM)] * 2,
        scratch_shapes=[
            pltpu.VMEM((nf, ndp, rows, width_attn), bf16),
            pltpu.VMEM((nf, ndp, rows, width_ffn), bf16),
            pltpu.VMEM((2, size, columns), bf16),
            pltpu.VMEM((size, columns), f32),
            pltpu.VMEM((size, size), f32),
            pltpu.VMEM((2, size, size), bf16),
            pltpu.VMEM((2, size, size), bf16),
            pltpu.VMEM((size, size), bf16),
            pltpu.VMEM((size, size), bf16),
            pltpu.VMEM((1, size), f32),
            pltpu.VMEM((size, 1), f32),
            pltpu.VMEM((1, 1), f32),
            pltpu.VMEM((size, width_ffn), bf16),
            pltpu.VMEM((size, width_ffn), f32),
            pltpu.VMEM((ndp, rows, width_attn), bf16),
            pltpu.VMEM((ndp, rows, width_ffn), bf16),
            dma,
            dma((ROLES,)),
            dma((ndp,)),
            dma((ndp, side - 1)),
            dma((ndp, side, side - 1)),
            dma((nf, ndp)),
            dma((2, size // tall)),
            dma((2, size // tall)),
            dma((ndp,)),
            dma((ROLES,)),
            dma((nf,)),
        ],
        compiler_params=pltpu.CompilerParams(
            collective_id=1, has_side_effects=True, vmem_limit_bytes=60 * 1024 * 1024
        ),
    )(attn_low, ffn_whole)


def update_kernel(
    attn_w,
    ffn_w,
    vectors,
    attn_mom,
    ffn_mom,
    vec_mom,
    attn_ema,
    ffn_ema,
    vec_ema,
    attn_grad,
    up_grad,
    down_grad,
    vec_grad,
    attn_ortho,
    ffn_ortho,
    attn_new,
    ffn_new,
    vec_new,
    attn_mom_new,
    ffn_mom_new,
    vec_mom_new,
    attn_ema_new,
    ffn_ema_new,
    vec_ema_new,
    *,
    vector_rate,
):
    for index in range(4):
        rate = attn_rates[index]
        attn_mom_new[index] = matrix_decay * attn_mom[index] + attn_grad[index]
        new = attn_w[index] * (1.0 - weight_decay * rate) - rate * attn_ortho[index].astype(jnp.float32)
        attn_new[index] = new
        attn_ema_new[index] = average_decay * attn_ema[index] + (1.0 - average_decay) * new
    width = ffn_ortho.shape[-1]
    shape_factor = math.sqrt(FF / D)
    for index, grad in enumerate((up_grad, down_grad)):
        ffn_mom_new[index] = matrix_decay * ffn_mom[index] + grad[...]
        for half in range(2):
            at = slice(half * width, (half + 1) * width)
            ortho = ffn_ortho[index, half].astype(jnp.float32)
            new = ffn_w[index, :, at] * (1.0 - weight_decay) - shape_factor * ortho
            ffn_new[index, :, at] = new
            ffn_ema_new[index, :, at] = average_decay * ffn_ema[index, :, at] + (1.0 - average_decay) * new
    mom = vector_decay * vec_mom[...] + vec_grad[...]
    vec_mom_new[...] = mom
    new = vectors[...] - vector_rate * mom
    vec_new[...] = new
    vec_ema_new[...] = average_decay * vec_ema[...] + (1.0 - average_decay) * new


def update_all(vector_rate, *operands):
    states = operands[:9]
    return pl.pallas_call(
        functools.partial(update_kernel, vector_rate=vector_rate),
        name="update",
        out_shape=[jax.ShapeDtypeStruct(states[index % 3].shape, jnp.float32) for index in range(9)],
        in_specs=[pl.BlockSpec(memory_space=pltpu.VMEM)] * len(operands),
        out_specs=[pl.BlockSpec(memory_space=pltpu.VMEM)] * 9,
        compiler_params=pltpu.CompilerParams(vmem_limit_bytes=60 * 1024 * 1024),
    )(*operands)


ROOM = pltpu.CompilerParams(vmem_limit_bytes=56 * 1024 * 1024)
ROOT_HALF = math.sqrt(0.5)
BELL = 1.0 / math.sqrt(2.0 * math.pi)


def flat(block):
    return block.reshape(-1, block.shape[-1])


def head_lanes(values, head):
    if values.shape[1] == HDIM:
        return values
    lane = lax.broadcasted_iota(jnp.int32, values.shape, 1)
    return jnp.where(lax.div(lane, HDIM) == head, values, jnp.zeros_like(values))


def normalize(values):
    center = values - jnp.mean(values, axis=1, keepdims=True)
    inverse = lax.rsqrt(jnp.mean(center * center, axis=1, keepdims=True) + ln_epsilon)
    return center * inverse, inverse


def normalize_back(grad, scaled, inverse):
    return inverse * (
        grad
        - jnp.mean(grad, axis=1, keepdims=True)
        - scaled * jnp.mean(grad * scaled, axis=1, keepdims=True)
    )


def row_sum(values):
    return jnp.sum(values.astype(jnp.float32), axis=0, keepdims=True)


def forward_kernel(
    ndp,
    nf,
    tokens_ref,
    label_ref,
    cotangent_ref,
    attn_w,
    ffn_w,
    vectors_ref,
    attn_out,
    up_out,
    down_out,
    blocks_out,
    active_out,
    slope_out,
    vec_out,
    mixture_out,
    total_out,
    scaled_out,
    inverse_out,
    low_out,
    layer_out,
    d_second_out,
    sums_out,
    attn_shard,
    up_shard,
    down_shard,
    three_weight,
    out_weight,
    ffn_weight,
    vec_land,
    bias,
    bias_up,
    blocks,
    parts,
    active,
    slope,
    total,
    own_sem,
    own_recv,
    pair_recv,
    z_send,
    first_send,
    second_send,
    pair_send,
    load_sem,
    store_sem,
):
    chunks, turned = 4, 3
    wholes = (attn_out, up_out, down_out)
    z, core, y, x, nz, side = place(ndp, nf)
    dp, fs = z * 2 + core, y * side + x
    rows, width_attn = attn_w.shape[1:]
    width_ffn, share = ffn_w.shape[2], vectors_ref.shape[1]
    count = tokens_ref.shape[0]
    width = ffn_weight.shape[-1]
    per = width_ffn // width

    attn_shard[4 * rows :] = jnp.zeros((16, width_attn), jnp.bfloat16)
    attn_shard[4 * rows : 4 * rows + 12, :share] = vectors_ref[...].astype(jnp.bfloat16)
    for index in range(4):
        attn_shard[index * rows : (index + 1) * rows] = attn_w[index].astype(jnp.bfloat16)
    up_shard[...] = ffn_w[0].astype(jnp.bfloat16)
    down_shard[...] = ffn_w[1].astype(jnp.bfloat16)
    greet(line_partners(ndp, nf))

    halves = slice(0, width_ffn // 2), slice(width_ffn // 2, width_ffn)
    shards = (attn_shard, up_shard, down_shard.at[:, halves[0]], down_shard.at[:, halves[1]])

    def row_slot(chunk, plane_at, row):
        if chunk < 2:
            return wholes[chunk].at[plane_at, row]
        return down_out.at[plane_at, row, :, halves[chunk - 2]]

    def slot(chunk, plane_at, z_at):
        return row_slot(chunk, plane_at, z_at * 2 + core)

    def source(chunk, plane_at, z_at, own):
        return shards[chunk] if own else slot(chunk, plane_at, z_at)

    def along(first, step):
        x_at = jnp.where(first, lax.rem(x + step, side), x)
        y_at = jnp.where(first, y, lax.rem(y + step, side))
        return y_at * side + x_at

    def first_copy(chunk, z_at, step, own):
        peer = along(lax.rem(z_at, 2) == 0, step)
        return remote(
            source(chunk, fs, z_at, own),
            slot(chunk, fs, z_at),
            first_send.at[chunk, z_at, step - 1],
            own_recv.at[chunk, fs, z_at],
            (dp, peer),
        )

    def second_copy(chunk, plane_at, z_at, step, own, line):
        peer = along(lax.rem(z_at, 2) != 0, step)
        return remote(
            source(chunk, plane_at, z_at, own),
            slot(chunk, plane_at, z_at),
            second_send.at[chunk, z_at, line, step - 1],
            own_recv.at[chunk, plane_at, z_at],
            (dp, peer),
        )

    def pair_copy(chunk, plane_at, z_at, own):
        return remote(
            source(chunk, plane_at, z_at, own),
            slot(chunk, plane_at, z_at),
            pair_send.at[chunk, plane_at, z_at],
            pair_recv.at[chunk, plane_at, z_at],
            (z * 2 + 1 - core, fs),
        )

    def z_copy(chunk, plane_at, z_at, up, own):
        return remote(
            source(chunk, plane_at, z_at, own),
            slot(chunk, plane_at, z_at),
            z_send.at[chunk, plane_at, z_at, up],
            own_recv.at[chunk, plane_at, z_at],
            ((z + (1 if up else -1)) * 2 + core, fs),
        )

    def along_z(chunk, plane_at, z_at, own, act):
        @pl.when(jnp.logical_and(z_at <= z, z < nz - 1))
        def _():
            act(z_copy(chunk, plane_at, z_at, 1, own))

        @pl.when(jnp.logical_and(z_at >= z, z > 0))
        def _():
            act(z_copy(chunk, plane_at, z_at, 0, own))

    def begin(copy):
        copy.start()

    def arrived(chunk, plane_at, z_at):
        here = slot(chunk, plane_at, z_at)
        remote(here, here, own_sem.at[chunk], own_recv.at[chunk, plane_at, z_at], (dp, fs)).wait_recv()

    def pass_on(chunk, z_at, own):
        for step in range(1, side):
            first_copy(chunk, z_at, step, own).start()
            second_copy(chunk, fs, z_at, step, own, 0).start()
        pair_copy(chunk, fs, z_at, own).start()

    def own_copy(chunk):
        return pltpu.make_async_copy(shards[chunk], slot(chunk, fs, z), own_sem.at[chunk])

    def near_first(body):
        def each(index):
            far = 1 + lax.div(index, 2)
            z_at = jnp.where(lax.rem(index, 2) == 0, z - far, z + far)

            @pl.when(jnp.logical_and(z_at >= 0, z_at < nz))
            def _():
                body(z_at)

        loop(2 * (nz - 1), each)

    def from_z(chunk):
        def each(z_at):
            arrived(chunk, fs, z_at)
            along_z(chunk, fs, z_at, False, begin)
            pass_on(chunk, z_at, False)

        near_first(each)

    def from_first(chunk):
        def each(z_at):
            for line in range(1, side):
                plane_at = along(lax.rem(z_at, 2) == 0, line)
                arrived(chunk, plane_at, z_at)
                for step in range(1, side):
                    second_copy(chunk, plane_at, z_at, step, False, line).start()
                pair_copy(chunk, plane_at, z_at, False).start()

        each(z)
        near_first(each)

    def last_places(z_at):
        x_first = lax.rem(z_at, 2) == 0
        for line in range(side):
            for step in range(1, side):
                near_x, far_y = lax.rem(x + line, side), lax.rem(y + step, side)
                far_x, near_y = lax.rem(x + step, side), lax.rem(y + line, side)
                yield jnp.where(x_first, far_y * side + near_x, near_y * side + far_x)

    def from_second(chunk):
        def each(z_at):
            for plane_at in last_places(z_at):
                arrived(chunk, plane_at, z_at)
                pair_copy(chunk, plane_at, z_at, False).start()

        each(z)
        near_first(each)

    def turned_first():
        for line in range(1, side):
            plane_at = along(lax.rem(z, 2) == 0, line)
            arrived(turned, plane_at, z)
            for step in range(1, side):
                second_copy(turned, plane_at, z, step, False, line).start()
            along_z(turned, plane_at, z, False, begin)
            pair_copy(turned, plane_at, z, False).start()

    def turned_second():
        for plane_at in last_places(z):
            arrived(turned, plane_at, z)
            along_z(turned, plane_at, z, False, begin)
            pair_copy(turned, plane_at, z, False).start()

    def turned_z(far):
        for z_at in (z - far, z + far):
            @pl.when(jnp.logical_and(z_at >= 0, z_at < nz))
            def _(z_at=z_at):
                def each(step):
                    plane_at = lax.rem(fs + step, nf)
                    arrived(turned, plane_at, z_at)
                    along_z(turned, plane_at, z_at, False, begin)
                    pair_copy(turned, plane_at, z_at, False).start()

                loop(nf, each)

    def from_pair(chunk):
        own_copy(chunk).wait()

        def each(index):
            plane_at, z_at = lax.rem(index, nf), lax.div(index, nf)
            there = row_slot(chunk, plane_at, z_at * 2 + 1 - core)
            remote(
                there, there, own_sem.at[chunk], pair_recv.at[chunk, plane_at, z_at], (dp, fs)
            ).wait_recv()

        loop(nf * nz, each)

    for chunk in (0, turned, 1, 2):
        own_copy(chunk).start(priority=1)
        along_z(chunk, fs, z, True, begin)
        pass_on(chunk, z, True)

    from_z(0)
    from_first(0)
    turned_first()
    from_z(1)
    from_second(0)
    turned_second()
    from_pair(0)

    def load(index, source, target):
        return pltpu.make_async_copy(source, target, load_sem.at[index])

    def attn_load(index, block, at):
        per_block = ndp // nf
        if index == 0:
            return load(at, attn_out.at[block, :, pl.ds(0, 3 * rows)], three_weight.at[at])
        return load(
            2 + at,
            attn_out.at[:, pl.ds(block * per_block, per_block), pl.ds(3 * rows, rows)],
            out_weight.at[at],
        )

    vec_copy = load(4, attn_out.at[:, :, pl.ds(4 * rows, 16)], vec_land)
    vec_copy.start(priority=1)
    for index in range(2):
        attn_load(index, 0, 0).start(priority=1)
    vec_copy.wait()
    for row in range(ndp):
        for column in range(nf):
            left = (row * nf + column) * share
            vec_out[:, left : left + share] = vec_land[column, row, :, :share].astype(jnp.float32)
    for index in range(nf):
        at = slice(index * width_attn, (index + 1) * width_attn)
        bias[index, 0:1] = vec_out[0:1, at]
        bias[index, 1:2] = vec_out[1:2, at]
    for index in range(FF // width):
        left = index * width
        bias_up[index] = vec_out[5 + left // D : 6 + left // D, left % D : left % D + width]
    label_row = label_ref[...].astype(jnp.float32)
    label_col = jnp.transpose(jnp.broadcast_to(label_row, (128, count)))[:, 0:1]
    tokens = tokens_ref[...]
    lane = lax.broadcasted_iota(jnp.int32, (count, 128), 1)
    total[...] = jnp.broadcast_to(vec_out[2:3], (count, D))

    def attn_turn(block):
        at = lax.rem(block, 2)

        @pl.when(block < nf - 1)
        def _():
            for index in range(2):
                attn_load(index, block + 1, 1 - at).start(priority=1)

        attn_load(0, block, at).wait()
        attn_load(1, block, at).wait()
        weights = [flat(three_weight[at, :, index * rows : (index + 1) * rows]) for index in range(3)]
        queries = (product(tokens, weights[0]) + bias[block, 0:1]).astype(jnp.bfloat16)
        keys_all = product(tokens, weights[1]).astype(jnp.bfloat16)
        values_all = (product(tokens, weights[2]) + bias[block, 1:2]).astype(jnp.bfloat16)
        for index, values in enumerate((queries, keys_all, values_all)):
            blocks[block, index] = values
        pltpu.make_async_copy(blocks.at[block], blocks_out.at[block], store_sem.at[block]).start(priority=1)
        allowed = label_col == label_row
        totals = jnp.zeros((count, 128), jnp.float32)
        mixture = jnp.zeros((count, width_attn), jnp.float32)
        for head in range(width_attn // HDIM):
            scores = contract_cols(head_lanes(queries, head) * score_scale, keys_all)
            scores = jnp.where(allowed, scores, -1e30)
            top = jnp.max(scores, axis=1, keepdims=True)
            exponent = jnp.exp(scores - top)
            weight = jnp.sum(exponent, axis=1, keepdims=True)
            attention = (exponent * (1.0 / weight)).astype(jnp.bfloat16)
            totals = jnp.where(lane == head, top + jnp.log(weight), totals)
            mixture += product(attention, head_lanes(values_all, head))
        mixture = mixture.astype(jnp.bfloat16)
        parts[block] = mixture
        total_out[block] = jnp.transpose(totals)[:8]
        for index in range(nf):
            side_at = slice(index * width_attn, (index + 1) * width_attn)
            total[:, side_at] += product(mixture, flat(out_weight[at, index]))

        @pl.when(block == 0)
        def _():
            from_z(2)
            turned_z(1)

        @pl.when(block == nf - 2)
        def _():
            from_first(1)
            turned_z(2)

    loop(nf, attn_turn)

    def first_norm(index):
        at = pl.ds(pl.multiple_of(index * NORM_ROWS, NORM_ROWS), NORM_ROWS)
        scaled, inverse = normalize(tokens_ref[at].astype(jnp.float32) + total[at])
        scaled_out[at] = scaled
        inverse_out[at] = inverse
        normed = scaled * vec_out[3:4] + vec_out[4:5]
        low_out[at] = normed.astype(jnp.bfloat16)
        total[at] = normed + vec_out[9:10]

    loop(count // NORM_ROWS, first_norm)
    for index in range(nf):
        mixture_out[:, index * width_attn : (index + 1) * width_attn] = parts[index]

    def ffn_load(chunk, step, at):
        block, part = lax.div(step, per), lax.rem(step, per)
        left = pl.multiple_of(part * width, width)
        return load(5 + at, wholes[chunk].at[block, :, :, pl.ds(left, width)], ffn_weight.at[at])

    def ffn_steps(chunk, body, between, first=0, stride=1):
        ffn_load(chunk, first, 0).start(priority=1)
        count_steps = FF // width // stride

        def each(index):
            at, step = lax.rem(index, 2), first + index * stride

            @pl.when(index < count_steps - 1)
            def _():
                ffn_load(chunk, step + stride, 1 - at).start(priority=1)

            ffn_load(chunk, step, at).wait()
            body(step, at)
            between(step)

        loop(count_steps, each)

    def keep(step):
        column = pl.ds(pl.multiple_of(step * width, width), width)
        return (
            pltpu.make_async_copy(active.at[step], active_out.at[:, column], store_sem.at[nf]),
            pltpu.make_async_copy(slope.at[lax.rem(step, 2)], slope_out.at[:, column], store_sem.at[nf + 1]),
        )

    def up_step(step, at):
        up_proj = product(low_out[...], flat(ffn_weight[at])) + bias_up[step]
        half = 0.5 * (1.0 + lax.erf(up_proj * ROOT_HALF))

        @pl.when(step > 0)
        def _():
            for copy in keep(step - 1):
                copy.wait()

        active[step] = (up_proj * half).astype(jnp.bfloat16)
        slope[lax.rem(step, 2)] = (half + up_proj * (BELL * jnp.exp(-0.5 * up_proj * up_proj))).astype(
            jnp.bfloat16
        )
        for copy in keep(step):
            copy.start(priority=1)

    def down_step(step, at):
        total[...] += contract_cols(active[step], flat(ffn_weight[at]))

    def between_up(step):
        @pl.when(step == 0)
        def _():
            for far in range(3, nz):
                turned_z(far)

        @pl.when(step == FF // width // 2)
        def _():
            from_first(2)

    from_second(1)
    from_pair(1)
    ffn_steps(1, up_step, between_up)
    for copy in keep(FF // width - 1):
        copy.wait()
    from_second(2)
    from_pair(turned)
    ffn_steps(2, down_step, lambda step: None, 1, 2)
    from_pair(2)
    ffn_steps(2, down_step, lambda step: None, 0, 2)
    sums_out[...] = jnp.zeros((8, D), jnp.float32)

    def second_norm(index):
        at = pl.ds(pl.multiple_of(index * NORM_ROWS, NORM_ROWS), NORM_ROWS)
        scaled, inverse = normalize(total[at])
        layer_out[at] = (scaled * vec_out[10:11] + vec_out[11:12]).astype(jnp.bfloat16)
        grad = cotangent_ref[at].astype(jnp.float32)
        d_second = normalize_back(grad * vec_out[10:11], scaled, inverse)
        d_second_out[at] = d_second
        sums_out[0:1] += row_sum(d_second.astype(jnp.bfloat16))
        sums_out[1:2] += row_sum(grad * scaled)
        sums_out[2:3] += row_sum(grad)

    loop(count // NORM_ROWS, second_norm)

    def stored(block):
        pltpu.make_async_copy(blocks.at[block], blocks_out.at[block], store_sem.at[block]).wait()

    loop(nf, stored)
    for chunk in range(chunks):
        def finish(z_at):
            def sent():
                for step in range(1, side):
                    first_copy(chunk, z_at, step, False).wait_send()
                    for line in range(side):
                        second_copy(chunk, fs, z_at, step, False, line).wait_send()

            if chunk == turned:
                pl.when(z_at == z)(sent)
            else:
                sent()
                along_z(chunk, fs, z_at, False, lambda copy: copy.wait_send())

            def each(plane_at):
                pair_copy(chunk, plane_at, z_at, False).wait_send()
                if chunk == turned:
                    along_z(chunk, plane_at, z_at, False, lambda copy: copy.wait_send())

            loop(nf, each)

        loop(nz, finish)


def forward(ndp, nf, tokens, segments, cotangent, attn_w, ffn_w, vectors):
    nz, side, chunks = ndp // 2, math.isqrt(nf), 4
    count = tokens.shape[0]
    rows, width_attn = attn_w.shape[1:]
    width_ffn = ffn_w.shape[2]
    width = width_ffn // 2
    bf16, f32 = jnp.bfloat16, jnp.float32
    dma = pltpu.SemaphoreType.DMA
    anywhere, inside = pl.BlockSpec(memory_space=pl.ANY), pl.BlockSpec(memory_space=pltpu.VMEM)
    shape = jax.ShapeDtypeStruct
    return pl.pallas_call(
        functools.partial(forward_kernel, ndp, nf),
        name="forward",
        out_shape=[
            shape((nf, ndp, 4 * rows + 16, width_attn), bf16),
            shape((nf, ndp, rows, width_ffn), bf16),
            shape((nf, ndp, rows, width_ffn), bf16),
            shape((nf, 3, count, width_attn), bf16),
            shape((count, FF), bf16),
            shape((count, FF), bf16),
            shape((16, D), f32),
            shape((count, D), bf16),
            shape((nf, 8, count), f32),
            shape((count, D), f32),
            shape((count, 1), f32),
            shape((count, D), bf16),
            shape((count, D), bf16),
            shape((count, D), f32),
            shape((8, D), f32),
        ],
        in_specs=[inside] * 6,
        out_specs=[anywhere] * 6 + [inside] * 9,
        scratch_shapes=[
            pltpu.VMEM((4 * rows + 16, width_attn), bf16),
            pltpu.VMEM((rows, width_ffn), bf16),
            pltpu.VMEM((rows, width_ffn), bf16),
            pltpu.VMEM((2, ndp, 3 * rows, width_attn), bf16),
            pltpu.VMEM((2, nf, ndp // nf, rows, width_attn), bf16),
            pltpu.VMEM((2, ndp, rows, width), bf16),
            pltpu.VMEM((nf, ndp, 16, width_attn), bf16),
            pltpu.VMEM((nf, 8, width_attn), f32),
            pltpu.VMEM((FF // width, 1, width), f32),
            pltpu.VMEM((nf, 3, count, width_attn), bf16),
            pltpu.VMEM((nf, count, width_attn), bf16),
            pltpu.VMEM((FF // width, count, width), bf16),
            pltpu.VMEM((2, count, width), bf16),
            pltpu.VMEM((count, D), f32),
            dma((chunks,)),
            dma((chunks, nf, nz)),
            dma((chunks, nf, nz)),
            dma((chunks, nf, nz, 2)),
            dma((chunks, nz, side - 1)),
            dma((chunks, nz, side, side - 1)),
            dma((chunks, nf, nz)),
            dma((7,)),
            dma((nf + 2,)),
        ],
        compiler_params=pltpu.CompilerParams(
            collective_id=2, has_side_effects=True, vmem_limit_bytes=60 * 1024 * 1024
        ),
    )(tokens, segments[None, :], cotangent, attn_w, ffn_w, vectors)


def backward_kernel(
    ndp,
    nf,
    d_second_ref,
    low_ref,
    scaled_ref,
    inverse_ref,
    vec_ref,
    active_ref,
    slope_ref,
    up_ref,
    down_ref,
    tokens_ref,
    label_ref,
    blocks_ref,
    mixture_ref,
    total_ref,
    attn_ref,
    tail_ref,
    attn_mom,
    ffn_mom,
    input_grad,
    up_out,
    down_out,
    attn_out,
    vec_out,
    attn_low,
    ffn_low,
    ffn_whole,
    held_up,
    held_down,
    held_attn,
    first_up,
    first_down,
    first_attn,
    second_up,
    second_down,
    second_attn,
    z_up,
    z_down,
    z_attn,
    first_turned,
    second_turned,
    z_turned,
    stages_out,
    land,
    ffn_weight,
    ffn_act,
    attn_weight,
    attn_block,
    wide_low,
    wide_two,
    turned_one,
    turned_two,
    branch,
    bias_up_sum,
    query_sum,
    value_sum,
    vec_land,
    load_sem,
    step_sem,
    pair_send,
    pair_recv,
    first_send,
    first_recv,
    second_send,
    second_recv,
    z_send,
    z_recv,
    vec_send,
    vec_recv,
    piece_own,
    piece_send,
    piece_recv,
    piece_first,
    piece_second,
    piece_plane,
    turned_send,
    turned_recv,
):
    z, core, y, x, nz, side = place(ndp, nf)
    dp, fs = z * 2 + core, y * side + x
    other = (z * 2 + 1 - core, fs)
    chunks, turned = 3, 3
    rows, width_ffn = held_up.shape[2:]
    half_width = width_ffn // 2
    held, outs = (held_up, held_down, held_attn), (up_out, down_out, attn_out)
    from_first = (first_up, first_down, first_attn, first_turned)
    from_second = (second_up, second_down, second_attn, second_turned)
    from_z = (z_up, z_down, z_attn)
    width_attn = held_attn.shape[-1]
    width = ffn_weight.shape[-1]
    per = width_ffn // width
    greet(all_partners(ndp, nf))

    def place_of(turn):
        step = nf - 1 - turn
        return lax.rem(y + lax.div(step, side), side) * side + lax.rem(x + lax.rem(step, side), side)

    def sums(chunk, z_at, plane_at):
        if chunk == 1:
            return held_down.at[z_at, plane_at, :, pl.ds(0, half_width)]
        if chunk == turned:
            return held_down.at[z_at, plane_at, :, pl.ds(half_width, half_width)]
        return held[chunk].at[z_at, plane_at]

    def add(target, source):
        target[...] = target[...] + source[...]

    def first_land(chunk, z_at, step, line):
        return from_first[chunk].at[0 if chunk == turned else z_at, step - 1, line]

    def second_land(chunk, z_at, step):
        return from_second[chunk].at[0 if chunk == turned else z_at, step - 1]

    def first_copy(chunk, z_at, line, step):
        x_first = lax.rem(z_at, 2) == 0
        near, far = lax.rem(x + step, side), lax.rem(y + step, side)
        to = jnp.where(x_first, y * side + near, far * side + x)
        at = jnp.where(
            x_first,
            lax.rem(y + line, side) * side + near,
            far * side + lax.rem(x + line, side),
        )
        return remote(
            sums(chunk, z_at, at),
            first_land(chunk, z_at, step, line),
            first_send.at[chunk, z_at, step - 1, line],
            first_recv.at[chunk, z_at, step - 1, line],
            (dp, to),
        )

    lag = 2
    total_steps = nf * per + nf
    schedule = {}
    for sent, base, stride, late in (((0, 1), 0, per, lag), ((2,), nf * per, 1, 1)):
        for turns in ((0,), tuple(range(1, nf - 1))):
            ready = min(base + (turns[-1] + 1) * stride - 1 + late, total_steps)
            for z_at in range(0, nz, 2):
                schedule.setdefault(ready, []).extend((chunk, turns, z_at) for chunk in sent)

    def send_first(chunk, turns, z_from, z_count=2):
        def each(z_at):
            x_first = lax.rem(z_at, 2) == 0
            for turn in turns:
                step_x, step_y = (nf - 1 - turn) % side, (nf - 1 - turn) // side
                step = jnp.where(x_first, step_x, step_y)
                line = jnp.where(x_first, step_y, step_x)

                @pl.when(step > 0)
                def _(line=line, step=step):
                    first_copy(chunk, z_at, line, step).start()

        loop(z_from + z_count, each, z_from)

    def sends_at(step, steps):
        for when in steps:
            @pl.when(step == when)
            def _(when=when):
                for chunk, turns, z_at in schedule.get(when, ()):
                    send_first(chunk, turns, z_at)

    def line_place(z_at, line):
        x_first = lax.rem(z_at, 2) == 0
        return jnp.where(
            x_first, lax.rem(y + line, side) * side + x, y * side + lax.rem(x + line, side)
        )

    def second_copy(chunk, z_at, step):
        to = line_place(z_at, step)
        return remote(
            sums(chunk, z_at, to),
            second_land(chunk, z_at, step),
            second_send.at[chunk, z_at, step - 1],
            second_recv.at[chunk, z_at, step - 1],
            (dp, to),
        )

    def z_copy(chunk, step):
        z_at = lax.rem(z + step, nz)
        return remote(
            sums(chunk, z_at, fs),
            from_z[chunk].at[step - 1],
            z_send.at[chunk, step - 1],
            z_recv.at[chunk, step - 1],
            (z_at * 2 + core, fs),
        )

    def take_first(chunk, lines):
        def each(hop):
            z_at = lax.rem(z + 1 + hop, nz)
            for line in lines:
                at = line_place(z_at, line)
                for step in range(1, side):
                    first_copy(chunk, z_at, line, step).wait_recv()
                    add(sums(chunk, z_at, at), first_land(chunk, z_at, step, line))
                if line:
                    second_copy(chunk, z_at, line).start()

        if chunk == turned:
            each(nz - 1)
        else:
            loop(nz, each)

    def turned_copy(plane_at, step):
        z_at = lax.rem(z + step, nz)
        return remote(
            sums(turned, z_at, plane_at),
            z_turned.at[step - 1, plane_at],
            turned_send.at[step - 1, plane_at],
            turned_recv.at[step - 1, plane_at],
            (z_at * 2 + core, fs),
        )

    def turned_start(turns):
        for turn in turns:
            for step in range(1, nz):
                turned_copy(place_of(turn), step).start()

    def turned_take(turns):
        for turn in turns:
            plane_at = place_of(turn)
            for step in range(1, nz):
                turned_copy(plane_at, step).wait_recv()
                add(sums(turned, z, plane_at), z_turned.at[step - 1, plane_at])
        send_first(turned, turns, z, 1)

    def take_second(chunk):
        def each(hop):
            z_at = lax.rem(z + 1 + hop, nz)
            for step in range(1, side):
                second_copy(chunk, z_at, step).wait_recv()
                add(sums(chunk, z_at, fs), second_land(chunk, z_at, step))

            @pl.when(hop < nz - 1)
            def _():
                z_copy(chunk, hop + 1).start()

        loop(nz, each)

    def moments(chunk):
        source = ffn_mom.at[chunk] if chunk < 2 else attn_mom
        return pltpu.make_async_copy(source, outs[chunk], load_sem.at[3 + chunk])

    def take_z(chunk):
        moments(chunk).wait()
        total = sums(chunk, z, fs)[...].astype(jnp.float32)
        for step in range(1, nz):
            z_copy(chunk, step).wait_recv()
            total += from_z[chunk][step - 1].astype(jnp.float32)
        if chunk == 0:
            low = (matrix_decay * up_out[...] + total).astype(jnp.bfloat16)
            up_out[...] = total
            ffn_low[0, 0] = low[:, :half_width]
            ffn_low[0, 1] = low[:, half_width:]
        elif chunk == 1:
            for step in range(1, side):
                second_copy(turned, z, step).wait_recv()
                add(sums(turned, z, fs), second_land(turned, z, step))
            for index, value in enumerate((total, sums(turned, z, fs)[...].astype(jnp.float32))):
                at = slice(index * half_width, (index + 1) * half_width)
                ffn_low[1, index] = (matrix_decay * down_out[:, at] + value).astype(jnp.bfloat16)
                down_out[:, at] = value
        else:
            attn_low[...] = (matrix_decay * attn_out[...] + total).astype(jnp.bfloat16)
            attn_out[...] = total

    vec_rounds = [[other]]
    vec_rounds.append([(dp, y * side + lax.rem(x + step, side)) for step in range(1, side)])
    vec_rounds.append([(dp, lax.rem(y + step, side) * side + x) for step in range(1, side)])
    vec_rounds.append([(lax.rem(z + step, nz) * 2 + core, fs) for step in range(1, nz)])
    starts = [sum(len(group) for group in vec_rounds[:index]) for index in range(4)]

    def vec_copy(index, step):
        at = starts[index] + step
        return remote(
            vec_land.at[index], vec_land.at[4 + at], vec_send.at[at], vec_recv.at[at], vec_rounds[index][step]
        )

    def vec_start(index):
        for step in range(len(vec_rounds[index])):
            vec_copy(index, step).start()

    def vec_take(index):
        total = vec_land[index]
        for step in range(len(vec_rounds[index])):
            vec_copy(index, step).wait_recv()
            total += vec_land[4 + starts[index] + step]
        if index < 3:
            vec_land[index + 1] = total
            vec_start(index + 1)
        else:
            vec_out[...] = total

    def split(values, keep, give):
        parts = values.astype(jnp.bfloat16).reshape(nz, 2, rows, values.shape[1])
        for which in range(2):
            @pl.when(core == which)
            def _(which=which):
                keep(parts[:, which])
                give(parts[:, 1 - which])

    def piece_copy(matrix, half):
        return remote(
            ffn_low.at[matrix, half],
            ffn_whole.at[fs, dp],
            piece_send.at[2 * matrix + half],
            piece_recv.at[dp],
            (2 + 2 * matrix + half, fs),
        )

    def piece_local(matrix, half):
        return pltpu.make_async_copy(ffn_low.at[matrix, half], ffn_whole.at[fs, dp], piece_own)

    def start_pieces(matrix):
        for half in range(2):
            @pl.when(dp != 2 + 2 * matrix + half)
            def _(half=half):
                piece_copy(matrix, half).start()

            @pl.when(dp == 2 + 2 * matrix + half)
            def _(half=half):
                piece_local(matrix, half).start(priority=1)

    crossing = Crossing(
        ndp, nf, ffn_whole, piece_own, piece_recv, piece_first, piece_second, piece_plane, ffn_low.at[0, 0]
    )
    runs_ffn = jnp.logical_and(dp >= 2, dp < 6)

    def ffn_loads(slot, turn, part):
        block = place_of(turn)
        at = pl.ds(part * width, width)
        column = pl.ds(pl.multiple_of(block * width_ffn + part * width, width), width)
        pairs = (
            (up_ref.at[block, :, :, at], ffn_weight.at[slot, 0]),
            (down_ref.at[block, :, :, at], ffn_weight.at[slot, 1]),
            (active_ref.at[:, column], ffn_act.at[slot, 0]),
            (slope_ref.at[:, column], ffn_act.at[slot, 1]),
        )
        return [
            pltpu.make_async_copy(source, target, step_sem.at[slot, index])
            for index, (source, target) in enumerate(pairs)
        ]

    def load(index, source, target):
        return pltpu.make_async_copy(source, target, load_sem.at[index])

    load(0, low_ref, wide_low).start(priority=1)
    load(1, d_second_ref, input_grad).start(priority=1)
    for copy in ffn_loads(0, 0, 0):
        copy.start(priority=1)
    load(2, tokens_ref, wide_two).start(priority=1)
    for chunk in range(chunks):
        moments(chunk).start(priority=1)
    load(0, low_ref, wide_low).wait()
    turned_one[...] = jnp.transpose(wide_low[...])
    load(1, d_second_ref, input_grad).wait()
    wide_low[...] = input_grad[...].astype(jnp.bfloat16)
    turned_two[...] = jnp.transpose(wide_low[...])

    def pair_copy(step):
        stage, slot = lax.rem(step, lag), lax.rem(step, 2 * lag)
        return remote(stages_out.at[stage], land.at[slot], pair_send.at[stage], pair_recv.at[slot], other)

    def pair_take(step):
        pair_copy(step).wait()
        slot = lax.rem(step, 2 * lag)

        @pl.when(step < nf * per)
        def _():
            block, part = place_of(lax.div(step, per)), lax.rem(step, per)
            for index in range(2):
                for which in range(per):
                    @pl.when(part == which)
                    def _(index=index, which=which):
                        for half in range(2):
                            left = which * width + half * width_attn
                            at = slice(left, left + width_attn)
                            held[index][:, block, :, at] += land[slot, :, 2 * index + half]

        @pl.when(step >= nf * per)
        def _():
            held_attn[:, place_of(step - nf * per)] += land[slot]

    def ffn_turn(turn):
        block = place_of(turn)
        for part in range(per):
            now = turn * per + part
            slot = lax.rem(now, 2)
            if part < per - 1:
                for copy in ffn_loads(1 - slot, turn, part + 1):
                    copy.start(priority=1)
            else:
                @pl.when(turn < nf - 1)
                def _():
                    for copy in ffn_loads(1 - slot, turn + 1, 0):
                        copy.start(priority=1)

            for copy in ffn_loads(slot, turn, part):
                copy.wait()
            d_active = product(wide_low[...], flat(ffn_weight[slot, 1]))
            d_up = (d_active * ffn_act[slot, 1].astype(jnp.float32)).astype(jnp.bfloat16)
            bias_up_sum[block * per + part] = row_sum(d_up)
            input_grad[...] += contract_cols(d_up, flat(ffn_weight[slot, 0]))

            @pl.when(now >= lag)
            def _():
                pair_take(now - lag)

            sends_at(now, range(nf * per))

            @pl.when(now == per - 1 + lag)
            def _():
                turned_start((0,))

            @pl.when(now == (nf - 1) * per - 1 + lag)
            def _():
                turned_start(range(1, nf - 1))
            at = slice(part * width, (part + 1) * width)
            for index in range(2):

                def keep(values, index=index):
                    held[index][:, block, :, at] = values

                def give(values, index=index):
                    for half in range(2):
                        side_at = slice(half * width_attn, (half + 1) * width_attn)
                        stages_out[lax.rem(now, lag), :, 2 * index + half] = values[:, :, side_at]

                if index == 0:
                    split(product(turned_one[...], d_up), keep, give)
                else:
                    split(product(turned_two[...], ffn_act[slot, 0]), keep, give)
            pair_copy(now).start()

    loop(nf, ffn_turn)

    load(2, tokens_ref, wide_two).wait()
    turned_one[...] = jnp.transpose(wide_two[...])
    load(0, mixture_ref, wide_two).start(priority=1)

    def attn_load(index, turn):
        block = place_of(turn)
        per_block = ndp // nf
        source, target = (
            (attn_ref.at[block, :, pl.ds(0, 3 * rows)], attn_weight[0]),
            (
                attn_ref.at[:, pl.ds(block * per_block, per_block), pl.ds(3 * rows, rows)],
                attn_weight[1],
            ),
            (blocks_ref.at[block], attn_block),
        )[index]
        return pltpu.make_async_copy(source, target, step_sem.at[0, index])

    for index in range(3):
        attn_load(index, 0).start(priority=1)
    vec_land[0] = jnp.zeros((16, D), jnp.float32)
    vec_land[0, 9:12] = tail_ref[0:3]

    def norm_back(index):
        at = pl.ds(pl.multiple_of(index * NORM_ROWS, NORM_ROWS), NORM_ROWS)
        grad = input_grad[at]
        scaled = scaled_ref[at]
        d_first = normalize_back(grad * vec_ref[3:4], scaled, inverse_ref[at])
        input_grad[at] = d_first
        low = d_first.astype(jnp.bfloat16)
        vec_land[0, 2:3] += row_sum(low)
        vec_land[0, 3:4] += row_sum(grad * scaled)
        vec_land[0, 4:5] += row_sum(grad)
        for column in range(nf):
            branch[column, at] = low[:, column * width_attn : (column + 1) * width_attn]

    loop(tokens_ref.shape[0] // NORM_ROWS, norm_back)
    label_row = label_ref[...].astype(jnp.float32)
    label_col = jnp.transpose(jnp.broadcast_to(label_row, (128, label_row.shape[1])))[:, 0:1]
    load(0, mixture_ref, wide_two).wait()
    turned_two[...] = jnp.transpose(wide_two[...])

    def attn_turn(turn):
        block = place_of(turn)
        now = nf * per + turn

        def load_next(index):
            @pl.when(turn < nf - 1)
            def _():
                attn_load(index, turn + 1).start(priority=1)

        for index in range(3):
            attn_load(index, turn).wait()
        count = tokens_ref.shape[0]
        zero = jnp.zeros((count, width_attn), jnp.float32)
        d_mixture = zero
        for index in range(nf):
            d_mixture += contract_cols(branch[index], flat(attn_weight[1][index]))
        load_next(1)
        d_mixture = d_mixture.astype(jnp.bfloat16)
        queries, keys_all, values_all = (attn_block[index] for index in range(3))
        allowed = label_col == label_row
        d_queries, d_keys, d_values = zero, zero, zero
        for head in range(width_attn // HDIM):
            my_queries = head_lanes(queries, head) * score_scale
            my_mixture = head_lanes(d_mixture, head)
            scores = contract_cols(keys_all, my_queries) - total_ref[block, head : head + 1, :]
            attention = jnp.where(allowed, jnp.exp(scores), 0.0)
            d_attention = contract_cols(values_all, my_mixture)
            inner = jnp.sum(d_attention * attention, axis=0, keepdims=True)
            d_scores = (attention * (d_attention - inner)).astype(jnp.bfloat16)
            d_keys += product(d_scores, my_queries)
            d_values += product(attention.astype(jnp.bfloat16), my_mixture)
            d_queries += contract_rows(d_scores, head_lanes(keys_all, head) * score_scale)
        load_next(2)
        grads = [values.astype(jnp.bfloat16) for values in (d_queries, d_keys, d_values)]
        query_sum[block] = row_sum(grads[0])
        value_sum[block] = row_sum(grads[2])
        moved = jnp.zeros((count, D), jnp.float32)
        for index in range(3):
            weight = attn_weight[0][:, index * rows : (index + 1) * rows]
            moved += contract_cols(grads[index], flat(weight))
        input_grad[...] += moved
        load_next(0)

        @pl.when(turn == 0)
        def _():
            pair_take(now - 2)

        pair_take(now - 1)
        for index in range(4):
            flipped, grad = (turned_one, grads[index]) if index < 3 else (turned_two, branch[block])

            def keep(values, index=index):
                held_attn[:, block, index] = values

            def give(values, index=index):
                stages_out[lax.rem(now, lag), :, index] = values

            split(product(flipped[...], grad), keep, give)
        pair_copy(now).start()
        sends_at(now, range(nf * per, total_steps))

        @pl.when(turn == 0)
        def _():
            turned_start((nf - 1,))

        @pl.when(turn == nf - 4)
        def _():
            turned_take((0,))
            take_first(0, range(1, side))
            take_first(1, range(1, side))

        @pl.when(turn == nf - 3)
        def _():
            turned_take(range(1, nf - 1))
            take_first(0, (0,))
            take_first(1, (0,))

        @pl.when(turn == nf - 2)
        def _():
            take_first(turned, range(1, side))

        @pl.when(turn == nf - 1)
        def _():
            turned_take((nf - 1,))
            take_first(turned, (0,))

        @pl.when(turn == nf - 2)
        def _():
            take_second(0)
            take_second(1)

    loop(nf, attn_turn)
    for index in range(nf):
        at = slice(index * width_attn, (index + 1) * width_attn)
        vec_land[0, 0:1, at] = query_sum[index]
        vec_land[0, 1:2, at] = value_sum[index]
    for index in range(nf * per):
        left = index * width
        vec_land[0, 5 + left // D : 6 + left // D, left % D : left % D + width] = bias_up_sum[index]
    vec_start(0)
    pair_take(total_steps - 1)
    sends_at(total_steps, (total_steps,))

    take_first(2, range(1, side))
    take_z(0)
    start_pieces(0)
    take_z(1)
    start_pieces(1)
    vec_take(0)
    take_first(2, (0,))
    take_second(2)
    vec_take(1)

    @pl.when(runs_ffn)
    def _():
        crossing.take()

    vec_take(2)
    take_z(2)
    vec_take(3)

    @pl.when(runs_ffn)
    def _():
        crossing.pass_on()
        crossing.near()
        crossing.far()
        crossing.finish()

    for matrix in range(2):
        for half in range(2):
            @pl.when(dp != 2 + 2 * matrix + half)
            def _(matrix=matrix, half=half):
                piece_copy(matrix, half).wait_send()

    def turned_sent(plane_at):
        for step in range(1, nz):
            turned_copy(plane_at, step).wait_send()

    loop(nf, turned_sent)
    for step in range(1, side):
        second_copy(turned, z, step).wait_send()
        for line in range(side):
            first_copy(turned, z, line, step).wait_send()
    for chunk in range(chunks):

        def finish(z_at):
            for step in range(1, side):
                second_copy(chunk, z_at, step).wait_send()
                for line in range(side):
                    first_copy(chunk, z_at, line, step).wait_send()

        loop(nz, finish)
        for step in range(1, nz):
            z_copy(chunk, step).wait_send()
    for index in range(4):
        for step in range(len(vec_rounds[index])):
            vec_copy(index, step).wait_send()


def backward_kernel_entry(ndp, nf, *refs):
    at = 18 + 8 + 15 + 2 + 2
    backward_kernel(ndp, nf, *refs[:at], refs[at : at + 2], *refs[at + 2 :])


def backward(
    ndp, nf, d_second, low, scaled, inverse, vectors, active, slope, up_all, down_all,
    tokens, segments, blocks, mixture, totals, attn_all, tail_sums, attn_mom, ffn_mom,
):
    nz, side = ndp // 2, math.isqrt(nf)
    count = tokens.shape[0]
    rows, width_ffn = up_all.shape[2:]
    width_attn = attn_all.shape[-1]
    width = 2 * width_attn
    bf16, f32 = jnp.bfloat16, jnp.float32
    dma = pltpu.SemaphoreType.DMA
    anywhere, inside = pl.BlockSpec(memory_space=pl.ANY), pl.BlockSpec(memory_space=pltpu.VMEM)
    shapes = [(rows, width_ffn), (rows, width_ffn), (4, rows, width_attn)]
    vec_copies = 1 + 2 * (side - 1) + nz - 1
    half = (rows, width_ffn // 2)
    sums = [pltpu.VMEM((nz, nf) + shape, bf16) for shape in shapes]
    for lead in ((nz, side - 1, side), (nz, side - 1), (nz - 1,)):
        sums += [pltpu.VMEM(lead + shape, bf16) for shape in (shapes[0], half, shapes[2])]
    sums += [pltpu.VMEM(lead + half, bf16) for lead in ((1, side - 1, side), (1, side - 1), (nz - 1, nf))]
    return pl.pallas_call(
        functools.partial(backward_kernel_entry, ndp, nf),
        name="backward",
        out_shape=[jax.ShapeDtypeStruct((count, D), f32)]
        + [jax.ShapeDtypeStruct(shape, f32) for shape in shapes]
        + [
            jax.ShapeDtypeStruct((16, D), f32),
            jax.ShapeDtypeStruct(attn_mom.shape, bf16),
            jax.ShapeDtypeStruct((2, 2, rows, width_ffn // 2), bf16),
            jax.ShapeDtypeStruct((nf, ndp, rows, width_ffn // 2), bf16),
        ],
        in_specs=[
            anywhere,
            anywhere,
            inside,
            inside,
            inside,
            anywhere,
            anywhere,
            anywhere,
            anywhere,
            anywhere,
            inside,
            anywhere,
            anywhere,
            inside,
            anywhere,
            inside,
            anywhere,
            anywhere,
        ],
        out_specs=[inside] * 7 + [anywhere],
        scratch_shapes=sums
        + [
            pltpu.VMEM((2, nz, 4, rows, width_attn), bf16),
            pltpu.VMEM((4, nz, 4, rows, width_attn), bf16),
            pltpu.VMEM((2, 2, ndp, rows, width), bf16),
            pltpu.VMEM((2, 2, count, width), bf16),
            pltpu.VMEM((ndp, 3 * rows, width_attn), bf16),
            pltpu.VMEM((nf, ndp // nf, rows, width_attn), bf16),
            pltpu.VMEM((3, count, width_attn), bf16),
            pltpu.VMEM((count, D), bf16),
            pltpu.VMEM((count, D), bf16),
            pltpu.VMEM((D, count), bf16),
            pltpu.VMEM((D, count), bf16),
            pltpu.VMEM((nf, count, width_attn), bf16),
            pltpu.VMEM((FF // width, 1, width), f32),
            pltpu.VMEM((nf, 1, width_attn), f32),
            pltpu.VMEM((nf, 1, width_attn), f32),
            pltpu.VMEM((4 + vec_copies, 16, D), f32),
            dma((6,)),
            dma((2, 4)),
            dma((2,)),
            dma((4,)),
            dma((4, nz, side - 1, side)),
            dma((4, nz, side - 1, side)),
            dma((4, nz, side - 1)),
            dma((4, nz, side - 1)),
            dma((3, nz - 1)),
            dma((3, nz - 1)),
            dma((vec_copies,)),
            dma((vec_copies,)),
            dma,
            dma((4,)),
            dma((ndp,)),
            dma((ndp, side - 1)),
            dma((ndp, side, side - 1)),
            dma((nf, ndp)),
            dma((nz - 1, nf)),
            dma((nz - 1, nf)),
        ],
        compiler_params=pltpu.CompilerParams(
            collective_id=3, has_side_effects=True, vmem_limit_bytes=63 * 1024 * 1024
        ),
    )(
        d_second, low, scaled, inverse, vectors, active, slope, up_all, down_all,
        tokens, segments[None, :], blocks, mixture, totals, attn_all, tail_sums, attn_mom, ffn_mom,
    )


def on_device(
    tokens,
    segments,
    cotangent,
    attn_w,
    ffn_w,
    vectors,
    attn_mom,
    ffn_mom,
    vec_mom,
    attn_ema,
    ffn_ema,
    vec_ema,
):
    ndp, nf = lax.axis_size("dp"), lax.axis_size("fsdp")
    share = vectors.shape[1]
    (
        attn_all, up_all, down_all, blocks, active, slope, vec_full, mixture, totals, scaled, inverse, low,
        layer_out, d_second, tail_sums,
    ) = forward(ndp, nf, tokens, segments, cotangent, attn_w, ffn_w, vectors)
    input_grad, up_grad, down_grad, attn_grad, vec_sum, attn_piece, _, ffn_whole = backward(
        ndp, nf, d_second, low, scaled, inverse, vec_full, active, slope, up_all, down_all,
        tokens, segments, blocks, mixture, totals, attn_all, tail_sums, attn_mom, ffn_mom,
    )
    mine = (lax.axis_index("dp") * nf + lax.axis_index("fsdp")) * share
    vec_grad = lax.dynamic_slice(vec_sum, (0, mine), (12, share))
    attn_ortho, ffn_ortho = orthogonalize(ndp, nf, attn_piece, ffn_whole)
    total_tokens = tokens.shape[0] * ndp * nf
    updated = update_all(
        vector_step / math.sqrt(total_tokens),
        attn_w,
        ffn_w,
        vectors,
        attn_mom,
        ffn_mom,
        vec_mom,
        attn_ema,
        ffn_ema,
        vec_ema,
        attn_grad,
        up_grad,
        down_grad,
        vec_grad,
        attn_ortho,
        ffn_ortho,
    )
    return (layer_out, input_grad, *updated, vec_grad[2])


def solution(mesh):
    in_specs = (
        P(("dp", "fsdp"), None),
        P(("dp", "fsdp")),
        P(("dp", "fsdp"), None),
        P(None, "dp", "fsdp"),
        P(None, "dp", "fsdp"),
        P(None, ("dp", "fsdp")),
        P(None, "dp", "fsdp"),
        P(None, "dp", "fsdp"),
        P(None, ("dp", "fsdp")),
        P(None, "dp", "fsdp"),
        P(None, "dp", "fsdp"),
        P(None, ("dp", "fsdp")),
    )
    out_specs = (
        P(("dp", "fsdp"), None),
        P(("dp", "fsdp"), None),
        P(None, "dp", "fsdp"),
        P(None, "dp", "fsdp"),
        P(None, ("dp", "fsdp")),
        P(None, "dp", "fsdp"),
        P(None, "dp", "fsdp"),
        P(None, ("dp", "fsdp")),
        P(None, "dp", "fsdp"),
        P(None, "dp", "fsdp"),
        P(None, ("dp", "fsdp")),
        P(("dp", "fsdp")),
    )
    return jax.shard_map(
        on_device, mesh=mesh, in_specs=in_specs, out_specs=out_specs, check_vma=False
    )
```
